32 devices in a mesh: seq: 4 (over y, core), fsdp: 2 (over x), batch: 4 (over z).
Axes of the slice: x: 2, y: 2, z: 4, core: 2. Of those that a mesh axis runs over, the one named last changes fastest.
Arguments:
- hidden: bfloat16 [8, 512, 2048], P(('fsdp', 'batch'), 'seq'), may hold values from -6 to 6
- in_weight: bfloat16 [2048, 2208], P(('fsdp', 'batch')), may hold values from -0.125 to 0.125
- read_starts: int32 [8, 4], P(('fsdp', 'batch')), may hold values from 1 to 511
- conv_weight: float32 [2, 4, 2176], replicated, may hold values from -3 to 3
- conv_bias: float32 [2, 2176], replicated, may hold values from -0.5 to 0.5
- dt_bias: float32 [2, 32], replicated, may hold values from -4.5 to -2.5
- decay: float32 [2, 32], replicated, may hold values from 9.765625e-05 to 0.7
- skip: float32 [2, 32], replicated, may hold values from 0.5 to 1.5
- norm_gain: float32 [2, 2048], replicated, may hold values from 0.5 to 1.5
Outputs:
- mixed: bfloat16 [8, 512, 2048], P(('fsdp', 'batch'), 'seq')
The draws below stay inside these ranges and needn't reach their ends.
All inputs are finite; a program needn't handle non-finite values.
Results may differ from the reference program's by a relative error of at most 0.0051.
Values may be sent and summed in bfloat16 or wider, within the bound.
No kernel may reach another device: no remote copies, remote signals or barrier semaphores. Data moves between devices by JAX's collectives and lax.ppermute only.
A program may use at most 128 MiB of HBM per device.

```python
import math
import jax
import jax.numpy as jnp
from jax import lax

D = 2048
HEADS = 32
HEAD_DIM = 64
STATE = 64
KERNEL = 4
BLOCK = 128
BOUNDS = 4
INNER = 2048
CONV_CH = 2176
PROJ = 2208
LENGTH = 512
BATCH = 8


def set_ends(entries, stream_key, smallest, high):
    shape = entries.shape
    spot = [jax.random.randint(jax.random.fold_in(stream_key, axis), (), 0, shape[axis]) for axis in range(len(shape))]
    entries = entries.at[tuple(spot)].set(smallest)
    longest = shape.index(max(shape))
    spot[longest] = (spot[longest] + 1) % shape[longest]
    return entries.at[tuple(spot)].set(high)


def shard_levels(rng, extent, shards, low, largest):
    def one(axis_at, blocks):
        draws = jax.random.uniform(jax.random.fold_in(jax.random.fold_in(rng, 6), axis_at), (blocks,), jnp.float32, low / len(shards), largest / len(shards))
        return jnp.repeat(jnp.exp(draws), extent[axis_at] // blocks).reshape((-1,) + (1,) * (len(extent) - axis_at - 1))

    gain = one(*shards[0])
    for cut in shards[1:]:
        gain = gain * one(*cut)
    return gain


def bell_draw(key, dims, deviation, reach, cuts=(), held_as=jnp.bfloat16):
    level = shard_levels(key, dims, cuts, -0.22, 0.18) if cuts else 1.0
    array = jax.random.normal(key, dims, jnp.float32) * deviation * level
    return jnp.minimum(jnp.maximum(array, -reach), reach).astype(held_as)


def setup_inputs(seed: int = 0) -> dict:
    key_list = jax.random.split(jax.random.key(seed), 10)
    return {
        "hidden": bell_draw(key_list[0], (BATCH, LENGTH, D), 1.0, 6.0, ((0, 8), (1, 4))),
        "in_weight": bell_draw(key_list[1], (D, PROJ), D ** -0.5, 0.125, ((0, 8),)),
        "read_starts": set_ends(jax.random.randint(key_list[2], (BATCH, BOUNDS), 1, LENGTH), jax.random.fold_in(key_list[2], 1), 1, LENGTH - 1).astype(jnp.int32),
        "conv_weight": bell_draw(key_list[3], (2, KERNEL, CONV_CH), KERNEL ** -0.5, 3.0, (), jnp.float32),
        "conv_bias": jnp.clip(jax.random.uniform(key_list[4], (2, CONV_CH), jnp.float32, -0.5, 0.5), -0.5, 0.5),
        "dt_bias": jnp.clip(jax.random.uniform(key_list[5], (2, HEADS), jnp.float32, -4.5, -2.5), -4.5, -2.5),
        "decay": jnp.clip(jnp.exp(jax.random.uniform(key_list[6], (2, HEADS), jnp.float32, math.log(9.765625145519152e-05), math.log(0.7))), 9.765625145519152e-05, 0.7),
        "skip": jnp.clip(jax.random.uniform(key_list[7], (2, HEADS), jnp.float32, 0.5, 1.5), 0.5, 1.5),
        "norm_gain": jnp.clip(1.0 + 0.1 * jax.random.normal(key_list[8], (2, INNER), jnp.float32), 0.5, 1.5),
    }


def conv_silu(padded, weight, bias):
    length = padded.shape[0] - weight.shape[0] + 1
    total = jnp.broadcast_to(bias[None, :], (length, bias.shape[0]))
    for tap in range(weight.shape[0]):
        total = total + weight[tap][None, :] * padded[tap:tap + length].astype(jnp.float32)
    return jax.nn.silu(total).astype(jnp.bfloat16)

def block_parts(x_part, b_part, c_part, step_size, log_rate, resets):
    length = x_part.shape[0]
    running = jnp.cumsum(log_rate, axis=0)
    resets_seen = jnp.cumsum(resets)
    scores = jnp.dot(c_part, b_part.T, preferred_element_type=jnp.float32)
    positions = jnp.arange(length)
    allowed = (positions[:, None] >= positions[None, :]) & (resets_seen[:, None] == resets_seen[None, :])
    log_gaps = jnp.minimum(running[:, None, :] - running[None, :, :], 0.0)
    weights = jnp.where(allowed[:, :, None], jnp.exp(log_gaps), 0.0) * scores[:, :, None] * step_size[None, :, :]
    weights = weights.astype(jnp.bfloat16)
    values = x_part.reshape(length, HEADS, HEAD_DIM)
    inner_part = jnp.einsum('tsh,shp->thp', weights.astype(jnp.float32), values.astype(jnp.float32), precision=lax.Precision.HIGHEST)
    last_same = resets_seen == resets_seen[-1]
    tail_weight = jnp.where(last_same[:, None], jnp.exp(running[-1][None, :] - running), 0.0) * step_size
    inputs = (tail_weight[:, :, None] * values.astype(jnp.float32)).astype(jnp.bfloat16)
    local_end = jnp.einsum('shp,sn->hpn', inputs.astype(jnp.float32), b_part.astype(jnp.float32), precision=lax.Precision.HIGHEST)
    lead_fade = jnp.where((resets_seen == 0)[:, None], jnp.exp(running), 0.0)
    block_fade = jnp.where(resets_seen[-1] == 0, jnp.exp(running[-1]), 0.0)
    return (inner_part, local_end, lead_fade, block_fade)

def direction(conv_out, step_cols, resets, bias_step, rates, direct, gains):
    length = conv_out.shape[0]
    blocks = length // BLOCK
    step_size = jax.nn.softplus(step_cols.astype(jnp.float32) + bias_step[None, :])
    log_rate = -step_size * rates[None, :]
    items = (conv_out[:, :INNER].reshape(blocks, BLOCK, INNER), conv_out[:, INNER:INNER + STATE].reshape(blocks, BLOCK, STATE), conv_out[:, INNER + STATE:].reshape(blocks, BLOCK, STATE), step_size.reshape(blocks, BLOCK, HEADS), log_rate.reshape(blocks, BLOCK, HEADS), resets.reshape(blocks, BLOCK))

    def one_block(state, item):
        x_part, b_part, c_part, step_here, rate_here, reset_here = item
        inner_part, local_end, lead_fade, block_fade = block_parts(x_part, b_part, c_part, step_here, rate_here, reset_here)
        rounded = lax.optimization_barrier(state.astype(jnp.bfloat16)).astype(jnp.float32)
        carried = jnp.einsum('tn,hpn->thp', c_part.astype(jnp.float32), rounded, precision=lax.Precision.HIGHEST)
        direct_part = direct[None, :, None] * x_part.reshape(BLOCK, HEADS, HEAD_DIM).astype(jnp.float32)
        output = inner_part + lead_fade[:, :, None] * carried + direct_part
        return (block_fade[:, None, None] * state + local_end, output)
    start_state = jnp.zeros((HEADS, HEAD_DIM, STATE), jnp.float32)
    _, outputs = lax.scan(one_block, start_state, items)
    result = outputs.reshape(length, HEADS, HEAD_DIM)
    scale = lax.rsqrt(lax.optimization_barrier(jnp.mean(result * result, axis=-1, keepdims=True)) + 1e-05)
    return (result * scale * gains.reshape(HEADS, HEAD_DIM)).reshape(length, INNER)

def reference(hidden, in_weight, read_starts, conv_weight, conv_bias, dt_bias, decay, skip, norm_gain):

    def one_sequence(item):
        tokens, marks = item
        projected = jnp.dot(tokens, in_weight, preferred_element_type=jnp.float32).astype(jnp.bfloat16)
        positions = jnp.arange(LENGTH, dtype=jnp.int32)
        starts_here = jnp.any(positions[:, None] == marks[None, :], axis=1).astype(jnp.float32)
        starts_next = jnp.any((positions + 1)[:, None] == marks[None, :], axis=1).astype(jnp.float32)
        xbc = projected[:, :CONV_CH]
        margin = KERNEL - 1
        zero_rows = jnp.zeros((margin, CONV_CH), jnp.bfloat16)
        forward_in = conv_silu(jnp.concatenate([zero_rows, xbc], axis=0), conv_weight[0], conv_bias[0])
        backward_in = conv_silu(jnp.flip(jnp.concatenate([xbc, zero_rows], axis=0), 0), conv_weight[1], conv_bias[1])
        step_cols = projected[:, CONV_CH:]
        forward_out = direction(forward_in, step_cols, starts_here, dt_bias[0], decay[0], skip[0], norm_gain[0])
        backward_out = direction(backward_in, jnp.flip(step_cols, 0), jnp.flip(starts_next, 0), dt_bias[1], decay[1], skip[1], norm_gain[1])
        return (forward_out + jnp.flip(backward_out, 0)).astype(jnp.bfloat16)
    return lax.map(one_sequence, (hidden, read_starts))
```

```python
import functools

import jax
import jax.numpy as jnp
from jax import lax
from jax.experimental import pallas as pl
from jax.experimental.pallas import tpu as pltpu
from jax.sharding import PartitionSpec as P

HEADS = 32
HEAD_DIM = 64
STATE = 64
KERNEL = 4
BLOCK = 128
INNER = 2048
CONV_CH = 2176


def prefix(value, axis, join, neutral, backward):
    count, mine = (lax.axis_size(axis), lax.axis_index(axis))
    pieces = jax.tree.map(lambda part: lax.all_gather(part, axis), value)
    if backward:
        pieces = jax.tree.map(lambda part: part[::-1], pieces)
        mine = count - 1 - mine
    running = jax.tree.map(
        lambda part, zero: jnp.full_like(part, 0) + jnp.asarray(zero, part.dtype), value, neutral
    )

    def turn(position, running):
        longer = join(running, jax.tree.map(lambda part: part[position], pieces))
        return jax.tree.map(lambda new, old: jnp.where(position < mine, new, old), longer, running)

    return lax.fori_loop(0, count - 1, turn, running)


def extended_2(value, sides, width):
    for axis, dim in sides:
        size, length = (lax.axis_size(axis), value.shape[dim])
        up = [(i, (i + 1) % size) for i in range(size - 1)]
        down = [(j, i) for i, j in up]
        last = lax.slice_in_dim(value, length - width, length, axis=dim)
        initial = lax.slice_in_dim(value, 0, width, axis=dim)
        before = lax.ppermute(last, axis, up)
        after = lax.ppermute(initial, axis, down)
        value = jnp.concatenate([before, value, after], axis=dim)
    return value


def conv_silu(padded, weight, bias):
    length = padded.shape[0] - weight.shape[0] + 1
    total = jnp.broadcast_to(bias[None, :], (length, bias.shape[0]))
    for tap in range(weight.shape[0]):
        total = total + weight[tap][None, :] * padded[tap : tap + length].astype(jnp.float32)
    return jax.nn.silu(total).astype(jnp.bfloat16)


def block_parts(x_part, b_part, c_part, step_size, log_rate, resets):
    length = x_part.shape[0]
    running = jnp.cumsum(log_rate, axis=0)
    running_heads = running.T
    step_heads = step_size.T
    resets_seen = jnp.cumsum(resets)
    scores = jnp.dot(c_part, b_part.T, preferred_element_type=jnp.float32)
    positions = jnp.arange(length)
    allowed = (positions[:, None] >= positions[None, :]) & (
        resets_seen[:, None] == resets_seen[None, :]
    )
    log_gaps = jnp.minimum(running_heads[:, :, None] - running_heads[:, None, :], 0.0)
    weights = (
        jnp.where(allowed[None, :, :], jnp.exp(log_gaps), 0.0)
        * scores[None, :, :]
        * step_heads[:, None, :]
    )
    weights = weights.astype(jnp.bfloat16)
    values = x_part.reshape(length, HEADS, HEAD_DIM)
    inner_part = jnp.einsum("hts,shp->thp", weights, values, preferred_element_type=jnp.float32)
    last_same = resets_seen == resets_seen[-1]
    tail_weight = (
        jnp.where(last_same[:, None], jnp.exp(running[-1][None, :] - running), 0.0) * step_size
    )
    inputs = (tail_weight[:, :, None] * values.astype(jnp.float32)).astype(jnp.bfloat16)
    local_end = jnp.einsum("shp,sn->hpn", inputs, b_part, preferred_element_type=jnp.float32)
    lead_fade = jnp.where((resets_seen == 0)[:, None], jnp.exp(running), 0.0)
    block_fade = jnp.where(resets_seen[-1] == 0, jnp.exp(running[-1]), 0.0)
    return (inner_part, local_end, lead_fade, block_fade)


def chain_combine(earlier, later):
    return (earlier[0] * later[0], later[0][:, None] * earlier[1] + later[1])


def direction(conv_out, step_cols, resets, bias_step, rates, direct, gains, backward):
    length = conv_out.shape[0]
    blocks = length // BLOCK
    x_part = conv_out[:, :INNER]
    b_part = conv_out[:, INNER : INNER + STATE]
    c_part = conv_out[:, INNER + STATE :]
    step_size = jax.nn.softplus(step_cols.astype(jnp.float32) + bias_step[None, :])
    log_rate = -step_size * rates[None, :]
    inner_part, local_end, lead_fade, block_fade = jax.vmap(block_parts)(
        x_part.reshape(blocks, BLOCK, INNER),
        b_part.reshape(blocks, BLOCK, STATE),
        c_part.reshape(blocks, BLOCK, STATE),
        step_size.reshape(blocks, BLOCK, HEADS),
        log_rate.reshape(blocks, BLOCK, HEADS),
        resets.reshape(blocks, BLOCK),
    )
    carried_state = jnp.zeros((HEADS, HEAD_DIM, STATE), jnp.float32)
    carried_fade = jnp.ones((HEADS,), jnp.float32)
    entering = carried_state
    fades_before = carried_fade
    carried_state = block_fade[0][:, None, None] * carried_state + local_end[0]
    carried_fade = block_fade[0] * carried_fade
    summary = (carried_fade, carried_state.reshape(HEADS, HEAD_DIM * STATE))
    identity = (jnp.ones((HEADS,), jnp.float32), jnp.zeros((HEADS, HEAD_DIM * STATE), jnp.float32))
    if backward:
        incoming = prefix(summary, "seq", chain_combine, identity, True)
    else:
        incoming = prefix(summary, "seq", chain_combine, identity, False)
    incoming_state = incoming[1].reshape(HEADS, HEAD_DIM, STATE)
    states = jnp.stack([fades_before[:, None, None] * incoming_state + entering])
    rounded = states.astype(jnp.bfloat16)
    carried = jnp.einsum(
        "btn,bhpn->bthp",
        c_part.reshape(blocks, BLOCK, STATE),
        rounded,
        preferred_element_type=jnp.float32,
    )
    direct_part = direct[None, None, :, None] * x_part.reshape(
        blocks, BLOCK, HEADS, HEAD_DIM
    ).astype(jnp.float32)
    result = (inner_part + lead_fade[..., None] * carried + direct_part).reshape(
        length, HEADS, HEAD_DIM
    )
    scale = lax.rsqrt(jnp.mean(result * result, axis=-1, keepdims=True) + 1e-05)
    return (result * scale * gains.reshape(HEADS, HEAD_DIM)).reshape(length, INNER)


def project(rows_in, in_weight):
    total = jnp.dot(
        rows_in,
        lax.all_gather(in_weight, ("fsdp", "batch"), axis=0, tiled=True),
        preferred_element_type=jnp.float32,
    )
    return total.astype(jnp.bfloat16)


def on_sections(
    hidden, in_weight, read_starts, conv_weight, conv_bias, dt_bias, decay, skip, norm_gain
):
    tokens = hidden[0]
    length = tokens.shape[0]
    margin = KERNEL - 1
    projected = project(tokens, in_weight)
    extended = extended_2(projected[:, :CONV_CH], (("seq", 0),), margin)
    forward_in = conv_silu(extended[: length + margin], conv_weight[0], conv_bias[0])
    backward_in = conv_silu(jnp.flip(extended[margin:], 0), conv_weight[1], conv_bias[1])
    step_cols = projected[:, CONV_CH:]
    positions = lax.axis_index("seq") * length + jnp.arange(length, dtype=jnp.int32)
    marks = read_starts[0]
    starts_here = jnp.any(positions[:, None] == marks[None, :], axis=1).astype(jnp.float32)
    starts_next = jnp.any((positions + 1)[:, None] == marks[None, :], axis=1).astype(jnp.float32)
    forward_out = direction(
        forward_in, step_cols, starts_here, dt_bias[0], decay[0], skip[0], norm_gain[0], False
    )
    backward_out = direction(
        backward_in,
        jnp.flip(step_cols, 0),
        jnp.flip(starts_next, 0),
        dt_bias[1],
        decay[1],
        skip[1],
        norm_gain[1],
        True,
    )
    mixed = forward_out + jnp.flip(backward_out, 0)
    return mixed.astype(jnp.bfloat16)[None]


LANES = 128
SIDE = 256
EDGE = 8


def split_two(value):
    high = value.astype(jnp.bfloat16)
    low = (value - high.astype(jnp.float32)).astype(jnp.bfloat16)
    return high, low


def mixer_kernel(
    heads,
    shards,
    ids,
    marks,
    *refs,
):
    pieces, refs = refs[:4], refs[4:]
    weights, refs = refs[:shards], refs[shards:]
    sides, refs = refs[:4], refs[4:]
    conv_w, conv_b, step_bias, rates, direct, gains = refs[:6]
    outs, refs = refs[6:10], refs[10:]
    rows_in, w_own, w_side, padded, xs, cs, bs, steps, cums, tails, leads, fades, turned, total, state, sems = refs
    seq, fsdp, batch = ids[0], ids[1], ids[2]
    ring = shards // 2
    depth = w_own.shape[0] // shards
    part = depth // 4
    columns = heads * HEAD_DIM
    chunks = columns // LANES
    length = rows_in.shape[0]
    blocks = length // BLOCK

    copies = []
    for mask in range(4):
        place = pl.multiple_of((seq ^ mask) * BLOCK, BLOCK)
        copies.append((pieces[mask], rows_in.at[pl.ds(place, BLOCK)]))
    for side in range(2):
        for turn in range(ring):
            shard = (fsdp ^ side) * ring + lax.rem(batch + ring - turn, ring)
            place = pl.multiple_of(shard * depth, depth)
            at = side * ring + turn
            copies.append((weights[at], w_own.at[pl.ds(place, depth)]))
            for mask in range(4):
                place_side = pl.multiple_of(shard * depth + (seq ^ mask) * part, part)
                copies.append((sides[mask].at[at], w_side.at[pl.ds(place_side, part)]))
    copies = [pltpu.make_async_copy(a, b, sems.at[i]) for i, (a, b) in enumerate(copies)]
    for copy in copies:
        copy.start()
    lane = lax.broadcasted_iota(jnp.int32, (BLOCK, LANES), 1)
    row = lax.broadcasted_iota(jnp.int32, (BLOCK, LANES), 0)
    edge = jnp.zeros((EDGE, LANES), jnp.float32)
    for c in range(chunks + 1):
        padded[c, 0:EDGE, :] = edge
        padded[c, EDGE + length :, :] = edge
    total[...] = jnp.zeros_like(total)
    state[...] = jnp.zeros_like(state)
    for copy in copies:
        copy.wait()

    side_out = jnp.dot(rows_in[...], w_side[...], preferred_element_type=jnp.float32)
    side_out = side_out.astype(jnp.bfloat16).astype(jnp.float32)
    padded[chunks, EDGE : EDGE + length, :] = side_out[:, :LANES]
    steps[...] = side_out[:, LANES:]
    for n in range(columns // SIDE):
        part_out = jnp.dot(
            rows_in[...], w_own[:, n * SIDE : (n + 1) * SIDE], preferred_element_type=jnp.float32
        )
        part_out = part_out.astype(jnp.bfloat16).astype(jnp.float32)
        for k in range(SIDE // LANES):
            padded[n * (SIDE // LANES) + k, EDGE : EDGE + length, :] = part_out[
                :, k * LANES : (k + 1) * LANES
            ]

    own_at = pl.multiple_of(seq * columns, columns)
    short = 64

    def conv_rows(i, carry):
        at = pl.multiple_of(i * short, short)
        for c in range(chunks + 1):
            taps = [padded[c, pl.ds(at + EDGE - 3 + k, short), :] for k in range(7)]
            if c < chunks:
                lanes = pl.ds(pl.multiple_of(own_at + c * LANES, LANES), LANES)
            else:
                lanes = pl.ds(INNER, LANES)
            for d in range(2):
                acc = conv_b[d : d + 1, lanes] + conv_w[d, 0:1, lanes] * taps[0 if d == 0 else 6]
                for k in range(1, KERNEL):
                    acc = acc + conv_w[d, k : k + 1, lanes] * taps[k if d == 0 else 6 - k]
                half = 0.5 * acc
                value = half + half * jnp.tanh(half)
                if c < chunks:
                    xs[d, pl.ds(at, short), c * LANES : (c + 1) * LANES] = value.astype(jnp.bfloat16)
                else:
                    upper = lax.broadcasted_iota(jnp.int32, (short, LANES), 1) >= STATE
                    cs[d, pl.ds(at, short), :] = jnp.where(upper, value, 0.0).astype(jnp.bfloat16)
                    bs[d, pl.ds(at, short), :] = jnp.where(
                        upper, pltpu.roll(value, STATE, 1), 0.0
                    ).astype(jnp.bfloat16)
        return carry

    lax.fori_loop(0, length // short, conv_rows, 0)

    backward_lane = ((lane >= heads) & (lane < 2 * heads)) | (lane == 2 * heads + 1)
    head_lane = lane < 2 * heads
    lower = jnp.where(row >= lane, 1.0, 0.0)
    upper_sum = jnp.where(row <= lane, 1.0, 0.0)

    def decays(b, carry):
        at = pl.multiple_of(b * BLOCK, BLOCK)
        columns_in = steps[pl.ds(at, BLOCK), :]
        mine = pltpu.roll(columns_in, lax.rem(LANES - seq * heads, LANES), 1)
        both = jnp.where(lane < heads, mine, pltpu.roll(mine, heads, 1)) + step_bias[...]
        step = jnp.maximum(both, 0.0) + jnp.log1p(jnp.exp(-jnp.abs(both)))
        rate = -step * rates[...]
        position = row + b * BLOCK
        here = position == marks[0]
        after = position + 1 == marks[0]
        for m in range(1, 4):
            here = here | (position == marks[m])
            after = after | (position + 1 == marks[m])
        here = jnp.where(here, 1.0, 0.0)
        after = jnp.where(after, 1.0, 0.0)
        rate = jnp.where(
            head_lane, rate, jnp.where(lane == 2 * heads, here, jnp.where(lane == 2 * heads + 1, after, 0.0))
        )
        ahead = jnp.dot(lower, rate, precision=lax.Precision.HIGHEST, preferred_element_type=jnp.float32)
        behind = jnp.dot(upper_sum, rate, precision=lax.Precision.HIGHEST, preferred_element_type=jnp.float32)
        cum = jnp.where(backward_lane, behind, ahead)
        seen = jnp.where(
            backward_lane,
            jnp.broadcast_to(cum[:, 2 * heads + 1 : 2 * heads + 2], (BLOCK, LANES)),
            jnp.broadcast_to(cum[:, 2 * heads : 2 * heads + 1], (BLOCK, LANES)),
        )
        last = jnp.where(backward_lane[:1], cum[:1], cum[BLOCK - 1 :])
        seen_last = jnp.where(backward_lane[:1], seen[:1], seen[BLOCK - 1 :])
        tail = jnp.where((seen == seen_last) & head_lane, jnp.exp(last - cum) * step, 0.0)
        lead = jnp.where((seen == 0.0) & head_lane, jnp.exp(cum), 0.0)
        fade = jnp.where((seen_last == 0.0) & head_lane[:1], jnp.exp(last), 0.0)
        cums[b] = cum
        tails[b] = tail
        leads[b] = lead
        fades[b] = jnp.broadcast_to(fade, (8, LANES))
        turned[b] = jnp.where(head_lane, jnp.log(step) - cum, cum).T
        return carry

    lax.fori_loop(0, blocks, decays, 0)

    own_lanes = pl.ds(own_at, columns)
    spread_row = lax.broadcasted_iota(jnp.int32, (LANES, columns), 0)
    spread_head = lax.broadcasted_iota(jnp.int32, (LANES, columns), 1) // HEAD_DIM
    spreads = [
        jnp.where(spread_row == spread_head + d * heads, 1.0, 0.0).astype(jnp.bfloat16) for d in range(2)
    ]
    same = jnp.where(row // HEAD_DIM == lane // HEAD_DIM, 1.0 / HEAD_DIM, 0.0).astype(jnp.bfloat16)
    left = lane < HEAD_DIM

    def widen(value, d):
        high, low = split_two(value)
        return jnp.dot(high, spreads[d], preferred_element_type=jnp.float32) + jnp.dot(
            low, spreads[d], preferred_element_type=jnp.float32
        )

    def scan_step(i, carry):
        for d in range(2):
            b = i if d == 0 else blocks - 1 - i
            at = pl.ds(pl.multiple_of(b * BLOCK, BLOCK), BLOCK)
            c_part = cs[d, at, :]
            b_part = bs[d, at, :]
            scores = lax.dot_general(
                c_part, b_part, (((1,), (1,)), ((), ())), preferred_element_type=jnp.float32
            )
            cum = cums[b]
            seen_at = 2 * heads + d
            ordered = (row >= lane) if d == 0 else (row <= lane)
            allowed = ordered & (cum[:, seen_at : seen_at + 1] == turned[b, seen_at : seen_at + 1, :])
            barred = jnp.where(allowed, 0.0, -1e30)
            before = state[d]
            carried = jnp.dot(c_part, before.astype(jnp.bfloat16), preferred_element_type=jnp.float32)
            lead = widen(leads[b], d)
            tail = widen(tails[b], d)
            fade = widen(fades[b], d)[:1]
            x_all = xs[d, at, :]
            x_wide = x_all.astype(jnp.float32)
            inputs = (tail * x_wide).astype(jnp.bfloat16)
            local_end = lax.dot_general(
                b_part, inputs, (((0,), (0,)), ((), ())), preferred_element_type=jnp.float32
            )
            state[d] = fade * before + local_end
            for p in range(chunks):
                pair = []
                for h in (2 * p + d * heads, 2 * p + 1 + d * heads):
                    gap = cum[:, h : h + 1] + (turned[b, h : h + 1, :] + barred)
                    pair.append((jnp.exp(gap) * scores).astype(jnp.bfloat16))
                lanes = slice(p * LANES, (p + 1) * LANES)
                x_pair = x_wide[:, lanes]
                x_two = jnp.concatenate(
                    [
                        jnp.where(left, x_pair, 0.0).astype(jnp.bfloat16),
                        jnp.where(left, 0.0, x_pair).astype(jnp.bfloat16),
                    ],
                    axis=0,
                )
                inner = jnp.dot(jnp.concatenate(pair, axis=1), x_two, preferred_element_type=jnp.float32)
                at_lanes = pl.ds(pl.multiple_of(own_at + p * LANES, LANES), LANES)
                y = inner + lead[:, lanes] * carried[:, lanes] + direct[d : d + 1, at_lanes] * x_pair
                high, low = split_two(y * y)
                mean = jnp.dot(high, same, preferred_element_type=jnp.float32) + jnp.dot(
                    low, same, preferred_element_type=jnp.float32
                )
                scale = lax.rsqrt(mean + 1e-05)
                total[at, lanes] += y * scale * gains[d : d + 1, at_lanes]
        return carry

    lax.fori_loop(0, blocks, scan_step, 0)
    for mask in range(4):
        at = pl.ds(pl.multiple_of((seq ^ mask) * BLOCK, BLOCK), BLOCK)
        outs[mask][...] = total[at, :].astype(jnp.bfloat16)


def ring_up(value, axis):
    count = lax.axis_size(axis)
    return lax.ppermute(value, axis, [(i, (i + 1) % count) for i in range(count)])


def swap(value, axis, mask):
    count = lax.axis_size(axis)
    return lax.ppermute(value, axis, [(i, i ^ mask) for i in range(count)])


def gather_rows(piece):
    mine = [piece]
    for _ in range(lax.axis_size("batch") - 1):
        mine.append(ring_up(mine[-1], "batch"))
    return mine + [swap(part, "fsdp", 1) for part in mine]


def on_heads(
    hidden, in_weight, read_starts, conv_weight, conv_bias, dt_bias, decay, skip, norm_gain
):
    tokens = hidden[0]
    section = tokens.shape[0]
    count = lax.axis_size("seq")
    seq = lax.axis_index("seq")
    heads = HEADS // count
    columns = heads * HEAD_DIM
    depth = in_weight.shape[0]
    part = depth // count
    shards = lax.axis_size("fsdp") * lax.axis_size("batch")
    side = lax.dynamic_slice(in_weight, (seq * part, INNER), (part, in_weight.shape[1] - INNER))
    side = jnp.pad(side, ((0, 0), (0, SIDE - side.shape[1])))
    own = lax.dynamic_slice(in_weight, (0, seq * columns), (depth, columns))
    side_mine = jnp.stack(gather_rows(side))
    across = swap(tokens, "seq", 2)
    pieces = [tokens, swap(tokens, "seq", 1), across, swap(across, "seq", 1)]
    side_across = swap(side_mine, "seq", 2)
    sides = [side_mine, swap(side_mine, "seq", 1), side_across, swap(side_across, "seq", 1)]
    weights = gather_rows(own)

    def for_lanes(value):
        mine = lax.dynamic_slice(value, (0, seq * heads), (2, heads)).reshape(1, 2 * heads)
        return jnp.pad(mine, ((0, 0), (0, LANES - 2 * heads)))

    length = section * count
    blocks = length // BLOCK
    ids = jnp.stack([seq, lax.axis_index("fsdp"), lax.axis_index("batch")]).astype(jnp.int32)
    in_smem = pl.BlockSpec(memory_space=pltpu.SMEM)
    in_vmem = pl.BlockSpec(memory_space=pltpu.VMEM)
    anywhere = pl.BlockSpec(memory_space=pl.ANY)
    chunks = columns // LANES
    results = pl.pallas_call(
        functools.partial(mixer_kernel, heads, shards),
        out_shape=[jax.ShapeDtypeStruct((section, columns), jnp.bfloat16)] * count,
        in_specs=[in_smem] * 2 + [anywhere] * (count + shards + count) + [in_vmem] * 6,
        out_specs=[in_vmem] * count,
        scratch_shapes=[
            pltpu.VMEM((length, tokens.shape[1]), jnp.bfloat16),
            pltpu.VMEM((depth * shards, columns), jnp.bfloat16),
            pltpu.VMEM((depth * shards, SIDE), jnp.bfloat16),
            pltpu.VMEM((chunks + 1, length + 2 * EDGE, LANES), jnp.float32),
            pltpu.VMEM((2, length, columns), jnp.bfloat16),
            pltpu.VMEM((2, length, LANES), jnp.bfloat16),
            pltpu.VMEM((2, length, LANES), jnp.bfloat16),
            pltpu.VMEM((length, LANES), jnp.float32),
            pltpu.VMEM((blocks, BLOCK, LANES), jnp.float32),
            pltpu.VMEM((blocks, BLOCK, LANES), jnp.float32),
            pltpu.VMEM((blocks, BLOCK, LANES), jnp.float32),
            pltpu.VMEM((blocks, 8, LANES), jnp.float32),
            pltpu.VMEM((blocks, BLOCK, LANES), jnp.float32),
            pltpu.VMEM((length, columns), jnp.float32),
            pltpu.VMEM((2, LANES, columns), jnp.float32),
            pltpu.SemaphoreType.DMA((count + shards + count * shards,)),
        ],
        compiler_params=pltpu.CompilerParams(vmem_limit_bytes=40 * 1024 * 1024),
    )(
        ids,
        read_starts[0],
        *pieces,
        *weights,
        *sides,
        conv_weight,
        conv_bias,
        for_lanes(dt_bias),
        for_lanes(decay),
        jnp.repeat(skip, HEAD_DIM, axis=1),
        norm_gain,
    )
    received = [results[0]] + [swap(results[mask], "seq", mask) for mask in range(1, count)]
    mixed = jnp.zeros((section, INNER), jnp.bfloat16)
    for mask in range(count):
        mixed = lax.dynamic_update_slice(mixed, received[mask], (0, (seq ^ mask) * columns))
    return mixed[None]


def solution(mesh):
    in_specs = (
        P(("fsdp", "batch"), "seq", None),
        P(("fsdp", "batch"), None),
        P(("fsdp", "batch"), None),
        P(),
        P(),
        P(),
        P(),
        P(),
        P(),
    )
    out_specs = P(("fsdp", "batch"), "seq", None)
    by_heads = mesh.shape["seq"] == 4 and mesh.shape["fsdp"] == 2

    def mixer(hidden, *rest):
        whole = by_heads and hidden.shape[1] == mesh.shape["seq"] * BLOCK
        return jax.shard_map(
            on_heads if whole else on_sections,
            mesh=mesh,
            in_specs=in_specs,
            out_specs=out_specs,
            check_vma=False,
        )(hidden, *rest)

    return mixer
```

```python
import functools

import jax
import jax.numpy as jnp
from jax import lax
from jax.experimental import pallas as pl
from jax.experimental.pallas import tpu as pltpu
from jax.sharding import PartitionSpec as P

HEADS = 32
HEAD_DIM = 64
STATE = 64
KERNEL = 4
BLOCK = 128
INNER = 2048
CONV_CH = 2176


def prefix(value, axis, join, neutral, backward):
    count, mine = (lax.axis_size(axis), lax.axis_index(axis))
    pieces = jax.tree.map(lambda part: lax.all_gather(part, axis), value)
    if backward:
        pieces = jax.tree.map(lambda part: part[::-1], pieces)
        mine = count - 1 - mine
    running = jax.tree.map(
        lambda part, zero: jnp.full_like(part, 0) + jnp.asarray(zero, part.dtype), value, neutral
    )

    def turn(position, running):
        longer = join(running, jax.tree.map(lambda part: part[position], pieces))
        return jax.tree.map(lambda new, old: jnp.where(position < mine, new, old), longer, running)

    return lax.fori_loop(0, count - 1, turn, running)


def extended_2(value, sides, width):
    for axis, dim in sides:
        size, length = (lax.axis_size(axis), value.shape[dim])
        up = [(i, (i + 1) % size) for i in range(size - 1)]
        down = [(j, i) for i, j in up]
        last = lax.slice_in_dim(value, length - width, length, axis=dim)
        initial = lax.slice_in_dim(value, 0, width, axis=dim)
        before = lax.ppermute(last, axis, up)
        after = lax.ppermute(initial, axis, down)
        value = jnp.concatenate([before, value, after], axis=dim)
    return value


def conv_silu(padded, weight, bias):
    length = padded.shape[0] - weight.shape[0] + 1
    total = jnp.broadcast_to(bias[None, :], (length, bias.shape[0]))
    for tap in range(weight.shape[0]):
        total = total + weight[tap][None, :] * padded[tap : tap + length].astype(jnp.float32)
    return jax.nn.silu(total).astype(jnp.bfloat16)


def block_parts(x_part, b_part, c_part, step_size, log_rate, resets):
    length = x_part.shape[0]
    running = jnp.cumsum(log_rate, axis=0)
    running_heads = running.T
    step_heads = step_size.T
    resets_seen = jnp.cumsum(resets)
    scores = jnp.dot(c_part, b_part.T, preferred_element_type=jnp.float32)
    positions = jnp.arange(length)
    allowed = (positions[:, None] >= positions[None, :]) & (
        resets_seen[:, None] == resets_seen[None, :]
    )
    log_gaps = jnp.minimum(running_heads[:, :, None] - running_heads[:, None, :], 0.0)
    weights = (
        jnp.where(allowed[None, :, :], jnp.exp(log_gaps), 0.0)
        * scores[None, :, :]
        * step_heads[:, None, :]
    )
    weights = weights.astype(jnp.bfloat16)
    values = x_part.reshape(length, HEADS, HEAD_DIM)
    inner_part = jnp.einsum("hts,shp->thp", weights, values, preferred_element_type=jnp.float32)
    last_same = resets_seen == resets_seen[-1]
    tail_weight = (
        jnp.where(last_same[:, None], jnp.exp(running[-1][None, :] - running), 0.0) * step_size
    )
    inputs = (tail_weight[:, :, None] * values.astype(jnp.float32)).astype(jnp.bfloat16)
    local_end = jnp.einsum("shp,sn->hpn", inputs, b_part, preferred_element_type=jnp.float32)
    lead_fade = jnp.where((resets_seen == 0)[:, None], jnp.exp(running), 0.0)
    block_fade = jnp.where(resets_seen[-1] == 0, jnp.exp(running[-1]), 0.0)
    return (inner_part, local_end, lead_fade, block_fade)


def chain_combine(earlier, later):
    return (earlier[0] * later[0], later[0][:, None] * earlier[1] + later[1])


def direction(conv_out, step_cols, resets, bias_step, rates, direct, gains, backward):
    length = conv_out.shape[0]
    blocks = length // BLOCK
    x_part = conv_out[:, :INNER]
    b_part = conv_out[:, INNER : INNER + STATE]
    c_part = conv_out[:, INNER + STATE :]
    step_size = jax.nn.softplus(step_cols.astype(jnp.float32) + bias_step[None, :])
    log_rate = -step_size * rates[None, :]
    inner_part, local_end, lead_fade, block_fade = jax.vmap(block_parts)(
        x_part.reshape(blocks, BLOCK, INNER),
        b_part.reshape(blocks, BLOCK, STATE),
        c_part.reshape(blocks, BLOCK, STATE),
        step_size.reshape(blocks, BLOCK, HEADS),
        log_rate.reshape(blocks, BLOCK, HEADS),
        resets.reshape(blocks, BLOCK),
    )
    carried_state = jnp.zeros((HEADS, HEAD_DIM, STATE), jnp.float32)
    carried_fade = jnp.ones((HEADS,), jnp.float32)
    entering = carried_state
    fades_before = carried_fade
    carried_state = block_fade[0][:, None, None] * carried_state + local_end[0]
    carried_fade = block_fade[0] * carried_fade
    summary = (carried_fade, carried_state.reshape(HEADS, HEAD_DIM * STATE))
    identity = (jnp.ones((HEADS,), jnp.float32), jnp.zeros((HEADS, HEAD_DIM * STATE), jnp.float32))
    if backward:
        incoming = prefix(summary, "seq", chain_combine, identity, True)
    else:
        incoming = prefix(summary, "seq", chain_combine, identity, False)
    incoming_state = incoming[1].reshape(HEADS, HEAD_DIM, STATE)
    states = jnp.stack([fades_before[:, None, None] * incoming_state + entering])
    rounded = states.astype(jnp.bfloat16)
    carried = jnp.einsum(
        "btn,bhpn->bthp",
        c_part.reshape(blocks, BLOCK, STATE),
        rounded,
        preferred_element_type=jnp.float32,
    )
    direct_part = direct[None, None, :, None] * x_part.reshape(
        blocks, BLOCK, HEADS, HEAD_DIM
    ).astype(jnp.float32)
    result = (inner_part + lead_fade[..., None] * carried + direct_part).reshape(
        length, HEADS, HEAD_DIM
    )
    scale = lax.rsqrt(jnp.mean(result * result, axis=-1, keepdims=True) + 1e-05)
    return (result * scale * gains.reshape(HEADS, HEAD_DIM)).reshape(length, INNER)


def project(rows_in, in_weight):
    total = jnp.dot(
        rows_in,
        lax.all_gather(in_weight, ("fsdp", "batch"), axis=0, tiled=True),
        preferred_element_type=jnp.float32,
    )
    return total.astype(jnp.bfloat16)


def on_sections(
    hidden, in_weight, read_starts, conv_weight, conv_bias, dt_bias, decay, skip, norm_gain
):
    tokens = hidden[0]
    length = tokens.shape[0]
    margin = KERNEL - 1
    projected = project(tokens, in_weight)
    extended = extended_2(projected[:, :CONV_CH], (("seq", 0),), margin)
    forward_in = conv_silu(extended[: length + margin], conv_weight[0], conv_bias[0])
    backward_in = conv_silu(jnp.flip(extended[margin:], 0), conv_weight[1], conv_bias[1])
    step_cols = projected[:, CONV_CH:]
    positions = lax.axis_index("seq") * length + jnp.arange(length, dtype=jnp.int32)
    marks = read_starts[0]
    starts_here = jnp.any(positions[:, None] == marks[None, :], axis=1).astype(jnp.float32)
    starts_next = jnp.any((positions + 1)[:, None] == marks[None, :], axis=1).astype(jnp.float32)
    forward_out = direction(
        forward_in, step_cols, starts_here, dt_bias[0], decay[0], skip[0], norm_gain[0], False
    )
    backward_out = direction(
        backward_in,
        jnp.flip(step_cols, 0),
        jnp.flip(starts_next, 0),
        dt_bias[1],
        decay[1],
        skip[1],
        norm_gain[1],
        True,
    )
    mixed = forward_out + jnp.flip(backward_out, 0)
    return mixed.astype(jnp.bfloat16)[None]


LANES = 128
SIDE = 256
EDGE = 8


def ring_order(count):
    return [i if i < count else 3 * count - 1 - i for i in range(2 * count)]


def split_three(value):
    parts = []
    for _ in range(3):
        parts.append(value.astype(jnp.bfloat16))
        value = value - parts[-1].astype(jnp.float32)
    return parts


def mixer_kernel(heads, shards, ids, marks, *refs):
    pieces, refs = refs[:4], refs[4:]
    weights, refs = refs[: shards - 1], refs[shards - 1 :]
    ends, refs = refs[:2], refs[2:]
    own_side, refs = refs[0], refs[1:]
    swapped, refs = refs[: shards // 2], refs[shards // 2 :]
    conv_w, conv_b, step_bias, rates, direct, gains = refs[:6]
    outs, refs = refs[6:10], refs[10:]
    rows_in, w_own, w_side, padded, xs, cs, bs, steps, refs = (*refs[:8], refs[8:])
    cums, tails, leads, fades, turned, barred, spread, columns_of, total, state = refs
    seq, core = ids[0], ids[1]
    columns = heads * HEAD_DIM
    depth = own_side.shape[1]
    side_rows = own_side.shape[0]
    half_side = side_rows // 2
    chunks = columns // LANES
    length = rows_in.shape[0]
    blocks = length // BLOCK
    cut = ends[0].shape[0]

    lane = lax.broadcasted_iota(jnp.int32, (BLOCK, LANES), 1)
    row = lax.broadcasted_iota(jnp.int32, (BLOCK, LANES), 0)

    for mask in range(4):
        rows_in[mask * BLOCK : (mask + 1) * BLOCK, :] = pieces[mask][...]
    mine = pl.ds(pl.multiple_of(core * half_side, 16), half_side)
    other = pl.ds(pl.multiple_of((1 - core) * half_side, 16), half_side)
    w_side[side_rows:, :] = jnp.zeros((SIDE - side_rows, w_side.shape[1]), jnp.bfloat16)
    for n in range(shards):
        at = pl.ds(pl.multiple_of(ids[2 + n] * depth, depth), depth)
        if n < shards - 1:
            w_own[:, at] = weights[n][:columns, :]
            if n:
                w_side[mine, at] = weights[n][columns:, :]
        else:
            w_own[:cut, at] = ends[0][...]
            w_own[cut:, at] = ends[1][: columns - cut, :]
            w_side[mine, at] = ends[1][columns - cut :, :]
        if n:
            w_side[other, at] = swapped[(n - 1) // 2][pl.ds((n - 1) % 2 * half_side, half_side), :]
        else:
            w_side[:side_rows, at] = own_side[...]
    edge = jnp.zeros((EDGE, LANES), jnp.float32)
    for c in range(chunks + 1):
        padded[c, 0:EDGE, :] = edge
        padded[c, EDGE + length :, :] = edge

    def project_in(weight):
        out = lax.dot_general(
            rows_in[...], weight, (((1,), (1,)), ((), ())), preferred_element_type=jnp.float32
        )
        return out.astype(jnp.bfloat16).astype(jnp.float32)

    def keep(c, value):
        for mask in range(4):
            place = pl.multiple_of((seq ^ mask) * BLOCK, BLOCK)
            padded[c, pl.ds(EDGE + place, BLOCK), :] = value[mask * BLOCK : (mask + 1) * BLOCK, :]

    side_out = project_in(w_side[...])
    keep(chunks, side_out[:, :LANES])
    for mask in range(4):
        place = pl.multiple_of((seq ^ mask) * BLOCK, BLOCK)
        steps[pl.ds(place, BLOCK), :] = side_out[mask * BLOCK : (mask + 1) * BLOCK, LANES:]
    for n in range(columns // SIDE):
        part_out = project_in(w_own[n * SIDE : (n + 1) * SIDE, :])
        for k in range(SIDE // LANES):
            keep(n * (SIDE // LANES) + k, part_out[:, k * LANES : (k + 1) * LANES])

    own_at = pl.multiple_of(seq * columns, columns)
    short = 64

    def conv_rows(i, carry):
        at = pl.multiple_of(i * short, short)
        for c in range(chunks + 1):
            taps = [padded[c, pl.ds(at + EDGE - 3 + k, short), :] for k in range(7)]
            if c < chunks:
                lanes = pl.ds(pl.multiple_of(own_at + c * LANES, LANES), LANES)
            else:
                lanes = pl.ds(INNER, LANES)
            for d in range(2):
                acc = conv_b[d : d + 1, lanes] + conv_w[d, 0:1, lanes] * taps[0 if d == 0 else 6]
                for k in range(1, KERNEL):
                    acc = acc + conv_w[d, k : k + 1, lanes] * taps[k if d == 0 else 6 - k]
                half = 0.5 * acc
                value = half + half * jnp.tanh(half)
                if c < chunks:
                    xs[d, pl.ds(at, short), c * LANES : (c + 1) * LANES] = value.astype(jnp.bfloat16)
                else:
                    upper = lax.broadcasted_iota(jnp.int32, (short, LANES), 1) >= STATE
                    cs[d, pl.ds(at, short), :] = jnp.where(upper, value, 0.0).astype(jnp.bfloat16)
                    bs[d, pl.ds(at, short), :] = jnp.where(
                        upper, pltpu.roll(value, STATE, 1), 0.0
                    ).astype(jnp.bfloat16)
        return carry

    lax.fori_loop(0, length // short, conv_rows, 0)

    backward_lane = ((lane >= heads) & (lane < 2 * heads)) | (lane == 2 * heads + 1)
    head_lane = lane < 2 * heads
    lower = jnp.where(row >= lane, 1.0, 0.0).astype(jnp.bfloat16)
    upper_sum = jnp.where(row <= lane, 1.0, 0.0).astype(jnp.bfloat16)

    def decays(b, carry):
        at = pl.multiple_of(b * BLOCK, BLOCK)
        columns_in = steps[pl.ds(at, BLOCK), :]
        mine = pltpu.roll(columns_in, lax.rem(LANES - seq * heads, LANES), 1)
        both = jnp.where(lane < heads, mine, pltpu.roll(mine, heads, 1)) + step_bias[...]
        step = jnp.maximum(both, 0.0) + jnp.log1p(jnp.exp(-jnp.abs(both)))
        rate = -step * rates[...]
        position = row + b * BLOCK
        here = position == marks[0]
        after = position + 1 == marks[0]
        for m in range(1, 4):
            here = here | (position == marks[m])
            after = after | (position + 1 == marks[m])
        here = jnp.where(here, 1.0, 0.0)
        after = jnp.where(after, 1.0, 0.0)
        rate = jnp.where(
            head_lane, rate, jnp.where(lane == 2 * heads, here, jnp.where(lane == 2 * heads + 1, after, 0.0))
        )
        parts = split_three(rate)
        ahead = sum(jnp.dot(lower, p, preferred_element_type=jnp.float32) for p in parts)
        behind = sum(jnp.dot(upper_sum, p, preferred_element_type=jnp.float32) for p in parts)
        cum = jnp.where(backward_lane, behind, ahead)
        seen = jnp.where(
            backward_lane,
            jnp.broadcast_to(cum[:, 2 * heads + 1 : 2 * heads + 2], (BLOCK, LANES)),
            jnp.broadcast_to(cum[:, 2 * heads : 2 * heads + 1], (BLOCK, LANES)),
        )
        last = jnp.where(backward_lane[:1], cum[:1], cum[BLOCK - 1 :])
        seen_last = jnp.where(backward_lane[:1], seen[:1], seen[BLOCK - 1 :])
        tail = jnp.where((seen == seen_last) & head_lane, jnp.exp(last - cum) * step, 0.0)
        lead = jnp.where((seen == 0.0) & head_lane, jnp.exp(cum), 0.0)
        fade = jnp.where((seen_last == 0.0) & head_lane[:1], jnp.exp(last), 0.0)
        parts = split_three(jnp.where(head_lane, cum, 0.0))
        joined = parts[0].astype(jnp.float32)
        for k in range(1, 3):
            joined = joined + pltpu.roll(parts[k].astype(jnp.float32), 2 * heads * k, 1)
        cums[b] = joined.astype(jnp.bfloat16)
        tails[b] = tail.astype(jnp.bfloat16)
        leads[b] = lead.astype(jnp.bfloat16)
        high = fade.astype(jnp.bfloat16).astype(jnp.float32)
        fades[b] = jnp.broadcast_to(high + pltpu.roll(fade - high, 2 * heads, 1), (16, LANES)).astype(
            jnp.bfloat16
        )
        shown = jnp.where(head_lane, jnp.log(step) - cum, cum).T
        turned[b] = shown
        for d in range(2):
            ordered = (row >= lane) if d == 0 else (row <= lane)
            seen_at = 2 * heads + d
            allowed = ordered & (cum[:, seen_at : seen_at + 1] == shown[seen_at : seen_at + 1, :])
            barred[d, b] = jnp.where(allowed, 0.0, -1e30)
        return carry

    lax.fori_loop(0, blocks, decays, 0)

    def head_columns(width, group, d):
        at_row = lax.broadcasted_iota(jnp.int32, (LANES, width), 0)
        head = lax.broadcasted_iota(jnp.int32, (LANES, width), 1) // group + d * heads
        hit = (at_row == head) | (at_row == head + 2 * heads) | (at_row == head + 4 * heads)
        return jnp.where(hit, 1.0, 0.0).astype(jnp.bfloat16)

    for d in range(2):
        spread[d] = head_columns(columns, HEAD_DIM, d)
        columns_of[d] = head_columns(heads * LANES, LANES, d)
    total[...] = jnp.zeros_like(total)
    state[...] = jnp.zeros_like(state)
    same = jnp.where(row // HEAD_DIM == lane // HEAD_DIM, 1.0 / HEAD_DIM, 0.0).astype(jnp.bfloat16)
    left = lane < HEAD_DIM

    def scan_step(i, carry):
        for d in range(2):
            b = i if d == 0 else blocks - 1 - i
            at = pl.ds(pl.multiple_of(b * BLOCK, BLOCK), BLOCK)
            c_part = cs[d, at, :]
            b_part = bs[d, at, :]
            scores = lax.dot_general(
                c_part, b_part, (((1,), (1,)), ((), ())), preferred_element_type=jnp.float32
            )
            bar = barred[d, b]
            before = state[d]
            carried = jnp.dot(c_part, before.astype(jnp.bfloat16), preferred_element_type=jnp.float32)
            lead = jnp.dot(leads[b], spread[d], preferred_element_type=jnp.float32)
            tail = jnp.dot(tails[b], spread[d], preferred_element_type=jnp.float32)
            fade = jnp.dot(fades[b], spread[d], preferred_element_type=jnp.float32)[:1]
            shown = jnp.dot(cums[b], columns_of[d], preferred_element_type=jnp.float32)
            x_all = xs[d, at, :]
            x_wide = x_all.astype(jnp.float32)
            inputs = (tail * x_wide).astype(jnp.bfloat16)
            local_end = lax.dot_general(
                b_part, inputs, (((0,), (0,)), ((), ())), preferred_element_type=jnp.float32
            )
            state[d] = fade * before + local_end
            for p in range(chunks):
                pair = []
                for h in (2 * p, 2 * p + 1):
                    at_row = d * heads + h
                    gap = shown[:, h * LANES : (h + 1) * LANES] + (turned[b, at_row : at_row + 1, :] + bar)
                    pair.append((jnp.exp(gap) * scores).astype(jnp.bfloat16))
                lanes = slice(p * LANES, (p + 1) * LANES)
                x_pair = x_all[:, lanes]
                none = jnp.zeros_like(x_pair)
                x_two = jnp.concatenate([jnp.where(left, x_pair, none), jnp.where(left, none, x_pair)], axis=0)
                inner = jnp.dot(jnp.concatenate(pair, axis=1), x_two, preferred_element_type=jnp.float32)
                at_lanes = pl.ds(pl.multiple_of(own_at + p * LANES, LANES), LANES)
                y = inner + lead[:, lanes] * carried[:, lanes] + direct[d : d + 1, at_lanes] * x_wide[:, lanes]
                mean = jnp.dot((y * y).astype(jnp.bfloat16), same, preferred_element_type=jnp.float32)
                scale = lax.rsqrt(mean + 1e-05)
                total[at, lanes] += y * scale * gains[d : d + 1, at_lanes]
        return carry

    lax.fori_loop(0, blocks, scan_step, 0)
    for mask in range(4):
        at = pl.ds(pl.multiple_of((seq ^ mask) * BLOCK, BLOCK), BLOCK)
        outs[mask][...] = total[at, :].astype(jnp.bfloat16)


def mix(heads, ids, marks, pieces, weights, ends, own_side, swapped, params):
    conv_weight, conv_bias, dt_bias, decay, skip, norm_gain = params
    shards = len(weights) + 1
    section, width = pieces[0].shape
    columns = heads * HEAD_DIM
    length = section * len(pieces)
    blocks = length // BLOCK
    chunks = columns // LANES
    in_smem = pl.BlockSpec(memory_space=pltpu.SMEM)
    in_vmem = pl.BlockSpec(memory_space=pltpu.VMEM)
    operands = (*pieces, *weights, *ends, own_side, *swapped, conv_weight, conv_bias, dt_bias, decay, skip, norm_gain)
    scratch = [
        ((length, width), jnp.bfloat16),
        ((columns, width), jnp.bfloat16),
        ((SIDE, width), jnp.bfloat16),
        ((chunks + 1, length + 2 * EDGE, LANES), jnp.float32),
        ((2, length, columns), jnp.bfloat16),
        ((2, length, LANES), jnp.bfloat16),
        ((2, length, LANES), jnp.bfloat16),
        ((length, LANES), jnp.float32),
        ((blocks, BLOCK, LANES), jnp.bfloat16),
        ((blocks, BLOCK, LANES), jnp.bfloat16),
        ((blocks, BLOCK, LANES), jnp.bfloat16),
        ((blocks, 16, LANES), jnp.bfloat16),
        ((blocks, BLOCK, LANES), jnp.float32),
        ((2, blocks, BLOCK, LANES), jnp.float32),
        ((2, LANES, columns), jnp.bfloat16),
        ((2, LANES, heads * LANES), jnp.bfloat16),
        ((length, columns), jnp.float32),
        ((2, LANES, columns), jnp.float32),
    ]
    return pl.pallas_call(
        functools.partial(mixer_kernel, heads, shards),
        out_shape=[jax.ShapeDtypeStruct((section, columns), jnp.bfloat16)] * len(pieces),
        in_specs=[in_smem] * 2 + [in_vmem] * len(operands),
        out_specs=[in_vmem] * len(pieces),
        scratch_shapes=[pltpu.VMEM(*one) for one in scratch],
        compiler_params=pltpu.CompilerParams(vmem_limit_bytes=32 * 1024 * 1024),
    )(ids, marks, *operands)


def turn(value, way):
    order = ring_order(lax.axis_size("batch"))
    count = len(order)
    return lax.ppermute(value, ("fsdp", "batch"), [(order[i], order[(i + way) % count]) for i in range(count)])


def swap(value, axis, mask):
    return lax.ppermute(value, axis, [(i, i ^ mask) for i in range(lax.axis_size(axis))])


def on_heads(hidden, in_weight, read_starts, conv_weight, conv_bias, dt_bias, decay, skip, norm_gain):
    tokens = hidden[0]
    count = lax.axis_size("seq")
    seq = lax.axis_index("seq")
    core = seq % 2
    heads = HEADS // count
    columns = heads * HEAD_DIM
    by_column = in_weight.T
    side_rows = by_column.shape[0] - INNER
    half_side = side_rows // 2
    own_side = by_column[INNER:]
    own = lax.dynamic_slice_in_dim(by_column, seq * columns, columns, axis=0)
    own = jnp.concatenate([own, lax.dynamic_slice_in_dim(own_side, core * half_side, half_side, axis=0)])

    order = ring_order(lax.axis_size("batch"))
    shards = len(order)
    up, down = [own], [own]
    for _ in range(shards // 2 - 1):
        up.append(turn(up[-1], 1))
        down.append(turn(down[-1], -1))
    cut = own.shape[0] // 32 * 16 + 16
    ends = [turn(up[-1][:cut], 1), turn(down[-1][cut:], -1)]
    weights = [own]
    for a, b in zip(up[1:], down[1:]):
        weights += [a, b]
    sides = [one[columns:] for one in weights[1:]] + [ends[1][columns - cut :]]
    swapped = [swap(jnp.concatenate(sides[i : i + 2]), "seq", 1) for i in range(0, shards - 1, 2)]
    across = swap(tokens, "seq", 2)
    pieces = [tokens, swap(tokens, "seq", 1), across, swap(across, "seq", 1)]

    place = jnp.asarray([order.index(i) for i in range(shards)], jnp.int32)[
        lax.axis_index("fsdp") * lax.axis_size("batch") + lax.axis_index("batch")
    ]
    steps = [0]
    for i in range(1, shards // 2):
        steps += [-i, i]
    steps.append(shards // 2)
    shard_ids = jnp.asarray(order, jnp.int32)[(place + jnp.asarray(steps, jnp.int32)) % shards]
    ids = jnp.concatenate([jnp.stack([seq, core]).astype(jnp.int32), shard_ids])

    def for_lanes(value):
        mine = lax.dynamic_slice(value, (0, seq * heads), (2, heads)).reshape(1, 2 * heads)
        return jnp.pad(mine, ((0, 0), (0, LANES - 2 * heads)))

    wide_skip = jnp.repeat(skip, HEAD_DIM, axis=1)
    params = (conv_weight, conv_bias, for_lanes(dt_bias), for_lanes(decay), wide_skip, norm_gain)
    results = mix(heads, ids, read_starts[0], pieces, weights, ends, own_side, swapped, params)
    received = [results[0]] + [swap(results[mask], "seq", mask) for mask in range(1, count)]
    mixed = jnp.zeros((tokens.shape[0], INNER), jnp.bfloat16)
    for mask in range(count):
        mixed = lax.dynamic_update_slice(mixed, received[mask], (0, (seq ^ mask) * columns))
    return mixed[None]


def solution(mesh):
    in_specs = (
        P(("fsdp", "batch"), "seq", None),
        P(("fsdp", "batch"), None),
        P(("fsdp", "batch"), None),
        P(),
        P(),
        P(),
        P(),
        P(),
        P(),
    )
    out_specs = P(("fsdp", "batch"), "seq", None)
    by_heads = mesh.shape["seq"] == 4 and mesh.shape["fsdp"] == 2

    def mixer(hidden, *rest):
        whole = by_heads and hidden.shape[1] == mesh.shape["seq"] * BLOCK
        return jax.shard_map(
            on_heads if whole else on_sections,
            mesh=mesh,
            in_specs=in_specs,
            out_specs=out_specs,
            check_vma=False,
        )(hidden, *rest)

    return mixer
```

```python
import functools

import jax
import jax.numpy as jnp
from jax import lax
from jax.experimental import pallas as pl
from jax.experimental.pallas import tpu as pltpu
from jax.sharding import PartitionSpec as P

HEADS = 32
HEAD_DIM = 64
STATE = 64
KERNEL = 4
BLOCK = 128
INNER = 2048
CONV_CH = 2176


def prefix(value, axis, join, neutral, backward):
    count, mine = (lax.axis_size(axis), lax.axis_index(axis))
    pieces = jax.tree.map(lambda part: lax.all_gather(part, axis), value)
    if backward:
        pieces = jax.tree.map(lambda part: part[::-1], pieces)
        mine = count - 1 - mine
    running = jax.tree.map(
        lambda part, zero: jnp.full_like(part, 0) + jnp.asarray(zero, part.dtype), value, neutral
    )

    def turn(position, running):
        longer = join(running, jax.tree.map(lambda part: part[position], pieces))
        return jax.tree.map(lambda new, old: jnp.where(position < mine, new, old), longer, running)

    return lax.fori_loop(0, count - 1, turn, running)


def extended_2(value, sides, width):
    for axis, dim in sides:
        size, length = (lax.axis_size(axis), value.shape[dim])
        up = [(i, (i + 1) % size) for i in range(size - 1)]
        down = [(j, i) for i, j in up]
        last = lax.slice_in_dim(value, length - width, length, axis=dim)
        initial = lax.slice_in_dim(value, 0, width, axis=dim)
        before = lax.ppermute(last, axis, up)
        after = lax.ppermute(initial, axis, down)
        value = jnp.concatenate([before, value, after], axis=dim)
    return value


def conv_silu(padded, weight, bias):
    length = padded.shape[0] - weight.shape[0] + 1
    total = jnp.broadcast_to(bias[None, :], (length, bias.shape[0]))
    for tap in range(weight.shape[0]):
        total = total + weight[tap][None, :] * padded[tap : tap + length].astype(jnp.float32)
    return jax.nn.silu(total).astype(jnp.bfloat16)


def block_parts(x_part, b_part, c_part, step_size, log_rate, resets):
    length = x_part.shape[0]
    running = jnp.cumsum(log_rate, axis=0)
    running_heads = running.T
    step_heads = step_size.T
    resets_seen = jnp.cumsum(resets)
    scores = jnp.dot(c_part, b_part.T, preferred_element_type=jnp.float32)
    positions = jnp.arange(length)
    allowed = (positions[:, None] >= positions[None, :]) & (
        resets_seen[:, None] == resets_seen[None, :]
    )
    log_gaps = jnp.minimum(running_heads[:, :, None] - running_heads[:, None, :], 0.0)
    weights = (
        jnp.where(allowed[None, :, :], jnp.exp(log_gaps), 0.0)
        * scores[None, :, :]
        * step_heads[:, None, :]
    )
    weights = weights.astype(jnp.bfloat16)
    values = x_part.reshape(length, HEADS, HEAD_DIM)
    inner_part = jnp.einsum("hts,shp->thp", weights, values, preferred_element_type=jnp.float32)
    last_same = resets_seen == resets_seen[-1]
    tail_weight = (
        jnp.where(last_same[:, None], jnp.exp(running[-1][None, :] - running), 0.0) * step_size
    )
    inputs = (tail_weight[:, :, None] * values.astype(jnp.float32)).astype(jnp.bfloat16)
    local_end = jnp.einsum("shp,sn->hpn", inputs, b_part, preferred_element_type=jnp.float32)
    lead_fade = jnp.where((resets_seen == 0)[:, None], jnp.exp(running), 0.0)
    block_fade = jnp.where(resets_seen[-1] == 0, jnp.exp(running[-1]), 0.0)
    return (inner_part, local_end, lead_fade, block_fade)


def chain_combine(earlier, later):
    return (earlier[0] * later[0], later[0][:, None] * earlier[1] + later[1])


def direction(conv_out, step_cols, resets, bias_step, rates, direct, gains, backward):
    length = conv_out.shape[0]
    blocks = length // BLOCK
    x_part = conv_out[:, :INNER]
    b_part = conv_out[:, INNER : INNER + STATE]
    c_part = conv_out[:, INNER + STATE :]
    step_size = jax.nn.softplus(step_cols.astype(jnp.float32) + bias_step[None, :])
    log_rate = -step_size * rates[None, :]
    inner_part, local_end, lead_fade, block_fade = jax.vmap(block_parts)(
        x_part.reshape(blocks, BLOCK, INNER),
        b_part.reshape(blocks, BLOCK, STATE),
        c_part.reshape(blocks, BLOCK, STATE),
        step_size.reshape(blocks, BLOCK, HEADS),
        log_rate.reshape(blocks, BLOCK, HEADS),
        resets.reshape(blocks, BLOCK),
    )
    carried_state = jnp.zeros((HEADS, HEAD_DIM, STATE), jnp.float32)
    carried_fade = jnp.ones((HEADS,), jnp.float32)
    entering = carried_state
    fades_before = carried_fade
    carried_state = block_fade[0][:, None, None] * carried_state + local_end[0]
    carried_fade = block_fade[0] * carried_fade
    summary = (carried_fade, carried_state.reshape(HEADS, HEAD_DIM * STATE))
    identity = (jnp.ones((HEADS,), jnp.float32), jnp.zeros((HEADS, HEAD_DIM * STATE), jnp.float32))
    if backward:
        incoming = prefix(summary, "seq", chain_combine, identity, True)
    else:
        incoming = prefix(summary, "seq", chain_combine, identity, False)
    incoming_state = incoming[1].reshape(HEADS, HEAD_DIM, STATE)
    states = jnp.stack([fades_before[:, None, None] * incoming_state + entering])
    rounded = states.astype(jnp.bfloat16)
    carried = jnp.einsum(
        "btn,bhpn->bthp",
        c_part.reshape(blocks, BLOCK, STATE),
        rounded,
        preferred_element_type=jnp.float32,
    )
    direct_part = direct[None, None, :, None] * x_part.reshape(
        blocks, BLOCK, HEADS, HEAD_DIM
    ).astype(jnp.float32)
    result = (inner_part + lead_fade[..., None] * carried + direct_part).reshape(
        length, HEADS, HEAD_DIM
    )
    scale = lax.rsqrt(jnp.mean(result * result, axis=-1, keepdims=True) + 1e-05)
    return (result * scale * gains.reshape(HEADS, HEAD_DIM)).reshape(length, INNER)


def project(rows_in, in_weight):
    total = jnp.dot(
        rows_in,
        lax.all_gather(in_weight, ("fsdp", "batch"), axis=0, tiled=True),
        preferred_element_type=jnp.float32,
    )
    return total.astype(jnp.bfloat16)


def on_sections(
    hidden, in_weight, read_starts, conv_weight, conv_bias, dt_bias, decay, skip, norm_gain
):
    tokens = hidden[0]
    length = tokens.shape[0]
    margin = KERNEL - 1
    projected = project(tokens, in_weight)
    extended = extended_2(projected[:, :CONV_CH], (("seq", 0),), margin)
    forward_in = conv_silu(extended[: length + margin], conv_weight[0], conv_bias[0])
    backward_in = conv_silu(jnp.flip(extended[margin:], 0), conv_weight[1], conv_bias[1])
    step_cols = projected[:, CONV_CH:]
    positions = lax.axis_index("seq") * length + jnp.arange(length, dtype=jnp.int32)
    marks = read_starts[0]
    starts_here = jnp.any(positions[:, None] == marks[None, :], axis=1).astype(jnp.float32)
    starts_next = jnp.any((positions + 1)[:, None] == marks[None, :], axis=1).astype(jnp.float32)
    forward_out = direction(
        forward_in, step_cols, starts_here, dt_bias[0], decay[0], skip[0], norm_gain[0], False
    )
    backward_out = direction(
        backward_in,
        jnp.flip(step_cols, 0),
        jnp.flip(starts_next, 0),
        dt_bias[1],
        decay[1],
        skip[1],
        norm_gain[1],
        True,
    )
    mixed = forward_out + jnp.flip(backward_out, 0)
    return mixed.astype(jnp.bfloat16)[None]


LANES = 128
SIDE = 256
EDGE = 8


def ring_order(count):
    return [i if i < count else 3 * count - 1 - i for i in range(2 * count)]


def split_parts(value, count):
    parts = []
    for _ in range(count):
        parts.append(value.astype(jnp.bfloat16))
        value = value - parts[-1].astype(jnp.float32)
    return parts


def mixer_kernel(heads, ring, *refs):
    shards = 2 * ring
    pieces, refs = refs[:4], refs[4:]
    weights, refs = refs[: shards - 1], refs[shards - 1 :]
    ends, refs = refs[:2], refs[2:]
    marks_in, conv_w_in, conv_b_in, step_bias_in, decay_in, skip_in, gain_in = refs[:7]
    outs, refs = refs[7:11], refs[11:]
    conv_w, conv_b, per_head, gains, marks, sems = refs[:6]
    rows_in, w_own, w_side, padded, xs, cs, bs, cums, leads, tails, turned, barred, fade_wide, state, ys, mixed = refs[6:]
    seq, fsdp, batch = lax.axis_index("seq"), lax.axis_index("fsdp"), lax.axis_index("batch")
    columns = heads * HEAD_DIM
    depth = weights[0].shape[1]
    side_rows = weights[0].shape[0] - columns
    chunks = columns // LANES
    length = rows_in.shape[0]
    blocks = length // BLOCK
    cut = ends[0].shape[0]
    own_at = pl.multiple_of(seq * columns, columns)

    own_lanes = pl.ds(own_at, columns)
    side_lanes = pl.ds(INNER, LANES)
    narrow = pl.ds(0, HEADS)
    copies = [
        (conv_w_in.at[:, :, own_lanes], conv_w.at[:, :, pl.ds(0, columns)]),
        (conv_w_in.at[:, :, side_lanes], conv_w.at[:, :, pl.ds(columns, LANES)]),
        (conv_b_in.at[:, own_lanes], conv_b.at[:, pl.ds(0, columns)]),
        (conv_b_in.at[:, side_lanes], conv_b.at[:, pl.ds(columns, LANES)]),
        (step_bias_in, per_head.at[0]),
        (decay_in, per_head.at[1]),
        (skip_in, per_head.at[2]),
        (gain_in.at[:, own_lanes], gains),
        (marks_in, marks),
    ]
    copies = [pltpu.make_async_copy(a, b, sems.at[i]) for i, (a, b) in enumerate(copies)]
    for copy in copies:
        copy.start()

    lane = lax.broadcasted_iota(jnp.int32, (BLOCK, LANES), 1)
    row = lax.broadcasted_iota(jnp.int32, (BLOCK, LANES), 0)

    for mask in range(4):
        rows_in[mask * BLOCK : (mask + 1) * BLOCK, :] = pieces[mask][...]
    w_side[side_rows:, :] = jnp.zeros((SIDE - side_rows, w_side.shape[1]), jnp.bfloat16)
    position = jnp.where(fsdp == 0, batch, shards - 1 - batch)
    for n in range(shards):
        away = 0 if n == 0 else (shards // 2 if n == shards - 1 else (-1) ** n * ((n + 1) // 2))
        there = lax.rem(position + shards + away, shards)
        shard = jnp.where(there < ring, there, 3 * ring - 1 - there)
        at = pl.ds(pl.multiple_of(shard * depth, depth), depth)
        if n < shards - 1:
            w_own[:, at] = weights[n][:columns, :]
            w_side[:side_rows, at] = weights[n][columns:, :]
        else:
            w_own[:cut, at] = ends[0][...]
            w_own[cut:, at] = ends[1][: columns - cut, :]
            w_side[:side_rows, at] = ends[1][columns - cut :, :]
    edge = jnp.zeros((EDGE, LANES), jnp.float32)
    for c in range(chunks + 1):
        padded[c, 0:EDGE, :] = edge
        padded[c, EDGE + length :, :] = edge
    state[...] = jnp.zeros_like(state)

    places = [pl.multiple_of((seq ^ mask) * BLOCK, BLOCK) for mask in range(4)]

    def project_in(weight):
        out = lax.dot_general(
            rows_in[...], weight, (((1,), (1,)), ((), ())), preferred_element_type=jnp.float32
        )
        return out.astype(jnp.bfloat16).astype(jnp.float32)

    def keep(c, value):
        for mask in range(4):
            padded[c, pl.ds(EDGE + places[mask], BLOCK), :] = value[mask * BLOCK : (mask + 1) * BLOCK, :]

    side_out = project_in(w_side[...])
    keep(chunks, side_out[:, :LANES])
    for n in range(columns // SIDE):
        part_out = project_in(w_own[n * SIDE : (n + 1) * SIDE, :])
        for k in range(SIDE // LANES):
            keep(n * (SIDE // LANES) + k, part_out[:, k * LANES : (k + 1) * LANES])
    for copy in copies:
        copy.wait()

    backward_lane = ((lane >= heads) & (lane < 2 * heads)) | (lane == 2 * heads + 1)
    head_lane = lane < 2 * heads
    lower = jnp.where(row >= lane, 1.0, 0.0).astype(jnp.bfloat16)
    upper = jnp.where(row <= lane, 1.0, 0.0).astype(jnp.bfloat16)
    to_first = lax.rem(LANES - seq * heads, LANES)

    def own_heads(k):
        both = jnp.concatenate([per_head[k], jnp.zeros((2, LANES - HEADS), jnp.float32)], axis=1)
        both = pltpu.roll(both, to_first, 1)
        ahead, behind = both[0:1, :], pltpu.roll(both, heads, 1)[1:2, :]
        value = jnp.where(lane[:1] < heads, ahead, behind)
        return jnp.where(head_lane[:1], value, 0.0)

    step_bias, rates, direct = own_heads(0), own_heads(1), own_heads(2)

    def head_columns(d):
        at_row = lax.broadcasted_iota(jnp.int32, (LANES, columns), 0)
        head = lax.broadcasted_iota(jnp.int32, (LANES, columns), 1) // HEAD_DIM + d * heads
        hit = (at_row == head) | (at_row == head + 2 * heads) | (at_row == head + 4 * heads)
        return jnp.where(hit, 1.0, 0.0).astype(jnp.bfloat16)

    spread = [head_columns(d) for d in range(2)]

    def packed(value, count):
        parts = split_parts(value, count)
        joined = parts[0].astype(jnp.float32)
        for k in range(1, count):
            joined = joined + pltpu.roll(parts[k].astype(jnp.float32), 2 * heads * k, 1)
        return joined

    fades = []
    for mask in range(4):
        place = places[mask]
        b = seq ^ mask
        mine = pltpu.roll(side_out[mask * BLOCK : (mask + 1) * BLOCK, LANES:], to_first, 1)
        both = jnp.where(lane < heads, mine, pltpu.roll(mine, heads, 1)) + step_bias
        step = jnp.maximum(both, 0.0) + jnp.log1p(jnp.exp(-jnp.abs(both)))
        rate = -step * rates
        here_at = row + place
        here = here_at == marks[:, 0:1]
        after = here_at + 1 == marks[:, 0:1]
        for m in range(1, marks.shape[1]):
            here = here | (here_at == marks[:, m : m + 1])
            after = after | (here_at + 1 == marks[:, m : m + 1])
        start = (here & (lane == 2 * heads)) | (after & (lane == 2 * heads + 1))
        rate = jnp.where(head_lane, rate, jnp.where(start, 1.0, 0.0))
        parts = split_parts(rate, 3)
        ahead = sum(jnp.dot(lower, p, preferred_element_type=jnp.float32) for p in parts)
        behind = sum(jnp.dot(upper, p, preferred_element_type=jnp.float32) for p in parts)
        cum = jnp.where(backward_lane, behind, ahead)
        seen_ahead = jnp.broadcast_to(cum[:, 2 * heads : 2 * heads + 1], (BLOCK, LANES))
        seen_behind = jnp.broadcast_to(cum[:, 2 * heads + 1 : 2 * heads + 2], (BLOCK, LANES))
        seen = jnp.where(backward_lane, seen_behind, seen_ahead)
        last = jnp.where(backward_lane[:1], cum[:1], cum[BLOCK - 1 :])
        seen_last = jnp.where(backward_lane[:1], seen[:1], seen[BLOCK - 1 :])
        tail = jnp.where((seen == seen_last) & head_lane, jnp.exp(last - cum) * step, 0.0)
        lead = jnp.where((seen == 0.0) & head_lane, jnp.exp(cum), 0.0)
        fade = jnp.where((seen_last == 0.0) & head_lane[:1], jnp.exp(last), 0.0)
        fades.append(packed(jnp.broadcast_to(fade, (8, LANES)), 2)[:1])
        at = pl.ds(place, BLOCK)
        cums[at, :] = cum
        for d in range(2):
            leads[d, at, :] = jnp.dot(
                lead.astype(jnp.bfloat16), spread[d], preferred_element_type=jnp.float32
            ).astype(jnp.bfloat16)
            tails[d, at, :] = jnp.dot(
                tail.astype(jnp.bfloat16), spread[d], preferred_element_type=jnp.float32
            ).astype(jnp.bfloat16)
        shown = jnp.where(head_lane, jnp.log(step) - cum, cum).T
        turned[b] = shown
        for d in range(2):
            ordered = (row >= lane) if d == 0 else (row <= lane)
            seen_row = shown[2 * heads + d : 2 * heads + d + 1, :]
            allowed = ordered & ((seen_ahead if d == 0 else seen_behind) == seen_row)
            barred[d, b] = jnp.where(allowed, 0.0, -1e30)
    fades.append(packed(jnp.broadcast_to(direct, (8, LANES)), 3)[:1])
    rows_wide = jnp.concatenate(fades + [jnp.zeros((11, LANES), jnp.float32)], axis=0).astype(jnp.bfloat16)
    wide = [jnp.dot(rows_wide, spread[d], preferred_element_type=jnp.float32) for d in range(2)]
    for d in range(2):
        for mask in range(4):
            fade_wide[d, seq ^ mask] = jnp.broadcast_to(wide[d][mask : mask + 1, :], (8, columns))
    skips = [wide[d][4:5, :] for d in range(2)]

    short = 64

    def conv_rows(i, carry):
        at = pl.multiple_of(i * short, short)
        for c in range(chunks + 1):
            taps = [padded[c, pl.ds(at + EDGE - 3 + k, short), :] for k in range(7)]
            lanes = slice(c * LANES, (c + 1) * LANES)
            for d in range(2):
                acc = conv_b[d : d + 1, lanes] + conv_w[d, 0:1, lanes] * taps[0 if d == 0 else 6]
                for k in range(1, KERNEL):
                    acc = acc + conv_w[d, k : k + 1, lanes] * taps[k if d == 0 else 6 - k]
                half = 0.5 * acc
                value = half + half * jnp.tanh(half)
                if c < chunks:
                    xs[d, pl.ds(at, short), lanes] = value.astype(jnp.bfloat16)
                else:
                    high = lax.broadcasted_iota(jnp.int32, (short, LANES), 1) >= STATE
                    cs[d, pl.ds(at, short), :] = jnp.where(high, value, 0.0).astype(jnp.bfloat16)
                    bs[d, pl.ds(at, short), :] = jnp.where(
                        high, pltpu.roll(value, STATE, 1), 0.0
                    ).astype(jnp.bfloat16)
        return carry

    lax.fori_loop(0, length // short, conv_rows, 0)

    group = SIDE // HEAD_DIM
    lane_head = lax.broadcasted_iota(jnp.int32, (BLOCK, SIDE), 1) // HEAD_DIM

    def scan_step(i, carry):
        for d in range(2):
            b = i if d == 0 else blocks - 1 - i
            at = pl.ds(pl.multiple_of(b * BLOCK, BLOCK), BLOCK)
            c_part = cs[d, at, :]
            b_part = bs[d, at, :]
            scores = lax.dot_general(
                c_part, b_part, (((1,), (1,)), ((), ())), preferred_element_type=jnp.float32
            )
            bar = barred[d, b]
            before = state[d]
            carried = jnp.dot(c_part, before.astype(jnp.bfloat16), preferred_element_type=jnp.float32)
            x_all = xs[d, at, :]
            inputs = tails[d, at, :] * x_all
            local_end = lax.dot_general(
                b_part, inputs, (((0,), (0,)), ((), ())), preferred_element_type=jnp.float32
            )
            state[d] = fade_wide[d, b][:1] * before + local_end
            for q in range(columns // SIDE):
                some = []
                for h in range(q * group, (q + 1) * group):
                    at_row = d * heads + h
                    gap = cums[at, at_row : at_row + 1] + (turned[b, at_row : at_row + 1, :] + bar)
                    some.append((jnp.exp(gap) * scores).astype(jnp.bfloat16))
                lanes = slice(q * SIDE, (q + 1) * SIDE)
                x_part = x_all[:, lanes]
                none = jnp.zeros_like(x_part)
                spaced = jnp.concatenate([jnp.where(lane_head == h, x_part, none) for h in range(group)], axis=0)
                inner = jnp.dot(jnp.concatenate(some, axis=1), spaced, preferred_element_type=jnp.float32)
                ys[d, at, lanes] = (
                    inner
                    + leads[d, at, lanes].astype(jnp.float32) * carried[:, lanes]
                    + skips[d][:, lanes] * x_part.astype(jnp.float32)
                )
        return carry

    lax.fori_loop(0, blocks, scan_step, 0)

    head_row = lax.broadcasted_iota(jnp.int32, (SIDE, SIDE), 0) // HEAD_DIM
    head_col = lax.broadcasted_iota(jnp.int32, (SIDE, SIDE), 1) // HEAD_DIM
    same = jnp.where(head_row == head_col, 1.0 / HEAD_DIM, 0.0).astype(jnp.bfloat16)
    for q in range(columns // SIDE):
        lanes = slice(q * SIDE, (q + 1) * SIDE)
        both = 0.0
        for d in range(2):
            y = ys[d, :, lanes]
            mean = jnp.dot((y * y).astype(jnp.bfloat16), same, preferred_element_type=jnp.float32)
            both = both + y * lax.rsqrt(mean + 1e-05) * gains[d : d + 1, lanes]
        mixed[:, lanes] = both.astype(jnp.bfloat16)
    for mask in range(4):
        outs[mask][...] = mixed[pl.ds(places[mask], BLOCK), :]


def mix(heads, ring, pieces, weights, ends, params):
    section, width = pieces[0].shape
    columns = heads * HEAD_DIM
    length = section * len(pieces)
    blocks = length // BLOCK
    chunks = columns // LANES
    in_hbm = pl.BlockSpec(memory_space=pltpu.HBM)
    in_vmem = pl.BlockSpec(memory_space=pltpu.VMEM)
    operands = (*pieces, *weights, *ends)
    scratch = [
        pltpu.VMEM((2, KERNEL, columns + LANES), jnp.float32),
        pltpu.VMEM((2, columns + LANES), jnp.float32),
        pltpu.VMEM((3, 2, HEADS), jnp.float32),
        pltpu.VMEM((2, columns), jnp.float32),
        pltpu.VMEM(params[0].shape, jnp.int32),
        pltpu.SemaphoreType.DMA((9,)),
        pltpu.VMEM((length, width), jnp.bfloat16),
        pltpu.VMEM((columns, width), jnp.bfloat16),
        pltpu.VMEM((SIDE, width), jnp.bfloat16),
        pltpu.VMEM((chunks + 1, length + 2 * EDGE, LANES), jnp.float32),
        pltpu.VMEM((2, length, columns), jnp.bfloat16),
        pltpu.VMEM((2, length, LANES), jnp.bfloat16),
        pltpu.VMEM((2, length, LANES), jnp.bfloat16),
        pltpu.VMEM((length, LANES), jnp.float32),
        pltpu.VMEM((2, length, columns), jnp.bfloat16),
        pltpu.VMEM((2, length, columns), jnp.bfloat16),
        pltpu.VMEM((blocks, BLOCK, LANES), jnp.float32),
        pltpu.VMEM((2, blocks, BLOCK, LANES), jnp.float32),
        pltpu.VMEM((2, blocks, 8, columns), jnp.float32),
        pltpu.VMEM((2, LANES, columns), jnp.float32),
        pltpu.VMEM((2, length, columns), jnp.float32),
        pltpu.VMEM((length, columns), jnp.bfloat16),
    ]
    return pl.pallas_call(
        functools.partial(mixer_kernel, heads, ring),
        out_shape=[jax.ShapeDtypeStruct((section, columns), jnp.bfloat16)] * len(pieces),
        in_specs=[in_vmem] * len(operands) + [in_hbm] * len(params),
        out_specs=[in_vmem] * len(pieces),
        scratch_shapes=scratch,
        compiler_params=pltpu.CompilerParams(vmem_limit_bytes=36 * 1024 * 1024),
    )(*operands, *params)


def turn(value, way):
    order = ring_order(lax.axis_size("batch"))
    count = len(order)
    return lax.ppermute(value, ("fsdp", "batch"), [(order[i], order[(i + way) % count]) for i in range(count)])


def swap(value, axis, mask):
    return lax.ppermute(value, axis, [(i, i ^ mask) for i in range(lax.axis_size(axis))])


def on_heads(hidden, in_weight, read_starts, conv_weight, conv_bias, dt_bias, decay, skip, norm_gain):
    tokens = hidden[0]
    count = lax.axis_size("seq")
    seq = lax.axis_index("seq")
    heads = HEADS // count
    columns = heads * HEAD_DIM
    by_column = in_weight.T
    own = jnp.concatenate(
        [lax.dynamic_slice_in_dim(by_column, seq * columns, columns, axis=0), by_column[INNER:]]
    )

    ring = lax.axis_size("batch")
    up, down = [own], [own]
    for _ in range(ring - 1):
        up.append(turn(up[-1], 1))
        down.append(turn(down[-1], -1))
    cut = own.shape[0] // 32 * 16
    ends = [turn(up[-1][:cut], 1), turn(down[-1][cut:], -1)]
    weights = [own]
    for a, b in zip(up[1:], down[1:]):
        weights += [a, b]
    across = swap(tokens, "seq", 2)
    pieces = [tokens, swap(tokens, "seq", 1), across, swap(across, "seq", 1)]
    params = (read_starts, conv_weight, conv_bias, dt_bias, decay, skip, norm_gain)
    results = mix(heads, ring, pieces, weights, ends, params)
    received = [results[0]] + [swap(results[mask], "seq", mask) for mask in range(1, count)]
    mixed = jnp.zeros((tokens.shape[0], INNER), jnp.bfloat16)
    for mask in range(count):
        mixed = lax.dynamic_update_slice(mixed, received[mask], (0, (seq ^ mask) * columns))
    return mixed[None]


def solution(mesh):
    in_specs = (
        P(("fsdp", "batch"), "seq", None),
        P(("fsdp", "batch"), None),
        P(("fsdp", "batch"), None),
        P(),
        P(),
        P(),
        P(),
        P(),
        P(),
    )
    out_specs = P(("fsdp", "batch"), "seq", None)
    by_heads = mesh.shape["seq"] == 4 and mesh.shape["fsdp"] == 2

    def mixer(hidden, *rest):
        whole = by_heads and hidden.shape[1] == mesh.shape["seq"] * BLOCK
        return jax.shard_map(
            on_heads if whole else on_sections,
            mesh=mesh,
            in_specs=in_specs,
            out_specs=out_specs,
            check_vma=False,
        )(hidden, *rest)

    return mixer
```

```python
import functools

import jax
import jax.numpy as jnp
from jax import lax
from jax.experimental import pallas as pl
from jax.experimental.pallas import tpu as pltpu
from jax.sharding import PartitionSpec as P

HEADS = 32
HEAD_DIM = 64
STATE = 64
KERNEL = 4
BLOCK = 128
INNER = 2048
CONV_CH = 2176


def prefix(value, axis, join, neutral, backward):
    count, mine = (lax.axis_size(axis), lax.axis_index(axis))
    pieces = jax.tree.map(lambda part: lax.all_gather(part, axis), value)
    if backward:
        pieces = jax.tree.map(lambda part: part[::-1], pieces)
        mine = count - 1 - mine
    running = jax.tree.map(
        lambda part, zero: jnp.full_like(part, 0) + jnp.asarray(zero, part.dtype), value, neutral
    )

    def turn(position, running):
        longer = join(running, jax.tree.map(lambda part: part[position], pieces))
        return jax.tree.map(lambda new, old: jnp.where(position < mine, new, old), longer, running)

    return lax.fori_loop(0, count - 1, turn, running)


def extended_2(value, sides, width):
    for axis, dim in sides:
        size, length = (lax.axis_size(axis), value.shape[dim])
        up = [(i, (i + 1) % size) for i in range(size - 1)]
        down = [(j, i) for i, j in up]
        last = lax.slice_in_dim(value, length - width, length, axis=dim)
        initial = lax.slice_in_dim(value, 0, width, axis=dim)
        before = lax.ppermute(last, axis, up)
        after = lax.ppermute(initial, axis, down)
        value = jnp.concatenate([before, value, after], axis=dim)
    return value


def conv_silu(padded, weight, bias):
    length = padded.shape[0] - weight.shape[0] + 1
    total = jnp.broadcast_to(bias[None, :], (length, bias.shape[0]))
    for tap in range(weight.shape[0]):
        total = total + weight[tap][None, :] * padded[tap : tap + length].astype(jnp.float32)
    return jax.nn.silu(total).astype(jnp.bfloat16)


def block_parts(x_part, b_part, c_part, step_size, log_rate, resets):
    length = x_part.shape[0]
    running = jnp.cumsum(log_rate, axis=0)
    running_heads = running.T
    step_heads = step_size.T
    resets_seen = jnp.cumsum(resets)
    scores = jnp.dot(c_part, b_part.T, preferred_element_type=jnp.float32)
    positions = jnp.arange(length)
    allowed = (positions[:, None] >= positions[None, :]) & (
        resets_seen[:, None] == resets_seen[None, :]
    )
    log_gaps = jnp.minimum(running_heads[:, :, None] - running_heads[:, None, :], 0.0)
    weights = (
        jnp.where(allowed[None, :, :], jnp.exp(log_gaps), 0.0)
        * scores[None, :, :]
        * step_heads[:, None, :]
    )
    weights = weights.astype(jnp.bfloat16)
    values = x_part.reshape(length, HEADS, HEAD_DIM)
    inner_part = jnp.einsum("hts,shp->thp", weights, values, preferred_element_type=jnp.float32)
    last_same = resets_seen == resets_seen[-1]
    tail_weight = (
        jnp.where(last_same[:, None], jnp.exp(running[-1][None, :] - running), 0.0) * step_size
    )
    inputs = (tail_weight[:, :, None] * values.astype(jnp.float32)).astype(jnp.bfloat16)
    local_end = jnp.einsum("shp,sn->hpn", inputs, b_part, preferred_element_type=jnp.float32)
    lead_fade = jnp.where((resets_seen == 0)[:, None], jnp.exp(running), 0.0)
    block_fade = jnp.where(resets_seen[-1] == 0, jnp.exp(running[-1]), 0.0)
    return (inner_part, local_end, lead_fade, block_fade)


def chain_combine(earlier, later):
    return (earlier[0] * later[0], later[0][:, None] * earlier[1] + later[1])


def direction(conv_out, step_cols, resets, bias_step, rates, direct, gains, backward):
    length = conv_out.shape[0]
    blocks = length // BLOCK
    x_part = conv_out[:, :INNER]
    b_part = conv_out[:, INNER : INNER + STATE]
    c_part = conv_out[:, INNER + STATE :]
    step_size = jax.nn.softplus(step_cols.astype(jnp.float32) + bias_step[None, :])
    log_rate = -step_size * rates[None, :]
    inner_part, local_end, lead_fade, block_fade = jax.vmap(block_parts)(
        x_part.reshape(blocks, BLOCK, INNER),
        b_part.reshape(blocks, BLOCK, STATE),
        c_part.reshape(blocks, BLOCK, STATE),
        step_size.reshape(blocks, BLOCK, HEADS),
        log_rate.reshape(blocks, BLOCK, HEADS),
        resets.reshape(blocks, BLOCK),
    )
    carried_state = jnp.zeros((HEADS, HEAD_DIM, STATE), jnp.float32)
    carried_fade = jnp.ones((HEADS,), jnp.float32)
    entering = carried_state
    fades_before = carried_fade
    carried_state = block_fade[0][:, None, None] * carried_state + local_end[0]
    carried_fade = block_fade[0] * carried_fade
    summary = (carried_fade, carried_state.reshape(HEADS, HEAD_DIM * STATE))
    identity = (jnp.ones((HEADS,), jnp.float32), jnp.zeros((HEADS, HEAD_DIM * STATE), jnp.float32))
    if backward:
        incoming = prefix(summary, "seq", chain_combine, identity, True)
    else:
        incoming = prefix(summary, "seq", chain_combine, identity, False)
    incoming_state = incoming[1].reshape(HEADS, HEAD_DIM, STATE)
    states = jnp.stack([fades_before[:, None, None] * incoming_state + entering])
    rounded = states.astype(jnp.bfloat16)
    carried = jnp.einsum(
        "btn,bhpn->bthp",
        c_part.reshape(blocks, BLOCK, STATE),
        rounded,
        preferred_element_type=jnp.float32,
    )
    direct_part = direct[None, None, :, None] * x_part.reshape(
        blocks, BLOCK, HEADS, HEAD_DIM
    ).astype(jnp.float32)
    result = (inner_part + lead_fade[..., None] * carried + direct_part).reshape(
        length, HEADS, HEAD_DIM
    )
    scale = lax.rsqrt(jnp.mean(result * result, axis=-1, keepdims=True) + 1e-05)
    return (result * scale * gains.reshape(HEADS, HEAD_DIM)).reshape(length, INNER)


def project(rows_in, in_weight):
    total = jnp.dot(
        rows_in,
        lax.all_gather(in_weight, ("fsdp", "batch"), axis=0, tiled=True),
        preferred_element_type=jnp.float32,
    )
    return total.astype(jnp.bfloat16)


def on_sections(
    hidden, in_weight, read_starts, conv_weight, conv_bias, dt_bias, decay, skip, norm_gain
):
    tokens = hidden[0]
    length = tokens.shape[0]
    margin = KERNEL - 1
    projected = project(tokens, in_weight)
    extended = extended_2(projected[:, :CONV_CH], (("seq", 0),), margin)
    forward_in = conv_silu(extended[: length + margin], conv_weight[0], conv_bias[0])
    backward_in = conv_silu(jnp.flip(extended[margin:], 0), conv_weight[1], conv_bias[1])
    step_cols = projected[:, CONV_CH:]
    positions = lax.axis_index("seq") * length + jnp.arange(length, dtype=jnp.int32)
    marks = read_starts[0]
    starts_here = jnp.any(positions[:, None] == marks[None, :], axis=1).astype(jnp.float32)
    starts_next = jnp.any((positions + 1)[:, None] == marks[None, :], axis=1).astype(jnp.float32)
    forward_out = direction(
        forward_in, step_cols, starts_here, dt_bias[0], decay[0], skip[0], norm_gain[0], False
    )
    backward_out = direction(
        backward_in,
        jnp.flip(step_cols, 0),
        jnp.flip(starts_next, 0),
        dt_bias[1],
        decay[1],
        skip[1],
        norm_gain[1],
        True,
    )
    mixed = forward_out + jnp.flip(backward_out, 0)
    return mixed.astype(jnp.bfloat16)[None]


LANES = 128
SIDE = 256
EDGE = 8
GROUP = 32


def ring_order(count):
    return [i if i < count else 3 * count - 1 - i for i in range(2 * count)]


def split_parts(value, count):
    parts = []
    for _ in range(count):
        parts.append(value.astype(jnp.bfloat16))
        value = value - parts[-1].astype(jnp.float32)
    return parts


def lane_row():
    lane = lax.broadcasted_iota(jnp.int32, (BLOCK, LANES), 1)
    row = lax.broadcasted_iota(jnp.int32, (BLOCK, LANES), 0)
    return lane, row


def shard_at(away, ring):
    fsdp, batch = lax.axis_index("fsdp"), lax.axis_index("batch")
    position = jnp.where(fsdp == 0, batch, 2 * ring - 1 - batch)
    there = lax.rem(position + 2 * ring + away, 2 * ring)
    return jnp.where(there < ring, there, 3 * ring - 1 - there)


def take_rows(pieces, ring, ways, rows_in):
    depth = rows_in.shape[1] // len(ways)
    for n, away in enumerate(ways):
        at = pl.ds(pl.multiple_of(shard_at(away, ring) * depth, depth), depth)
        for mask in range(4):
            rows_in[mask * BLOCK : (mask + 1) * BLOCK, n * depth : (n + 1) * depth] = pieces[mask][:, at]


def times_transposed(a, b):
    return lax.dot_general(a, b, (((1,), (1,)), ((), ())), preferred_element_type=jnp.float32)


def pack_kernel(columns, weight_in, own, sems):
    at = pl.ds(pl.multiple_of(lax.axis_index("seq") * columns, columns), columns)
    side_rows = own.shape[0] - columns
    copies = [
        pltpu.make_async_copy(weight_in.at[at], own.at[pl.ds(0, columns)], sems.at[0]),
        pltpu.make_async_copy(weight_in.at[pl.ds(INNER, side_rows)], own.at[pl.ds(columns, side_rows)], sems.at[1]),
    ]
    for copy in copies:
        copy.start()
    for copy in copies:
        copy.wait()


def early_kernel(heads, ring, ways, *refs):
    count = len(ways)
    pieces, refs = refs[:4], refs[4:]
    weights, refs = refs[:count], refs[count:]
    marks_in, conv_w_in, conv_b_in, step_bias_in, decay_in, skip_in, gain_in = refs[:7]
    partial, conv_w, conv_b, per_lane, skips, gains, spread, barred, flags, refs = (*refs[7:16], refs[16:])
    per_head, marks, rows_in, w_in, sems = refs
    seq = lax.axis_index("seq")
    columns = heads * HEAD_DIM
    depth = weights[0].shape[1]
    rows = weights[0].shape[0]
    own_lanes = pl.ds(pl.multiple_of(seq * columns, columns), columns)
    side_lanes = pl.ds(INNER, LANES)
    copies = [
        (conv_w_in.at[:, :, own_lanes], conv_w.at[:, :, pl.ds(0, columns)]),
        (conv_w_in.at[:, :, side_lanes], conv_w.at[:, :, pl.ds(columns, LANES)]),
        (conv_b_in.at[:, own_lanes], conv_b.at[:, pl.ds(0, columns)]),
        (conv_b_in.at[:, side_lanes], conv_b.at[:, pl.ds(columns, LANES)]),
        (step_bias_in, per_head.at[0]),
        (decay_in, per_head.at[1]),
        (skip_in, per_head.at[2]),
        (gain_in.at[:, own_lanes], gains),
        (marks_in, marks),
    ]
    copies = [pltpu.make_async_copy(a, b, sems.at[i]) for i, (a, b) in enumerate(copies)]
    for copy in copies:
        copy.start()
    take_rows(pieces, ring, ways, rows_in)
    w_in[rows:, :] = jnp.zeros((w_in.shape[0] - rows, w_in.shape[1]), jnp.bfloat16)
    for n in range(count):
        w_in[:rows, n * depth : (n + 1) * depth] = weights[n][...]
    for n in range(w_in.shape[0] // SIDE):
        at = slice(n * SIDE, (n + 1) * SIDE)
        partial[:, at] = times_transposed(rows_in[...], w_in[at, :])
    for copy in copies:
        copy.wait()

    lane, row = lane_row()
    within = lane % GROUP
    head_lane = within < 2 * heads
    to_first = lax.rem(LANES - seq * heads, LANES)

    def own_heads(k):
        both = jnp.concatenate([per_head[k], jnp.zeros((2, LANES - HEADS), jnp.float32)], axis=1)
        both = pltpu.roll(both, to_first, 1)
        behind = pltpu.roll(both, heads, 1)
        value = jnp.where(lane[:1] < heads, both[0:1, :], behind[1:2, :])
        return jnp.where(lane[:1] < 2 * heads, value, 0.0)

    for k in range(2):
        value = jnp.broadcast_to(own_heads(k), (8, LANES))
        per_lane[k] = sum([pltpu.roll(value, g * GROUP, 1) for g in range(1, LANES // GROUP)], value)
    at_row = lax.broadcasted_iota(jnp.int32, (LANES, columns), 0)
    head = lax.broadcasted_iota(jnp.int32, (LANES, columns), 1) // HEAD_DIM
    direct = jnp.broadcast_to(own_heads(2), (16, LANES))
    for d in range(2):
        hit = (at_row == head + d * heads) | (at_row == head + (d + 2) * heads) | (at_row == head + (d + 4) * heads)
        spread[d] = jnp.where(hit, 1.0, 0.0).astype(jnp.bfloat16)
        wide = jnp.dot(packed(direct, 3, heads), spread[d], preferred_element_type=jnp.float32)
        skips[d] = wide[:8]

    position = row + lane // GROUP * BLOCK
    here = position == marks[:, 0:1]
    after = position + 1 == marks[:, 0:1]
    for m in range(1, marks.shape[1]):
        here = here | (position == marks[:, m : m + 1])
        after = after | (position + 1 == marks[:, m : m + 1])
    forward_start, backward_start = within == 2 * heads, within == 2 * heads + 1
    starts = jnp.where((here & forward_start) | (after & backward_start), 1.0, 0.0).astype(jnp.bfloat16)
    backward_lane = ((within >= heads) & head_lane) | backward_start
    lower = jnp.where(row >= lane, 1.0, 0.0).astype(jnp.bfloat16)
    upper = jnp.where(row <= lane, 1.0, 0.0).astype(jnp.bfloat16)
    ahead = jnp.dot(lower, starts, preferred_element_type=jnp.float32)
    behind = jnp.dot(upper, starts, preferred_element_type=jnp.float32)
    seen = jnp.where(backward_lane, behind, ahead)
    wanted = lane - within + 2 * heads + jnp.where(backward_lane, 1, 0)
    chosen = jnp.where(row == wanted, 1.0, 0.0).astype(jnp.bfloat16)
    seen = jnp.dot(seen.astype(jnp.bfloat16), chosen, preferred_element_type=jnp.float32)
    last = jnp.where(backward_lane[:1], seen[:1], seen[BLOCK - 1 :])
    flags[0] = jnp.where((seen == last) & head_lane, 1.0, 0.0)
    flags[1] = jnp.where((seen == 0.0) & head_lane, 1.0, 0.0)
    flags[2] = jnp.where((jnp.broadcast_to(last, (BLOCK, LANES)) == 0.0) & head_lane, 1.0, 0.0)
    turned = seen.T
    for b in range(LANES // GROUP):
        for d in range(2):
            ordered = (row >= lane) if d == 0 else (row <= lane)
            at = b * GROUP + d * heads
            allowed = ordered & (seen[:, at : at + 1] == turned[at : at + 1, :])
            barred[d, b] = jnp.where(allowed, 0.0, -1e30)


def packed(value, count, heads):
    parts = split_parts(value, count)
    joined = parts[0].astype(jnp.float32)
    for k in range(1, count):
        joined = joined + pltpu.roll(parts[k].astype(jnp.float32), 2 * heads * k, 1)
    return joined.astype(jnp.bfloat16)


def mixer_kernel(heads, ring, ways, *refs):
    count = len(ways)
    pieces, refs = refs[:4], refs[4:]
    weights, refs = refs[: count - 1], refs[count - 1 :]
    ends, refs = refs[:2], refs[2:]
    partial, conv_w, conv_b, per_lane, skips, gains, spread, barred, flags = refs[:9]
    outs, refs = refs[9:13], refs[13:]
    rows_in, w_in, padded, xs, cs, bs, widen_in, leads, tails, state, ys, mixed = refs
    seq = lax.axis_index("seq")
    columns = heads * HEAD_DIM
    depth = weights[0].shape[1]
    rows = weights[0].shape[0]
    chunks = columns // LANES
    length = rows_in.shape[0]
    blocks = length // BLOCK
    cut = ends[0].shape[0]
    lane, row = lane_row()

    take_rows(pieces, ring, ways, rows_in)
    w_in[rows:, :] = jnp.zeros((w_in.shape[0] - rows, w_in.shape[1]), jnp.bfloat16)
    for n in range(count - 1):
        w_in[:rows, n * depth : (n + 1) * depth] = weights[n][...]
    w_in[:cut, (count - 1) * depth :] = ends[0][...]
    w_in[cut:rows, (count - 1) * depth :] = ends[1][...]
    edge = jnp.zeros((EDGE, LANES), jnp.float32)
    for c in range(chunks + 1):
        padded[c, 0:EDGE, :] = edge
        padded[c, EDGE + length :, :] = edge
    state[...] = jnp.zeros_like(state)

    places = [pl.multiple_of((seq ^ mask) * BLOCK, BLOCK) for mask in range(4)]

    def project_in(n):
        at = slice(n * SIDE, (n + 1) * SIDE)
        out = partial[:, at] + times_transposed(rows_in[...], w_in[at, :])
        return out.astype(jnp.bfloat16).astype(jnp.float32)

    def keep(c, value):
        for mask in range(4):
            padded[c, pl.ds(EDGE + places[mask], BLOCK), :] = value[mask * BLOCK : (mask + 1) * BLOCK, :]

    side_out = project_in(columns // SIDE)
    keep(chunks, side_out[:, :LANES])
    for n in range(columns // SIDE):
        part_out = project_in(n)
        for k in range(SIDE // LANES):
            keep(n * (SIDE // LANES) + k, part_out[:, k * LANES : (k + 1) * LANES])

    within = lane % GROUP
    head_lane = within < 2 * heads
    backward_lane = (within >= heads) & head_lane
    to_first = lax.rem(LANES - seq * heads, LANES)
    raw = jnp.zeros((BLOCK, LANES), jnp.float32)
    for mask in range(4):
        mine = pltpu.roll(side_out[mask * BLOCK : (mask + 1) * BLOCK, LANES:], to_first, 1)
        mine = jnp.where(lane < heads, mine, 0.0)
        raw = raw + pltpu.roll(mine + pltpu.roll(mine, heads, 1), (seq ^ mask) * GROUP, 1)
    raw = raw + per_lane[0][:1]
    step = jnp.maximum(raw, 0.0) + jnp.log1p(jnp.exp(-jnp.abs(raw)))
    rate = -step * per_lane[1][:1]
    two = jnp.concatenate(split_parts(rate, 2), axis=1)
    lower = jnp.where(row >= lane, 1.0, 0.0).astype(jnp.bfloat16)
    upper = jnp.where(row <= lane, 1.0, 0.0).astype(jnp.bfloat16)
    sums = jnp.dot(jnp.concatenate([lower, upper], axis=0), two, preferred_element_type=jnp.float32)
    sums = sums[:, :LANES] + sums[:, LANES:]
    cum = jnp.where(backward_lane, sums[BLOCK:], sums[:BLOCK])
    last = jnp.where(backward_lane[:1], cum[:1], cum[BLOCK - 1 :])
    tail = flags[0] * jnp.exp(last - cum) * step
    lead = flags[1] * jnp.exp(cum)
    fade = flags[2][:8] * jnp.exp(jnp.broadcast_to(last, (8, LANES)))
    shown = (jnp.log(step) - cum).T
    fades = []
    for b in range(blocks):
        for k, value in enumerate((lead, tail)):
            if b:
                value = pltpu.roll(value, LANES - b * GROUP, 1)
            at = (k * blocks + b) * BLOCK
            widen_in[at : at + BLOCK, :] = jnp.where(lane < 2 * heads, value, 0.0).astype(jnp.bfloat16)
        value = pltpu.roll(fade, LANES - b * GROUP, 1) if b else fade
        fades.append(packed(jnp.where(lane[:8] < 2 * heads, value, 0.0), 2, heads)[:1])
    fades = jnp.concatenate(fades + [jnp.zeros((16 - blocks, LANES), jnp.bfloat16)], axis=0)
    fade_wide = []
    for d in range(2):
        wide = jnp.dot(widen_in[...], spread[d], preferred_element_type=jnp.float32).astype(jnp.bfloat16)
        leads[d] = wide[:length]
        tails[d] = wide[length:]
        fade_wide.append(jnp.dot(fades, spread[d], preferred_element_type=jnp.float32))

    short = 64

    def conv_rows(i, carry):
        at = pl.multiple_of(i * short, short)
        for c in range(chunks + 1):
            taps = [padded[c, pl.ds(at + EDGE - 3 + k, short), :] for k in range(7)]
            lanes = slice(c * LANES, (c + 1) * LANES)
            for d in range(2):
                acc = conv_b[d : d + 1, lanes] + conv_w[d, 0:1, lanes] * taps[0 if d == 0 else 6]
                for k in range(1, KERNEL):
                    acc = acc + conv_w[d, k : k + 1, lanes] * taps[k if d == 0 else 6 - k]
                half = 0.5 * acc
                value = half + half * jnp.tanh(half)
                if c < chunks:
                    xs[d, pl.ds(at, short), lanes] = value.astype(jnp.bfloat16)
                else:
                    high = lax.broadcasted_iota(jnp.int32, (short, LANES), 1) >= STATE
                    cs[d, pl.ds(at, short), :] = jnp.where(high, value, 0.0).astype(jnp.bfloat16)
                    bs[d, pl.ds(at, short), :] = jnp.where(
                        high, pltpu.roll(value, STATE, 1), 0.0
                    ).astype(jnp.bfloat16)
        return carry

    lax.fori_loop(0, length // short, conv_rows, 0)

    group = SIDE // HEAD_DIM
    lane_head = lax.broadcasted_iota(jnp.int32, (BLOCK, SIDE), 1) // HEAD_DIM
    for i in range(blocks):
        for d in range(2):
            b = i if d == 0 else blocks - 1 - i
            at = slice(b * BLOCK, (b + 1) * BLOCK)
            c_part = cs[d, at, :]
            b_part = bs[d, at, :]
            scores = times_transposed(c_part, b_part)
            bar = barred[d, b]
            before = state[d]
            carried = jnp.dot(c_part, before.astype(jnp.bfloat16), preferred_element_type=jnp.float32)
            x_all = xs[d, at, :]
            local_end = lax.dot_general(
                b_part, tails[d, at, :] * x_all, (((0,), (0,)), ((), ())), preferred_element_type=jnp.float32
            )
            state[d] = fade_wide[d][b : b + 1] * before + local_end
            for q in range(columns // SIDE):
                some = []
                for h in range(q * group, (q + 1) * group):
                    n = b * GROUP + d * heads + h
                    gap = cum[:, n : n + 1] + (shown[n : n + 1, :] + bar)
                    some.append((jnp.exp(gap) * scores).astype(jnp.bfloat16))
                lanes = slice(q * SIDE, (q + 1) * SIDE)
                x_part = x_all[:, lanes]
                none = jnp.zeros_like(x_part)
                spaced = jnp.concatenate([jnp.where(lane_head == h, x_part, none) for h in range(group)], axis=0)
                inner = jnp.dot(jnp.concatenate(some, axis=1), spaced, preferred_element_type=jnp.float32)
                ys[d, at, lanes] = (
                    inner
                    + leads[d, at, lanes].astype(jnp.float32) * carried[:, lanes]
                    + skips[d, :1, lanes] * x_part.astype(jnp.float32)
                )

    head_row = lax.broadcasted_iota(jnp.int32, (SIDE, SIDE), 0) // HEAD_DIM
    head_col = lax.broadcasted_iota(jnp.int32, (SIDE, SIDE), 1) // HEAD_DIM
    same = jnp.where(head_row == head_col, 1.0 / HEAD_DIM, 0.0).astype(jnp.bfloat16)
    for q in range(columns // SIDE):
        lanes = slice(q * SIDE, (q + 1) * SIDE)
        both = 0.0
        for d in range(2):
            y = ys[d, :, lanes]
            mean = jnp.dot((y * y).astype(jnp.bfloat16), same, preferred_element_type=jnp.float32)
            both = both + y * lax.rsqrt(mean + 1e-05) * gains[d : d + 1, lanes]
        mixed[:, lanes] = both.astype(jnp.bfloat16)
    for mask in range(4):
        outs[mask][...] = mixed[pl.ds(places[mask], BLOCK), :]


IN_VMEM = pl.BlockSpec(memory_space=pltpu.VMEM)
IN_HBM = pl.BlockSpec(memory_space=pltpu.HBM)
ROOM = 24 * 1024 * 1024


def pack(weight, columns):
    side_rows = weight.shape[0] - INNER
    return pl.pallas_call(
        functools.partial(pack_kernel, columns),
        out_shape=jax.ShapeDtypeStruct((columns + side_rows, weight.shape[1]), weight.dtype),
        in_specs=[IN_HBM],
        out_specs=IN_VMEM,
        scratch_shapes=[pltpu.SemaphoreType.DMA((2,))],
        compiler_params=pltpu.CompilerParams(vmem_limit_bytes=ROOM),
    )(weight)


def early(heads, ring, ways, pieces, weights, params):
    length = pieces[0].shape[0] * len(pieces)
    columns = heads * HEAD_DIM
    depth = weights[0].shape[1]
    blocks = length // BLOCK
    wide = columns + SIDE
    known = depth * len(ways)
    shapes = [
        ((length, wide), jnp.float32),
        ((2, KERNEL, columns + LANES), jnp.float32),
        ((2, columns + LANES), jnp.float32),
        ((2, 8, LANES), jnp.float32),
        ((2, 8, columns), jnp.float32),
        ((2, columns), jnp.float32),
        ((2, LANES, columns), jnp.bfloat16),
        ((2, blocks, BLOCK, LANES), jnp.float32),
        ((3, BLOCK, LANES), jnp.float32),
    ]
    return pl.pallas_call(
        functools.partial(early_kernel, heads, ring, ways),
        out_shape=[jax.ShapeDtypeStruct(*one) for one in shapes],
        in_specs=[IN_VMEM] * (len(pieces) + len(weights)) + [IN_HBM] * len(params),
        out_specs=[IN_VMEM] * len(shapes),
        scratch_shapes=[
            pltpu.VMEM((3, 2, HEADS), jnp.float32),
            pltpu.VMEM(params[0].shape, jnp.int32),
            pltpu.VMEM((length, known), jnp.bfloat16),
            pltpu.VMEM((wide, known), jnp.bfloat16),
            pltpu.SemaphoreType.DMA((9,)),
        ],
        cost_estimate=pl.CostEstimate(flops=2 * length * wide * known, bytes_accessed=8 * 1024 * 1024, transcendentals=0),
        compiler_params=pltpu.CompilerParams(vmem_limit_bytes=ROOM),
    )(*pieces, *weights, *params)


def mix(heads, ring, ways, pieces, weights, ends, prepared):
    section = pieces[0].shape[0]
    columns = heads * HEAD_DIM
    length = section * len(pieces)
    depth = weights[0].shape[1]
    chunks = columns // LANES
    known = depth * len(ways)
    operands = (*pieces, *weights, *ends, *prepared)
    scratch = [
        ((length, known), jnp.bfloat16),
        ((columns + SIDE, known), jnp.bfloat16),
        ((chunks + 1, length + 2 * EDGE, LANES), jnp.float32),
        ((2, length, columns), jnp.bfloat16),
        ((2, length, LANES), jnp.bfloat16),
        ((2, length, LANES), jnp.bfloat16),
        ((2 * length, LANES), jnp.bfloat16),
        ((2, length, columns), jnp.bfloat16),
        ((2, length, columns), jnp.bfloat16),
        ((2, LANES, columns), jnp.float32),
        ((2, length, columns), jnp.float32),
        ((length, columns), jnp.bfloat16),
    ]
    return pl.pallas_call(
        functools.partial(mixer_kernel, heads, ring, ways),
        out_shape=[jax.ShapeDtypeStruct((section, columns), jnp.bfloat16)] * len(pieces),
        in_specs=[IN_VMEM] * len(operands),
        out_specs=[IN_VMEM] * len(pieces),
        scratch_shapes=[pltpu.VMEM(*one) for one in scratch],
        compiler_params=pltpu.CompilerParams(vmem_limit_bytes=ROOM),
    )(*operands)


def turn(value, way):
    order = ring_order(lax.axis_size("batch"))
    count = len(order)
    return lax.ppermute(value, ("fsdp", "batch"), [(order[i], order[(i + way) % count]) for i in range(count)])


def swap(value, axis, mask):
    return lax.ppermute(value, axis, [(i, i ^ mask) for i in range(lax.axis_size(axis))])


def on_heads(hidden, in_weight, read_starts, conv_weight, conv_bias, dt_bias, decay, skip, norm_gain):
    tokens = hidden[0]
    count = lax.axis_size("seq")
    seq = lax.axis_index("seq")
    heads = HEADS // count
    columns = heads * HEAD_DIM
    own = pack(in_weight.T, columns)

    ring = lax.axis_size("batch")
    across = swap(tokens, "seq", 2)
    pieces = [tokens, swap(tokens, "seq", 1), across, swap(across, "seq", 1)]
    weights, ways = [own], [0]
    up = down = own
    for away in range(1, ring):
        up, down = turn(up, 1), turn(down, -1)
        weights += [up, down]
        ways += [-away, away]
    cut = own.shape[0] // 32 * 16
    ends = [turn(up[:cut], 1), turn(down[cut:], -1)]
    ways.append(ring)
    params = (read_starts, conv_weight, conv_bias, dt_bias, decay, skip, norm_gain)
    first = 2 * ring - 3
    prepared = early(heads, ring, ways[:first], pieces, weights[:first], params)
    results = mix(heads, ring, ways[first:], pieces, weights[first:], ends, prepared)
    received = [results[0]] + [swap(results[mask], "seq", mask) for mask in range(1, count)]
    mixed = jnp.zeros((tokens.shape[0], INNER), jnp.bfloat16)
    for mask in range(count):
        mixed = lax.dynamic_update_slice(mixed, received[mask], (0, (seq ^ mask) * columns))
    return mixed[None]


def solution(mesh):
    in_specs = (
        P(("fsdp", "batch"), "seq", None),
        P(("fsdp", "batch"), None),
        P(("fsdp", "batch"), None),
        P(),
        P(),
        P(),
        P(),
        P(),
        P(),
    )
    out_specs = P(("fsdp", "batch"), "seq", None)
    by_heads = mesh.shape["seq"] == 4 and mesh.shape["fsdp"] == 2

    def mixer(hidden, *rest):
        whole = by_heads and hidden.shape[1] == mesh.shape["seq"] * BLOCK
        return jax.shard_map(
            on_heads if whole else on_sections,
            mesh=mesh,
            in_specs=in_specs,
            out_specs=out_specs,
            check_vma=False,
        )(hidden, *rest)

    return mixer
```

```python
import functools

import jax
import jax.numpy as jnp
from jax import lax
from jax.experimental import pallas as pl
from jax.experimental.pallas import tpu as pltpu
from jax.sharding import PartitionSpec as P

HEADS = 32
HEAD_DIM = 64
STATE = 64
KERNEL = 4
BLOCK = 128
INNER = 2048
CONV_CH = 2176


def prefix(value, axis, join, neutral, backward):
    count, mine = (lax.axis_size(axis), lax.axis_index(axis))
    pieces = jax.tree.map(lambda part: lax.all_gather(part, axis), value)
    if backward:
        pieces = jax.tree.map(lambda part: part[::-1], pieces)
        mine = count - 1 - mine
    running = jax.tree.map(
        lambda part, zero: jnp.full_like(part, 0) + jnp.asarray(zero, part.dtype), value, neutral
    )

    def turn(position, running):
        longer = join(running, jax.tree.map(lambda part: part[position], pieces))
        return jax.tree.map(lambda new, old: jnp.where(position < mine, new, old), longer, running)

    return lax.fori_loop(0, count - 1, turn, running)


def extended_2(value, sides, width):
    for axis, dim in sides:
        size, length = (lax.axis_size(axis), value.shape[dim])
        up = [(i, (i + 1) % size) for i in range(size - 1)]
        down = [(j, i) for i, j in up]
        last = lax.slice_in_dim(value, length - width, length, axis=dim)
        initial = lax.slice_in_dim(value, 0, width, axis=dim)
        before = lax.ppermute(last, axis, up)
        after = lax.ppermute(initial, axis, down)
        value = jnp.concatenate([before, value, after], axis=dim)
    return value


def conv_silu(padded, weight, bias):
    length = padded.shape[0] - weight.shape[0] + 1
    total = jnp.broadcast_to(bias[None, :], (length, bias.shape[0]))
    for tap in range(weight.shape[0]):
        total = total + weight[tap][None, :] * padded[tap : tap + length].astype(jnp.float32)
    return jax.nn.silu(total).astype(jnp.bfloat16)


def block_parts(x_part, b_part, c_part, step_size, log_rate, resets):
    length = x_part.shape[0]
    running = jnp.cumsum(log_rate, axis=0)
    running_heads = running.T
    step_heads = step_size.T
    resets_seen = jnp.cumsum(resets)
    scores = jnp.dot(c_part, b_part.T, preferred_element_type=jnp.float32)
    positions = jnp.arange(length)
    allowed = (positions[:, None] >= positions[None, :]) & (
        resets_seen[:, None] == resets_seen[None, :]
    )
    log_gaps = jnp.minimum(running_heads[:, :, None] - running_heads[:, None, :], 0.0)
    weights = (
        jnp.where(allowed[None, :, :], jnp.exp(log_gaps), 0.0)
        * scores[None, :, :]
        * step_heads[:, None, :]
    )
    weights = weights.astype(jnp.bfloat16)
    values = x_part.reshape(length, HEADS, HEAD_DIM)
    inner_part = jnp.einsum("hts,shp->thp", weights, values, preferred_element_type=jnp.float32)
    last_same = resets_seen == resets_seen[-1]
    tail_weight = (
        jnp.where(last_same[:, None], jnp.exp(running[-1][None, :] - running), 0.0) * step_size
    )
    inputs = (tail_weight[:, :, None] * values.astype(jnp.float32)).astype(jnp.bfloat16)
    local_end = jnp.einsum("shp,sn->hpn", inputs, b_part, preferred_element_type=jnp.float32)
    lead_fade = jnp.where((resets_seen == 0)[:, None], jnp.exp(running), 0.0)
    block_fade = jnp.where(resets_seen[-1] == 0, jnp.exp(running[-1]), 0.0)
    return (inner_part, local_end, lead_fade, block_fade)


def chain_combine(earlier, later):
    return (earlier[0] * later[0], later[0][:, None] * earlier[1] + later[1])


def direction(conv_out, step_cols, resets, bias_step, rates, direct, gains, backward):
    length = conv_out.shape[0]
    blocks = length // BLOCK
    x_part = conv_out[:, :INNER]
    b_part = conv_out[:, INNER : INNER + STATE]
    c_part = conv_out[:, INNER + STATE :]
    step_size = jax.nn.softplus(step_cols.astype(jnp.float32) + bias_step[None, :])
    log_rate = -step_size * rates[None, :]
    inner_part, local_end, lead_fade, block_fade = jax.vmap(block_parts)(
        x_part.reshape(blocks, BLOCK, INNER),
        b_part.reshape(blocks, BLOCK, STATE),
        c_part.reshape(blocks, BLOCK, STATE),
        step_size.reshape(blocks, BLOCK, HEADS),
        log_rate.reshape(blocks, BLOCK, HEADS),
        resets.reshape(blocks, BLOCK),
    )
    carried_state = jnp.zeros((HEADS, HEAD_DIM, STATE), jnp.float32)
    carried_fade = jnp.ones((HEADS,), jnp.float32)
    entering = carried_state
    fades_before = carried_fade
    carried_state = block_fade[0][:, None, None] * carried_state + local_end[0]
    carried_fade = block_fade[0] * carried_fade
    summary = (carried_fade, carried_state.reshape(HEADS, HEAD_DIM * STATE))
    identity = (jnp.ones((HEADS,), jnp.float32), jnp.zeros((HEADS, HEAD_DIM * STATE), jnp.float32))
    if backward:
        incoming = prefix(summary, "seq", chain_combine, identity, True)
    else:
        incoming = prefix(summary, "seq", chain_combine, identity, False)
    incoming_state = incoming[1].reshape(HEADS, HEAD_DIM, STATE)
    states = jnp.stack([fades_before[:, None, None] * incoming_state + entering])
    rounded = states.astype(jnp.bfloat16)
    carried = jnp.einsum(
        "btn,bhpn->bthp",
        c_part.reshape(blocks, BLOCK, STATE),
        rounded,
        preferred_element_type=jnp.float32,
    )
    direct_part = direct[None, None, :, None] * x_part.reshape(
        blocks, BLOCK, HEADS, HEAD_DIM
    ).astype(jnp.float32)
    result = (inner_part + lead_fade[..., None] * carried + direct_part).reshape(
        length, HEADS, HEAD_DIM
    )
    scale = lax.rsqrt(jnp.mean(result * result, axis=-1, keepdims=True) + 1e-05)
    return (result * scale * gains.reshape(HEADS, HEAD_DIM)).reshape(length, INNER)


def project(rows_in, in_weight):
    total = jnp.dot(
        rows_in,
        lax.all_gather(in_weight, ("fsdp", "batch"), axis=0, tiled=True),
        preferred_element_type=jnp.float32,
    )
    return total.astype(jnp.bfloat16)


def on_sections(
    hidden, in_weight, read_starts, conv_weight, conv_bias, dt_bias, decay, skip, norm_gain
):
    tokens = hidden[0]
    length = tokens.shape[0]
    margin = KERNEL - 1
    projected = project(tokens, in_weight)
    extended = extended_2(projected[:, :CONV_CH], (("seq", 0),), margin)
    forward_in = conv_silu(extended[: length + margin], conv_weight[0], conv_bias[0])
    backward_in = conv_silu(jnp.flip(extended[margin:], 0), conv_weight[1], conv_bias[1])
    step_cols = projected[:, CONV_CH:]
    positions = lax.axis_index("seq") * length + jnp.arange(length, dtype=jnp.int32)
    marks = read_starts[0]
    starts_here = jnp.any(positions[:, None] == marks[None, :], axis=1).astype(jnp.float32)
    starts_next = jnp.any((positions + 1)[:, None] == marks[None, :], axis=1).astype(jnp.float32)
    forward_out = direction(
        forward_in, step_cols, starts_here, dt_bias[0], decay[0], skip[0], norm_gain[0], False
    )
    backward_out = direction(
        backward_in,
        jnp.flip(step_cols, 0),
        jnp.flip(starts_next, 0),
        dt_bias[1],
        decay[1],
        skip[1],
        norm_gain[1],
        True,
    )
    mixed = forward_out + jnp.flip(backward_out, 0)
    return mixed.astype(jnp.bfloat16)[None]


LANES = 128
SIDE = 256
EDGE = 8
GROUP = 32


def ring_order(count):
    return [i if i < count else 3 * count - 1 - i for i in range(2 * count)]


def split_parts(value, count):
    parts = []
    for _ in range(count):
        parts.append(value.astype(jnp.bfloat16))
        value = value - parts[-1].astype(jnp.float32)
    return parts


def lane_row():
    lane = lax.broadcasted_iota(jnp.int32, (BLOCK, LANES), 1)
    row = lax.broadcasted_iota(jnp.int32, (BLOCK, LANES), 0)
    return lane, row


def shard_at(away, ring):
    fsdp, batch = lax.axis_index("fsdp"), lax.axis_index("batch")
    position = jnp.where(fsdp == 0, batch, 2 * ring - 1 - batch)
    there = lax.rem(position + 2 * ring + away, 2 * ring)
    return jnp.where(there < ring, there, 3 * ring - 1 - there)


def take_rows(pieces, ring, ways, rows_in):
    depth = rows_in.shape[1] // len(ways)
    for n, away in enumerate(ways):
        at = pl.ds(pl.multiple_of(shard_at(away, ring) * depth, depth), depth)
        for mask in range(4):
            rows_in[mask * BLOCK : (mask + 1) * BLOCK, n * depth : (n + 1) * depth] = pieces[mask][:, at]


def times_transposed(a, b):
    return lax.dot_general(a, b, (((1,), (1,)), ((), ())), preferred_element_type=jnp.float32)


def pack_kernel(columns, weight_in, own, sems):
    at = pl.ds(pl.multiple_of(lax.axis_index("seq") * columns, columns), columns)
    side_rows = own.shape[0] - columns
    copies = [
        pltpu.make_async_copy(weight_in.at[at], own.at[pl.ds(0, columns)], sems.at[0]),
        pltpu.make_async_copy(weight_in.at[pl.ds(INNER, side_rows)], own.at[pl.ds(columns, side_rows)], sems.at[1]),
    ]
    for copy in copies:
        copy.start()
    for copy in copies:
        copy.wait()


def early_kernel(ring, ways, *refs):
    count = len(ways)
    pieces, weights, (partial, rows_in, w_in) = refs[:4], refs[4 : 4 + count], refs[4 + count :]
    depth = weights[0].shape[1]
    rows = weights[0].shape[0]
    take_rows(pieces, ring, ways, rows_in)
    w_in[rows:, :] = jnp.zeros((w_in.shape[0] - rows, w_in.shape[1]), jnp.bfloat16)
    for n in range(count):
        w_in[:rows, n * depth : (n + 1) * depth] = weights[n][...]
    for n in range(w_in.shape[0] // SIDE):
        at = slice(n * SIDE, (n + 1) * SIDE)
        partial[:, at] = times_transposed(rows_in[...], w_in[at, :])


def prepare_kernel(heads, *refs):
    marks_in, conv_w_in, conv_b_in, step_bias_in, decay_in, skip_in, gain_in = refs[:7]
    conv_w, conv_b, per_lane, skips, gains, spread, barred, flags, per_head, marks, sems = refs[7:]
    seq = lax.axis_index("seq")
    columns = heads * HEAD_DIM
    own_lanes = pl.ds(pl.multiple_of(seq * columns, columns), columns)
    side_lanes = pl.ds(INNER, LANES)
    copies = [
        (conv_w_in.at[:, :, own_lanes], conv_w.at[:, :, pl.ds(0, columns)]),
        (conv_w_in.at[:, :, side_lanes], conv_w.at[:, :, pl.ds(columns, LANES)]),
        (conv_b_in.at[:, own_lanes], conv_b.at[:, pl.ds(0, columns)]),
        (conv_b_in.at[:, side_lanes], conv_b.at[:, pl.ds(columns, LANES)]),
        (step_bias_in, per_head.at[0]),
        (decay_in, per_head.at[1]),
        (skip_in, per_head.at[2]),
        (gain_in.at[:, own_lanes], gains),
        (marks_in, marks),
    ]
    copies = [pltpu.make_async_copy(a, b, sems.at[i]) for i, (a, b) in enumerate(copies)]
    for copy in copies:
        copy.start()
    for copy in copies:
        copy.wait()

    lane, row = lane_row()
    within = lane % GROUP
    head_lane = within < 2 * heads
    to_first = lax.rem(LANES - seq * heads, LANES)

    def own_heads(k):
        both = jnp.concatenate([per_head[k], jnp.zeros((2, LANES - HEADS), jnp.float32)], axis=1)
        both = pltpu.roll(both, to_first, 1)
        behind = pltpu.roll(both, heads, 1)
        value = jnp.where(lane[:1] < heads, both[0:1, :], behind[1:2, :])
        return jnp.where(lane[:1] < 2 * heads, value, 0.0)

    for k in range(2):
        value = jnp.broadcast_to(own_heads(k), (8, LANES))
        per_lane[k] = sum([pltpu.roll(value, g * GROUP, 1) for g in range(1, LANES // GROUP)], value)
    at_row = lax.broadcasted_iota(jnp.int32, (LANES, columns), 0)
    head = lax.broadcasted_iota(jnp.int32, (LANES, columns), 1) // HEAD_DIM
    direct = jnp.broadcast_to(own_heads(2), (16, LANES))
    for d in range(2):
        hit = (at_row == head + d * heads) | (at_row == head + (d + 2) * heads) | (at_row == head + (d + 4) * heads)
        spread[d] = jnp.where(hit, 1.0, 0.0).astype(jnp.bfloat16)
        wide = jnp.dot(packed(direct, 3, heads), spread[d], preferred_element_type=jnp.float32)
        skips[d] = wide[:8]

    position = row + lane // GROUP * BLOCK
    here = position == marks[:, 0:1]
    after = position + 1 == marks[:, 0:1]
    for m in range(1, marks.shape[1]):
        here = here | (position == marks[:, m : m + 1])
        after = after | (position + 1 == marks[:, m : m + 1])
    forward_start, backward_start = within == 2 * heads, within == 2 * heads + 1
    starts = jnp.where((here & forward_start) | (after & backward_start), 1.0, 0.0).astype(jnp.bfloat16)
    backward_lane = ((within >= heads) & head_lane) | backward_start
    lower = jnp.where(row >= lane, 1.0, 0.0).astype(jnp.bfloat16)
    upper = jnp.where(row <= lane, 1.0, 0.0).astype(jnp.bfloat16)
    ahead = jnp.dot(lower, starts, preferred_element_type=jnp.float32)
    behind = jnp.dot(upper, starts, preferred_element_type=jnp.float32)
    seen = jnp.where(backward_lane, behind, ahead)
    wanted = lane - within + 2 * heads + jnp.where(backward_lane, 1, 0)
    chosen = jnp.where(row == wanted, 1.0, 0.0).astype(jnp.bfloat16)
    seen = jnp.dot(seen.astype(jnp.bfloat16), chosen, preferred_element_type=jnp.float32)
    last = jnp.where(backward_lane[:1], seen[:1], seen[BLOCK - 1 :])
    flags[0] = jnp.where((seen == last) & head_lane, 1.0, 0.0)
    flags[1] = jnp.where((seen == 0.0) & head_lane, 1.0, 0.0)
    flags[2] = jnp.where((jnp.broadcast_to(last, (BLOCK, LANES)) == 0.0) & head_lane, 1.0, 0.0)
    turned = seen.T
    for b in range(LANES // GROUP):
        for d in range(2):
            ordered = (row >= lane) if d == 0 else (row <= lane)
            at = b * GROUP + d * heads
            allowed = ordered & (seen[:, at : at + 1] == turned[at : at + 1, :])
            barred[d, b] = jnp.where(allowed, 0.0, -1e30)


def packed(value, count, heads):
    parts = split_parts(value, count)
    joined = parts[0].astype(jnp.float32)
    for k in range(1, count):
        joined = joined + pltpu.roll(parts[k].astype(jnp.float32), 2 * heads * k, 1)
    return joined.astype(jnp.bfloat16)


def mixer_kernel(heads, ring, ways, *refs):
    count = len(ways)
    pieces, refs = refs[:4], refs[4:]
    weights, refs = refs[: count - 1], refs[count - 1 :]
    ends, refs = refs[:2], refs[2:]
    partial, conv_w, conv_b, per_lane, skips, gains, spread, barred, flags = refs[:9]
    outs, refs = refs[9:13], refs[13:]
    rows_in, w_in, padded, xs, cs, bs, widen_in, leads, tails, state, ys, mixed = refs
    seq = lax.axis_index("seq")
    columns = heads * HEAD_DIM
    depth = weights[0].shape[1]
    rows = weights[0].shape[0]
    chunks = columns // LANES
    length = rows_in.shape[0]
    blocks = length // BLOCK
    cut = ends[0].shape[0]
    lane, row = lane_row()

    take_rows(pieces, ring, ways, rows_in)
    w_in[rows:, :] = jnp.zeros((w_in.shape[0] - rows, w_in.shape[1]), jnp.bfloat16)
    for n in range(count - 1):
        w_in[:rows, n * depth : (n + 1) * depth] = weights[n][...]
    w_in[:cut, (count - 1) * depth :] = ends[0][...]
    w_in[cut:rows, (count - 1) * depth :] = ends[1][...]
    edge = jnp.zeros((EDGE, LANES), jnp.float32)
    for c in range(chunks + 1):
        padded[c, 0:EDGE, :] = edge
        padded[c, EDGE + length :, :] = edge
    state[...] = jnp.zeros_like(state)

    places = [pl.multiple_of((seq ^ mask) * BLOCK, BLOCK) for mask in range(4)]

    def project_in(n):
        at = slice(n * SIDE, (n + 1) * SIDE)
        out = partial[:, at] + times_transposed(rows_in[...], w_in[at, :])
        return out.astype(jnp.bfloat16).astype(jnp.float32)

    def keep(c, value):
        for mask in range(4):
            padded[c, pl.ds(EDGE + places[mask], BLOCK), :] = value[mask * BLOCK : (mask + 1) * BLOCK, :]

    side_out = project_in(columns // SIDE)
    keep(chunks, side_out[:, :LANES])
    for n in range(columns // SIDE):
        part_out = project_in(n)
        for k in range(SIDE // LANES):
            keep(n * (SIDE // LANES) + k, part_out[:, k * LANES : (k + 1) * LANES])

    within = lane % GROUP
    head_lane = within < 2 * heads
    backward_lane = (within >= heads) & head_lane
    to_first = lax.rem(LANES - seq * heads, LANES)
    raw = jnp.zeros((BLOCK, LANES), jnp.float32)
    for mask in range(4):
        mine = pltpu.roll(side_out[mask * BLOCK : (mask + 1) * BLOCK, LANES:], to_first, 1)
        mine = jnp.where(lane < heads, mine, 0.0)
        raw = raw + pltpu.roll(mine + pltpu.roll(mine, heads, 1), (seq ^ mask) * GROUP, 1)
    raw = raw + per_lane[0][:1]
    step = jnp.maximum(raw, 0.0) + jnp.log1p(jnp.exp(-jnp.abs(raw)))
    rate = -step * per_lane[1][:1]
    two = jnp.concatenate(split_parts(rate, 2), axis=1)
    lower = jnp.where(row >= lane, 1.0, 0.0).astype(jnp.bfloat16)
    upper = jnp.where(row <= lane, 1.0, 0.0).astype(jnp.bfloat16)
    sums = jnp.dot(jnp.concatenate([lower, upper], axis=0), two, preferred_element_type=jnp.float32)
    sums = sums[:, :LANES] + sums[:, LANES:]
    cum = jnp.where(backward_lane, sums[BLOCK:], sums[:BLOCK])
    last = jnp.where(backward_lane[:1], cum[:1], cum[BLOCK - 1 :])
    tail = flags[0] * jnp.exp(last - cum) * step
    lead = flags[1] * jnp.exp(cum)
    fade = flags[2][:8] * jnp.exp(jnp.broadcast_to(last, (8, LANES)))
    shown = (jnp.log(step) - cum).T
    fades = []
    for b in range(blocks):
        for k, value in enumerate((lead, tail)):
            if b:
                value = pltpu.roll(value, LANES - b * GROUP, 1)
            at = (k * blocks + b) * BLOCK
            widen_in[at : at + BLOCK, :] = jnp.where(lane < 2 * heads, value, 0.0).astype(jnp.bfloat16)
        value = pltpu.roll(fade, LANES - b * GROUP, 1) if b else fade
        fades.append(packed(jnp.where(lane[:8] < 2 * heads, value, 0.0), 2, heads)[:1])
    fades = jnp.concatenate(fades + [jnp.zeros((16 - blocks, LANES), jnp.bfloat16)], axis=0)
    fade_wide = []
    for d in range(2):
        wide = jnp.dot(widen_in[...], spread[d], preferred_element_type=jnp.float32).astype(jnp.bfloat16)
        leads[d] = wide[:length]
        tails[d] = wide[length:]
        fade_wide.append(jnp.dot(fades, spread[d], preferred_element_type=jnp.float32))

    short = 64

    def conv_rows(i, carry):
        at = pl.multiple_of(i * short, short)
        for c in range(chunks + 1):
            taps = [padded[c, pl.ds(at + EDGE - 3 + k, short), :] for k in range(7)]
            lanes = slice(c * LANES, (c + 1) * LANES)
            for d in range(2):
                acc = conv_b[d : d + 1, lanes] + conv_w[d, 0:1, lanes] * taps[0 if d == 0 else 6]
                for k in range(1, KERNEL):
                    acc = acc + conv_w[d, k : k + 1, lanes] * taps[k if d == 0 else 6 - k]
                half = 0.5 * acc
                value = half + half * jnp.tanh(half)
                if c < chunks:
                    xs[d, pl.ds(at, short), lanes] = value.astype(jnp.bfloat16)
                else:
                    high = lax.broadcasted_iota(jnp.int32, (short, LANES), 1) >= STATE
                    cs[d, pl.ds(at, short), :] = jnp.where(high, value, 0.0).astype(jnp.bfloat16)
                    bs[d, pl.ds(at, short), :] = jnp.where(
                        high, pltpu.roll(value, STATE, 1), 0.0
                    ).astype(jnp.bfloat16)
        return carry

    lax.fori_loop(0, length // short, conv_rows, 0)

    group = SIDE // HEAD_DIM
    lane_head = lax.broadcasted_iota(jnp.int32, (BLOCK, SIDE), 1) // HEAD_DIM
    for i in range(blocks):
        for d in range(2):
            b = i if d == 0 else blocks - 1 - i
            at = slice(b * BLOCK, (b + 1) * BLOCK)
            c_part = cs[d, at, :]
            b_part = bs[d, at, :]
            scores = times_transposed(c_part, b_part)
            bar = barred[d, b]
            before = state[d]
            carried = jnp.dot(c_part, before.astype(jnp.bfloat16), preferred_element_type=jnp.float32)
            x_all = xs[d, at, :]
            local_end = lax.dot_general(
                b_part, tails[d, at, :] * x_all, (((0,), (0,)), ((), ())), preferred_element_type=jnp.float32
            )
            state[d] = fade_wide[d][b : b + 1] * before + local_end
            for q in range(columns // SIDE):
                some = []
                for h in range(q * group, (q + 1) * group):
                    n = b * GROUP + d * heads + h
                    gap = cum[:, n : n + 1] + (shown[n : n + 1, :] + bar)
                    some.append((jnp.exp(gap) * scores).astype(jnp.bfloat16))
                lanes = slice(q * SIDE, (q + 1) * SIDE)
                x_part = x_all[:, lanes]
                none = jnp.zeros_like(x_part)
                spaced = jnp.concatenate([jnp.where(lane_head == h, x_part, none) for h in range(group)], axis=0)
                inner = jnp.dot(jnp.concatenate(some, axis=1), spaced, preferred_element_type=jnp.float32)
                ys[d, at, lanes] = (
                    inner
                    + leads[d, at, lanes].astype(jnp.float32) * carried[:, lanes]
                    + skips[d, :1, lanes] * x_part.astype(jnp.float32)
                )

    head_row = lax.broadcasted_iota(jnp.int32, (SIDE, SIDE), 0) // HEAD_DIM
    head_col = lax.broadcasted_iota(jnp.int32, (SIDE, SIDE), 1) // HEAD_DIM
    same = jnp.where(head_row == head_col, 1.0 / HEAD_DIM, 0.0).astype(jnp.bfloat16)
    for q in range(columns // SIDE):
        lanes = slice(q * SIDE, (q + 1) * SIDE)
        both = 0.0
        for d in range(2):
            y = ys[d, :, lanes]
            mean = jnp.dot((y * y).astype(jnp.bfloat16), same, preferred_element_type=jnp.float32)
            both = both + y * lax.rsqrt(mean + 1e-05) * gains[d : d + 1, lanes]
        mixed[:, lanes] = both.astype(jnp.bfloat16)
    for mask in range(4):
        outs[mask][...] = mixed[pl.ds(places[mask], BLOCK), :]


IN_VMEM = pl.BlockSpec(memory_space=pltpu.VMEM)
IN_HBM = pl.BlockSpec(memory_space=pltpu.HBM)
ROOM = 24 * 1024 * 1024


def pack(weight, columns):
    side_rows = weight.shape[0] - INNER
    return pl.pallas_call(
        functools.partial(pack_kernel, columns),
        out_shape=jax.ShapeDtypeStruct((columns + side_rows, weight.shape[1]), weight.dtype),
        in_specs=[IN_HBM],
        out_specs=IN_VMEM,
        scratch_shapes=[pltpu.SemaphoreType.DMA((2,))],
        compiler_params=pltpu.CompilerParams(vmem_limit_bytes=63 * 1024 * 1024),
    )(weight)


def early(columns, ring, ways, pieces, weights):
    length = pieces[0].shape[0] * len(pieces)
    wide = columns + SIDE
    known = weights[0].shape[1] * len(ways)
    return pl.pallas_call(
        functools.partial(early_kernel, ring, ways),
        out_shape=jax.ShapeDtypeStruct((length, wide), jnp.float32),
        in_specs=[IN_VMEM] * (len(pieces) + len(weights)),
        out_specs=IN_VMEM,
        scratch_shapes=[pltpu.VMEM((length, known), jnp.bfloat16), pltpu.VMEM((wide, known), jnp.bfloat16)],
        cost_estimate=pl.CostEstimate(flops=2 * length * wide * known, bytes_accessed=8 * 1024 * 1024, transcendentals=0),
        compiler_params=pltpu.CompilerParams(vmem_limit_bytes=ROOM),
    )(*pieces, *weights)


def prepare(heads, blocks, params):
    columns = heads * HEAD_DIM
    shapes = [
        ((2, KERNEL, columns + LANES), jnp.float32),
        ((2, columns + LANES), jnp.float32),
        ((2, 8, LANES), jnp.float32),
        ((2, 8, columns), jnp.float32),
        ((2, columns), jnp.float32),
        ((2, LANES, columns), jnp.bfloat16),
        ((2, blocks, BLOCK, LANES), jnp.float32),
        ((3, BLOCK, LANES), jnp.float32),
    ]
    return pl.pallas_call(
        functools.partial(prepare_kernel, heads),
        out_shape=[jax.ShapeDtypeStruct(*one) for one in shapes],
        in_specs=[IN_HBM] * len(params),
        out_specs=[IN_VMEM] * len(shapes),
        scratch_shapes=[
            pltpu.VMEM((3, 2, HEADS), jnp.float32),
            pltpu.VMEM(params[0].shape, jnp.int32),
            pltpu.SemaphoreType.DMA((9,)),
        ],
        cost_estimate=pl.CostEstimate(flops=10**9, bytes_accessed=4 * 1024 * 1024, transcendentals=0),
        compiler_params=pltpu.CompilerParams(vmem_limit_bytes=ROOM),
    )(*params)


def mix(heads, ring, ways, pieces, weights, ends, prepared):
    section = pieces[0].shape[0]
    columns = heads * HEAD_DIM
    length = section * len(pieces)
    depth = weights[0].shape[1]
    chunks = columns // LANES
    known = depth * len(ways)
    operands = (*pieces, *weights, *ends, *prepared)
    scratch = [
        ((length, known), jnp.bfloat16),
        ((columns + SIDE, known), jnp.bfloat16),
        ((chunks + 1, length + 2 * EDGE, LANES), jnp.float32),
        ((2, length, columns), jnp.bfloat16),
        ((2, length, LANES), jnp.bfloat16),
        ((2, length, LANES), jnp.bfloat16),
        ((2 * length, LANES), jnp.bfloat16),
        ((2, length, columns), jnp.bfloat16),
        ((2, length, columns), jnp.bfloat16),
        ((2, LANES, columns), jnp.float32),
        ((2, length, columns), jnp.float32),
        ((length, columns), jnp.bfloat16),
    ]
    return pl.pallas_call(
        functools.partial(mixer_kernel, heads, ring, ways),
        out_shape=[jax.ShapeDtypeStruct((section, columns), jnp.bfloat16)] * len(pieces),
        in_specs=[IN_VMEM] * len(operands),
        out_specs=[IN_VMEM] * len(pieces),
        scratch_shapes=[pltpu.VMEM(*one) for one in scratch],
        compiler_params=pltpu.CompilerParams(vmem_limit_bytes=ROOM),
    )(*operands)


def turn(value, way):
    order = ring_order(lax.axis_size("batch"))
    count = len(order)
    return lax.ppermute(value, ("fsdp", "batch"), [(order[i], order[(i + way) % count]) for i in range(count)])


def swap(value, axis, mask):
    return lax.ppermute(value, axis, [(i, i ^ mask) for i in range(lax.axis_size(axis))])


def on_heads(hidden, in_weight, read_starts, conv_weight, conv_bias, dt_bias, decay, skip, norm_gain):
    tokens = hidden[0]
    count = lax.axis_size("seq")
    seq = lax.axis_index("seq")
    heads = HEADS // count
    columns = heads * HEAD_DIM
    own = pack(in_weight.T, columns)

    ring = lax.axis_size("batch")
    across = swap(tokens, "seq", 2)
    pieces = [tokens, swap(tokens, "seq", 1), across, swap(across, "seq", 1)]
    weights, ways = [own], [0]
    params = (read_starts, conv_weight, conv_bias, dt_bias, decay, skip, norm_gain)
    prepared = prepare(heads, count * tokens.shape[0] // BLOCK, params)
    up = down = own
    for away in range(1, ring):
        up, down = turn(up, 1), turn(down, -1)
        if away == ring - 2:
            up, down, prepared = lax.optimization_barrier((up, down, prepared))
        weights += [up, down]
        ways += [-away, away]
    first = 2 * ring - 3
    partial = early(columns, ring, ways[:first], pieces, weights[:first])
    up, down, partial = lax.optimization_barrier((up, down, partial))
    cut = own.shape[0] // 32 * 16
    ends = [turn(up[:cut], 1), turn(down[cut:], -1)]
    ways.append(ring)
    prepared = (partial, *prepared)
    results = mix(heads, ring, ways[first:], pieces, weights[first:], ends, prepared)
    received = [results[0]] + [swap(results[mask], "seq", mask) for mask in range(1, count)]
    mixed = jnp.zeros((tokens.shape[0], INNER), jnp.bfloat16)
    for mask in range(count):
        mixed = lax.dynamic_update_slice(mixed, received[mask], (0, (seq ^ mask) * columns))
    return mixed[None]


def solution(mesh):
    in_specs = (
        P(("fsdp", "batch"), "seq", None),
        P(("fsdp", "batch"), None),
        P(("fsdp", "batch"), None),
        P(),
        P(),
        P(),
        P(),
        P(),
        P(),
    )
    out_specs = P(("fsdp", "batch"), "seq", None)
    by_heads = mesh.shape["seq"] == 4 and mesh.shape["fsdp"] == 2

    def mixer(hidden, *rest):
        whole = by_heads and hidden.shape[1] == mesh.shape["seq"] * BLOCK
        return jax.shard_map(
            on_heads if whole else on_sections,
            mesh=mesh,
            in_specs=in_specs,
            out_specs=out_specs,
            check_vma=False,
        )(hidden, *rest)

    return mixer
```

```python
import functools

import jax
import jax.numpy as jnp
from jax import lax
from jax.experimental import pallas as pl
from jax.experimental.pallas import tpu as pltpu
from jax.sharding import PartitionSpec as P

HEADS = 32
HEAD_DIM = 64
STATE = 64
KERNEL = 4
BLOCK = 128
INNER = 2048
CONV_CH = 2176


def prefix(value, axis, join, neutral, backward):
    count, mine = (lax.axis_size(axis), lax.axis_index(axis))
    pieces = jax.tree.map(lambda part: lax.all_gather(part, axis), value)
    if backward:
        pieces = jax.tree.map(lambda part: part[::-1], pieces)
        mine = count - 1 - mine
    running = jax.tree.map(
        lambda part, zero: jnp.full_like(part, 0) + jnp.asarray(zero, part.dtype), value, neutral
    )

    def turn(position, running):
        longer = join(running, jax.tree.map(lambda part: part[position], pieces))
        return jax.tree.map(lambda new, old: jnp.where(position < mine, new, old), longer, running)

    return lax.fori_loop(0, count - 1, turn, running)


def extended_2(value, sides, width):
    for axis, dim in sides:
        size, length = (lax.axis_size(axis), value.shape[dim])
        up = [(i, (i + 1) % size) for i in range(size - 1)]
        down = [(j, i) for i, j in up]
        last = lax.slice_in_dim(value, length - width, length, axis=dim)
        initial = lax.slice_in_dim(value, 0, width, axis=dim)
        before = lax.ppermute(last, axis, up)
        after = lax.ppermute(initial, axis, down)
        value = jnp.concatenate([before, value, after], axis=dim)
    return value


def conv_silu(padded, weight, bias):
    length = padded.shape[0] - weight.shape[0] + 1
    total = jnp.broadcast_to(bias[None, :], (length, bias.shape[0]))
    for tap in range(weight.shape[0]):
        total = total + weight[tap][None, :] * padded[tap : tap + length].astype(jnp.float32)
    return jax.nn.silu(total).astype(jnp.bfloat16)


def block_parts(x_part, b_part, c_part, step_size, log_rate, resets):
    length = x_part.shape[0]
    running = jnp.cumsum(log_rate, axis=0)
    running_heads = running.T
    step_heads = step_size.T
    resets_seen = jnp.cumsum(resets)
    scores = jnp.dot(c_part, b_part.T, preferred_element_type=jnp.float32)
    positions = jnp.arange(length)
    allowed = (positions[:, None] >= positions[None, :]) & (
        resets_seen[:, None] == resets_seen[None, :]
    )
    log_gaps = jnp.minimum(running_heads[:, :, None] - running_heads[:, None, :], 0.0)
    weights = (
        jnp.where(allowed[None, :, :], jnp.exp(log_gaps), 0.0)
        * scores[None, :, :]
        * step_heads[:, None, :]
    )
    weights = weights.astype(jnp.bfloat16)
    values = x_part.reshape(length, HEADS, HEAD_DIM)
    inner_part = jnp.einsum("hts,shp->thp", weights, values, preferred_element_type=jnp.float32)
    last_same = resets_seen == resets_seen[-1]
    tail_weight = (
        jnp.where(last_same[:, None], jnp.exp(running[-1][None, :] - running), 0.0) * step_size
    )
    inputs = (tail_weight[:, :, None] * values.astype(jnp.float32)).astype(jnp.bfloat16)
    local_end = jnp.einsum("shp,sn->hpn", inputs, b_part, preferred_element_type=jnp.float32)
    lead_fade = jnp.where((resets_seen == 0)[:, None], jnp.exp(running), 0.0)
    block_fade = jnp.where(resets_seen[-1] == 0, jnp.exp(running[-1]), 0.0)
    return (inner_part, local_end, lead_fade, block_fade)


def chain_combine(earlier, later):
    return (earlier[0] * later[0], later[0][:, None] * earlier[1] + later[1])


def direction(conv_out, step_cols, resets, bias_step, rates, direct, gains, backward):
    length = conv_out.shape[0]
    blocks = length // BLOCK
    x_part = conv_out[:, :INNER]
    b_part = conv_out[:, INNER : INNER + STATE]
    c_part = conv_out[:, INNER + STATE :]
    step_size = jax.nn.softplus(step_cols.astype(jnp.float32) + bias_step[None, :])
    log_rate = -step_size * rates[None, :]
    inner_part, local_end, lead_fade, block_fade = jax.vmap(block_parts)(
        x_part.reshape(blocks, BLOCK, INNER),
        b_part.reshape(blocks, BLOCK, STATE),
        c_part.reshape(blocks, BLOCK, STATE),
        step_size.reshape(blocks, BLOCK, HEADS),
        log_rate.reshape(blocks, BLOCK, HEADS),
        resets.reshape(blocks, BLOCK),
    )
    carried_state = jnp.zeros((HEADS, HEAD_DIM, STATE), jnp.float32)
    carried_fade = jnp.ones((HEADS,), jnp.float32)
    entering = carried_state
    fades_before = carried_fade
    carried_state = block_fade[0][:, None, None] * carried_state + local_end[0]
    carried_fade = block_fade[0] * carried_fade
    summary = (carried_fade, carried_state.reshape(HEADS, HEAD_DIM * STATE))
    identity = (jnp.ones((HEADS,), jnp.float32), jnp.zeros((HEADS, HEAD_DIM * STATE), jnp.float32))
    if backward:
        incoming = prefix(summary, "seq", chain_combine, identity, True)
    else:
        incoming = prefix(summary, "seq", chain_combine, identity, False)
    incoming_state = incoming[1].reshape(HEADS, HEAD_DIM, STATE)
    states = jnp.stack([fades_before[:, None, None] * incoming_state + entering])
    rounded = states.astype(jnp.bfloat16)
    carried = jnp.einsum(
        "btn,bhpn->bthp",
        c_part.reshape(blocks, BLOCK, STATE),
        rounded,
        preferred_element_type=jnp.float32,
    )
    direct_part = direct[None, None, :, None] * x_part.reshape(
        blocks, BLOCK, HEADS, HEAD_DIM
    ).astype(jnp.float32)
    result = (inner_part + lead_fade[..., None] * carried + direct_part).reshape(
        length, HEADS, HEAD_DIM
    )
    scale = lax.rsqrt(jnp.mean(result * result, axis=-1, keepdims=True) + 1e-05)
    return (result * scale * gains.reshape(HEADS, HEAD_DIM)).reshape(length, INNER)


def project(rows_in, in_weight):
    total = jnp.dot(
        rows_in,
        lax.all_gather(in_weight, ("fsdp", "batch"), axis=0, tiled=True),
        preferred_element_type=jnp.float32,
    )
    return total.astype(jnp.bfloat16)


def on_sections(
    hidden, in_weight, read_starts, conv_weight, conv_bias, dt_bias, decay, skip, norm_gain
):
    tokens = hidden[0]
    length = tokens.shape[0]
    margin = KERNEL - 1
    projected = project(tokens, in_weight)
    extended = extended_2(projected[:, :CONV_CH], (("seq", 0),), margin)
    forward_in = conv_silu(extended[: length + margin], conv_weight[0], conv_bias[0])
    backward_in = conv_silu(jnp.flip(extended[margin:], 0), conv_weight[1], conv_bias[1])
    step_cols = projected[:, CONV_CH:]
    positions = lax.axis_index("seq") * length + jnp.arange(length, dtype=jnp.int32)
    marks = read_starts[0]
    starts_here = jnp.any(positions[:, None] == marks[None, :], axis=1).astype(jnp.float32)
    starts_next = jnp.any((positions + 1)[:, None] == marks[None, :], axis=1).astype(jnp.float32)
    forward_out = direction(
        forward_in, step_cols, starts_here, dt_bias[0], decay[0], skip[0], norm_gain[0], False
    )
    backward_out = direction(
        backward_in,
        jnp.flip(step_cols, 0),
        jnp.flip(starts_next, 0),
        dt_bias[1],
        decay[1],
        skip[1],
        norm_gain[1],
        True,
    )
    mixed = forward_out + jnp.flip(backward_out, 0)
    return mixed.astype(jnp.bfloat16)[None]


LANES = 128
SIDE = 256
EDGE = 8
GROUP = 32
HEADER = 16


def ring_order(count):
    return [i if i < count else 3 * count - 1 - i for i in range(2 * count)]


def split_parts(value, count):
    parts = []
    for _ in range(count):
        parts.append(value.astype(jnp.bfloat16))
        value = value - parts[-1].astype(jnp.float32)
    return parts


def lane_row():
    lane = lax.broadcasted_iota(jnp.int32, (BLOCK, LANES), 1)
    row = lax.broadcasted_iota(jnp.int32, (BLOCK, LANES), 0)
    return lane, row


def shard_at(away, ring):
    fsdp, batch = lax.axis_index("fsdp"), lax.axis_index("batch")
    position = jnp.where(fsdp == 0, batch, 2 * ring - 1 - batch)
    there = lax.rem(position + 2 * ring + away, 2 * ring)
    return jnp.where(there < ring, there, 3 * ring - 1 - there)


def take_rows(pieces, ring, ways, rows_in):
    depth = rows_in.shape[1] // len(ways)
    for n, away in enumerate(ways):
        at = pl.ds(pl.multiple_of(shard_at(away, ring) * depth, depth), depth)
        for mask in range(4):
            rows_in[mask * BLOCK : (mask + 1) * BLOCK, n * depth : (n + 1) * depth] = pieces[mask][:, at]


def times_transposed(a, b):
    return lax.dot_general(a, b, (((1,), (1,)), ((), ())), preferred_element_type=jnp.float32)


def pack_kernel(columns, weight_in, own, side, sems):
    seq = lax.axis_index("seq")
    half = side.shape[0]
    few = own.shape[0] - columns - half
    mine = pl.multiple_of(INNER + seq % 2 * half, half)
    other = pl.multiple_of(INNER + (1 - seq % 2) * half, half)
    steps_at = pl.multiple_of(INNER + 2 * half + seq // 2 * few, few)
    copies = [
        (weight_in.at[pl.ds(pl.multiple_of(seq * columns, columns), columns)], own.at[pl.ds(0, columns)]),
        (weight_in.at[pl.ds(mine, half)], own.at[pl.ds(columns, half)]),
        (weight_in.at[pl.ds(steps_at, few)], own.at[pl.ds(columns + half, few)]),
        (weight_in.at[pl.ds(other, half)], side),
    ]
    copies = [pltpu.make_async_copy(a, b, sems.at[i]) for i, (a, b) in enumerate(copies)]
    for copy in copies:
        copy.start()
    for copy in copies:
        copy.wait()


def first_gather_kernel(columns, own, side, up, down, out, sent):
    rows, depth = own.shape
    half = side.shape[0]
    other = columns + LANES
    out[rows:, :] = jnp.zeros((out.shape[0] - rows, out.shape[1]), out.dtype)
    for n, weight in enumerate((own, up, down)):
        out[:rows, n * depth : (n + 1) * depth] = weight[...]
    out[other : other + half, :depth] = side[...]
    sent[:half, :] = up[columns : columns + half, :]
    sent[half:, :] = down[columns : columns + half, :]


def next_gather_kernel(columns, at, held, swapped, up, down, out, sent):
    del held
    rows, depth = up.shape
    half = swapped.shape[0] // 2
    other = columns + LANES
    for n, weight in enumerate((up, down)):
        out[:rows, (at + n) * depth : (at + n + 1) * depth] = weight[...]
        out[other : other + half, (at + n - 2) * depth : (at + n - 1) * depth] = swapped[n * half : (n + 1) * half, :]
    sent[:half, :] = up[columns : columns + half, :]
    sent[half:, :] = down[columns : columns + half, :]


def split_kernel(columns, up, down, up_part, down_part, sent, crossing):
    cut = up_part.shape[0]
    half = crossing.shape[0]
    up_part[...] = up[:cut, :]
    down_part[...] = down[cut:, :]
    sent[:half, :] = up[columns : columns + half, :]
    sent[half:, :] = down[columns : columns + half, :]
    crossing[...] = down[columns : columns + half, :]


def early_kernel(columns, ring, ways, first, *refs):
    pieces = refs[:4]
    gathered, swapped, table, partial, rest, rows_in, side = refs[4:]
    length = rows_in.shape[0]
    half, depth = swapped.shape[0] // 2, swapped.shape[1]
    take_rows(pieces, ring, ways[:first], rows_in)
    take_rows(pieces, ring, ways[first:], rest)
    for n in range(columns // SIDE):
        at = slice(n * SIDE, (n + 1) * SIDE)
        partial[:length, at] = times_transposed(rows_in[...], gathered[at, :])
    side[...] = gathered[columns:, :]
    for n in range(2):
        side[LANES : LANES + half, (first - 2 + n) * depth : (first - 1 + n) * depth] = swapped[n * half : (n + 1) * half, :]
    partial[:length, columns:] = times_transposed(rows_in[...], side[...])
    partial[length:, : table.shape[1]] = table[...]


def second_kernel(columns, partial, rest, up, down, swapped, out, w_in):
    rows, depth = up.shape
    length = rest.shape[0]
    half = swapped.shape[0] // 2
    other = columns + LANES
    w_in[rows:, :] = jnp.zeros((w_in.shape[0] - rows, w_in.shape[1]), jnp.bfloat16)
    for n, weight in enumerate((up, down)):
        w_in[:rows, n * depth : (n + 1) * depth] = weight[...]
        w_in[other : other + half, n * depth : (n + 1) * depth] = swapped[n * half : (n + 1) * half, :]
    for n in range(w_in.shape[0] // SIDE):
        at = slice(n * SIDE, (n + 1) * SIDE)
        out[:length, at] = partial[:length, at] + times_transposed(rest[:, : 2 * depth], w_in[at, :])
    out[length:, :] = partial[length:, :]


def prepare_kernel(heads, *refs):
    marks_in, conv_w_in, conv_b_in, step_bias_in, decay_in, skip_in, gain_in = refs[:7]
    table, conv_w, conv_b, gains, per_head, marks, sems = refs[7:]
    seq = lax.axis_index("seq")
    columns = heads * HEAD_DIM
    own_lanes = pl.ds(pl.multiple_of(seq * columns, columns), columns)
    side_lanes = pl.ds(INNER, LANES)
    copies = [
        (conv_w_in.at[:, :, own_lanes], conv_w.at[:, :, pl.ds(0, columns)]),
        (conv_w_in.at[:, :, side_lanes], conv_w.at[:, :, pl.ds(columns, LANES)]),
        (conv_b_in.at[:, own_lanes], conv_b.at[:, pl.ds(0, columns)]),
        (conv_b_in.at[:, side_lanes], conv_b.at[:, pl.ds(columns, LANES)]),
        (step_bias_in, per_head.at[0]),
        (decay_in, per_head.at[1]),
        (skip_in, per_head.at[2]),
        (gain_in.at[:, own_lanes], gains),
        (marks_in, marks),
    ]
    copies = [pltpu.make_async_copy(a, b, sems.at[i]) for i, (a, b) in enumerate(copies)]
    for copy in copies:
        copy.start()
    for copy in copies:
        copy.wait()

    lane, row = lane_row()
    within = lane % GROUP
    head_lane = within < 2 * heads
    to_first = lax.rem(LANES - seq * heads, LANES)

    def own_heads(k):
        both = jnp.concatenate([per_head[k], jnp.zeros((2, LANES - HEADS), jnp.float32)], axis=1)
        both = pltpu.roll(both, to_first, 1)
        behind = pltpu.roll(both, heads, 1)
        value = jnp.where(lane[:1] < heads, both[0:1, :], behind[1:2, :])
        return jnp.where(lane[:1] < 2 * heads, value, 0.0)

    for d in range(2):
        table[d * KERNEL : (d + 1) * KERNEL, :] = conv_w[d]
    table[8:10, :] = conv_b[...]
    for k in range(2):
        value = jnp.broadcast_to(own_heads(k), (8, LANES))
        value = sum([pltpu.roll(value, g * GROUP, 1) for g in range(1, LANES // GROUP)], value)
        table[10 + k : 11 + k, :LANES] = value[:1]
    direct = packed(jnp.broadcast_to(own_heads(2), (16, LANES)), 3, heads)
    for d in range(2):
        wide = jnp.dot(direct, head_columns(heads, d), preferred_element_type=jnp.float32)
        table[12 + d : 13 + d, :columns] = wide[:1]
    table[14:16, :columns] = gains[...]

    position = row + lane // GROUP * BLOCK
    here = position == marks[:, 0:1]
    after = position + 1 == marks[:, 0:1]
    for m in range(1, marks.shape[1]):
        here = here | (position == marks[:, m : m + 1])
        after = after | (position + 1 == marks[:, m : m + 1])
    forward_start, backward_start = within == 2 * heads, within == 2 * heads + 1
    starts = jnp.where((here & forward_start) | (after & backward_start), 1.0, 0.0).astype(jnp.bfloat16)
    backward_lane = ((within >= heads) & head_lane) | backward_start
    lower = jnp.where(row >= lane, 1.0, 0.0).astype(jnp.bfloat16)
    upper = jnp.where(row <= lane, 1.0, 0.0).astype(jnp.bfloat16)
    ahead = jnp.dot(lower, starts, preferred_element_type=jnp.float32)
    behind = jnp.dot(upper, starts, preferred_element_type=jnp.float32)
    seen = jnp.where(backward_lane, behind, ahead)
    wanted = lane - within + 2 * heads + jnp.where(backward_lane, 1, 0)
    chosen = jnp.where(row == wanted, 1.0, 0.0).astype(jnp.bfloat16)
    seen = jnp.dot(seen.astype(jnp.bfloat16), chosen, preferred_element_type=jnp.float32)
    last = jnp.where(backward_lane[:1], seen[:1], seen[BLOCK - 1 :])
    table[HEADER:, 0:LANES] = jnp.where((seen == last) & head_lane, 1.0, 0.0)
    table[HEADER:, LANES : 2 * LANES] = jnp.where((seen == 0.0) & head_lane, 1.0, 0.0)
    last = jnp.broadcast_to(last, (BLOCK, LANES))
    table[HEADER:, 2 * LANES : 3 * LANES] = jnp.where((last == 0.0) & head_lane, 1.0, 0.0)
    table[HEADER:, 3 * LANES : 4 * LANES] = seen


def head_columns(heads, d):
    at_row = lax.broadcasted_iota(jnp.int32, (LANES, heads * HEAD_DIM), 0)
    head = lax.broadcasted_iota(jnp.int32, (LANES, heads * HEAD_DIM), 1) // HEAD_DIM + d * heads
    hit = (at_row == head) | (at_row == head + 2 * heads) | (at_row == head + 4 * heads)
    return jnp.where(hit, 1.0, 0.0).astype(jnp.bfloat16)


def packed(value, count, heads):
    parts = split_parts(value, count)
    joined = parts[0].astype(jnp.float32)
    for k in range(1, count):
        joined = joined + pltpu.roll(parts[k].astype(jnp.float32), 2 * heads * k, 1)
    return joined.astype(jnp.bfloat16)


def mixer_kernel(heads, partial, rest, up_end, down_end, far, *refs):
    outs, refs = refs[:4], refs[4:]
    w_end, padded, xs, cs, bs, widen_in, leads, tails, state, ys, mixed = refs
    seq = lax.axis_index("seq")
    columns = heads * HEAD_DIM
    depth = up_end.shape[1]
    cut, rows = up_end.shape[0], up_end.shape[0] + down_end.shape[0]
    chunks = columns // LANES
    length = rest.shape[0]
    blocks = length // BLOCK
    lane, row = lane_row()

    def table(first, last, lanes):
        return partial[length + first : length + last, lanes]

    w_end[:cut, :] = up_end[...]
    w_end[cut:rows, :] = down_end[...]
    half = far.shape[0]
    other = columns + LANES
    w_end[rows:other, :] = jnp.zeros((other - rows, depth), jnp.bfloat16)
    w_end[other : other + half, :] = far[...]
    w_end[other + half :, :] = jnp.zeros((w_end.shape[0] - other - half, depth), jnp.bfloat16)
    edge = jnp.zeros((EDGE, LANES), jnp.float32)
    for c in range(chunks + 1):
        padded[c, 0:EDGE, :] = edge
        padded[c, EDGE + length :, :] = edge
    state[...] = jnp.zeros_like(state)

    places = [pl.multiple_of((seq ^ mask) * BLOCK, BLOCK) for mask in range(4)]

    def project_in(n):
        at = slice(n * SIDE, (n + 1) * SIDE)
        return times_transposed(rest[:, 2 * depth :], w_end[at, :])

    def rounded(value):
        return value.astype(jnp.bfloat16).astype(jnp.float32)

    def keep(c, value):
        for mask in range(4):
            padded[c, pl.ds(EDGE + places[mask], BLOCK), :] = value[mask * BLOCK : (mask + 1) * BLOCK, :]

    side_out = project_in(columns // SIDE)
    mine = rounded(side_out[:, :LANES] + partial[:length, columns:other])
    others = rounded(side_out[:, LANES:] + partial[:length, other:])
    even = jnp.broadcast_to(seq, mine.shape) % 2 == 0
    low, high = jnp.where(even, mine, others), jnp.where(even, others, mine)
    left = lax.broadcasted_iota(jnp.int32, mine.shape, 1) < half
    keep(chunks, jnp.where(left, low, pltpu.roll(high, half, 1)))
    for n in range(columns // SIDE):
        part_out = rounded(project_in(n) + partial[:length, n * SIDE : (n + 1) * SIDE])
        for k in range(SIDE // LANES):
            keep(n * (SIDE // LANES) + k, part_out[:, k * LANES : (k + 1) * LANES])

    within = lane % GROUP
    head_lane = within < 2 * heads
    backward_lane = (within >= heads) & head_lane
    to_first = LANES - half - seq % 2 * heads
    raw = jnp.zeros((BLOCK, LANES), jnp.float32)
    for mask in range(4):
        own_steps = pltpu.roll(mine[mask * BLOCK : (mask + 1) * BLOCK, :], to_first, 1)
        own_steps = jnp.where(lane < heads, own_steps, 0.0)
        raw = raw + pltpu.roll(own_steps + pltpu.roll(own_steps, heads, 1), (seq ^ mask) * GROUP, 1)
    raw = raw + table(10, 11, slice(0, LANES))
    step = jnp.maximum(raw, 0.0) + jnp.log1p(jnp.exp(-jnp.abs(raw)))
    rate = -step * table(11, 12, slice(0, LANES))
    two = jnp.concatenate(split_parts(rate, 2), axis=1)
    lower = jnp.where(row >= lane, 1.0, 0.0).astype(jnp.bfloat16)
    upper = jnp.where(row <= lane, 1.0, 0.0).astype(jnp.bfloat16)
    sums = jnp.dot(jnp.concatenate([lower, upper], axis=0), two, preferred_element_type=jnp.float32)
    sums = sums[:, :LANES] + sums[:, LANES:]
    cum = jnp.where(backward_lane, sums[BLOCK:], sums[:BLOCK])
    last = jnp.where(backward_lane[:1], cum[:1], cum[BLOCK - 1 :])
    flags = [table(HEADER, HEADER + BLOCK, slice(k * LANES, (k + 1) * LANES)) for k in range(4)]
    tail = flags[0] * jnp.exp(last - cum) * step
    lead = flags[1] * jnp.exp(cum)
    fade = flags[2][:8] * jnp.exp(jnp.broadcast_to(last, (8, LANES)))
    seen = flags[3]
    seen_turned = seen.T
    spread = [head_columns(heads, d) for d in range(2)]
    shown = (jnp.log(step) - cum).T
    fades = []
    for b in range(blocks):
        for k, value in enumerate((lead, tail)):
            if b:
                value = pltpu.roll(value, LANES - b * GROUP, 1)
            at = (k * blocks + b) * BLOCK
            widen_in[at : at + BLOCK, :] = jnp.where(lane < 2 * heads, value, 0.0).astype(jnp.bfloat16)
        value = pltpu.roll(fade, LANES - b * GROUP, 1) if b else fade
        fades.append(packed(jnp.where(lane[:8] < 2 * heads, value, 0.0), 2, heads)[:1])
    fades = jnp.concatenate(fades + [jnp.zeros((16 - blocks, LANES), jnp.bfloat16)], axis=0)
    fade_wide = []
    for d in range(2):
        wide = jnp.dot(widen_in[...], spread[d], preferred_element_type=jnp.float32).astype(jnp.bfloat16)
        leads[d] = wide[:length]
        tails[d] = wide[length:]
        fade_wide.append(jnp.dot(fades, spread[d], preferred_element_type=jnp.float32))

    short = 64

    def conv_rows(i, carry):
        at = pl.multiple_of(i * short, short)
        for c in range(chunks + 1):
            taps = [padded[c, pl.ds(at + EDGE - 3 + k, short), :] for k in range(7)]
            lanes = slice(c * LANES, (c + 1) * LANES)
            for d in range(2):
                acc = table(8 + d, 9 + d, lanes)
                for k in range(KERNEL):
                    n = d * KERNEL + k
                    acc = acc + table(n, n + 1, lanes) * taps[k if d == 0 else 6 - k]
                half = 0.5 * acc
                value = half + half * jnp.tanh(half)
                if c < chunks:
                    xs[d, pl.ds(at, short), lanes] = value.astype(jnp.bfloat16)
                else:
                    high = lax.broadcasted_iota(jnp.int32, (short, LANES), 1) >= STATE
                    cs[d, pl.ds(at, short), :] = jnp.where(high, value, 0.0).astype(jnp.bfloat16)
                    bs[d, pl.ds(at, short), :] = jnp.where(
                        high, pltpu.roll(value, STATE, 1), 0.0
                    ).astype(jnp.bfloat16)
        return carry

    lax.fori_loop(0, length // short, conv_rows, 0)

    group = SIDE // HEAD_DIM
    lane_head = lax.broadcasted_iota(jnp.int32, (BLOCK, SIDE), 1) // HEAD_DIM
    for i in range(blocks):
        for d in range(2):
            b = i if d == 0 else blocks - 1 - i
            at = slice(b * BLOCK, (b + 1) * BLOCK)
            c_part = cs[d, at, :]
            b_part = bs[d, at, :]
            scores = times_transposed(c_part, b_part)
            ordered = (row >= lane) if d == 0 else (row <= lane)
            n = b * GROUP + d * heads
            bar = jnp.where(ordered & (seen[:, n : n + 1] == seen_turned[n : n + 1, :]), 0.0, -1e30)
            before = state[d]
            carried = jnp.dot(c_part, before.astype(jnp.bfloat16), preferred_element_type=jnp.float32)
            x_all = xs[d, at, :]
            local_end = lax.dot_general(
                b_part, tails[d, at, :] * x_all, (((0,), (0,)), ((), ())), preferred_element_type=jnp.float32
            )
            state[d] = fade_wide[d][b : b + 1] * before + local_end
            for q in range(columns // SIDE):
                some = []
                for h in range(q * group, (q + 1) * group):
                    n = b * GROUP + d * heads + h
                    gap = cum[:, n : n + 1] + (shown[n : n + 1, :] + bar)
                    some.append((jnp.exp(gap) * scores).astype(jnp.bfloat16))
                lanes = slice(q * SIDE, (q + 1) * SIDE)
                x_part = x_all[:, lanes]
                none = jnp.zeros_like(x_part)
                spaced = jnp.concatenate([jnp.where(lane_head == h, x_part, none) for h in range(group)], axis=0)
                inner = jnp.dot(jnp.concatenate(some, axis=1), spaced, preferred_element_type=jnp.float32)
                ys[d, at, lanes] = (
                    inner
                    + leads[d, at, lanes].astype(jnp.float32) * carried[:, lanes]
                    + table(12 + d, 13 + d, lanes) * x_part.astype(jnp.float32)
                )

    head_row = lax.broadcasted_iota(jnp.int32, (SIDE, SIDE), 0) // HEAD_DIM
    head_col = lax.broadcasted_iota(jnp.int32, (SIDE, SIDE), 1) // HEAD_DIM
    same = jnp.where(head_row == head_col, 1.0 / HEAD_DIM, 0.0).astype(jnp.bfloat16)
    for q in range(columns // SIDE):
        lanes = slice(q * SIDE, (q + 1) * SIDE)
        both = 0.0
        for d in range(2):
            y = ys[d, :, lanes]
            mean = jnp.dot((y * y).astype(jnp.bfloat16), same, preferred_element_type=jnp.float32)
            both = both + y * lax.rsqrt(mean + 1e-05) * table(14 + d, 15 + d, lanes)
        mixed[:, lanes] = both.astype(jnp.bfloat16)
    for mask in range(4):
        outs[mask][...] = mixed[pl.ds(places[mask], BLOCK), :]


IN_VMEM = pl.BlockSpec(memory_space=pltpu.VMEM)
IN_HBM = pl.BlockSpec(memory_space=pltpu.HBM)
ROOM = 24 * 1024 * 1024


def call(kernel, shapes, scratch, *operands, space=IN_VMEM, aliases=None):
    shapes = [jax.ShapeDtypeStruct(*one) for one in shapes]
    return pl.pallas_call(
        kernel,
        out_shape=shapes,
        in_specs=[space] * len(operands),
        out_specs=[IN_VMEM] * len(shapes),
        scratch_shapes=scratch,
        input_output_aliases=aliases or {},
        compiler_params=pltpu.CompilerParams(vmem_limit_bytes=ROOM),
    )(*operands)


def pack(weight, columns):
    depth = weight.shape[1]
    few = 2 * columns // HEAD_DIM
    shapes = [((columns + STATE + few, depth), weight.dtype), ((STATE, depth), weight.dtype)]
    scratch = [pltpu.SemaphoreType.DMA((4,))]
    return call(functools.partial(pack_kernel, columns), shapes, scratch, weight, space=IN_HBM)


def first_gather(columns, shape, own, side, up, down):
    shapes = [(shape, own.dtype), ((2 * side.shape[0], side.shape[1]), own.dtype)]
    return call(functools.partial(first_gather_kernel, columns), shapes, [], own, side, up, down)


def next_gather(columns, at, held, swapped, up, down):
    shapes = [(held.shape, held.dtype), (swapped.shape, held.dtype)]
    kernel = functools.partial(next_gather_kernel, columns, at)
    return call(kernel, shapes, [], held, swapped, up, down, aliases={0: 0})


def split(columns, up, down):
    rows, depth = up.shape
    cut = rows // 32 * 16
    shapes = [(cut, depth), (rows - cut, depth), (2 * STATE, depth), (STATE, depth)]
    shapes = [(one, up.dtype) for one in shapes]
    return call(functools.partial(split_kernel, columns), shapes, [], up, down)


def prepare(heads, params):
    columns = heads * HEAD_DIM
    scratch = [
        pltpu.VMEM((2, KERNEL, columns + LANES), jnp.float32),
        pltpu.VMEM((2, columns + LANES), jnp.float32),
        pltpu.VMEM((2, columns), jnp.float32),
        pltpu.VMEM((3, 2, HEADS), jnp.float32),
        pltpu.VMEM(params[0].shape, jnp.int32),
        pltpu.SemaphoreType.DMA((9,)),
    ]
    shape = ((HEADER + BLOCK, columns + LANES), jnp.float32)
    return call(functools.partial(prepare_kernel, heads), [shape], scratch, *params, space=IN_HBM)[0]


def early(columns, ring, ways, pieces, gathered, swapped, table):
    length = pieces[0].shape[0] * len(pieces)
    wide, known = gathered.shape
    first = 2 * ring - 3
    depth = known // first
    shapes = [
        ((length + table.shape[0], wide), jnp.float32),
        ((length, depth * len(ways) - known), jnp.bfloat16),
    ]
    scratch = [pltpu.VMEM((length, known), jnp.bfloat16), pltpu.VMEM((SIDE, known), jnp.bfloat16)]
    kernel = functools.partial(early_kernel, columns, ring, ways, first)
    return call(kernel, shapes, scratch, *pieces, gathered, swapped, table)


def second(columns, partial, rest, up, down, swapped):
    scratch = [pltpu.VMEM((partial.shape[1], 2 * up.shape[1]), jnp.bfloat16)]
    shapes = [(partial.shape, jnp.float32)]
    return call(functools.partial(second_kernel, columns), shapes, scratch, partial, rest, up, down, swapped)[0]


def mix(heads, count, partial, rest, *others):
    columns = heads * HEAD_DIM
    length = rest.shape[0]
    scratch = [
        ((columns + SIDE, others[0].shape[1]), jnp.bfloat16),
        ((columns // LANES + 1, length + 2 * EDGE, LANES), jnp.float32),
        ((2, length, columns), jnp.bfloat16),
        ((2, length, LANES), jnp.bfloat16),
        ((2, length, LANES), jnp.bfloat16),
        ((2 * length, LANES), jnp.bfloat16),
        ((2, length, columns), jnp.bfloat16),
        ((2, length, columns), jnp.bfloat16),
        ((2, LANES, columns), jnp.float32),
        ((2, length, columns), jnp.float32),
        ((length, columns), jnp.bfloat16),
    ]
    shapes = [((length // count, columns), jnp.bfloat16)] * count
    scratch = [pltpu.VMEM(*one) for one in scratch]
    return call(functools.partial(mixer_kernel, heads), shapes, scratch, partial, rest, *others)


def turn(value, way):
    order = ring_order(lax.axis_size("batch"))
    count = len(order)
    return lax.ppermute(value, ("fsdp", "batch"), [(order[i], order[(i + way) % count]) for i in range(count)])


def turn_across(value, way):
    order = ring_order(lax.axis_size("batch"))
    count = len(order)
    pairs = []
    for s in range(lax.axis_size("seq")):
        pairs += [(s * count + order[i], (s ^ 1) * count + order[(i + way) % count]) for i in range(count)]
    return lax.ppermute(value, ("seq", "fsdp", "batch"), pairs)


def swap(value, axis, mask):
    return lax.ppermute(value, axis, [(i, i ^ mask) for i in range(lax.axis_size(axis))])


def on_heads(hidden, in_weight, read_starts, conv_weight, conv_bias, dt_bias, decay, skip, norm_gain):
    tokens = hidden[0]
    count = lax.axis_size("seq")
    seq = lax.axis_index("seq")
    heads = HEADS // count
    columns = heads * HEAD_DIM
    own, side = pack(in_weight.T, columns)

    ring = lax.axis_size("batch")
    late, _ = lax.optimization_barrier((tokens, own))
    across = swap(late, "seq", 2)
    pieces = [tokens, swap(tokens, "seq", 1), across, swap(across, "seq", 1)]
    table = prepare(heads, (read_starts, conv_weight, conv_bias, dt_bias, decay, skip, norm_gain))
    first = 2 * ring - 3
    ways = [0]
    up = down = own
    for away in range(1, ring):
        before = up, down
        up, down = turn(up, 1), turn(down, -1)
        ways += [-away, away]
        if away == 1:
            beside = table
        elif away == 2:
            gathered, sent = first_gather(columns, (columns + SIDE, first * own.shape[1]), own, side, *before)
            beside = swapped = swap(sent, "seq", 1)
        elif away < ring - 1:
            gathered, sent = next_gather(columns, 2 * away - 3, gathered, swapped, *before)
            beside = swapped = swap(sent, "seq", 1)
        else:
            gathered, sent = next_gather(columns, 2 * away - 3, gathered, swapped, *before)
            swapped = swap(sent, "seq", 1)
            partial, rest = early(columns, ring, tuple(ways) + (ring,), pieces, gathered, swapped, table)
            beside = partial
        up, _ = lax.optimization_barrier((up, beside))
        down, _ = lax.optimization_barrier((down, beside))
    up_part, down_part, sent, crossing = split(columns, up, down)
    ends = [turn(up_part, 1), turn(down_part, -1)]
    far = turn_across(crossing, -1)
    partial = second(columns, partial, rest, up, down, swap(sent, "seq", 1))
    results = mix(heads, count, partial, rest, *ends, far)
    received = [results[0]] + [swap(results[mask], "seq", mask) for mask in range(1, count)]
    mixed = jnp.zeros((tokens.shape[0], INNER), jnp.bfloat16)
    for mask in range(count):
        mixed = lax.dynamic_update_slice(mixed, received[mask], (0, (seq ^ mask) * columns))
    return mixed[None]


def solution(mesh):
    in_specs = (
        P(("fsdp", "batch"), "seq", None),
        P(("fsdp", "batch"), None),
        P(("fsdp", "batch"), None),
        P(),
        P(),
        P(),
        P(),
        P(),
        P(),
    )
    out_specs = P(("fsdp", "batch"), "seq", None)
    by_heads = mesh.shape["seq"] == 4 and mesh.shape["fsdp"] == 2

    def mixer(hidden, *rest):
        whole = by_heads and hidden.shape[1] == mesh.shape["seq"] * BLOCK
        return jax.shard_map(
            on_heads if whole else on_sections,
            mesh=mesh,
            in_specs=in_specs,
            out_specs=out_specs,
            check_vma=False,
        )(hidden, *rest)

    return mixer
```

```python
import functools

import jax
import jax.numpy as jnp
from jax import lax
from jax.experimental import pallas as pl
from jax.experimental.pallas import tpu as pltpu
from jax.sharding import PartitionSpec as P

HEADS = 32
HEAD_DIM = 64
STATE = 64
KERNEL = 4
BLOCK = 128
INNER = 2048
CONV_CH = 2176


def prefix(value, axis, join, neutral, backward):
    count, mine = (lax.axis_size(axis), lax.axis_index(axis))
    pieces = jax.tree.map(lambda part: lax.all_gather(part, axis), value)
    if backward:
        pieces = jax.tree.map(lambda part: part[::-1], pieces)
        mine = count - 1 - mine
    running = jax.tree.map(
        lambda part, zero: jnp.full_like(part, 0) + jnp.asarray(zero, part.dtype), value, neutral
    )

    def turn(position, running):
        longer = join(running, jax.tree.map(lambda part: part[position], pieces))
        return jax.tree.map(lambda new, old: jnp.where(position < mine, new, old), longer, running)

    return lax.fori_loop(0, count - 1, turn, running)


def extended_2(value, sides, width):
    for axis, dim in sides:
        size, length = (lax.axis_size(axis), value.shape[dim])
        up = [(i, (i + 1) % size) for i in range(size - 1)]
        down = [(j, i) for i, j in up]
        last = lax.slice_in_dim(value, length - width, length, axis=dim)
        initial = lax.slice_in_dim(value, 0, width, axis=dim)
        before = lax.ppermute(last, axis, up)
        after = lax.ppermute(initial, axis, down)
        value = jnp.concatenate([before, value, after], axis=dim)
    return value


def conv_silu(padded, weight, bias):
    length = padded.shape[0] - weight.shape[0] + 1
    total = jnp.broadcast_to(bias[None, :], (length, bias.shape[0]))
    for tap in range(weight.shape[0]):
        total = total + weight[tap][None, :] * padded[tap : tap + length].astype(jnp.float32)
    return jax.nn.silu(total).astype(jnp.bfloat16)


def block_parts(x_part, b_part, c_part, step_size, log_rate, resets):
    length = x_part.shape[0]
    running = jnp.cumsum(log_rate, axis=0)
    running_heads = running.T
    step_heads = step_size.T
    resets_seen = jnp.cumsum(resets)
    scores = jnp.dot(c_part, b_part.T, preferred_element_type=jnp.float32)
    positions = jnp.arange(length)
    allowed = (positions[:, None] >= positions[None, :]) & (
        resets_seen[:, None] == resets_seen[None, :]
    )
    log_gaps = jnp.minimum(running_heads[:, :, None] - running_heads[:, None, :], 0.0)
    weights = (
        jnp.where(allowed[None, :, :], jnp.exp(log_gaps), 0.0)
        * scores[None, :, :]
        * step_heads[:, None, :]
    )
    weights = weights.astype(jnp.bfloat16)
    values = x_part.reshape(length, HEADS, HEAD_DIM)
    inner_part = jnp.einsum("hts,shp->thp", weights, values, preferred_element_type=jnp.float32)
    last_same = resets_seen == resets_seen[-1]
    tail_weight = (
        jnp.where(last_same[:, None], jnp.exp(running[-1][None, :] - running), 0.0) * step_size
    )
    inputs = (tail_weight[:, :, None] * values.astype(jnp.float32)).astype(jnp.bfloat16)
    local_end = jnp.einsum("shp,sn->hpn", inputs, b_part, preferred_element_type=jnp.float32)
    lead_fade = jnp.where((resets_seen == 0)[:, None], jnp.exp(running), 0.0)
    block_fade = jnp.where(resets_seen[-1] == 0, jnp.exp(running[-1]), 0.0)
    return (inner_part, local_end, lead_fade, block_fade)


def chain_combine(earlier, later):
    return (earlier[0] * later[0], later[0][:, None] * earlier[1] + later[1])


def direction(conv_out, step_cols, resets, bias_step, rates, direct, gains, backward):
    length = conv_out.shape[0]
    blocks = length // BLOCK
    x_part = conv_out[:, :INNER]
    b_part = conv_out[:, INNER : INNER + STATE]
    c_part = conv_out[:, INNER + STATE :]
    step_size = jax.nn.softplus(step_cols.astype(jnp.float32) + bias_step[None, :])
    log_rate = -step_size * rates[None, :]
    inner_part, local_end, lead_fade, block_fade = jax.vmap(block_parts)(
        x_part.reshape(blocks, BLOCK, INNER),
        b_part.reshape(blocks, BLOCK, STATE),
        c_part.reshape(blocks, BLOCK, STATE),
        step_size.reshape(blocks, BLOCK, HEADS),
        log_rate.reshape(blocks, BLOCK, HEADS),
        resets.reshape(blocks, BLOCK),
    )
    carried_state = jnp.zeros((HEADS, HEAD_DIM, STATE), jnp.float32)
    carried_fade = jnp.ones((HEADS,), jnp.float32)
    entering = carried_state
    fades_before = carried_fade
    carried_state = block_fade[0][:, None, None] * carried_state + local_end[0]
    carried_fade = block_fade[0] * carried_fade
    summary = (carried_fade, carried_state.reshape(HEADS, HEAD_DIM * STATE))
    identity = (jnp.ones((HEADS,), jnp.float32), jnp.zeros((HEADS, HEAD_DIM * STATE), jnp.float32))
    if backward:
        incoming = prefix(summary, "seq", chain_combine, identity, True)
    else:
        incoming = prefix(summary, "seq", chain_combine, identity, False)
    incoming_state = incoming[1].reshape(HEADS, HEAD_DIM, STATE)
    states = jnp.stack([fades_before[:, None, None] * incoming_state + entering])
    rounded = states.astype(jnp.bfloat16)
    carried = jnp.einsum(
        "btn,bhpn->bthp",
        c_part.reshape(blocks, BLOCK, STATE),
        rounded,
        preferred_element_type=jnp.float32,
    )
    direct_part = direct[None, None, :, None] * x_part.reshape(
        blocks, BLOCK, HEADS, HEAD_DIM
    ).astype(jnp.float32)
    result = (inner_part + lead_fade[..., None] * carried + direct_part).reshape(
        length, HEADS, HEAD_DIM
    )
    scale = lax.rsqrt(jnp.mean(result * result, axis=-1, keepdims=True) + 1e-05)
    return (result * scale * gains.reshape(HEADS, HEAD_DIM)).reshape(length, INNER)


def project(rows_in, in_weight):
    total = jnp.dot(
        rows_in,
        lax.all_gather(in_weight, ("fsdp", "batch"), axis=0, tiled=True),
        preferred_element_type=jnp.float32,
    )
    return total.astype(jnp.bfloat16)


def on_sections(
    hidden, in_weight, read_starts, conv_weight, conv_bias, dt_bias, decay, skip, norm_gain
):
    tokens = hidden[0]
    length = tokens.shape[0]
    margin = KERNEL - 1
    projected = project(tokens, in_weight)
    extended = extended_2(projected[:, :CONV_CH], (("seq", 0),), margin)
    forward_in = conv_silu(extended[: length + margin], conv_weight[0], conv_bias[0])
    backward_in = conv_silu(jnp.flip(extended[margin:], 0), conv_weight[1], conv_bias[1])
    step_cols = projected[:, CONV_CH:]
    positions = lax.axis_index("seq") * length + jnp.arange(length, dtype=jnp.int32)
    marks = read_starts[0]
    starts_here = jnp.any(positions[:, None] == marks[None, :], axis=1).astype(jnp.float32)
    starts_next = jnp.any((positions + 1)[:, None] == marks[None, :], axis=1).astype(jnp.float32)
    forward_out = direction(
        forward_in, step_cols, starts_here, dt_bias[0], decay[0], skip[0], norm_gain[0], False
    )
    backward_out = direction(
        backward_in,
        jnp.flip(step_cols, 0),
        jnp.flip(starts_next, 0),
        dt_bias[1],
        decay[1],
        skip[1],
        norm_gain[1],
        True,
    )
    mixed = forward_out + jnp.flip(backward_out, 0)
    return mixed.astype(jnp.bfloat16)[None]


LANES = 128
SIDE = 256
EDGE = 8
GROUP = 32
HEADER = 16


def ring_order(count):
    return [i if i < count else 3 * count - 1 - i for i in range(2 * count)]


def split_parts(value, count):
    parts = []
    for _ in range(count):
        parts.append(value.astype(jnp.bfloat16))
        value = value - parts[-1].astype(jnp.float32)
    return parts


def lane_row():
    lane = lax.broadcasted_iota(jnp.int32, (BLOCK, LANES), 1)
    row = lax.broadcasted_iota(jnp.int32, (BLOCK, LANES), 0)
    return lane, row


def shard_at(away, ring):
    fsdp, batch = lax.axis_index("fsdp"), lax.axis_index("batch")
    position = jnp.where(fsdp == 0, batch, 2 * ring - 1 - batch)
    there = lax.rem(position + 2 * ring + away, 2 * ring)
    return jnp.where(there < ring, there, 3 * ring - 1 - there)


def take_rows(pieces, ring, ways, rows_in):
    depth = rows_in.shape[1] // len(ways)
    for n, away in enumerate(ways):
        at = pl.ds(pl.multiple_of(shard_at(away, ring) * depth, depth), depth)
        for mask in range(4):
            rows_in[mask * BLOCK : (mask + 1) * BLOCK, n * depth : (n + 1) * depth] = pieces[mask][:, at]


def times_transposed(a, b):
    return lax.dot_general(a, b, (((1,), (1,)), ((), ())), preferred_element_type=jnp.float32)


def pack_kernel(columns, weight_in, own, side, sems):
    seq = lax.axis_index("seq")
    half = side.shape[0]
    few = own.shape[0] - columns - half
    mine = pl.multiple_of(INNER + seq % 2 * half, half)
    other = pl.multiple_of(INNER + (1 - seq % 2) * half, half)
    steps_at = pl.multiple_of(INNER + 2 * half + seq // 2 * few, few)
    copies = [
        (weight_in.at[pl.ds(pl.multiple_of(seq * columns, columns), columns)], own.at[pl.ds(0, columns)]),
        (weight_in.at[pl.ds(mine, half)], own.at[pl.ds(columns, half)]),
        (weight_in.at[pl.ds(steps_at, few)], own.at[pl.ds(columns + half, few)]),
        (weight_in.at[pl.ds(other, half)], side),
    ]
    copies = [pltpu.make_async_copy(a, b, sems.at[i]) for i, (a, b) in enumerate(copies)]
    for copy in copies:
        copy.start()
    for copy in copies:
        copy.wait()


def first_gather_kernel(columns, own, side, up, down, out, sent):
    rows, depth = own.shape
    half = side.shape[0]
    other = columns + LANES
    out[rows:, :] = jnp.zeros((out.shape[0] - rows, out.shape[1]), out.dtype)
    for n, weight in enumerate((own, up, down)):
        out[:rows, n * depth : (n + 1) * depth] = weight[...]
    out[other : other + half, :depth] = side[...]
    sent[:half, :] = up[columns : columns + half, :]
    sent[half:, :] = down[columns : columns + half, :]


def next_gather_kernel(columns, at, held, swapped, up, down, out, sent):
    del held
    rows, depth = up.shape
    half = swapped.shape[0] // 2
    other = columns + LANES
    for n, weight in enumerate((up, down)):
        out[:rows, (at + n) * depth : (at + n + 1) * depth] = weight[...]
        out[other : other + half, (at + n - 2) * depth : (at + n - 1) * depth] = swapped[n * half : (n + 1) * half, :]
    sent[:half, :] = up[columns : columns + half, :]
    sent[half:, :] = down[columns : columns + half, :]


def split_kernel(columns, up, down, sent, crossing):
    half = crossing.shape[0]
    sent[:half, :] = up[columns : columns + half, :]
    sent[half:, :] = down[columns : columns + half, :]
    crossing[...] = down[columns : columns + half, :]


def early_kernel(columns, ring, ways, first, *refs):
    pieces = refs[:4]
    gathered, swapped, table, partial, rest, rows_in, side = refs[4:]
    length = rows_in.shape[0]
    half, depth = swapped.shape[0] // 2, swapped.shape[1]
    take_rows(pieces, ring, ways[:first], rows_in)
    take_rows(pieces, ring, ways[first:], rest)
    for n in range(columns // SIDE):
        at = slice(n * SIDE, (n + 1) * SIDE)
        partial[:length, at] = times_transposed(rows_in[...], gathered[at, :])
    side[...] = gathered[columns:, :]
    for n in range(2):
        side[LANES : LANES + half, (first - 2 + n) * depth : (first - 1 + n) * depth] = swapped[n * half : (n + 1) * half, :]
    partial[:length, columns:] = times_transposed(rows_in[...], side[...])
    other = columns + LANES
    partial[:BLOCK, other:] = partial[:BLOCK, other:] + pltpu.roll(table[HEADER:, :LANES], half, 1)
    partial[length:, : table.shape[1]] = table[:HEADER, :]


def second_kernel(columns, partial, rest, up, down, swapped, out, w_in, sems):
    rows, depth = up.shape
    length = rest.shape[0]
    half = swapped.shape[0] // 2
    other = columns + LANES
    copies = []
    for n in range(2):
        place = w_in.at[pl.ds(other, half), pl.ds(n * depth, depth)]
        copies.append(pltpu.make_async_copy(swapped.at[pl.ds(n * half, half)], place, sems.at[n]))
        copies[-1].start()
    w_in[rows:other, :] = jnp.zeros((other - rows, w_in.shape[1]), jnp.bfloat16)
    w_in[other + half :, :] = jnp.zeros((w_in.shape[0] - other - half, w_in.shape[1]), jnp.bfloat16)
    for n, weight in enumerate((up, down)):
        w_in[:rows, n * depth : (n + 1) * depth] = weight[...]
    for n in range(w_in.shape[0] // SIDE):
        at = slice(n * SIDE, (n + 1) * SIDE)
        if n == columns // SIDE:
            for copy in copies:
                copy.wait()
        out[:length, at] = partial[:length, at] + times_transposed(rest[:, : 2 * depth], w_in[at, :])
    out[length:, :] = partial[length:, :]


def prepare_kernel(heads, *refs):
    marks_in, conv_w_in, conv_b_in, step_bias_in, decay_in, skip_in, gain_in = refs[:7]
    table, conv_w, conv_b, gains, per_head, marks, sems = refs[7:]
    seq = lax.axis_index("seq")
    columns = heads * HEAD_DIM
    own_lanes = pl.ds(pl.multiple_of(seq * columns, columns), columns)
    side_lanes = pl.ds(INNER, LANES)
    copies = [
        (conv_w_in.at[:, :, own_lanes], conv_w.at[:, :, pl.ds(0, columns)]),
        (conv_w_in.at[:, :, side_lanes], conv_w.at[:, :, pl.ds(columns, LANES)]),
        (conv_b_in.at[:, own_lanes], conv_b.at[:, pl.ds(0, columns)]),
        (conv_b_in.at[:, side_lanes], conv_b.at[:, pl.ds(columns, LANES)]),
        (step_bias_in, per_head.at[0]),
        (decay_in, per_head.at[1]),
        (skip_in, per_head.at[2]),
        (gain_in.at[:, own_lanes], gains),
        (marks_in, marks),
    ]
    copies = [pltpu.make_async_copy(a, b, sems.at[i]) for i, (a, b) in enumerate(copies)]
    for copy in copies:
        copy.start()
    for copy in copies:
        copy.wait()

    lane, row = lane_row()
    within = lane % GROUP
    head_lane = within < 2 * heads
    to_first = lax.rem(LANES - seq * heads, LANES)

    def own_heads(k):
        both = jnp.concatenate([per_head[k], jnp.zeros((2, LANES - HEADS), jnp.float32)], axis=1)
        both = pltpu.roll(both, to_first, 1)
        behind = pltpu.roll(both, heads, 1)
        value = jnp.where(lane[:1] < heads, both[0:1, :], behind[1:2, :])
        return jnp.where(lane[:1] < 2 * heads, value, 0.0)

    for d in range(2):
        table[d * KERNEL : (d + 1) * KERNEL, :] = conv_w[d]
    table[8:10, :] = conv_b[...]
    for k in range(2):
        value = jnp.broadcast_to(own_heads(k), (8, LANES))
        value = sum([pltpu.roll(value, g * GROUP, 1) for g in range(1, LANES // GROUP)], value)
        table[10 + k : 11 + k, :LANES] = value[:1]
    direct = packed(jnp.broadcast_to(own_heads(2), (16, LANES)), 3, heads)
    for d in range(2):
        wide = jnp.dot(direct, head_columns(heads, d), preferred_element_type=jnp.float32)
        table[12 + d : 13 + d, :columns] = wide[:1]
    table[14:16, :columns] = gains[...]

    position = row + lane // GROUP * BLOCK
    here = position == marks[:, 0:1]
    after = position + 1 == marks[:, 0:1]
    for m in range(1, marks.shape[1]):
        here = here | (position == marks[:, m : m + 1])
        after = after | (position + 1 == marks[:, m : m + 1])
    forward_start, backward_start = within == 2 * heads, within == 2 * heads + 1
    starts = jnp.where((here & forward_start) | (after & backward_start), 1.0, 0.0).astype(jnp.bfloat16)
    backward_lane = ((within >= heads) & head_lane) | backward_start
    lower = jnp.where(row >= lane, 1.0, 0.0).astype(jnp.bfloat16)
    upper = jnp.where(row <= lane, 1.0, 0.0).astype(jnp.bfloat16)
    ahead = jnp.dot(lower, starts, preferred_element_type=jnp.float32)
    behind = jnp.dot(upper, starts, preferred_element_type=jnp.float32)
    seen = jnp.where(backward_lane, behind, ahead)
    wanted = lane - within + 2 * heads + jnp.where(backward_lane, 1, 0)
    chosen = jnp.where(row == wanted, 1.0, 0.0).astype(jnp.bfloat16)
    seen = jnp.dot(seen.astype(jnp.bfloat16), chosen, preferred_element_type=jnp.float32)
    chosen = (row == lane // 2 * GROUP + lane % 2 * heads) & (lane < 2 * LANES // GROUP)
    chosen = jnp.where(chosen, 1.0, 0.0).astype(jnp.bfloat16)
    table[HEADER:, :LANES] = jnp.dot(seen.astype(jnp.bfloat16), chosen, preferred_element_type=jnp.float32)


def head_columns(heads, d):
    at_row = lax.broadcasted_iota(jnp.int32, (LANES, heads * HEAD_DIM), 0)
    head = lax.broadcasted_iota(jnp.int32, (LANES, heads * HEAD_DIM), 1) // HEAD_DIM + d * heads
    hit = (at_row == head) | (at_row == head + 2 * heads) | (at_row == head + 4 * heads)
    return jnp.where(hit, 1.0, 0.0).astype(jnp.bfloat16)


def packed(value, count, heads):
    parts = split_parts(value, count)
    joined = parts[0].astype(jnp.float32)
    for k in range(1, count):
        joined = joined + pltpu.roll(parts[k].astype(jnp.float32), 2 * heads * k, 1)
    return joined.astype(jnp.bfloat16)


def mixer_kernel(heads, partial, rest, up_end, down_end, far, *refs):
    outs, refs = refs[:4], refs[4:]
    w_end, padded, xs, cs, bs, widen_in, leads, tails, state, ys, mixed = refs
    seq = lax.axis_index("seq")
    columns = heads * HEAD_DIM
    depth = up_end.shape[1]
    cut, rows = up_end.shape[0], up_end.shape[0] + down_end.shape[0]
    chunks = columns // LANES
    length = rest.shape[0]
    blocks = length // BLOCK
    lane, row = lane_row()

    def table(first, last, lanes):
        return partial[length + first : length + last, lanes]

    half = far.shape[0]
    other = columns + LANES
    w_end[:cut, :] = up_end[...]
    w_end[cut:rows, :] = down_end[...]
    w_end[other : other + half, :] = far[...]
    w_end[rows:other, :] = jnp.zeros((other - rows, depth), jnp.bfloat16)
    w_end[other + half :, :] = jnp.zeros((w_end.shape[0] - other - half, depth), jnp.bfloat16)
    edge = jnp.zeros((EDGE, LANES), jnp.float32)
    for c in range(chunks + 1):
        padded[c, 0:EDGE, :] = edge
        padded[c, EDGE + length :, :] = edge
    state[...] = jnp.zeros_like(state)

    places = [pl.multiple_of((seq ^ mask) * BLOCK, BLOCK) for mask in range(4)]

    def project_in(n):
        at = slice(n * SIDE, (n + 1) * SIDE)
        return times_transposed(rest[:, 2 * depth :], w_end[at, :])

    def rounded(value):
        return value.astype(jnp.bfloat16).astype(jnp.float32)

    def keep(c, value):
        for mask in range(4):
            padded[c, pl.ds(EDGE + places[mask], BLOCK), :] = value[mask * BLOCK : (mask + 1) * BLOCK, :]

    side_out = project_in(columns // SIDE)
    mine = rounded(side_out[:, :LANES] + partial[:length, columns:other])
    others = rounded(side_out[:, LANES:] + partial[:length, other:])
    even = jnp.broadcast_to(seq, mine.shape) % 2 == 0
    low, high = jnp.where(even, mine, others), jnp.where(even, others, mine)
    left = lax.broadcasted_iota(jnp.int32, mine.shape, 1) < half
    keep(chunks, jnp.where(left, low, pltpu.roll(high, half, 1)))
    for n in range(columns // SIDE):
        part_out = rounded(project_in(n) + partial[:length, n * SIDE : (n + 1) * SIDE])
        for k in range(SIDE // LANES):
            keep(n * (SIDE // LANES) + k, part_out[:, k * LANES : (k + 1) * LANES])

    within = lane % GROUP
    head_lane = within < 2 * heads
    backward_lane = (within >= heads) & head_lane
    to_first = LANES - half - seq % 2 * heads
    raw = jnp.zeros((BLOCK, LANES), jnp.float32)
    for mask in range(4):
        own_steps = pltpu.roll(mine[mask * BLOCK : (mask + 1) * BLOCK, :], to_first, 1)
        own_steps = jnp.where(lane < heads, own_steps, 0.0)
        raw = raw + pltpu.roll(own_steps + pltpu.roll(own_steps, heads, 1), (seq ^ mask) * GROUP, 1)
    raw = raw + table(10, 11, slice(0, LANES))
    step = jnp.maximum(raw, 0.0) + jnp.log1p(jnp.exp(-jnp.abs(raw)))
    rate = -step * table(11, 12, slice(0, LANES))
    two = jnp.concatenate(split_parts(rate, 2), axis=1)
    lower = jnp.where(row >= lane, 1.0, 0.0).astype(jnp.bfloat16)
    upper = jnp.where(row <= lane, 1.0, 0.0).astype(jnp.bfloat16)
    sums = jnp.dot(jnp.concatenate([lower, upper], axis=0), two, preferred_element_type=jnp.float32)
    sums = sums[:, :LANES] + sums[:, LANES:]
    cum = jnp.where(backward_lane, sums[BLOCK:], sums[:BLOCK])
    last = jnp.where(backward_lane[:1], cum[:1], cum[BLOCK - 1 :])
    chosen = jnp.where(row == lane // GROUP * 2 + jnp.where(backward_lane, 1, 0), 1.0, 0.0).astype(jnp.bfloat16)
    seen = pltpu.roll(partial[:BLOCK, other:], half, 1).astype(jnp.bfloat16)
    seen = jnp.dot(seen, chosen, preferred_element_type=jnp.float32)
    seen_last = jnp.where(backward_lane[:1], seen[:1], seen[BLOCK - 1 :])
    tail = jnp.where(seen == seen_last, jnp.exp(last - cum) * step, 0.0)
    lead = jnp.where(seen == 0.0, jnp.exp(cum), 0.0)
    last, seen_last = jnp.broadcast_to(last, (8, LANES)), jnp.broadcast_to(seen_last, (8, LANES))
    fade = jnp.where(seen_last == 0.0, jnp.exp(last), 0.0)
    seen_turned = seen.T
    spread = [head_columns(heads, d) for d in range(2)]
    shown = (jnp.log(step) - cum).T
    fades = []
    for b in range(blocks):
        for k, value in enumerate((lead, tail)):
            if b:
                value = pltpu.roll(value, LANES - b * GROUP, 1)
            at = (k * blocks + b) * BLOCK
            widen_in[at : at + BLOCK, :] = jnp.where(lane < 2 * heads, value, 0.0).astype(jnp.bfloat16)
        value = pltpu.roll(fade, LANES - b * GROUP, 1) if b else fade
        fades.append(packed(jnp.where(lane[:8] < 2 * heads, value, 0.0), 2, heads)[:1])
    fades = jnp.concatenate(fades + [jnp.zeros((16 - blocks, LANES), jnp.bfloat16)], axis=0)
    fade_wide = []
    for d in range(2):
        wide = jnp.dot(widen_in[...], spread[d], preferred_element_type=jnp.float32).astype(jnp.bfloat16)
        leads[d] = wide[:length]
        tails[d] = wide[length:]
        fade_wide.append(jnp.dot(fades, spread[d], preferred_element_type=jnp.float32))

    short = 64

    def conv_rows(i, carry):
        at = pl.multiple_of(i * short, short)
        for c in range(chunks + 1):
            taps = [padded[c, pl.ds(at + EDGE - 3 + k, short), :] for k in range(7)]
            lanes = slice(c * LANES, (c + 1) * LANES)
            for d in range(2):
                acc = table(8 + d, 9 + d, lanes)
                for k in range(KERNEL):
                    n = d * KERNEL + k
                    acc = acc + table(n, n + 1, lanes) * taps[k if d == 0 else 6 - k]
                half = 0.5 * acc
                value = half + half * jnp.tanh(half)
                if c < chunks:
                    xs[d, pl.ds(at, short), lanes] = value.astype(jnp.bfloat16)
                else:
                    high = lax.broadcasted_iota(jnp.int32, (short, LANES), 1) >= STATE
                    cs[d, pl.ds(at, short), :] = jnp.where(high, value, 0.0).astype(jnp.bfloat16)
                    bs[d, pl.ds(at, short), :] = jnp.where(
                        high, pltpu.roll(value, STATE, 1), 0.0
                    ).astype(jnp.bfloat16)
        return carry

    lax.fori_loop(0, length // short, conv_rows, 0)

    group = SIDE // HEAD_DIM
    lane_head = lax.broadcasted_iota(jnp.int32, (BLOCK, SIDE), 1) // HEAD_DIM
    for i in range(blocks):
        for d in range(2):
            b = i if d == 0 else blocks - 1 - i
            at = slice(b * BLOCK, (b + 1) * BLOCK)
            c_part = cs[d, at, :]
            b_part = bs[d, at, :]
            scores = times_transposed(c_part, b_part)
            ordered = (row >= lane) if d == 0 else (row <= lane)
            n = b * GROUP + d * heads
            bar = jnp.where(ordered & (seen[:, n : n + 1] == seen_turned[n : n + 1, :]), 0.0, -1e30)
            before = state[d]
            carried = jnp.dot(c_part, before.astype(jnp.bfloat16), preferred_element_type=jnp.float32)
            x_all = xs[d, at, :]
            local_end = lax.dot_general(
                b_part, tails[d, at, :] * x_all, (((0,), (0,)), ((), ())), preferred_element_type=jnp.float32
            )
            state[d] = fade_wide[d][b : b + 1] * before + local_end
            for q in range(columns // SIDE):
                some = []
                for h in range(q * group, (q + 1) * group):
                    n = b * GROUP + d * heads + h
                    gap = cum[:, n : n + 1] + (shown[n : n + 1, :] + bar)
                    some.append((jnp.exp(gap) * scores).astype(jnp.bfloat16))
                lanes = slice(q * SIDE, (q + 1) * SIDE)
                x_part = x_all[:, lanes]
                none = jnp.zeros_like(x_part)
                spaced = jnp.concatenate([jnp.where(lane_head == h, x_part, none) for h in range(group)], axis=0)
                inner = jnp.dot(jnp.concatenate(some, axis=1), spaced, preferred_element_type=jnp.float32)
                ys[d, at, lanes] = (
                    inner
                    + leads[d, at, lanes].astype(jnp.float32) * carried[:, lanes]
                    + table(12 + d, 13 + d, lanes) * x_part.astype(jnp.float32)
                )

    head_row = lax.broadcasted_iota(jnp.int32, (SIDE, SIDE), 0) // HEAD_DIM
    head_col = lax.broadcasted_iota(jnp.int32, (SIDE, SIDE), 1) // HEAD_DIM
    same = jnp.where(head_row == head_col, 1.0 / HEAD_DIM, 0.0).astype(jnp.bfloat16)
    for q in range(columns // SIDE):
        lanes = slice(q * SIDE, (q + 1) * SIDE)
        both = 0.0
        for d in range(2):
            y = ys[d, :, lanes]
            mean = jnp.dot((y * y).astype(jnp.bfloat16), same, preferred_element_type=jnp.float32)
            both = both + y * lax.rsqrt(mean + 1e-05) * table(14 + d, 15 + d, lanes)
        mixed[:, lanes] = both.astype(jnp.bfloat16)
    for mask in range(4):
        outs[mask][...] = mixed[pl.ds(places[mask], BLOCK), :]


IN_VMEM = pl.BlockSpec(memory_space=pltpu.VMEM)
IN_HBM = pl.BlockSpec(memory_space=pltpu.HBM)
ROOM = 24 * 1024 * 1024


def call(kernel, shapes, scratch, *operands, space=IN_VMEM, apart=0, aliases=None):
    shapes = [jax.ShapeDtypeStruct(*one) for one in shapes]
    return pl.pallas_call(
        kernel,
        out_shape=shapes,
        in_specs=[space] * (len(operands) - apart) + [pl.BlockSpec(memory_space=pl.ANY)] * apart,
        out_specs=[IN_VMEM] * len(shapes),
        scratch_shapes=scratch,
        input_output_aliases=aliases or {},
        compiler_params=pltpu.CompilerParams(vmem_limit_bytes=ROOM),
    )(*operands)


def pack(weight, columns):
    depth = weight.shape[1]
    few = 2 * columns // HEAD_DIM
    shapes = [((columns + STATE + few, depth), weight.dtype), ((STATE, depth), weight.dtype)]
    scratch = [pltpu.SemaphoreType.DMA((4,))]
    return call(functools.partial(pack_kernel, columns), shapes, scratch, weight, space=IN_HBM)


def first_gather(columns, shape, own, side, up, down):
    shapes = [(shape, own.dtype), ((2 * side.shape[0], side.shape[1]), own.dtype)]
    return call(functools.partial(first_gather_kernel, columns), shapes, [], own, side, up, down)


def next_gather(columns, at, held, swapped, up, down):
    shapes = [(held.shape, held.dtype), (swapped.shape, held.dtype)]
    kernel = functools.partial(next_gather_kernel, columns, at)
    return call(kernel, shapes, [], held, swapped, up, down, aliases={0: 0})


def split(columns, up, down):
    rows, depth = up.shape
    shapes = [(2 * STATE, depth), (STATE, depth)]
    shapes = [(one, up.dtype) for one in shapes]
    return call(functools.partial(split_kernel, columns), shapes, [], up, down)


def prepare(heads, params):
    columns = heads * HEAD_DIM
    scratch = [
        pltpu.VMEM((2, KERNEL, columns + LANES), jnp.float32),
        pltpu.VMEM((2, columns + LANES), jnp.float32),
        pltpu.VMEM((2, columns), jnp.float32),
        pltpu.VMEM((3, 2, HEADS), jnp.float32),
        pltpu.VMEM(params[0].shape, jnp.int32),
        pltpu.SemaphoreType.DMA((9,)),
    ]
    shape = ((HEADER + BLOCK, columns + LANES), jnp.float32)
    return call(functools.partial(prepare_kernel, heads), [shape], scratch, *params, space=IN_HBM)[0]


def early(columns, ring, ways, pieces, gathered, swapped, table):
    length = pieces[0].shape[0] * len(pieces)
    wide, known = gathered.shape
    first = 2 * ring - 3
    depth = known // first
    shapes = [
        ((length + HEADER, wide), jnp.float32),
        ((length, depth * len(ways) - known), jnp.bfloat16),
    ]
    scratch = [pltpu.VMEM((length, known), jnp.bfloat16), pltpu.VMEM((SIDE, known), jnp.bfloat16)]
    kernel = functools.partial(early_kernel, columns, ring, ways, first)
    return call(kernel, shapes, scratch, *pieces, gathered, swapped, table)


def second(columns, partial, rest, up, down, swapped):
    scratch = [pltpu.VMEM((partial.shape[1], 2 * up.shape[1]), jnp.bfloat16), pltpu.SemaphoreType.DMA((2,))]
    operands = (partial, rest, up, down, swapped)
    return call(functools.partial(second_kernel, columns), [(partial.shape, jnp.float32)], scratch, *operands, apart=1)[0]


def mix(heads, count, partial, rest, *others):
    columns = heads * HEAD_DIM
    length = rest.shape[0]
    scratch = [
        ((columns + SIDE, others[0].shape[1]), jnp.bfloat16),
        ((columns // LANES + 1, length + 2 * EDGE, LANES), jnp.float32),
        ((2, length, columns), jnp.bfloat16),
        ((2, length, LANES), jnp.bfloat16),
        ((2, length, LANES), jnp.bfloat16),
        ((2 * length, LANES), jnp.bfloat16),
        ((2, length, columns), jnp.bfloat16),
        ((2, length, columns), jnp.bfloat16),
        ((2, LANES, columns), jnp.float32),
        ((2, length, columns), jnp.float32),
        ((length, columns), jnp.bfloat16),
    ]
    shapes = [((length // count, columns), jnp.bfloat16)] * count
    scratch = [pltpu.VMEM(*one) for one in scratch]
    return call(functools.partial(mixer_kernel, heads), shapes, scratch, partial, rest, *others)


def turn(value, way):
    order = ring_order(lax.axis_size("batch"))
    count = len(order)
    return lax.ppermute(value, ("fsdp", "batch"), [(order[i], order[(i + way) % count]) for i in range(count)])


def turn_across(value, way):
    order = ring_order(lax.axis_size("batch"))
    count = len(order)
    pairs = []
    for s in range(lax.axis_size("seq")):
        pairs += [(s * count + order[i], (s ^ 1) * count + order[(i + way) % count]) for i in range(count)]
    return lax.ppermute(value, ("seq", "fsdp", "batch"), pairs)


def swap(value, axis, mask):
    return lax.ppermute(value, axis, [(i, i ^ mask) for i in range(lax.axis_size(axis))])


def on_heads(hidden, in_weight, read_starts, conv_weight, conv_bias, dt_bias, decay, skip, norm_gain):
    tokens = hidden[0]
    count = lax.axis_size("seq")
    seq = lax.axis_index("seq")
    heads = HEADS // count
    columns = heads * HEAD_DIM
    own, side = pack(in_weight.T, columns)

    ring = lax.axis_size("batch")
    late, _ = lax.optimization_barrier((tokens, own))
    across = swap(late, "seq", 2)
    pieces = [tokens, swap(tokens, "seq", 1), across, swap(across, "seq", 1)]
    table = prepare(heads, (read_starts, conv_weight, conv_bias, dt_bias, decay, skip, norm_gain))
    first = 2 * ring - 3
    ways = [0]
    up = down = own
    for away in range(1, ring):
        before = up, down
        up, down = turn(up, 1), turn(down, -1)
        ways += [-away, away]
        if away == 1:
            beside = table
        elif away == 2:
            gathered, sent = first_gather(columns, (columns + SIDE, first * own.shape[1]), own, side, *before)
            beside = swapped = swap(sent, "seq", 1)
        elif away < ring - 1:
            gathered, sent = next_gather(columns, 2 * away - 3, gathered, swapped, *before)
            beside = swapped = swap(sent, "seq", 1)
        else:
            gathered, sent = next_gather(columns, 2 * away - 3, gathered, swapped, *before)
            swapped = swap(sent, "seq", 1)
            partial, rest = early(columns, ring, tuple(ways) + (ring,), pieces, gathered, swapped, table)
            beside = partial
        up, _ = lax.optimization_barrier((up, beside))
        down, _ = lax.optimization_barrier((down, beside))
    cut = own.shape[0] // 32 * 16
    ends = [turn(up[:cut], 1), turn(down[cut:], -1)]
    sent, crossing = split(columns, up, down)
    far = turn_across(crossing, -1)
    partial = second(columns, partial, rest, up, down, swap(sent, "seq", 1))
    results = mix(heads, count, partial, rest, *ends, far)
    received = [results[0]] + [swap(results[mask], "seq", mask) for mask in range(1, count)]
    mixed = jnp.zeros((tokens.shape[0], INNER), jnp.bfloat16)
    for mask in range(count):
        mixed = lax.dynamic_update_slice(mixed, received[mask], (0, (seq ^ mask) * columns))
    return mixed[None]


def solution(mesh):
    in_specs = (
        P(("fsdp", "batch"), "seq", None),
        P(("fsdp", "batch"), None),
        P(("fsdp", "batch"), None),
        P(),
        P(),
        P(),
        P(),
        P(),
        P(),
    )
    out_specs = P(("fsdp", "batch"), "seq", None)
    by_heads = mesh.shape["seq"] == 4 and mesh.shape["fsdp"] == 2

    def mixer(hidden, *rest):
        whole = by_heads and hidden.shape[1] == mesh.shape["seq"] * BLOCK
        return jax.shard_map(
            on_heads if whole else on_sections,
            mesh=mesh,
            in_specs=in_specs,
            out_specs=out_specs,
            check_vma=False,
        )(hidden, *rest)

    return mixer
```

```python
import functools

import jax
import jax.numpy as jnp
from jax import lax
from jax.experimental import pallas as pl
from jax.experimental.pallas import tpu as pltpu
from jax.sharding import PartitionSpec as P

HEADS = 32
HEAD_DIM = 64
STATE = 64
KERNEL = 4
BLOCK = 128
INNER = 2048
CONV_CH = 2176


def prefix(value, axis, join, neutral, backward):
    count, mine = (lax.axis_size(axis), lax.axis_index(axis))
    pieces = jax.tree.map(lambda part: lax.all_gather(part, axis), value)
    if backward:
        pieces = jax.tree.map(lambda part: part[::-1], pieces)
        mine = count - 1 - mine
    running = jax.tree.map(
        lambda part, zero: jnp.full_like(part, 0) + jnp.asarray(zero, part.dtype), value, neutral
    )

    def turn(position, running):
        longer = join(running, jax.tree.map(lambda part: part[position], pieces))
        return jax.tree.map(lambda new, old: jnp.where(position < mine, new, old), longer, running)

    return lax.fori_loop(0, count - 1, turn, running)


def extended_2(value, sides, width):
    for axis, dim in sides:
        size, length = (lax.axis_size(axis), value.shape[dim])
        up = [(i, (i + 1) % size) for i in range(size - 1)]
        down = [(j, i) for i, j in up]
        last = lax.slice_in_dim(value, length - width, length, axis=dim)
        initial = lax.slice_in_dim(value, 0, width, axis=dim)
        before = lax.ppermute(last, axis, up)
        after = lax.ppermute(initial, axis, down)
        value = jnp.concatenate([before, value, after], axis=dim)
    return value


def conv_silu(padded, weight, bias):
    length = padded.shape[0] - weight.shape[0] + 1
    total = jnp.broadcast_to(bias[None, :], (length, bias.shape[0]))
    for tap in range(weight.shape[0]):
        total = total + weight[tap][None, :] * padded[tap : tap + length].astype(jnp.float32)
    return jax.nn.silu(total).astype(jnp.bfloat16)


def block_parts(x_part, b_part, c_part, step_size, log_rate, resets):
    length = x_part.shape[0]
    running = jnp.cumsum(log_rate, axis=0)
    running_heads = running.T
    step_heads = step_size.T
    resets_seen = jnp.cumsum(resets)
    scores = jnp.dot(c_part, b_part.T, preferred_element_type=jnp.float32)
    positions = jnp.arange(length)
    allowed = (positions[:, None] >= positions[None, :]) & (
        resets_seen[:, None] == resets_seen[None, :]
    )
    log_gaps = jnp.minimum(running_heads[:, :, None] - running_heads[:, None, :], 0.0)
    weights = (
        jnp.where(allowed[None, :, :], jnp.exp(log_gaps), 0.0)
        * scores[None, :, :]
        * step_heads[:, None, :]
    )
    weights = weights.astype(jnp.bfloat16)
    values = x_part.reshape(length, HEADS, HEAD_DIM)
    inner_part = jnp.einsum("hts,shp->thp", weights, values, preferred_element_type=jnp.float32)
    last_same = resets_seen == resets_seen[-1]
    tail_weight = (
        jnp.where(last_same[:, None], jnp.exp(running[-1][None, :] - running), 0.0) * step_size
    )
    inputs = (tail_weight[:, :, None] * values.astype(jnp.float32)).astype(jnp.bfloat16)
    local_end = jnp.einsum("shp,sn->hpn", inputs, b_part, preferred_element_type=jnp.float32)
    lead_fade = jnp.where((resets_seen == 0)[:, None], jnp.exp(running), 0.0)
    block_fade = jnp.where(resets_seen[-1] == 0, jnp.exp(running[-1]), 0.0)
    return (inner_part, local_end, lead_fade, block_fade)


def chain_combine(earlier, later):
    return (earlier[0] * later[0], later[0][:, None] * earlier[1] + later[1])


def direction(conv_out, step_cols, resets, bias_step, rates, direct, gains, backward):
    length = conv_out.shape[0]
    blocks = length // BLOCK
    x_part = conv_out[:, :INNER]
    b_part = conv_out[:, INNER : INNER + STATE]
    c_part = conv_out[:, INNER + STATE :]
    step_size = jax.nn.softplus(step_cols.astype(jnp.float32) + bias_step[None, :])
    log_rate = -step_size * rates[None, :]
    inner_part, local_end, lead_fade, block_fade = jax.vmap(block_parts)(
        x_part.reshape(blocks, BLOCK, INNER),
        b_part.reshape(blocks, BLOCK, STATE),
        c_part.reshape(blocks, BLOCK, STATE),
        step_size.reshape(blocks, BLOCK, HEADS),
        log_rate.reshape(blocks, BLOCK, HEADS),
        resets.reshape(blocks, BLOCK),
    )
    carried_state = jnp.zeros((HEADS, HEAD_DIM, STATE), jnp.float32)
    carried_fade = jnp.ones((HEADS,), jnp.float32)
    entering = carried_state
    fades_before = carried_fade
    carried_state = block_fade[0][:, None, None] * carried_state + local_end[0]
    carried_fade = block_fade[0] * carried_fade
    summary = (carried_fade, carried_state.reshape(HEADS, HEAD_DIM * STATE))
    identity = (jnp.ones((HEADS,), jnp.float32), jnp.zeros((HEADS, HEAD_DIM * STATE), jnp.float32))
    if backward:
        incoming = prefix(summary, "seq", chain_combine, identity, True)
    else:
        incoming = prefix(summary, "seq", chain_combine, identity, False)
    incoming_state = incoming[1].reshape(HEADS, HEAD_DIM, STATE)
    states = jnp.stack([fades_before[:, None, None] * incoming_state + entering])
    rounded = states.astype(jnp.bfloat16)
    carried = jnp.einsum(
        "btn,bhpn->bthp",
        c_part.reshape(blocks, BLOCK, STATE),
        rounded,
        preferred_element_type=jnp.float32,
    )
    direct_part = direct[None, None, :, None] * x_part.reshape(
        blocks, BLOCK, HEADS, HEAD_DIM
    ).astype(jnp.float32)
    result = (inner_part + lead_fade[..., None] * carried + direct_part).reshape(
        length, HEADS, HEAD_DIM
    )
    scale = lax.rsqrt(jnp.mean(result * result, axis=-1, keepdims=True) + 1e-05)
    return (result * scale * gains.reshape(HEADS, HEAD_DIM)).reshape(length, INNER)


def project(rows_in, in_weight):
    total = jnp.dot(
        rows_in,
        lax.all_gather(in_weight, ("fsdp", "batch"), axis=0, tiled=True),
        preferred_element_type=jnp.float32,
    )
    return total.astype(jnp.bfloat16)


def on_sections(
    hidden, in_weight, read_starts, conv_weight, conv_bias, dt_bias, decay, skip, norm_gain
):
    tokens = hidden[0]
    length = tokens.shape[0]
    margin = KERNEL - 1
    projected = project(tokens, in_weight)
    extended = extended_2(projected[:, :CONV_CH], (("seq", 0),), margin)
    forward_in = conv_silu(extended[: length + margin], conv_weight[0], conv_bias[0])
    backward_in = conv_silu(jnp.flip(extended[margin:], 0), conv_weight[1], conv_bias[1])
    step_cols = projected[:, CONV_CH:]
    positions = lax.axis_index("seq") * length + jnp.arange(length, dtype=jnp.int32)
    marks = read_starts[0]
    starts_here = jnp.any(positions[:, None] == marks[None, :], axis=1).astype(jnp.float32)
    starts_next = jnp.any((positions + 1)[:, None] == marks[None, :], axis=1).astype(jnp.float32)
    forward_out = direction(
        forward_in, step_cols, starts_here, dt_bias[0], decay[0], skip[0], norm_gain[0], False
    )
    backward_out = direction(
        backward_in,
        jnp.flip(step_cols, 0),
        jnp.flip(starts_next, 0),
        dt_bias[1],
        decay[1],
        skip[1],
        norm_gain[1],
        True,
    )
    mixed = forward_out + jnp.flip(backward_out, 0)
    return mixed.astype(jnp.bfloat16)[None]


LANES = 128
SIDE = 256
EDGE = 8
GROUP = 32
HEADER = 16


def ring_order(count):
    return [i if i < count else 3 * count - 1 - i for i in range(2 * count)]


def split_parts(value, count):
    parts = []
    for _ in range(count):
        parts.append(value.astype(jnp.bfloat16))
        value = value - parts[-1].astype(jnp.float32)
    return parts


def lane_row():
    lane = lax.broadcasted_iota(jnp.int32, (BLOCK, LANES), 1)
    row = lax.broadcasted_iota(jnp.int32, (BLOCK, LANES), 0)
    return lane, row


def shard_at(away, ring):
    fsdp, batch = lax.axis_index("fsdp"), lax.axis_index("batch")
    position = jnp.where(fsdp == 0, batch, 2 * ring - 1 - batch)
    there = lax.rem(position + 2 * ring + away, 2 * ring)
    return jnp.where(there < ring, there, 3 * ring - 1 - there)


def take_rows(pieces, ring, ways, rows_in):
    depth = rows_in.shape[1] // len(ways)
    for n, away in enumerate(ways):
        at = pl.ds(pl.multiple_of(shard_at(away, ring) * depth, depth), depth)
        for mask in range(4):
            rows_in[mask * BLOCK : (mask + 1) * BLOCK, n * depth : (n + 1) * depth] = pieces[mask][:, at]


def times_transposed(a, b):
    return lax.dot_general(a, b, (((1,), (1,)), ((), ())), preferred_element_type=jnp.float32)


def pack_kernel(columns, weight_in, own, side, sems):
    seq = lax.axis_index("seq")
    half = side.shape[0]
    few = own.shape[0] - columns - half
    mine = pl.multiple_of(INNER + seq % 2 * half, half)
    other = pl.multiple_of(INNER + (1 - seq % 2) * half, half)
    steps_at = pl.multiple_of(INNER + 2 * half + seq // 2 * few, few)
    copies = [
        (weight_in.at[pl.ds(pl.multiple_of(seq * columns, columns), columns)], own.at[pl.ds(0, columns)]),
        (weight_in.at[pl.ds(mine, half)], own.at[pl.ds(columns, half)]),
        (weight_in.at[pl.ds(steps_at, few)], own.at[pl.ds(columns + half, few)]),
        (weight_in.at[pl.ds(other, half)], side),
    ]
    copies = [pltpu.make_async_copy(a, b, sems.at[i]) for i, (a, b) in enumerate(copies)]
    for copy in copies:
        copy.start()
    for copy in copies:
        copy.wait()


def first_gather_kernel(columns, own, side, up, down, out, sent):
    rows, depth = own.shape
    half = side.shape[0]
    other = columns + LANES
    out[rows:, :] = jnp.zeros((out.shape[0] - rows, out.shape[1]), out.dtype)
    for n, weight in enumerate((own, up, down)):
        out[:rows, n * depth : (n + 1) * depth] = weight[...]
    out[other : other + half, :depth] = side[...]
    sent[:half, :] = up[columns : columns + half, :]
    sent[half:, :] = down[columns : columns + half, :]


def next_gather_kernel(columns, at, held, swapped, up, down, out, sent):
    del held
    rows, depth = up.shape
    half = swapped.shape[0] // 2
    other = columns + LANES
    for n, weight in enumerate((up, down)):
        out[:rows, (at + n) * depth : (at + n + 1) * depth] = weight[...]
        out[other : other + half, (at + n - 2) * depth : (at + n - 1) * depth] = swapped[n * half : (n + 1) * half, :]
    sent[:half, :] = up[columns : columns + half, :]
    sent[half:, :] = down[columns : columns + half, :]


def split_kernel(columns, up, down, sent, crossing):
    half = crossing.shape[0]
    sent[:half, :] = up[columns : columns + half, :]
    sent[half:, :] = down[columns : columns + half, :]
    crossing[...] = down[columns : columns + half, :]


def early_kernel(columns, ring, ways, first, *refs):
    pieces = refs[:4]
    gathered, swapped, table, partial, rest, rows_in, side = refs[4:]
    length = rows_in.shape[0]
    half, depth = swapped.shape[0] // 2, swapped.shape[1]
    take_rows(pieces, ring, ways[:first], rows_in)
    take_rows(pieces, ring, ways[first:], rest)
    for n in range(columns // SIDE):
        at = slice(n * SIDE, (n + 1) * SIDE)
        partial[:length, at] = times_transposed(rows_in[...], gathered[at, :])
    side[...] = gathered[columns:, :]
    for n in range(2):
        side[LANES : LANES + half, (first - 2 + n) * depth : (first - 1 + n) * depth] = swapped[n * half : (n + 1) * half, :]
    partial[:length, columns:] = times_transposed(rows_in[...], side[...])
    other = columns + LANES
    partial[:BLOCK, other:] = partial[:BLOCK, other:] + pltpu.roll(table[HEADER:, :LANES], half, 1)
    partial[length:, : table.shape[1]] = table[:HEADER, :]


def second_kernel(columns, partial, rest, up, down, swapped, out, w_in, sems):
    rows, depth = up.shape
    length = rest.shape[0]
    half = swapped.shape[0] // 2
    other = columns + LANES
    copies = []
    for n in range(2):
        place = w_in.at[pl.ds(other, half), pl.ds(n * depth, depth)]
        copies.append(pltpu.make_async_copy(swapped.at[pl.ds(n * half, half)], place, sems.at[n]))
        copies[-1].start()
    w_in[rows:other, :] = jnp.zeros((other - rows, w_in.shape[1]), jnp.bfloat16)
    w_in[other + half :, :] = jnp.zeros((w_in.shape[0] - other - half, w_in.shape[1]), jnp.bfloat16)
    for n, weight in enumerate((up, down)):
        w_in[:rows, n * depth : (n + 1) * depth] = weight[...]
    for n in range(w_in.shape[0] // SIDE):
        at = slice(n * SIDE, (n + 1) * SIDE)
        if n == columns // SIDE:
            for copy in copies:
                copy.wait()
        out[:length, at] = partial[:length, at] + times_transposed(rest[:, : 2 * depth], w_in[at, :])
    out[length:, :] = partial[length:, :]


def prepare_kernel(heads, *refs):
    marks_in, conv_w_in, conv_b_in, step_bias_in, decay_in, skip_in, gain_in = refs[:7]
    table, conv_w, conv_b, gains, per_head, marks, sems = refs[7:]
    seq = lax.axis_index("seq")
    columns = heads * HEAD_DIM
    own_lanes = pl.ds(pl.multiple_of(seq * columns, columns), columns)
    side_lanes = pl.ds(INNER, LANES)
    copies = [
        (conv_w_in.at[:, :, own_lanes], conv_w.at[:, :, pl.ds(0, columns)]),
        (conv_w_in.at[:, :, side_lanes], conv_w.at[:, :, pl.ds(columns, LANES)]),
        (conv_b_in.at[:, own_lanes], conv_b.at[:, pl.ds(0, columns)]),
        (conv_b_in.at[:, side_lanes], conv_b.at[:, pl.ds(columns, LANES)]),
        (step_bias_in, per_head.at[0]),
        (decay_in, per_head.at[1]),
        (skip_in, per_head.at[2]),
        (gain_in.at[:, own_lanes], gains),
        (marks_in, marks),
    ]
    copies = [pltpu.make_async_copy(a, b, sems.at[i]) for i, (a, b) in enumerate(copies)]
    for copy in copies:
        copy.start()
    for copy in copies:
        copy.wait()

    lane, row = lane_row()
    within = lane % GROUP
    head_lane = within < 2 * heads
    to_first = lax.rem(LANES - seq * heads, LANES)

    def own_heads(k):
        both = jnp.concatenate([per_head[k], jnp.zeros((2, LANES - HEADS), jnp.float32)], axis=1)
        both = pltpu.roll(both, to_first, 1)
        behind = pltpu.roll(both, heads, 1)
        value = jnp.where(lane[:1] < heads, both[0:1, :], behind[1:2, :])
        return jnp.where(lane[:1] < 2 * heads, value, 0.0)

    for d in range(2):
        table[d * KERNEL : (d + 1) * KERNEL, :] = conv_w[d]
    table[8:10, :] = conv_b[...]
    for k in range(2):
        value = jnp.broadcast_to(own_heads(k), (8, LANES))
        value = sum([pltpu.roll(value, g * GROUP, 1) for g in range(1, LANES // GROUP)], value)
        table[10 + k : 11 + k, :LANES] = value[:1]
    direct = packed(jnp.broadcast_to(own_heads(2), (16, LANES)), 3, heads)
    for d in range(2):
        wide = jnp.dot(direct, head_columns(heads, d), preferred_element_type=jnp.float32)
        table[12 + d : 13 + d, :columns] = wide[:1]
    table[14:16, :columns] = gains[...]

    position = row + lane // GROUP * BLOCK
    here = position == marks[:, 0:1]
    after = position + 1 == marks[:, 0:1]
    for m in range(1, marks.shape[1]):
        here = here | (position == marks[:, m : m + 1])
        after = after | (position + 1 == marks[:, m : m + 1])
    forward_start, backward_start = within == 2 * heads, within == 2 * heads + 1
    starts = jnp.where((here & forward_start) | (after & backward_start), 1.0, 0.0).astype(jnp.bfloat16)
    backward_lane = ((within >= heads) & head_lane) | backward_start
    lower = jnp.where(row >= lane, 1.0, 0.0).astype(jnp.bfloat16)
    upper = jnp.where(row <= lane, 1.0, 0.0).astype(jnp.bfloat16)
    ahead = jnp.dot(lower, starts, preferred_element_type=jnp.float32)
    behind = jnp.dot(upper, starts, preferred_element_type=jnp.float32)
    seen = jnp.where(backward_lane, behind, ahead)
    wanted = lane - within + 2 * heads + jnp.where(backward_lane, 1, 0)
    chosen = jnp.where(row == wanted, 1.0, 0.0).astype(jnp.bfloat16)
    seen = jnp.dot(seen.astype(jnp.bfloat16), chosen, preferred_element_type=jnp.float32)
    chosen = (row == lane // 2 * GROUP + lane % 2 * heads) & (lane < 2 * LANES // GROUP)
    chosen = jnp.where(chosen, 1.0, 0.0).astype(jnp.bfloat16)
    table[HEADER:, :LANES] = jnp.dot(seen.astype(jnp.bfloat16), chosen, preferred_element_type=jnp.float32)


def head_columns(heads, d):
    at_row = lax.broadcasted_iota(jnp.int32, (LANES, heads * HEAD_DIM), 0)
    head = lax.broadcasted_iota(jnp.int32, (LANES, heads * HEAD_DIM), 1) // HEAD_DIM + d * heads
    hit = (at_row == head) | (at_row == head + 2 * heads) | (at_row == head + 4 * heads)
    return jnp.where(hit, 1.0, 0.0).astype(jnp.bfloat16)


def packed(value, count, heads):
    parts = split_parts(value, count)
    joined = parts[0].astype(jnp.float32)
    for k in range(1, count):
        joined = joined + pltpu.roll(parts[k].astype(jnp.float32), 2 * heads * k, 1)
    return joined.astype(jnp.bfloat16)


def mixer_kernel(heads, partial, rest, up_end, down_end, far, *refs):
    outs, refs = refs[:4], refs[4:]
    w_end, padded, xs, cs, bs, widen_in, leads, tails, state, ys, mixed = refs
    seq = lax.axis_index("seq")
    columns = heads * HEAD_DIM
    depth = up_end.shape[1]
    cut, rows = up_end.shape[0], up_end.shape[0] + down_end.shape[0]
    chunks = columns // LANES
    length = rest.shape[0]
    blocks = length // BLOCK
    lane, row = lane_row()

    def table(first, last, lanes):
        return partial[length + first : length + last, lanes]

    half = far.shape[0]
    other = columns + LANES
    w_end[:cut, :] = up_end[...]
    w_end[cut:rows, :] = down_end[...]
    w_end[other : other + half, :] = far[...]
    w_end[rows:other, :] = jnp.zeros((other - rows, depth), jnp.bfloat16)
    w_end[other + half :, :] = jnp.zeros((w_end.shape[0] - other - half, depth), jnp.bfloat16)
    edge = jnp.zeros((EDGE, LANES), jnp.float32)
    for c in range(chunks + 1):
        padded[c, 0:EDGE, :] = edge
        padded[c, EDGE + length :, :] = edge
    state[...] = jnp.zeros_like(state)

    places = [pl.multiple_of((seq ^ mask) * BLOCK, BLOCK) for mask in range(4)]

    def project_in(n):
        at = slice(n * SIDE, (n + 1) * SIDE)
        return times_transposed(rest[:, 2 * depth :], w_end[at, :])

    def rounded(value):
        return value.astype(jnp.bfloat16).astype(jnp.float32)

    def keep(c, value):
        for mask in range(4):
            padded[c, pl.ds(EDGE + places[mask], BLOCK), :] = value[mask * BLOCK : (mask + 1) * BLOCK, :]

    side_out = project_in(columns // SIDE)
    mine = rounded(side_out[:, :LANES] + partial[:length, columns:other])
    others = rounded(side_out[:, LANES:] + partial[:length, other:])
    even = jnp.broadcast_to(seq, mine.shape) % 2 == 0
    low, high = jnp.where(even, mine, others), jnp.where(even, others, mine)
    left = lax.broadcasted_iota(jnp.int32, mine.shape, 1) < half
    keep(chunks, jnp.where(left, low, pltpu.roll(high, half, 1)))
    for n in range(columns // SIDE):
        part_out = rounded(project_in(n) + partial[:length, n * SIDE : (n + 1) * SIDE])
        for k in range(SIDE // LANES):
            keep(n * (SIDE // LANES) + k, part_out[:, k * LANES : (k + 1) * LANES])

    within = lane % GROUP
    head_lane = within < 2 * heads
    backward_lane = (within >= heads) & head_lane
    to_first = LANES - half - seq % 2 * heads
    raw = jnp.zeros((BLOCK, LANES), jnp.float32)
    for mask in range(4):
        own_steps = pltpu.roll(mine[mask * BLOCK : (mask + 1) * BLOCK, :], to_first, 1)
        own_steps = jnp.where(lane < heads, own_steps, 0.0)
        raw = raw + pltpu.roll(own_steps + pltpu.roll(own_steps, heads, 1), (seq ^ mask) * GROUP, 1)
    raw = raw + table(10, 11, slice(0, LANES))
    step = jnp.maximum(raw, 0.0) + jnp.log1p(jnp.exp(-jnp.abs(raw)))
    rate = -step * table(11, 12, slice(0, LANES))
    two = jnp.concatenate(split_parts(rate, 2), axis=1)
    lower = jnp.where(row >= lane, 1.0, 0.0).astype(jnp.bfloat16)
    upper = jnp.where(row <= lane, 1.0, 0.0).astype(jnp.bfloat16)
    sums = jnp.dot(jnp.concatenate([lower, upper], axis=0), two, preferred_element_type=jnp.float32)
    sums = sums[:, :LANES] + sums[:, LANES:]
    cum = jnp.where(backward_lane, sums[BLOCK:], sums[:BLOCK])
    last = jnp.where(backward_lane[:1], cum[:1], cum[BLOCK - 1 :])
    chosen = jnp.where(row == lane // GROUP * 2 + jnp.where(backward_lane, 1, 0), 1.0, 0.0).astype(jnp.bfloat16)
    seen = pltpu.roll(partial[:BLOCK, other:], half, 1).astype(jnp.bfloat16)
    seen = jnp.dot(seen, chosen, preferred_element_type=jnp.float32)
    seen_last = jnp.where(backward_lane[:1], seen[:1], seen[BLOCK - 1 :])
    tail = jnp.where(seen == seen_last, jnp.exp(last - cum) * step, 0.0)
    lead = jnp.where(seen == 0.0, jnp.exp(cum), 0.0)
    last, seen_last = jnp.broadcast_to(last, (8, LANES)), jnp.broadcast_to(seen_last, (8, LANES))
    fade = jnp.where(seen_last == 0.0, jnp.exp(last), 0.0)
    seen_turned = seen.T
    spread = [head_columns(heads, d) for d in range(2)]
    shown = (jnp.log(step) - cum).T
    fades = []
    for b in range(blocks):
        for k, value in enumerate((lead, tail)):
            if b:
                value = pltpu.roll(value, LANES - b * GROUP, 1)
            at = (k * blocks + b) * BLOCK
            widen_in[at : at + BLOCK, :] = jnp.where(lane < 2 * heads, value, 0.0).astype(jnp.bfloat16)
        value = pltpu.roll(fade, LANES - b * GROUP, 1) if b else fade
        fades.append(packed(jnp.where(lane[:8] < 2 * heads, value, 0.0), 2, heads)[:1])
    fades = jnp.concatenate(fades + [jnp.zeros((16 - blocks, LANES), jnp.bfloat16)], axis=0)
    fade_wide = []
    for d in range(2):
        wide = jnp.dot(widen_in[...], spread[d], preferred_element_type=jnp.float32).astype(jnp.bfloat16)
        leads[d] = wide[:length]
        tails[d] = wide[length:]
        fade_wide.append(jnp.dot(fades, spread[d], preferred_element_type=jnp.float32))

    short = 64

    def convolve(c, i):
        at = i * short
        taps = [padded[c, at + EDGE - 3 + k : at + EDGE - 3 + k + short, :] for k in range(7)]
        rows_at = slice(at, at + short)
        lanes = slice(c * LANES, (c + 1) * LANES)
        for d in range(2):
            acc = table(8 + d, 9 + d, lanes)
            for k in range(KERNEL):
                n = d * KERNEL + k
                acc = acc + table(n, n + 1, lanes) * taps[k if d == 0 else 6 - k]
            half = 0.5 * acc
            value = half + half * jnp.tanh(half)
            if c < chunks:
                xs[d, rows_at, lanes] = value.astype(jnp.bfloat16)
            else:
                high = lax.broadcasted_iota(jnp.int32, (short, LANES), 1) >= STATE
                cs[d, rows_at, :] = jnp.where(high, value, 0.0).astype(jnp.bfloat16)
                bs[d, rows_at, :] = jnp.where(high, pltpu.roll(value, STATE, 1), 0.0).astype(jnp.bfloat16)

    group = SIDE // HEAD_DIM
    lane_head = lax.broadcasted_iota(jnp.int32, (BLOCK, SIDE), 1) // HEAD_DIM
    known = {}

    def scan_block(q, d, b):
        at = slice(b * BLOCK, (b + 1) * BLOCK)
        lanes = slice(q * SIDE, (q + 1) * SIDE)
        c_part = cs[d, at, :]
        b_part = bs[d, at, :]
        if (d, b) not in known:
            ordered = (row >= lane) if d == 0 else (row <= lane)
            n = b * GROUP + d * heads
            bar = jnp.where(ordered & (seen[:, n : n + 1] == seen_turned[n : n + 1, :]), 0.0, -1e30)
            known[d, b] = times_transposed(c_part, b_part), bar
        scores, bar = known[d, b]
        before = state[d, :, lanes]
        carried = jnp.dot(c_part, before.astype(jnp.bfloat16), preferred_element_type=jnp.float32)
        x_part = xs[d, at, lanes]
        local_end = lax.dot_general(
            b_part, tails[d, at, lanes] * x_part, (((0,), (0,)), ((), ())), preferred_element_type=jnp.float32
        )
        state[d, :, lanes] = fade_wide[d][b : b + 1, lanes] * before + local_end
        some = []
        for h in range(q * group, (q + 1) * group):
            n = b * GROUP + d * heads + h
            gap = cum[:, n : n + 1] + (shown[n : n + 1, :] + bar)
            some.append((jnp.exp(gap) * scores).astype(jnp.bfloat16))
        none = jnp.zeros_like(x_part)
        spaced = jnp.concatenate([jnp.where(lane_head == h, x_part, none) for h in range(group)], axis=0)
        inner = jnp.dot(jnp.concatenate(some, axis=1), spaced, preferred_element_type=jnp.float32)
        ys[d, at, lanes] = (
            inner
            + leads[d, at, lanes].astype(jnp.float32) * carried
            + table(12 + d, 13 + d, lanes) * x_part.astype(jnp.float32)
        )

    in_group = SIDE // LANES
    for i in range(length // short):
        for c in (chunks, *range(in_group)):
            convolve(c, i)
    for q in range(columns // SIDE):
        for i in range(blocks):
            for d in range(2):
                scan_block(q, d, i if d == 0 else blocks - 1 - i)
            for c in range((q + 1) * in_group, min((q + 2) * in_group, chunks)):
                for part in range(BLOCK // short):
                    convolve(c, i * (BLOCK // short) + part)

    head_row = lax.broadcasted_iota(jnp.int32, (SIDE, SIDE), 0) // HEAD_DIM
    head_col = lax.broadcasted_iota(jnp.int32, (SIDE, SIDE), 1) // HEAD_DIM
    same = jnp.where(head_row == head_col, 1.0 / HEAD_DIM, 0.0).astype(jnp.bfloat16)
    for q in range(columns // SIDE):
        lanes = slice(q * SIDE, (q + 1) * SIDE)
        both = 0.0
        for d in range(2):
            y = ys[d, :, lanes]
            mean = jnp.dot((y * y).astype(jnp.bfloat16), same, preferred_element_type=jnp.float32)
            both = both + y * lax.rsqrt(mean + 1e-05) * table(14 + d, 15 + d, lanes)
        mixed[:, lanes] = both.astype(jnp.bfloat16)
    for mask in range(4):
        outs[mask][...] = mixed[pl.ds(places[mask], BLOCK), :]


IN_VMEM = pl.BlockSpec(memory_space=pltpu.VMEM)
IN_HBM = pl.BlockSpec(memory_space=pltpu.HBM)
ROOM = 24 * 1024 * 1024


def call(kernel, shapes, scratch, *operands, space=IN_VMEM, apart=0, aliases=None):
    shapes = [jax.ShapeDtypeStruct(*one) for one in shapes]
    return pl.pallas_call(
        kernel,
        out_shape=shapes,
        in_specs=[space] * (len(operands) - apart) + [pl.BlockSpec(memory_space=pl.ANY)] * apart,
        out_specs=[IN_VMEM] * len(shapes),
        scratch_shapes=scratch,
        input_output_aliases=aliases or {},
        compiler_params=pltpu.CompilerParams(vmem_limit_bytes=ROOM),
    )(*operands)


def pack(weight, columns):
    depth = weight.shape[1]
    few = 2 * columns // HEAD_DIM
    shapes = [((columns + STATE + few, depth), weight.dtype), ((STATE, depth), weight.dtype)]
    scratch = [pltpu.SemaphoreType.DMA((4,))]
    return call(functools.partial(pack_kernel, columns), shapes, scratch, weight, space=IN_HBM)


def first_gather(columns, shape, own, side, up, down):
    shapes = [(shape, own.dtype), ((2 * side.shape[0], side.shape[1]), own.dtype)]
    return call(functools.partial(first_gather_kernel, columns), shapes, [], own, side, up, down)


def next_gather(columns, at, held, swapped, up, down):
    shapes = [(held.shape, held.dtype), (swapped.shape, held.dtype)]
    kernel = functools.partial(next_gather_kernel, columns, at)
    return call(kernel, shapes, [], held, swapped, up, down, aliases={0: 0})


def split(columns, up, down):
    rows, depth = up.shape
    shapes = [(2 * STATE, depth), (STATE, depth)]
    shapes = [(one, up.dtype) for one in shapes]
    return call(functools.partial(split_kernel, columns), shapes, [], up, down)


def prepare(heads, params):
    columns = heads * HEAD_DIM
    scratch = [
        pltpu.VMEM((2, KERNEL, columns + LANES), jnp.float32),
        pltpu.VMEM((2, columns + LANES), jnp.float32),
        pltpu.VMEM((2, columns), jnp.float32),
        pltpu.VMEM((3, 2, HEADS), jnp.float32),
        pltpu.VMEM(params[0].shape, jnp.int32),
        pltpu.SemaphoreType.DMA((9,)),
    ]
    shape = ((HEADER + BLOCK, columns + LANES), jnp.float32)
    return call(functools.partial(prepare_kernel, heads), [shape], scratch, *params, space=IN_HBM)[0]


def early(columns, ring, ways, pieces, gathered, swapped, table):
    length = pieces[0].shape[0] * len(pieces)
    wide, known = gathered.shape
    first = 2 * ring - 3
    depth = known // first
    shapes = [
        ((length + HEADER, wide), jnp.float32),
        ((length, depth * len(ways) - known), jnp.bfloat16),
    ]
    scratch = [pltpu.VMEM((length, known), jnp.bfloat16), pltpu.VMEM((SIDE, known), jnp.bfloat16)]
    kernel = functools.partial(early_kernel, columns, ring, ways, first)
    return call(kernel, shapes, scratch, *pieces, gathered, swapped, table)


def second(columns, partial, rest, up, down, swapped):
    scratch = [pltpu.VMEM((partial.shape[1], 2 * up.shape[1]), jnp.bfloat16), pltpu.SemaphoreType.DMA((2,))]
    operands = (partial, rest, up, down, swapped)
    return call(functools.partial(second_kernel, columns), [(partial.shape, jnp.float32)], scratch, *operands, apart=1)[0]


def mix(heads, count, partial, rest, *others):
    columns = heads * HEAD_DIM
    length = rest.shape[0]
    scratch = [
        ((columns + SIDE, others[0].shape[1]), jnp.bfloat16),
        ((columns // LANES + 1, length + 2 * EDGE, LANES), jnp.float32),
        ((2, length, columns), jnp.bfloat16),
        ((2, length, LANES), jnp.bfloat16),
        ((2, length, LANES), jnp.bfloat16),
        ((2 * length, LANES), jnp.bfloat16),
        ((2, length, columns), jnp.bfloat16),
        ((2, length, columns), jnp.bfloat16),
        ((2, LANES, columns), jnp.float32),
        ((2, length, columns), jnp.float32),
        ((length, columns), jnp.bfloat16),
    ]
    shapes = [((length // count, columns), jnp.bfloat16)] * count
    scratch = [pltpu.VMEM(*one) for one in scratch]
    return call(functools.partial(mixer_kernel, heads), shapes, scratch, partial, rest, *others)


def turn(value, way):
    order = ring_order(lax.axis_size("batch"))
    count = len(order)
    return lax.ppermute(value, ("fsdp", "batch"), [(order[i], order[(i + way) % count]) for i in range(count)])


def turn_across(value, way):
    order = ring_order(lax.axis_size("batch"))
    count = len(order)
    pairs = []
    for s in range(lax.axis_size("seq")):
        pairs += [(s * count + order[i], (s ^ 1) * count + order[(i + way) % count]) for i in range(count)]
    return lax.ppermute(value, ("seq", "fsdp", "batch"), pairs)


def swap(value, axis, mask):
    return lax.ppermute(value, axis, [(i, i ^ mask) for i in range(lax.axis_size(axis))])


def on_heads(hidden, in_weight, read_starts, conv_weight, conv_bias, dt_bias, decay, skip, norm_gain):
    tokens = hidden[0]
    count = lax.axis_size("seq")
    seq = lax.axis_index("seq")
    heads = HEADS // count
    columns = heads * HEAD_DIM
    own, side = pack(in_weight.T, columns)

    ring = lax.axis_size("batch")
    late, _ = lax.optimization_barrier((tokens, own))
    across = swap(late, "seq", 2)
    pieces = [tokens, swap(tokens, "seq", 1), across, swap(across, "seq", 1)]
    table = prepare(heads, (read_starts, conv_weight, conv_bias, dt_bias, decay, skip, norm_gain))
    first = 2 * ring - 3
    ways = [0]
    up = down = own
    for away in range(1, ring):
        before = up, down
        up, down = turn(up, 1), turn(down, -1)
        ways += [-away, away]
        if away == 1:
            beside = table
        elif away == 2:
            gathered, sent = first_gather(columns, (columns + SIDE, first * own.shape[1]), own, side, *before)
            beside = swapped = swap(sent, "seq", 1)
        elif away < ring - 1:
            gathered, sent = next_gather(columns, 2 * away - 3, gathered, swapped, *before)
            beside = swapped = swap(sent, "seq", 1)
        else:
            gathered, sent = next_gather(columns, 2 * away - 3, gathered, swapped, *before)
            swapped = swap(sent, "seq", 1)
            partial, rest = early(columns, ring, tuple(ways) + (ring,), pieces, gathered, swapped, table)
            beside = partial
        up, _ = lax.optimization_barrier((up, beside))
        down, _ = lax.optimization_barrier((down, beside))
    cut = own.shape[0] // 32 * 16
    ends = [turn(up[:cut], 1), turn(down[cut:], -1)]
    sent, crossing = split(columns, up, down)
    far = turn_across(crossing, -1)
    partial = second(columns, partial, rest, up, down, swap(sent, "seq", 1))
    results = mix(heads, count, partial, rest, *ends, far)
    received = [results[0]] + [swap(results[mask], "seq", mask) for mask in range(1, count)]
    mixed = jnp.zeros((tokens.shape[0], INNER), jnp.bfloat16)
    for mask in range(count):
        mixed = lax.dynamic_update_slice(mixed, received[mask], (0, (seq ^ mask) * columns))
    return mixed[None]


def solution(mesh):
    in_specs = (
        P(("fsdp", "batch"), "seq", None),
        P(("fsdp", "batch"), None),
        P(("fsdp", "batch"), None),
        P(),
        P(),
        P(),
        P(),
        P(),
        P(),
    )
    out_specs = P(("fsdp", "batch"), "seq", None)
    by_heads = mesh.shape["seq"] == 4 and mesh.shape["fsdp"] == 2

    def mixer(hidden, *rest):
        whole = by_heads and hidden.shape[1] == mesh.shape["seq"] * BLOCK
        return jax.shard_map(
            on_heads if whole else on_sections,
            mesh=mesh,
            in_specs=in_specs,
            out_specs=out_specs,
            check_vma=False,
        )(hidden, *rest)

    return mixer
```

```python
import functools

import jax
import jax.numpy as jnp
from jax import lax
from jax.experimental import pallas as pl
from jax.experimental.pallas import tpu as pltpu
from jax.sharding import PartitionSpec as P

HEADS = 32
HEAD_DIM = 64
STATE = 64
KERNEL = 4
BLOCK = 128
INNER = 2048
CONV_CH = 2176


def prefix(value, axis, join, neutral, backward):
    count, mine = (lax.axis_size(axis), lax.axis_index(axis))
    pieces = jax.tree.map(lambda part: lax.all_gather(part, axis), value)
    if backward:
        pieces = jax.tree.map(lambda part: part[::-1], pieces)
        mine = count - 1 - mine
    running = jax.tree.map(
        lambda part, zero: jnp.full_like(part, 0) + jnp.asarray(zero, part.dtype), value, neutral
    )

    def turn(position, running):
        longer = join(running, jax.tree.map(lambda part: part[position], pieces))
        return jax.tree.map(lambda new, old: jnp.where(position < mine, new, old), longer, running)

    return lax.fori_loop(0, count - 1, turn, running)


def extended_2(value, sides, width):
    for axis, dim in sides:
        size, length = (lax.axis_size(axis), value.shape[dim])
        up = [(i, (i + 1) % size) for i in range(size - 1)]
        down = [(j, i) for i, j in up]
        last = lax.slice_in_dim(value, length - width, length, axis=dim)
        initial = lax.slice_in_dim(value, 0, width, axis=dim)
        before = lax.ppermute(last, axis, up)
        after = lax.ppermute(initial, axis, down)
        value = jnp.concatenate([before, value, after], axis=dim)
    return value


def conv_silu(padded, weight, bias):
    length = padded.shape[0] - weight.shape[0] + 1
    total = jnp.broadcast_to(bias[None, :], (length, bias.shape[0]))
    for tap in range(weight.shape[0]):
        total = total + weight[tap][None, :] * padded[tap : tap + length].astype(jnp.float32)
    return jax.nn.silu(total).astype(jnp.bfloat16)


def block_parts(x_part, b_part, c_part, step_size, log_rate, resets):
    length = x_part.shape[0]
    running = jnp.cumsum(log_rate, axis=0)
    running_heads = running.T
    step_heads = step_size.T
    resets_seen = jnp.cumsum(resets)
    scores = jnp.dot(c_part, b_part.T, preferred_element_type=jnp.float32)
    positions = jnp.arange(length)
    allowed = (positions[:, None] >= positions[None, :]) & (
        resets_seen[:, None] == resets_seen[None, :]
    )
    log_gaps = jnp.minimum(running_heads[:, :, None] - running_heads[:, None, :], 0.0)
    weights = (
        jnp.where(allowed[None, :, :], jnp.exp(log_gaps), 0.0)
        * scores[None, :, :]
        * step_heads[:, None, :]
    )
    weights = weights.astype(jnp.bfloat16)
    values = x_part.reshape(length, HEADS, HEAD_DIM)
    inner_part = jnp.einsum("hts,shp->thp", weights, values, preferred_element_type=jnp.float32)
    last_same = resets_seen == resets_seen[-1]
    tail_weight = (
        jnp.where(last_same[:, None], jnp.exp(running[-1][None, :] - running), 0.0) * step_size
    )
    inputs = (tail_weight[:, :, None] * values.astype(jnp.float32)).astype(jnp.bfloat16)
    local_end = jnp.einsum("shp,sn->hpn", inputs, b_part, preferred_element_type=jnp.float32)
    lead_fade = jnp.where((resets_seen == 0)[:, None], jnp.exp(running), 0.0)
    block_fade = jnp.where(resets_seen[-1] == 0, jnp.exp(running[-1]), 0.0)
    return (inner_part, local_end, lead_fade, block_fade)


def chain_combine(earlier, later):
    return (earlier[0] * later[0], later[0][:, None] * earlier[1] + later[1])


def direction(conv_out, step_cols, resets, bias_step, rates, direct, gains, backward):
    length = conv_out.shape[0]
    blocks = length // BLOCK
    x_part = conv_out[:, :INNER]
    b_part = conv_out[:, INNER : INNER + STATE]
    c_part = conv_out[:, INNER + STATE :]
    step_size = jax.nn.softplus(step_cols.astype(jnp.float32) + bias_step[None, :])
    log_rate = -step_size * rates[None, :]
    inner_part, local_end, lead_fade, block_fade = jax.vmap(block_parts)(
        x_part.reshape(blocks, BLOCK, INNER),
        b_part.reshape(blocks, BLOCK, STATE),
        c_part.reshape(blocks, BLOCK, STATE),
        step_size.reshape(blocks, BLOCK, HEADS),
        log_rate.reshape(blocks, BLOCK, HEADS),
        resets.reshape(blocks, BLOCK),
    )
    carried_state = jnp.zeros((HEADS, HEAD_DIM, STATE), jnp.float32)
    carried_fade = jnp.ones((HEADS,), jnp.float32)
    entering = carried_state
    fades_before = carried_fade
    carried_state = block_fade[0][:, None, None] * carried_state + local_end[0]
    carried_fade = block_fade[0] * carried_fade
    summary = (carried_fade, carried_state.reshape(HEADS, HEAD_DIM * STATE))
    identity = (jnp.ones((HEADS,), jnp.float32), jnp.zeros((HEADS, HEAD_DIM * STATE), jnp.float32))
    if backward:
        incoming = prefix(summary, "seq", chain_combine, identity, True)
    else:
        incoming = prefix(summary, "seq", chain_combine, identity, False)
    incoming_state = incoming[1].reshape(HEADS, HEAD_DIM, STATE)
    states = jnp.stack([fades_before[:, None, None] * incoming_state + entering])
    rounded = states.astype(jnp.bfloat16)
    carried = jnp.einsum(
        "btn,bhpn->bthp",
        c_part.reshape(blocks, BLOCK, STATE),
        rounded,
        preferred_element_type=jnp.float32,
    )
    direct_part = direct[None, None, :, None] * x_part.reshape(
        blocks, BLOCK, HEADS, HEAD_DIM
    ).astype(jnp.float32)
    result = (inner_part + lead_fade[..., None] * carried + direct_part).reshape(
        length, HEADS, HEAD_DIM
    )
    scale = lax.rsqrt(jnp.mean(result * result, axis=-1, keepdims=True) + 1e-05)
    return (result * scale * gains.reshape(HEADS, HEAD_DIM)).reshape(length, INNER)


def project(rows_in, in_weight):
    total = jnp.dot(
        rows_in,
        lax.all_gather(in_weight, ("fsdp", "batch"), axis=0, tiled=True),
        preferred_element_type=jnp.float32,
    )
    return total.astype(jnp.bfloat16)


def on_sections(
    hidden, in_weight, read_starts, conv_weight, conv_bias, dt_bias, decay, skip, norm_gain
):
    tokens = hidden[0]
    length = tokens.shape[0]
    margin = KERNEL - 1
    projected = project(tokens, in_weight)
    extended = extended_2(projected[:, :CONV_CH], (("seq", 0),), margin)
    forward_in = conv_silu(extended[: length + margin], conv_weight[0], conv_bias[0])
    backward_in = conv_silu(jnp.flip(extended[margin:], 0), conv_weight[1], conv_bias[1])
    step_cols = projected[:, CONV_CH:]
    positions = lax.axis_index("seq") * length + jnp.arange(length, dtype=jnp.int32)
    marks = read_starts[0]
    starts_here = jnp.any(positions[:, None] == marks[None, :], axis=1).astype(jnp.float32)
    starts_next = jnp.any((positions + 1)[:, None] == marks[None, :], axis=1).astype(jnp.float32)
    forward_out = direction(
        forward_in, step_cols, starts_here, dt_bias[0], decay[0], skip[0], norm_gain[0], False
    )
    backward_out = direction(
        backward_in,
        jnp.flip(step_cols, 0),
        jnp.flip(starts_next, 0),
        dt_bias[1],
        decay[1],
        skip[1],
        norm_gain[1],
        True,
    )
    mixed = forward_out + jnp.flip(backward_out, 0)
    return mixed.astype(jnp.bfloat16)[None]


LANES = 128
SIDE = 256
EDGE = 8
GROUP = 32
HEADER = 16


def ring_order(count):
    return [i if i < count else 3 * count - 1 - i for i in range(2 * count)]


def split_parts(value, count):
    parts = []
    for _ in range(count):
        parts.append(value.astype(jnp.bfloat16))
        value = value - parts[-1].astype(jnp.float32)
    return parts


def lane_row():
    lane = lax.broadcasted_iota(jnp.int32, (BLOCK, LANES), 1)
    row = lax.broadcasted_iota(jnp.int32, (BLOCK, LANES), 0)
    return lane, row


def shard_at(away, ring):
    fsdp, batch = lax.axis_index("fsdp"), lax.axis_index("batch")
    position = jnp.where(fsdp == 0, batch, 2 * ring - 1 - batch)
    there = lax.rem(position + 2 * ring + away, 2 * ring)
    return jnp.where(there < ring, there, 3 * ring - 1 - there)


def take_rows(pieces, ring, ways, rows_in):
    depth = rows_in.shape[1] // len(ways)
    for n, away in enumerate(ways):
        at = pl.ds(pl.multiple_of(shard_at(away, ring) * depth, depth), depth)
        for mask in range(4):
            rows_in[mask * BLOCK : (mask + 1) * BLOCK, n * depth : (n + 1) * depth] = pieces[mask][:, at]


def times_transposed(a, b):
    return lax.dot_general(a, b, (((1,), (1,)), ((), ())), preferred_element_type=jnp.float32)


def pack_kernel(columns, weight_in, own, side, sems):
    seq = lax.axis_index("seq")
    half = side.shape[0]
    few = own.shape[0] - columns - half
    mine = pl.multiple_of(INNER + seq % 2 * half, half)
    other = pl.multiple_of(INNER + (1 - seq % 2) * half, half)
    steps_at = pl.multiple_of(INNER + 2 * half + seq // 2 * few, few)
    copies = [
        (weight_in.at[pl.ds(pl.multiple_of(seq * columns, columns), columns)], own.at[pl.ds(0, columns)]),
        (weight_in.at[pl.ds(mine, half)], own.at[pl.ds(columns, half)]),
        (weight_in.at[pl.ds(steps_at, few)], own.at[pl.ds(columns + half, few)]),
        (weight_in.at[pl.ds(other, half)], side),
    ]
    copies = [pltpu.make_async_copy(a, b, sems.at[i]) for i, (a, b) in enumerate(copies)]
    for copy in copies:
        copy.start()
    for copy in copies:
        copy.wait()


def first_gather_kernel(columns, own, side, up, down, out, sent):
    rows, depth = own.shape
    half = side.shape[0]
    other = columns + LANES
    out[rows:, :] = jnp.zeros((out.shape[0] - rows, out.shape[1]), out.dtype)
    for n, weight in enumerate((own, up, down)):
        out[:rows, n * depth : (n + 1) * depth] = weight[...]
    out[other : other + half, :depth] = side[...]
    sent[:half, :] = up[columns : columns + half, :]
    sent[half:, :] = down[columns : columns + half, :]


def next_gather_kernel(columns, at, held, swapped, up, down, out, sent):
    del held
    rows, depth = up.shape
    half = swapped.shape[0] // 2
    other = columns + LANES
    for n, weight in enumerate((up, down)):
        out[:rows, (at + n) * depth : (at + n + 1) * depth] = weight[...]
        out[other : other + half, (at + n - 2) * depth : (at + n - 1) * depth] = swapped[n * half : (n + 1) * half, :]
    sent[:half, :] = up[columns : columns + half, :]
    sent[half:, :] = down[columns : columns + half, :]


def split_kernel(columns, up, down, sent, crossing):
    half = crossing.shape[0]
    sent[:half, :] = up[columns : columns + half, :]
    sent[half:, :] = down[columns : columns + half, :]
    crossing[...] = down[columns : columns + half, :]


def early_kernel(columns, ring, ways, first, *refs):
    pieces = refs[:4]
    gathered, swapped, table, partial, rest, rows_in, side = refs[4:]
    length = rows_in.shape[0]
    half, depth = swapped.shape[0] // 2, swapped.shape[1]
    take_rows(pieces, ring, ways[:first], rows_in)
    take_rows(pieces, ring, ways[first:], rest)
    for n in range(columns // SIDE):
        at = slice(n * SIDE, (n + 1) * SIDE)
        partial[:length, at] = times_transposed(rows_in[...], gathered[at, :])
    side[...] = gathered[columns:, :]
    for n in range(2):
        side[LANES : LANES + half, (first - 2 + n) * depth : (first - 1 + n) * depth] = swapped[n * half : (n + 1) * half, :]
    partial[:length, columns:] = times_transposed(rows_in[...], side[...])
    other = columns + LANES
    partial[:BLOCK, other:] = partial[:BLOCK, other:] + pltpu.roll(table[HEADER:, :LANES], half, 1)
    partial[length:, : table.shape[1]] = table[:HEADER, :]


def second_kernel(columns, partial, rest, up, down, swapped, out, w_in, sems):
    rows, depth = up.shape
    length = rest.shape[0]
    half = swapped.shape[0] // 2
    other = columns + LANES
    copies = []
    for n in range(2):
        place = w_in.at[pl.ds(other, half), pl.ds(n * depth, depth)]
        copies.append(pltpu.make_async_copy(swapped.at[pl.ds(n * half, half)], place, sems.at[n]))
        copies[-1].start()
    w_in[rows:other, :] = jnp.zeros((other - rows, w_in.shape[1]), jnp.bfloat16)
    w_in[other + half :, :] = jnp.zeros((w_in.shape[0] - other - half, w_in.shape[1]), jnp.bfloat16)
    for n, weight in enumerate((up, down)):
        w_in[:rows, n * depth : (n + 1) * depth] = weight[...]
    for n in range(w_in.shape[0] // SIDE):
        at = slice(n * SIDE, (n + 1) * SIDE)
        if n == columns // SIDE:
            for copy in copies:
                copy.wait()
        out[:length, at] = partial[:length, at] + times_transposed(rest[:, : 2 * depth], w_in[at, :])
    out[length:, :] = partial[length:, :]


def prepare_kernel(heads, *refs):
    marks_in, conv_w_in, conv_b_in, step_bias_in, decay_in, skip_in, gain_in = refs[:7]
    table, conv_w, conv_b, gains, per_head, marks, sems = refs[7:]
    seq = lax.axis_index("seq")
    columns = heads * HEAD_DIM
    own_lanes = pl.ds(pl.multiple_of(seq * columns, columns), columns)
    side_lanes = pl.ds(INNER, LANES)
    copies = [
        (conv_w_in.at[:, :, own_lanes], conv_w.at[:, :, pl.ds(0, columns)]),
        (conv_w_in.at[:, :, side_lanes], conv_w.at[:, :, pl.ds(columns, LANES)]),
        (conv_b_in.at[:, own_lanes], conv_b.at[:, pl.ds(0, columns)]),
        (conv_b_in.at[:, side_lanes], conv_b.at[:, pl.ds(columns, LANES)]),
        (step_bias_in, per_head.at[0]),
        (decay_in, per_head.at[1]),
        (skip_in, per_head.at[2]),
        (gain_in.at[:, own_lanes], gains),
        (marks_in, marks),
    ]
    copies = [pltpu.make_async_copy(a, b, sems.at[i]) for i, (a, b) in enumerate(copies)]
    for copy in copies:
        copy.start()
    for copy in copies:
        copy.wait()

    lane, row = lane_row()
    within = lane % GROUP
    head_lane = within < 2 * heads
    to_first = lax.rem(LANES - seq * heads, LANES)

    def own_heads(k):
        both = jnp.concatenate([per_head[k], jnp.zeros((2, LANES - HEADS), jnp.float32)], axis=1)
        both = pltpu.roll(both, to_first, 1)
        behind = pltpu.roll(both, heads, 1)
        value = jnp.where(lane[:1] < heads, both[0:1, :], behind[1:2, :])
        return jnp.where(lane[:1] < 2 * heads, value, 0.0)

    for d in range(2):
        table[d * KERNEL : (d + 1) * KERNEL, :] = conv_w[d]
    table[8:10, :] = conv_b[...]
    for k in range(2):
        value = jnp.broadcast_to(own_heads(k), (8, LANES))
        value = sum([pltpu.roll(value, g * GROUP, 1) for g in range(1, LANES // GROUP)], value)
        table[10 + k : 11 + k, :LANES] = value[:1]
    direct = packed(jnp.broadcast_to(own_heads(2), (16, LANES)), 3, heads)
    for d in range(2):
        wide = jnp.dot(direct, head_columns(heads, d), preferred_element_type=jnp.float32)
        table[12 + d : 13 + d, :columns] = wide[:1]
    table[14:16, :columns] = gains[...]

    position = row + lane // GROUP * BLOCK
    here = position == marks[:, 0:1]
    after = position + 1 == marks[:, 0:1]
    for m in range(1, marks.shape[1]):
        here = here | (position == marks[:, m : m + 1])
        after = after | (position + 1 == marks[:, m : m + 1])
    forward_start, backward_start = within == 2 * heads, within == 2 * heads + 1
    starts = jnp.where((here & forward_start) | (after & backward_start), 1.0, 0.0).astype(jnp.bfloat16)
    backward_lane = ((within >= heads) & head_lane) | backward_start
    lower = jnp.where(row >= lane, 1.0, 0.0).astype(jnp.bfloat16)
    upper = jnp.where(row <= lane, 1.0, 0.0).astype(jnp.bfloat16)
    ahead = jnp.dot(lower, starts, preferred_element_type=jnp.float32)
    behind = jnp.dot(upper, starts, preferred_element_type=jnp.float32)
    seen = jnp.where(backward_lane, behind, ahead)
    wanted = lane - within + 2 * heads + jnp.where(backward_lane, 1, 0)
    chosen = jnp.where(row == wanted, 1.0, 0.0).astype(jnp.bfloat16)
    seen = jnp.dot(seen.astype(jnp.bfloat16), chosen, preferred_element_type=jnp.float32)
    chosen = (row == lane // 2 * GROUP + lane % 2 * heads) & (lane < 2 * LANES // GROUP)
    chosen = jnp.where(chosen, 1.0, 0.0).astype(jnp.bfloat16)
    table[HEADER:, :LANES] = jnp.dot(seen.astype(jnp.bfloat16), chosen, preferred_element_type=jnp.float32)


def head_columns(heads, d):
    at_row = lax.broadcasted_iota(jnp.int32, (LANES, heads * HEAD_DIM), 0)
    head = lax.broadcasted_iota(jnp.int32, (LANES, heads * HEAD_DIM), 1) // HEAD_DIM + d * heads
    hit = (at_row == head) | (at_row == head + 2 * heads) | (at_row == head + 4 * heads)
    return jnp.where(hit, 1.0, 0.0).astype(jnp.bfloat16)


def packed(value, count, heads):
    parts = split_parts(value, count)
    joined = parts[0].astype(jnp.float32)
    for k in range(1, count):
        joined = joined + pltpu.roll(parts[k].astype(jnp.float32), 2 * heads * k, 1)
    return joined.astype(jnp.bfloat16)


def mixer_kernel(heads, partial, rest, up_end, down_end, far, *refs):
    outs, refs = refs[:4], refs[4:]
    w_end, padded, xs, cs, bs, widen_in, leads, tails, state, ys, mixed = refs
    seq = lax.axis_index("seq")
    columns = heads * HEAD_DIM
    depth = up_end.shape[1]
    cut, rows = up_end.shape[0], up_end.shape[0] + down_end.shape[0]
    chunks = columns // LANES
    length = rest.shape[0]
    blocks = length // BLOCK
    lane, row = lane_row()

    def table(first, last, lanes):
        return partial[length + first : length + last, lanes]

    half = far.shape[0]
    other = columns + LANES
    w_end[:cut, :] = up_end[...]
    w_end[cut:rows, :] = down_end[...]
    w_end[other : other + half, :] = far[...]
    w_end[rows:other, :] = jnp.zeros((other - rows, depth), jnp.bfloat16)
    w_end[other + half :, :] = jnp.zeros((w_end.shape[0] - other - half, depth), jnp.bfloat16)
    edge = jnp.zeros((EDGE, LANES), jnp.float32)
    for c in range(chunks + 1):
        padded[c, 0:EDGE, :] = edge
        padded[c, EDGE + length :, :] = edge
    state[...] = jnp.zeros_like(state)

    places = [pl.multiple_of((seq ^ mask) * BLOCK, BLOCK) for mask in range(4)]

    def project_in(n):
        at = slice(n * SIDE, (n + 1) * SIDE)
        return times_transposed(rest[:, 2 * depth :], w_end[at, :])

    def rounded(value):
        return value.astype(jnp.bfloat16).astype(jnp.float32)

    def keep(c, value):
        for mask in range(4):
            padded[c, pl.ds(EDGE + places[mask], BLOCK), :] = value[mask * BLOCK : (mask + 1) * BLOCK, :]

    side_out = project_in(columns // SIDE)
    mine = rounded(side_out[:, :LANES] + partial[:length, columns:other])
    others = rounded(side_out[:, LANES:] + partial[:length, other:])
    even = jnp.broadcast_to(seq, mine.shape) % 2 == 0
    low, high = jnp.where(even, mine, others), jnp.where(even, others, mine)
    left = lax.broadcasted_iota(jnp.int32, mine.shape, 1) < half
    keep(chunks, jnp.where(left, low, pltpu.roll(high, half, 1)))
    for n in range(columns // SIDE):
        part_out = rounded(project_in(n) + partial[:length, n * SIDE : (n + 1) * SIDE])
        for k in range(SIDE // LANES):
            keep(n * (SIDE // LANES) + k, part_out[:, k * LANES : (k + 1) * LANES])

    within = lane % GROUP
    head_lane = within < 2 * heads
    backward_lane = (within >= heads) & head_lane
    to_first = LANES - half - seq % 2 * heads
    raw = jnp.zeros((BLOCK, LANES), jnp.float32)
    for mask in range(4):
        own_steps = pltpu.roll(mine[mask * BLOCK : (mask + 1) * BLOCK, :], to_first, 1)
        own_steps = jnp.where(lane < heads, own_steps, 0.0)
        raw = raw + pltpu.roll(own_steps + pltpu.roll(own_steps, heads, 1), (seq ^ mask) * GROUP, 1)
    raw = raw + table(10, 11, slice(0, LANES))
    step = jnp.maximum(raw, 0.0) + jnp.log1p(jnp.exp(-jnp.abs(raw)))
    rate = -step * table(11, 12, slice(0, LANES))
    two = jnp.concatenate(split_parts(rate, 2), axis=1)
    lower = jnp.where(row >= lane, 1.0, 0.0).astype(jnp.bfloat16)
    upper = jnp.where(row <= lane, 1.0, 0.0).astype(jnp.bfloat16)
    sums = jnp.dot(jnp.concatenate([lower, upper], axis=0), two, preferred_element_type=jnp.float32)
    sums = sums[:, :LANES] + sums[:, LANES:]
    cum = jnp.where(backward_lane, sums[BLOCK:], sums[:BLOCK])
    last = jnp.where(backward_lane[:1], cum[:1], cum[BLOCK - 1 :])
    chosen = jnp.where(row == lane // GROUP * 2 + jnp.where(backward_lane, 1, 0), 1.0, 0.0).astype(jnp.bfloat16)
    seen = pltpu.roll(partial[:BLOCK, other:], half, 1).astype(jnp.bfloat16)
    seen = jnp.dot(seen, chosen, preferred_element_type=jnp.float32)
    seen_last = jnp.where(backward_lane[:1], seen[:1], seen[BLOCK - 1 :])
    tail = jnp.where(seen == seen_last, jnp.exp(last - cum) * step, 0.0)
    lead = jnp.where(seen == 0.0, jnp.exp(cum), 0.0)
    last, seen_last = jnp.broadcast_to(last, (8, LANES)), jnp.broadcast_to(seen_last, (8, LANES))
    fade = jnp.where(seen_last == 0.0, jnp.exp(last), 0.0)
    seen_turned = seen.T
    spread = [head_columns(heads, d) for d in range(2)]
    shown = (jnp.log(step) - cum).T
    fades = []
    for b in range(blocks):
        for k, value in enumerate((lead, tail)):
            if b:
                value = pltpu.roll(value, LANES - b * GROUP, 1)
            at = (k * blocks + b) * BLOCK
            widen_in[at : at + BLOCK, :] = jnp.where(lane < 2 * heads, value, 0.0).astype(jnp.bfloat16)
        value = pltpu.roll(fade, LANES - b * GROUP, 1) if b else fade
        fades.append(packed(jnp.where(lane[:8] < 2 * heads, value, 0.0), 2, heads)[:1])
    fades = jnp.concatenate(fades + [jnp.zeros((16 - blocks, LANES), jnp.bfloat16)], axis=0)
    fade_wide = []
    for d in range(2):
        wide = jnp.dot(widen_in[...], spread[d], preferred_element_type=jnp.float32).astype(jnp.bfloat16)
        leads[d] = wide[:length]
        tails[d] = wide[length:]
        fade_wide.append(jnp.dot(fades, spread[d], preferred_element_type=jnp.float32))

    short = 64

    def convolve(c, i):
        at = i * short
        taps = [padded[c, at + EDGE - 3 + k : at + EDGE - 3 + k + short, :] for k in range(7)]
        rows_at = slice(at, at + short)
        lanes = slice(c * LANES, (c + 1) * LANES)
        for d in range(2):
            acc = table(8 + d, 9 + d, lanes)
            for k in range(KERNEL):
                n = d * KERNEL + k
                acc = acc + table(n, n + 1, lanes) * taps[k if d == 0 else 6 - k]
            half = 0.5 * acc
            value = half + half * jnp.tanh(half)
            if c < chunks:
                xs[d, rows_at, lanes] = value.astype(jnp.bfloat16)
            else:
                high = lax.broadcasted_iota(jnp.int32, (short, LANES), 1) >= STATE
                cs[d, rows_at, :] = jnp.where(high, value, 0.0).astype(jnp.bfloat16)
                bs[d, rows_at, :] = jnp.where(high, pltpu.roll(value, STATE, 1), 0.0).astype(jnp.bfloat16)

    group = SIDE // HEAD_DIM
    lane_head = lax.broadcasted_iota(jnp.int32, (BLOCK, SIDE), 1) // HEAD_DIM
    known = {}

    def scan_block(q, d, b):
        at = slice(b * BLOCK, (b + 1) * BLOCK)
        lanes = slice(q * SIDE, (q + 1) * SIDE)
        c_part = cs[d, at, :]
        b_part = bs[d, at, :]
        if (d, b) not in known:
            ordered = (row >= lane) if d == 0 else (row <= lane)
            n = b * GROUP + d * heads
            bar = jnp.where(ordered & (seen[:, n : n + 1] == seen_turned[n : n + 1, :]), 0.0, -1e30)
            known[d, b] = times_transposed(c_part, b_part), bar
        scores, bar = known[d, b]
        before = state[d, :, lanes]
        carried = jnp.dot(c_part, before.astype(jnp.bfloat16), preferred_element_type=jnp.float32)
        x_part = xs[d, at, lanes]
        local_end = lax.dot_general(
            b_part, tails[d, at, lanes] * x_part, (((0,), (0,)), ((), ())), preferred_element_type=jnp.float32
        )
        state[d, :, lanes] = fade_wide[d][b : b + 1, lanes] * before + local_end
        some = []
        for h in range(q * group, (q + 1) * group):
            n = b * GROUP + d * heads + h
            gap = cum[:, n : n + 1] + (shown[n : n + 1, :] + bar)
            some.append((jnp.exp(gap) * scores).astype(jnp.bfloat16))
        none = jnp.zeros_like(x_part)
        spaced = jnp.concatenate([jnp.where(lane_head == h, x_part, none) for h in range(group)], axis=0)
        inner = jnp.dot(jnp.concatenate(some, axis=1), spaced, preferred_element_type=jnp.float32)
        ys[d, at, lanes] = (
            inner
            + leads[d, at, lanes].astype(jnp.float32) * carried
            + table(12 + d, 13 + d, lanes) * x_part.astype(jnp.float32)
        )

    in_group = SIDE // LANES
    for i in range(length // short):
        for c in (chunks, *range(in_group)):
            convolve(c, i)
    for q in range(columns // SIDE):
        for i in range(blocks):
            for d in range(2):
                scan_block(q, d, i if d == 0 else blocks - 1 - i)
            for c in range((q + 1) * in_group, min((q + 2) * in_group, chunks)):
                for part in range(BLOCK // short):
                    convolve(c, i * (BLOCK // short) + part)

    head_row = lax.broadcasted_iota(jnp.int32, (SIDE, SIDE), 0) // HEAD_DIM
    head_col = lax.broadcasted_iota(jnp.int32, (SIDE, SIDE), 1) // HEAD_DIM
    same = jnp.where(head_row == head_col, 1.0 / HEAD_DIM, 0.0).astype(jnp.bfloat16)
    for q in range(columns // SIDE):
        lanes = slice(q * SIDE, (q + 1) * SIDE)
        both = 0.0
        for d in range(2):
            y = ys[d, :, lanes]
            mean = jnp.dot((y * y).astype(jnp.bfloat16), same, preferred_element_type=jnp.float32)
            both = both + y * lax.rsqrt(mean + 1e-05) * table(14 + d, 15 + d, lanes)
        mixed[:, lanes] = both.astype(jnp.bfloat16)
    for mask in range(4):
        outs[mask][...] = mixed[pl.ds(places[mask], BLOCK), :]


IN_VMEM = pl.BlockSpec(memory_space=pltpu.VMEM)
IN_HBM = pl.BlockSpec(memory_space=pltpu.HBM)
ROOM = 24 * 1024 * 1024


def call(kernel, shapes, scratch, *operands, space=IN_VMEM, apart=0, aliases=None):
    shapes = [jax.ShapeDtypeStruct(*one) for one in shapes]
    return pl.pallas_call(
        kernel,
        out_shape=shapes,
        in_specs=[space] * (len(operands) - apart) + [pl.BlockSpec(memory_space=pl.ANY)] * apart,
        out_specs=[IN_VMEM] * len(shapes),
        scratch_shapes=scratch,
        input_output_aliases=aliases or {},
        compiler_params=pltpu.CompilerParams(vmem_limit_bytes=ROOM),
    )(*operands)


def pack(weight, columns):
    depth = weight.shape[1]
    few = 2 * columns // HEAD_DIM
    shapes = [((columns + STATE + few, depth), weight.dtype), ((STATE, depth), weight.dtype)]
    scratch = [pltpu.SemaphoreType.DMA((4,))]
    return call(functools.partial(pack_kernel, columns), shapes, scratch, weight, space=IN_HBM)


def first_gather(columns, shape, own, side, up, down):
    shapes = [(shape, own.dtype), ((2 * side.shape[0], side.shape[1]), own.dtype)]
    return call(functools.partial(first_gather_kernel, columns), shapes, [], own, side, up, down)


def next_gather(columns, at, held, swapped, up, down):
    shapes = [(held.shape, held.dtype), (swapped.shape, held.dtype)]
    kernel = functools.partial(next_gather_kernel, columns, at)
    return call(kernel, shapes, [], held, swapped, up, down, aliases={0: 0})


def split(columns, up, down):
    rows, depth = up.shape
    shapes = [(2 * STATE, depth), (STATE, depth)]
    shapes = [(one, up.dtype) for one in shapes]
    return call(functools.partial(split_kernel, columns), shapes, [], up, down)


def prepare(heads, params):
    columns = heads * HEAD_DIM
    scratch = [
        pltpu.VMEM((2, KERNEL, columns + LANES), jnp.float32),
        pltpu.VMEM((2, columns + LANES), jnp.float32),
        pltpu.VMEM((2, columns), jnp.float32),
        pltpu.VMEM((3, 2, HEADS), jnp.float32),
        pltpu.VMEM(params[0].shape, jnp.int32),
        pltpu.SemaphoreType.DMA((9,)),
    ]
    shape = ((HEADER + BLOCK, columns + LANES), jnp.float32)
    return call(functools.partial(prepare_kernel, heads), [shape], scratch, *params, space=IN_HBM)[0]


def early(columns, ring, ways, pieces, gathered, swapped, table):
    length = pieces[0].shape[0] * len(pieces)
    wide, known = gathered.shape
    first = 2 * ring - 3
    depth = known // first
    shapes = [
        ((length + HEADER, wide), jnp.float32),
        ((length, depth * len(ways) - known), jnp.bfloat16),
    ]
    scratch = [pltpu.VMEM((length, known), jnp.bfloat16), pltpu.VMEM((SIDE, known), jnp.bfloat16)]
    kernel = functools.partial(early_kernel, columns, ring, ways, first)
    return call(kernel, shapes, scratch, *pieces, gathered, swapped, table)


def second(columns, partial, rest, up, down, swapped):
    scratch = [pltpu.VMEM((partial.shape[1], 2 * up.shape[1]), jnp.bfloat16), pltpu.SemaphoreType.DMA((2,))]
    operands = (partial, rest, up, down, swapped)
    return call(functools.partial(second_kernel, columns), [(partial.shape, jnp.float32)], scratch, *operands, apart=1)[0]


def mix(heads, count, partial, rest, *others):
    columns = heads * HEAD_DIM
    length = rest.shape[0]
    scratch = [
        ((columns + SIDE, others[0].shape[1]), jnp.bfloat16),
        ((columns // LANES + 1, length + 2 * EDGE, LANES), jnp.float32),
        ((2, length, columns), jnp.bfloat16),
        ((2, length, LANES), jnp.bfloat16),
        ((2, length, LANES), jnp.bfloat16),
        ((2 * length, LANES), jnp.bfloat16),
        ((2, length, columns), jnp.bfloat16),
        ((2, length, columns), jnp.bfloat16),
        ((2, LANES, columns), jnp.float32),
        ((2, length, columns), jnp.float32),
        ((length, columns), jnp.bfloat16),
    ]
    shapes = [((length // count, columns), jnp.bfloat16)] * count
    scratch = [pltpu.VMEM(*one) for one in scratch]
    return call(functools.partial(mixer_kernel, heads), shapes, scratch, partial, rest, *others)


def turn(value, way):
    order = ring_order(lax.axis_size("batch"))
    count = len(order)
    return lax.ppermute(value, ("fsdp", "batch"), [(order[i], order[(i + way) % count]) for i in range(count)])


def turn_across(value, way):
    order = ring_order(lax.axis_size("batch"))
    count = len(order)
    pairs = []
    for s in range(lax.axis_size("seq")):
        pairs += [(s * count + order[i], (s ^ 1) * count + order[(i + way) % count]) for i in range(count)]
    return lax.ppermute(value, ("seq", "fsdp", "batch"), pairs)


def swap(value, axis, mask):
    return lax.ppermute(value, axis, [(i, i ^ mask) for i in range(lax.axis_size(axis))])


def on_heads(hidden, in_weight, read_starts, conv_weight, conv_bias, dt_bias, decay, skip, norm_gain):
    tokens = hidden[0]
    count = lax.axis_size("seq")
    seq = lax.axis_index("seq")
    heads = HEADS // count
    columns = heads * HEAD_DIM
    own, side = pack(in_weight.T, columns)

    ring = lax.axis_size("batch")
    late, _ = lax.optimization_barrier((tokens, own))
    across = swap(late, "seq", 2)
    pieces = [tokens, swap(tokens, "seq", 1), across, swap(across, "seq", 1)]
    table = prepare(heads, (read_starts, conv_weight, conv_bias, dt_bias, decay, skip, norm_gain))
    first = 2 * ring - 3
    ways = [0]
    up = down = own
    for away in range(1, ring):
        before = up, down
        up, down = turn(up, 1), turn(down, -1)
        ways += [-away, away]
        if away == 1:
            beside = table
        elif away == 2:
            gathered, sent = first_gather(columns, (columns + SIDE, first * own.shape[1]), own, side, *before)
            beside = swapped = swap(sent, "seq", 1)
        elif away < ring - 1:
            gathered, sent = next_gather(columns, 2 * away - 3, gathered, swapped, *before)
            beside = swapped = swap(sent, "seq", 1)
        else:
            gathered, sent = next_gather(columns, 2 * away - 3, gathered, swapped, *before)
            swapped = swap(sent, "seq", 1)
            partial, rest = early(columns, ring, tuple(ways) + (ring,), pieces, gathered, swapped, table)
            beside = partial
        up, _ = lax.optimization_barrier((up, beside))
        down, _ = lax.optimization_barrier((down, beside))
    cut = own.shape[0] * 2 // 5 // 16 * 16
    ends = [turn(up[:cut], 1), turn(down[cut:], -1)]
    sent, crossing = split(columns, up, down)
    far = turn_across(crossing, -1)
    partial = second(columns, partial, rest, up, down, swap(sent, "seq", 1))
    results = mix(heads, count, partial, rest, *ends, far)
    received = [results[0]] + [swap(results[mask], "seq", mask) for mask in range(1, count)]
    mixed = jnp.zeros((tokens.shape[0], INNER), jnp.bfloat16)
    for mask in range(count):
        mixed = lax.dynamic_update_slice(mixed, received[mask], (0, (seq ^ mask) * columns))
    return mixed[None]


def solution(mesh):
    in_specs = (
        P(("fsdp", "batch"), "seq", None),
        P(("fsdp", "batch"), None),
        P(("fsdp", "batch"), None),
        P(),
        P(),
        P(),
        P(),
        P(),
        P(),
    )
    out_specs = P(("fsdp", "batch"), "seq", None)
    by_heads = mesh.shape["seq"] == 4 and mesh.shape["fsdp"] == 2

    def mixer(hidden, *rest):
        whole = by_heads and hidden.shape[1] == mesh.shape["seq"] * BLOCK
        return jax.shard_map(
            on_heads if whole else on_sections,
            mesh=mesh,
            in_specs=in_specs,
            out_specs=out_specs,
            check_vma=False,
        )(hidden, *rest)

    return mixer
```

```python
import functools

import jax
import jax.numpy as jnp
from jax import lax
from jax.experimental import pallas as pl
from jax.experimental.pallas import tpu as pltpu
from jax.sharding import PartitionSpec as P

HEADS = 32
HEAD_DIM = 64
STATE = 64
KERNEL = 4
BLOCK = 128
INNER = 2048
CONV_CH = 2176


def prefix(value, axis, join, neutral, backward):
    count, mine = (lax.axis_size(axis), lax.axis_index(axis))
    pieces = jax.tree.map(lambda part: lax.all_gather(part, axis), value)
    if backward:
        pieces = jax.tree.map(lambda part: part[::-1], pieces)
        mine = count - 1 - mine
    running = jax.tree.map(
        lambda part, zero: jnp.full_like(part, 0) + jnp.asarray(zero, part.dtype), value, neutral
    )

    def turn(position, running):
        longer = join(running, jax.tree.map(lambda part: part[position], pieces))
        return jax.tree.map(lambda new, old: jnp.where(position < mine, new, old), longer, running)

    return lax.fori_loop(0, count - 1, turn, running)


def extended_2(value, sides, width):
    for axis, dim in sides:
        size, length = (lax.axis_size(axis), value.shape[dim])
        up = [(i, (i + 1) % size) for i in range(size - 1)]
        down = [(j, i) for i, j in up]
        last = lax.slice_in_dim(value, length - width, length, axis=dim)
        initial = lax.slice_in_dim(value, 0, width, axis=dim)
        before = lax.ppermute(last, axis, up)
        after = lax.ppermute(initial, axis, down)
        value = jnp.concatenate([before, value, after], axis=dim)
    return value


def conv_silu(padded, weight, bias):
    length = padded.shape[0] - weight.shape[0] + 1
    total = jnp.broadcast_to(bias[None, :], (length, bias.shape[0]))
    for tap in range(weight.shape[0]):
        total = total + weight[tap][None, :] * padded[tap : tap + length].astype(jnp.float32)
    return jax.nn.silu(total).astype(jnp.bfloat16)


def block_parts(x_part, b_part, c_part, step_size, log_rate, resets):
    length = x_part.shape[0]
    running = jnp.cumsum(log_rate, axis=0)
    running_heads = running.T
    step_heads = step_size.T
    resets_seen = jnp.cumsum(resets)
    scores = jnp.dot(c_part, b_part.T, preferred_element_type=jnp.float32)
    positions = jnp.arange(length)
    allowed = (positions[:, None] >= positions[None, :]) & (
        resets_seen[:, None] == resets_seen[None, :]
    )
    log_gaps = jnp.minimum(running_heads[:, :, None] - running_heads[:, None, :], 0.0)
    weights = (
        jnp.where(allowed[None, :, :], jnp.exp(log_gaps), 0.0)
        * scores[None, :, :]
        * step_heads[:, None, :]
    )
    weights = weights.astype(jnp.bfloat16)
    values = x_part.reshape(length, HEADS, HEAD_DIM)
    inner_part = jnp.einsum("hts,shp->thp", weights, values, preferred_element_type=jnp.float32)
    last_same = resets_seen == resets_seen[-1]
    tail_weight = (
        jnp.where(last_same[:, None], jnp.exp(running[-1][None, :] - running), 0.0) * step_size
    )
    inputs = (tail_weight[:, :, None] * values.astype(jnp.float32)).astype(jnp.bfloat16)
    local_end = jnp.einsum("shp,sn->hpn", inputs, b_part, preferred_element_type=jnp.float32)
    lead_fade = jnp.where((resets_seen == 0)[:, None], jnp.exp(running), 0.0)
    block_fade = jnp.where(resets_seen[-1] == 0, jnp.exp(running[-1]), 0.0)
    return (inner_part, local_end, lead_fade, block_fade)


def chain_combine(earlier, later):
    return (earlier[0] * later[0], later[0][:, None] * earlier[1] + later[1])


def direction(conv_out, step_cols, resets, bias_step, rates, direct, gains, backward):
    length = conv_out.shape[0]
    blocks = length // BLOCK
    x_part = conv_out[:, :INNER]
    b_part = conv_out[:, INNER : INNER + STATE]
    c_part = conv_out[:, INNER + STATE :]
    step_size = jax.nn.softplus(step_cols.astype(jnp.float32) + bias_step[None, :])
    log_rate = -step_size * rates[None, :]
    inner_part, local_end, lead_fade, block_fade = jax.vmap(block_parts)(
        x_part.reshape(blocks, BLOCK, INNER),
        b_part.reshape(blocks, BLOCK, STATE),
        c_part.reshape(blocks, BLOCK, STATE),
        step_size.reshape(blocks, BLOCK, HEADS),
        log_rate.reshape(blocks, BLOCK, HEADS),
        resets.reshape(blocks, BLOCK),
    )
    carried_state = jnp.zeros((HEADS, HEAD_DIM, STATE), jnp.float32)
    carried_fade = jnp.ones((HEADS,), jnp.float32)
    entering = carried_state
    fades_before = carried_fade
    carried_state = block_fade[0][:, None, None] * carried_state + local_end[0]
    carried_fade = block_fade[0] * carried_fade
    summary = (carried_fade, carried_state.reshape(HEADS, HEAD_DIM * STATE))
    identity = (jnp.ones((HEADS,), jnp.float32), jnp.zeros((HEADS, HEAD_DIM * STATE), jnp.float32))
    if backward:
        incoming = prefix(summary, "seq", chain_combine, identity, True)
    else:
        incoming = prefix(summary, "seq", chain_combine, identity, False)
    incoming_state = incoming[1].reshape(HEADS, HEAD_DIM, STATE)
    states = jnp.stack([fades_before[:, None, None] * incoming_state + entering])
    rounded = states.astype(jnp.bfloat16)
    carried = jnp.einsum(
        "btn,bhpn->bthp",
        c_part.reshape(blocks, BLOCK, STATE),
        rounded,
        preferred_element_type=jnp.float32,
    )
    direct_part = direct[None, None, :, None] * x_part.reshape(
        blocks, BLOCK, HEADS, HEAD_DIM
    ).astype(jnp.float32)
    result = (inner_part + lead_fade[..., None] * carried + direct_part).reshape(
        length, HEADS, HEAD_DIM
    )
    scale = lax.rsqrt(jnp.mean(result * result, axis=-1, keepdims=True) + 1e-05)
    return (result * scale * gains.reshape(HEADS, HEAD_DIM)).reshape(length, INNER)


def project(rows_in, in_weight):
    total = jnp.dot(
        rows_in,
        lax.all_gather(in_weight, ("fsdp", "batch"), axis=0, tiled=True),
        preferred_element_type=jnp.float32,
    )
    return total.astype(jnp.bfloat16)


def on_sections(
    hidden, in_weight, read_starts, conv_weight, conv_bias, dt_bias, decay, skip, norm_gain
):
    tokens = hidden[0]
    length = tokens.shape[0]
    margin = KERNEL - 1
    projected = project(tokens, in_weight)
    extended = extended_2(projected[:, :CONV_CH], (("seq", 0),), margin)
    forward_in = conv_silu(extended[: length + margin], conv_weight[0], conv_bias[0])
    backward_in = conv_silu(jnp.flip(extended[margin:], 0), conv_weight[1], conv_bias[1])
    step_cols = projected[:, CONV_CH:]
    positions = lax.axis_index("seq") * length + jnp.arange(length, dtype=jnp.int32)
    marks = read_starts[0]
    starts_here = jnp.any(positions[:, None] == marks[None, :], axis=1).astype(jnp.float32)
    starts_next = jnp.any((positions + 1)[:, None] == marks[None, :], axis=1).astype(jnp.float32)
    forward_out = direction(
        forward_in, step_cols, starts_here, dt_bias[0], decay[0], skip[0], norm_gain[0], False
    )
    backward_out = direction(
        backward_in,
        jnp.flip(step_cols, 0),
        jnp.flip(starts_next, 0),
        dt_bias[1],
        decay[1],
        skip[1],
        norm_gain[1],
        True,
    )
    mixed = forward_out + jnp.flip(backward_out, 0)
    return mixed.astype(jnp.bfloat16)[None]


LANES = 128
SIDE = 256
EDGE = 8
GROUP = 32
HEADER = 16


def ring_order(count):
    return [i if i < count else 3 * count - 1 - i for i in range(2 * count)]


def split_parts(value, count):
    parts = []
    for _ in range(count):
        parts.append(value.astype(jnp.bfloat16))
        value = value - parts[-1].astype(jnp.float32)
    return parts


def lane_row():
    lane = lax.broadcasted_iota(jnp.int32, (BLOCK, LANES), 1)
    row = lax.broadcasted_iota(jnp.int32, (BLOCK, LANES), 0)
    return lane, row


def shard_at(away, ring):
    fsdp, batch = lax.axis_index("fsdp"), lax.axis_index("batch")
    position = jnp.where(fsdp == 0, batch, 2 * ring - 1 - batch)
    there = lax.rem(position + 2 * ring + away, 2 * ring)
    return jnp.where(there < ring, there, 3 * ring - 1 - there)


def take_rows(pieces, ring, ways, rows_in):
    depth = rows_in.shape[1] // len(ways)
    for n, away in enumerate(ways):
        at = pl.ds(pl.multiple_of(shard_at(away, ring) * depth, depth), depth)
        for mask in range(4):
            rows_in[mask * BLOCK : (mask + 1) * BLOCK, n * depth : (n + 1) * depth] = pieces[mask][:, at]


def times_transposed(a, b):
    return lax.dot_general(a, b, (((1,), (1,)), ((), ())), preferred_element_type=jnp.float32)


def pack_kernel(columns, weight_in, own, side, sems):
    seq = lax.axis_index("seq")
    half = side.shape[0]
    few = own.shape[0] - columns - half
    mine = pl.multiple_of(INNER + seq % 2 * half, half)
    other = pl.multiple_of(INNER + (1 - seq % 2) * half, half)
    steps_at = pl.multiple_of(INNER + 2 * half + seq // 2 * few, few)
    copies = [
        (weight_in.at[pl.ds(pl.multiple_of(seq * columns, columns), columns)], own.at[pl.ds(0, columns)]),
        (weight_in.at[pl.ds(mine, half)], own.at[pl.ds(columns, half)]),
        (weight_in.at[pl.ds(steps_at, few)], own.at[pl.ds(columns + half, few)]),
        (weight_in.at[pl.ds(other, half)], side),
    ]
    copies = [pltpu.make_async_copy(a, b, sems.at[i]) for i, (a, b) in enumerate(copies)]
    for copy in copies:
        copy.start()
    for copy in copies:
        copy.wait()


def first_gather_kernel(columns, own, side, up, down, out, sent):
    rows, depth = own.shape
    half = side.shape[0]
    other = columns + LANES
    out[rows:, :] = jnp.zeros((out.shape[0] - rows, out.shape[1]), out.dtype)
    for n, weight in enumerate((own, up, down)):
        out[:rows, n * depth : (n + 1) * depth] = weight[...]
    out[other : other + half, :depth] = side[...]
    sent[:half, :] = up[columns : columns + half, :]
    sent[half:, :] = down[columns : columns + half, :]


def next_gather_kernel(columns, at, held, swapped, up, down, out, sent):
    del held
    rows, depth = up.shape
    half = swapped.shape[0] // 2
    other = columns + LANES
    for n, weight in enumerate((up, down)):
        out[:rows, (at + n) * depth : (at + n + 1) * depth] = weight[...]
        out[other : other + half, (at + n - 2) * depth : (at + n - 1) * depth] = swapped[n * half : (n + 1) * half, :]
    sent[:half, :] = up[columns : columns + half, :]
    sent[half:, :] = down[columns : columns + half, :]


def split_kernel(columns, up, down, sent, crossing):
    half = crossing.shape[0]
    sent[:half, :] = up[columns : columns + half, :]
    sent[half:, :] = down[columns : columns + half, :]
    crossing[...] = down[columns : columns + half, :]


def early_kernel(columns, ring, ways, first, *refs):
    pieces = refs[:4]
    gathered, swapped, table, partial, rest, rows_in, side = refs[4:]
    length = rows_in.shape[0]
    half, depth = swapped.shape[0] // 2, swapped.shape[1]
    take_rows(pieces, ring, ways[:first], rows_in)
    take_rows(pieces, ring, ways[first:], rest)
    for n in range(columns // SIDE):
        at = slice(n * SIDE, (n + 1) * SIDE)
        partial[:length, at] = times_transposed(rows_in[...], gathered[at, :])
    side[...] = gathered[columns:, :]
    for n in range(2):
        side[LANES : LANES + half, (first - 2 + n) * depth : (first - 1 + n) * depth] = swapped[n * half : (n + 1) * half, :]
    partial[:length, columns:] = times_transposed(rows_in[...], side[...])
    other = columns + LANES
    partial[:BLOCK, other:] = partial[:BLOCK, other:] + pltpu.roll(table[HEADER:, :LANES], half, 1)
    partial[length:, : table.shape[1]] = table[:HEADER, :]


def second_kernel(columns, partial, rest, up, down, swapped, out, w_in, sems):
    rows, depth = up.shape
    length = rest.shape[0]
    half = swapped.shape[0] // 2
    other = columns + LANES
    copies = []
    for n in range(2):
        place = w_in.at[pl.ds(other, half), pl.ds(n * depth, depth)]
        copies.append(pltpu.make_async_copy(swapped.at[pl.ds(n * half, half)], place, sems.at[n]))
        copies[-1].start()
    w_in[rows:other, :] = jnp.zeros((other - rows, w_in.shape[1]), jnp.bfloat16)
    w_in[other + half :, :] = jnp.zeros((w_in.shape[0] - other - half, w_in.shape[1]), jnp.bfloat16)
    for n, weight in enumerate((up, down)):
        w_in[:rows, n * depth : (n + 1) * depth] = weight[...]
    for n in range(w_in.shape[0] // SIDE):
        at = slice(n * SIDE, (n + 1) * SIDE)
        if n == columns // SIDE:
            for copy in copies:
                copy.wait()
        out[:length, at] = partial[:length, at] + times_transposed(rest[:, : 2 * depth], w_in[at, :])
    out[length:, :] = partial[length:, :]


def prepare_kernel(heads, *refs):
    marks_in, conv_w_in, conv_b_in, step_bias_in, decay_in, skip_in, gain_in = refs[:7]
    table, conv_w, conv_b, gains, per_head, marks, sems = refs[7:]
    seq = lax.axis_index("seq")
    columns = heads * HEAD_DIM
    own_lanes = pl.ds(pl.multiple_of(seq * columns, columns), columns)
    side_lanes = pl.ds(INNER, LANES)
    copies = [
        (conv_w_in.at[:, :, own_lanes], conv_w.at[:, :, pl.ds(0, columns)]),
        (conv_w_in.at[:, :, side_lanes], conv_w.at[:, :, pl.ds(columns, LANES)]),
        (conv_b_in.at[:, own_lanes], conv_b.at[:, pl.ds(0, columns)]),
        (conv_b_in.at[:, side_lanes], conv_b.at[:, pl.ds(columns, LANES)]),
        (step_bias_in, per_head.at[0]),
        (decay_in, per_head.at[1]),
        (skip_in, per_head.at[2]),
        (gain_in.at[:, own_lanes], gains),
        (marks_in, marks),
    ]
    copies = [pltpu.make_async_copy(a, b, sems.at[i]) for i, (a, b) in enumerate(copies)]
    for copy in copies:
        copy.start()
    for copy in copies:
        copy.wait()

    lane, row = lane_row()
    within = lane % GROUP
    head_lane = within < 2 * heads
    to_first = lax.rem(LANES - seq * heads, LANES)

    def own_heads(k):
        both = jnp.concatenate([per_head[k], jnp.zeros((2, LANES - HEADS), jnp.float32)], axis=1)
        both = pltpu.roll(both, to_first, 1)
        behind = pltpu.roll(both, heads, 1)
        value = jnp.where(lane[:1] < heads, both[0:1, :], behind[1:2, :])
        return jnp.where(lane[:1] < 2 * heads, value, 0.0)

    for d in range(2):
        table[d * KERNEL : (d + 1) * KERNEL, :] = conv_w[d]
    table[8:10, :] = conv_b[...]
    for k in range(2):
        value = jnp.broadcast_to(own_heads(k), (8, LANES))
        value = sum([pltpu.roll(value, g * GROUP, 1) for g in range(1, LANES // GROUP)], value)
        table[10 + k : 11 + k, :LANES] = value[:1]
    direct = packed(jnp.broadcast_to(own_heads(2), (16, LANES)), 3, heads)
    for d in range(2):
        wide = jnp.dot(direct, head_columns(heads, d), preferred_element_type=jnp.float32)
        table[12 + d : 13 + d, :columns] = wide[:1]
    table[14:16, :columns] = gains[...]

    position = row + lane // GROUP * BLOCK
    here = position == marks[:, 0:1]
    after = position + 1 == marks[:, 0:1]
    for m in range(1, marks.shape[1]):
        here = here | (position == marks[:, m : m + 1])
        after = after | (position + 1 == marks[:, m : m + 1])
    forward_start, backward_start = within == 2 * heads, within == 2 * heads + 1
    starts = jnp.where((here & forward_start) | (after & backward_start), 1.0, 0.0).astype(jnp.bfloat16)
    backward_lane = ((within >= heads) & head_lane) | backward_start
    lower = jnp.where(row >= lane, 1.0, 0.0).astype(jnp.bfloat16)
    upper = jnp.where(row <= lane, 1.0, 0.0).astype(jnp.bfloat16)
    ahead = jnp.dot(lower, starts, preferred_element_type=jnp.float32)
    behind = jnp.dot(upper, starts, preferred_element_type=jnp.float32)
    seen = jnp.where(backward_lane, behind, ahead)
    wanted = lane - within + 2 * heads + jnp.where(backward_lane, 1, 0)
    chosen = jnp.where(row == wanted, 1.0, 0.0).astype(jnp.bfloat16)
    seen = jnp.dot(seen.astype(jnp.bfloat16), chosen, preferred_element_type=jnp.float32)
    chosen = (row == lane // 2 * GROUP + lane % 2 * heads) & (lane < 2 * LANES // GROUP)
    chosen = jnp.where(chosen, 1.0, 0.0).astype(jnp.bfloat16)
    table[HEADER:, :LANES] = jnp.dot(seen.astype(jnp.bfloat16), chosen, preferred_element_type=jnp.float32)


def head_columns(heads, d):
    at_row = lax.broadcasted_iota(jnp.int32, (LANES, heads * HEAD_DIM), 0)
    head = lax.broadcasted_iota(jnp.int32, (LANES, heads * HEAD_DIM), 1) // HEAD_DIM + d * heads
    hit = (at_row == head) | (at_row == head + 2 * heads) | (at_row == head + 4 * heads)
    return jnp.where(hit, 1.0, 0.0).astype(jnp.bfloat16)


def packed(value, count, heads):
    parts = split_parts(value, count)
    joined = parts[0].astype(jnp.float32)
    for k in range(1, count):
        joined = joined + pltpu.roll(parts[k].astype(jnp.float32), 2 * heads * k, 1)
    return joined.astype(jnp.bfloat16)


def mixer_kernel(heads, partial, rest, up_end, down_end, far, *refs):
    outs, refs = refs[:4], refs[4:]
    w_end, padded, xs, cs, bs, widen_in, leads, tails, state, ys, mixed = refs
    seq = lax.axis_index("seq")
    columns = heads * HEAD_DIM
    depth = up_end.shape[1]
    cut, rows = up_end.shape[0], up_end.shape[0] + down_end.shape[0]
    chunks = columns // LANES
    length = rest.shape[0]
    blocks = length // BLOCK
    lane, row = lane_row()

    def table(first, last, lanes):
        return partial[length + first : length + last, lanes]

    half = far.shape[0]
    other = columns + LANES
    w_end[:cut, :] = up_end[...]
    w_end[cut:rows, :] = down_end[...]
    w_end[other : other + half, :] = far[...]
    w_end[rows:other, :] = jnp.zeros((other - rows, depth), jnp.bfloat16)
    w_end[other + half :, :] = jnp.zeros((w_end.shape[0] - other - half, depth), jnp.bfloat16)
    edge = jnp.zeros((EDGE, LANES), jnp.float32)
    for c in range(chunks + 1):
        padded[c, 0:EDGE, :] = edge
        padded[c, EDGE + length :, :] = edge
    state[...] = jnp.zeros_like(state)

    places = [pl.multiple_of((seq ^ mask) * BLOCK, BLOCK) for mask in range(4)]

    def project_in(n):
        at = slice(n * SIDE, (n + 1) * SIDE)
        return times_transposed(rest[:, 2 * depth :], w_end[at, :])

    def rounded(value):
        return value.astype(jnp.bfloat16).astype(jnp.float32)

    def keep(c, value):
        for mask in range(4):
            padded[c, pl.ds(EDGE + places[mask], BLOCK), :] = value[mask * BLOCK : (mask + 1) * BLOCK, :]

    side_out = project_in(columns // SIDE)
    mine = rounded(side_out[:, :LANES] + partial[:length, columns:other])
    others = rounded(side_out[:, LANES:] + partial[:length, other:])
    even = jnp.broadcast_to(seq, mine.shape) % 2 == 0
    low, high = jnp.where(even, mine, others), jnp.where(even, others, mine)
    left = lax.broadcasted_iota(jnp.int32, mine.shape, 1) < half
    keep(chunks, jnp.where(left, low, pltpu.roll(high, half, 1)))
    for n in range(columns // SIDE):
        part_out = rounded(project_in(n) + partial[:length, n * SIDE : (n + 1) * SIDE])
        for k in range(SIDE // LANES):
            keep(n * (SIDE // LANES) + k, part_out[:, k * LANES : (k + 1) * LANES])

    within = lane % GROUP
    head_lane = within < 2 * heads
    backward_lane = (within >= heads) & head_lane
    to_first = LANES - half - seq % 2 * heads
    raw = jnp.zeros((BLOCK, LANES), jnp.float32)
    for mask in range(4):
        own_steps = pltpu.roll(mine[mask * BLOCK : (mask + 1) * BLOCK, :], to_first, 1)
        own_steps = jnp.where(lane < heads, own_steps, 0.0)
        raw = raw + pltpu.roll(own_steps + pltpu.roll(own_steps, heads, 1), (seq ^ mask) * GROUP, 1)
    raw = raw + table(10, 11, slice(0, LANES))
    step = jnp.maximum(raw, 0.0) + jnp.log1p(jnp.exp(-jnp.abs(raw)))
    rate = -step * table(11, 12, slice(0, LANES))
    two = jnp.concatenate(split_parts(rate, 2), axis=1)
    lower = jnp.where(row >= lane, 1.0, 0.0).astype(jnp.bfloat16)
    upper = jnp.where(row <= lane, 1.0, 0.0).astype(jnp.bfloat16)
    sums = jnp.dot(jnp.concatenate([lower, upper], axis=0), two, preferred_element_type=jnp.float32)
    sums = sums[:, :LANES] + sums[:, LANES:]
    cum = jnp.where(backward_lane, sums[BLOCK:], sums[:BLOCK])
    last = jnp.where(backward_lane[:1], cum[:1], cum[BLOCK - 1 :])
    chosen = jnp.where(row == lane // GROUP * 2 + jnp.where(backward_lane, 1, 0), 1.0, 0.0).astype(jnp.bfloat16)
    seen = pltpu.roll(partial[:BLOCK, other:], half, 1).astype(jnp.bfloat16)
    seen = jnp.dot(seen, chosen, preferred_element_type=jnp.float32)
    seen_last = jnp.where(backward_lane[:1], seen[:1], seen[BLOCK - 1 :])
    tail = jnp.where(seen == seen_last, jnp.exp(last - cum) * step, 0.0)
    lead = jnp.where(seen == 0.0, jnp.exp(cum), 0.0)
    last, seen_last = jnp.broadcast_to(last, (8, LANES)), jnp.broadcast_to(seen_last, (8, LANES))
    fade = jnp.where(seen_last == 0.0, jnp.exp(last), 0.0)
    seen_turned = seen.T
    spread = [head_columns(heads, d) for d in range(2)]
    shown, step_turned = (-cum).T, step.T
    fades = []
    for b in range(blocks):
        for k, value in enumerate((lead, tail)):
            if b:
                value = pltpu.roll(value, LANES - b * GROUP, 1)
            at = (k * blocks + b) * BLOCK
            widen_in[at : at + BLOCK, :] = jnp.where(lane < 2 * heads, value, 0.0).astype(jnp.bfloat16)
        value = pltpu.roll(fade, LANES - b * GROUP, 1) if b else fade
        fades.append(packed(jnp.where(lane[:8] < 2 * heads, value, 0.0), 2, heads)[:1])
    fades = jnp.concatenate(fades + [jnp.zeros((16 - blocks, LANES), jnp.bfloat16)], axis=0)
    fade_wide = []
    for d in range(2):
        wide = jnp.dot(widen_in[...], spread[d], preferred_element_type=jnp.float32).astype(jnp.bfloat16)
        leads[d] = wide[:length]
        tails[d] = wide[length:]
        fade_wide.append(jnp.dot(fades, spread[d], preferred_element_type=jnp.float32))

    short = 64

    def convolve(c, i):
        at = i * short
        taps = [padded[c, at + EDGE - 3 + k : at + EDGE - 3 + k + short, :] for k in range(7)]
        rows_at = slice(at, at + short)
        lanes = slice(c * LANES, (c + 1) * LANES)
        for d in range(2):
            acc = table(8 + d, 9 + d, lanes)
            for k in range(KERNEL):
                n = d * KERNEL + k
                acc = acc + table(n, n + 1, lanes) * taps[k if d == 0 else 6 - k]
            half = 0.5 * acc
            value = half + half * jnp.tanh(half)
            if c < chunks:
                xs[d, rows_at, lanes] = value.astype(jnp.bfloat16)
            else:
                high = lax.broadcasted_iota(jnp.int32, (short, LANES), 1) >= STATE
                cs[d, rows_at, :] = jnp.where(high, value, 0.0).astype(jnp.bfloat16)
                bs[d, rows_at, :] = jnp.where(high, pltpu.roll(value, STATE, 1), 0.0).astype(jnp.bfloat16)

    group = SIDE // HEAD_DIM
    lane_head = lax.broadcasted_iota(jnp.int32, (BLOCK, SIDE), 1) // HEAD_DIM
    known = {}

    def scan_block(q, d, b):
        at = slice(b * BLOCK, (b + 1) * BLOCK)
        lanes = slice(q * SIDE, (q + 1) * SIDE)
        c_part = cs[d, at, :]
        b_part = bs[d, at, :]
        if (d, b) not in known:
            ordered = (row >= lane) if d == 0 else (row <= lane)
            n = b * GROUP + d * heads
            bar = jnp.where(ordered & (seen[:, n : n + 1] == seen_turned[n : n + 1, :]), 0.0, -1e30)
            known[d, b] = times_transposed(c_part, b_part), bar
        scores, bar = known[d, b]
        before = state[d, :, lanes]
        carried = jnp.dot(c_part, before.astype(jnp.bfloat16), preferred_element_type=jnp.float32)
        x_part = xs[d, at, lanes]
        local_end = lax.dot_general(
            b_part, tails[d, at, lanes] * x_part, (((0,), (0,)), ((), ())), preferred_element_type=jnp.float32
        )
        state[d, :, lanes] = fade_wide[d][b : b + 1, lanes] * before + local_end
        some = []
        for h in range(q * group, (q + 1) * group):
            n = b * GROUP + d * heads + h
            gap = cum[:, n : n + 1] + (shown[n : n + 1, :] + bar)
            some.append((jnp.exp(gap) * scores * step_turned[n : n + 1, :]).astype(jnp.bfloat16))
        none = jnp.zeros_like(x_part)
        spaced = jnp.concatenate([jnp.where(lane_head == h, x_part, none) for h in range(group)], axis=0)
        inner = jnp.dot(jnp.concatenate(some, axis=1), spaced, preferred_element_type=jnp.float32)
        ys[d, at, lanes] = (
            inner
            + leads[d, at, lanes].astype(jnp.float32) * carried
            + table(12 + d, 13 + d, lanes) * x_part.astype(jnp.float32)
        )

    in_group = SIDE // LANES
    for i in range(length // short):
        for c in (chunks, *range(in_group)):
            convolve(c, i)
    for q in range(columns // SIDE):
        for i in range(blocks):
            for d in range(2):
                scan_block(q, d, i if d == 0 else blocks - 1 - i)
            for c in range((q + 1) * in_group, min((q + 2) * in_group, chunks)):
                for part in range(BLOCK // short):
                    convolve(c, i * (BLOCK // short) + part)

    head_row = lax.broadcasted_iota(jnp.int32, (SIDE, SIDE), 0) // HEAD_DIM
    head_col = lax.broadcasted_iota(jnp.int32, (SIDE, SIDE), 1) // HEAD_DIM
    same = jnp.where(head_row == head_col, 1.0 / HEAD_DIM, 0.0).astype(jnp.bfloat16)
    for q in range(columns // SIDE):
        lanes = slice(q * SIDE, (q + 1) * SIDE)
        both = 0.0
        for d in range(2):
            y = ys[d, :, lanes]
            mean = jnp.dot((y * y).astype(jnp.bfloat16), same, preferred_element_type=jnp.float32)
            both = both + y * lax.rsqrt(mean + 1e-05) * table(14 + d, 15 + d, lanes)
        mixed[:, lanes] = both.astype(jnp.bfloat16)
    for mask in range(4):
        outs[mask][...] = mixed[pl.ds(places[mask], BLOCK), :]


IN_VMEM = pl.BlockSpec(memory_space=pltpu.VMEM)
IN_HBM = pl.BlockSpec(memory_space=pltpu.HBM)
ROOM = 24 * 1024 * 1024


def call(kernel, shapes, scratch, *operands, space=IN_VMEM, apart=0, aliases=None):
    shapes = [jax.ShapeDtypeStruct(*one) for one in shapes]
    return pl.pallas_call(
        kernel,
        out_shape=shapes,
        in_specs=[space] * (len(operands) - apart) + [pl.BlockSpec(memory_space=pl.ANY)] * apart,
        out_specs=[IN_VMEM] * len(shapes),
        scratch_shapes=scratch,
        input_output_aliases=aliases or {},
        compiler_params=pltpu.CompilerParams(vmem_limit_bytes=ROOM),
    )(*operands)


def pack(weight, columns):
    depth = weight.shape[1]
    few = 2 * columns // HEAD_DIM
    shapes = [((columns + STATE + few, depth), weight.dtype), ((STATE, depth), weight.dtype)]
    scratch = [pltpu.SemaphoreType.DMA((4,))]
    return call(functools.partial(pack_kernel, columns), shapes, scratch, weight, space=IN_HBM)


def first_gather(columns, shape, own, side, up, down):
    shapes = [(shape, own.dtype), ((2 * side.shape[0], side.shape[1]), own.dtype)]
    return call(functools.partial(first_gather_kernel, columns), shapes, [], own, side, up, down)


def next_gather(columns, at, held, swapped, up, down):
    shapes = [(held.shape, held.dtype), (swapped.shape, held.dtype)]
    kernel = functools.partial(next_gather_kernel, columns, at)
    return call(kernel, shapes, [], held, swapped, up, down, aliases={0: 0})


def split(columns, up, down):
    rows, depth = up.shape
    shapes = [(2 * STATE, depth), (STATE, depth)]
    shapes = [(one, up.dtype) for one in shapes]
    return call(functools.partial(split_kernel, columns), shapes, [], up, down)


def prepare(heads, params):
    columns = heads * HEAD_DIM
    scratch = [
        pltpu.VMEM((2, KERNEL, columns + LANES), jnp.float32),
        pltpu.VMEM((2, columns + LANES), jnp.float32),
        pltpu.VMEM((2, columns), jnp.float32),
        pltpu.VMEM((3, 2, HEADS), jnp.float32),
        pltpu.VMEM(params[0].shape, jnp.int32),
        pltpu.SemaphoreType.DMA((9,)),
    ]
    shape = ((HEADER + BLOCK, columns + LANES), jnp.float32)
    return call(functools.partial(prepare_kernel, heads), [shape], scratch, *params, space=IN_HBM)[0]


def early(columns, ring, ways, pieces, gathered, swapped, table):
    length = pieces[0].shape[0] * len(pieces)
    wide, known = gathered.shape
    first = 2 * ring - 3
    depth = known // first
    shapes = [
        ((length + HEADER, wide), jnp.float32),
        ((length, depth * len(ways) - known), jnp.bfloat16),
    ]
    scratch = [pltpu.VMEM((length, known), jnp.bfloat16), pltpu.VMEM((SIDE, known), jnp.bfloat16)]
    kernel = functools.partial(early_kernel, columns, ring, ways, first)
    return call(kernel, shapes, scratch, *pieces, gathered, swapped, table)


def second(columns, partial, rest, up, down, swapped):
    scratch = [pltpu.VMEM((partial.shape[1], 2 * up.shape[1]), jnp.bfloat16), pltpu.SemaphoreType.DMA((2,))]
    operands = (partial, rest, up, down, swapped)
    return call(functools.partial(second_kernel, columns), [(partial.shape, jnp.float32)], scratch, *operands, apart=1)[0]


def mix(heads, count, partial, rest, *others):
    columns = heads * HEAD_DIM
    length = rest.shape[0]
    scratch = [
        ((columns + SIDE, others[0].shape[1]), jnp.bfloat16),
        ((columns // LANES + 1, length + 2 * EDGE, LANES), jnp.float32),
        ((2, length, columns), jnp.bfloat16),
        ((2, length, LANES), jnp.bfloat16),
        ((2, length, LANES), jnp.bfloat16),
        ((2 * length, LANES), jnp.bfloat16),
        ((2, length, columns), jnp.bfloat16),
        ((2, length, columns), jnp.bfloat16),
        ((2, LANES, columns), jnp.float32),
        ((2, length, columns), jnp.float32),
        ((length, columns), jnp.bfloat16),
    ]
    shapes = [((length // count, columns), jnp.bfloat16)] * count
    scratch = [pltpu.VMEM(*one) for one in scratch]
    return call(functools.partial(mixer_kernel, heads), shapes, scratch, partial, rest, *others)


def turn(value, way):
    order = ring_order(lax.axis_size("batch"))
    count = len(order)
    return lax.ppermute(value, ("fsdp", "batch"), [(order[i], order[(i + way) % count]) for i in range(count)])


def turn_across(value, way):
    order = ring_order(lax.axis_size("batch"))
    count = len(order)
    pairs = []
    for s in range(lax.axis_size("seq")):
        pairs += [(s * count + order[i], (s ^ 1) * count + order[(i + way) % count]) for i in range(count)]
    return lax.ppermute(value, ("seq", "fsdp", "batch"), pairs)


def swap(value, axis, mask):
    return lax.ppermute(value, axis, [(i, i ^ mask) for i in range(lax.axis_size(axis))])


def on_heads(hidden, in_weight, read_starts, conv_weight, conv_bias, dt_bias, decay, skip, norm_gain):
    tokens = hidden[0]
    count = lax.axis_size("seq")
    seq = lax.axis_index("seq")
    heads = HEADS // count
    columns = heads * HEAD_DIM
    own, side = pack(in_weight.T, columns)

    ring = lax.axis_size("batch")
    late, _ = lax.optimization_barrier((tokens, own))
    across = swap(late, "seq", 2)
    pieces = [tokens, swap(tokens, "seq", 1), across, swap(across, "seq", 1)]
    table = prepare(heads, (read_starts, conv_weight, conv_bias, dt_bias, decay, skip, norm_gain))
    first = 2 * ring - 3
    ways = [0]
    up = down = own
    for away in range(1, ring):
        before = up, down
        up, down = turn(up, 1), turn(down, -1)
        ways += [-away, away]
        if away == 1:
            beside = table
        elif away == 2:
            gathered, sent = first_gather(columns, (columns + SIDE, first * own.shape[1]), own, side, *before)
            beside = swapped = swap(sent, "seq", 1)
        elif away < ring - 1:
            gathered, sent = next_gather(columns, 2 * away - 3, gathered, swapped, *before)
            beside = swapped = swap(sent, "seq", 1)
        else:
            gathered, sent = next_gather(columns, 2 * away - 3, gathered, swapped, *before)
            swapped = swap(sent, "seq", 1)
            partial, rest = early(columns, ring, tuple(ways) + (ring,), pieces, gathered, swapped, table)
            beside = partial
        up, _ = lax.optimization_barrier((up, beside))
        down, _ = lax.optimization_barrier((down, beside))
    cut = own.shape[0] * 2 // 5 // 16 * 16
    ends = [turn(up[:cut], 1), turn(down[cut:], -1)]
    sent, crossing = split(columns, up, down)
    far = turn_across(crossing, -1)
    partial = second(columns, partial, rest, up, down, swap(sent, "seq", 1))
    results = mix(heads, count, partial, rest, *ends, far)
    received = [results[0]] + [swap(results[mask], "seq", mask) for mask in range(1, count)]
    mixed = jnp.zeros((tokens.shape[0], INNER), jnp.bfloat16)
    for mask in range(count):
        mixed = lax.dynamic_update_slice(mixed, received[mask], (0, (seq ^ mask) * columns))
    return mixed[None]


def solution(mesh):
    in_specs = (
        P(("fsdp", "batch"), "seq", None),
        P(("fsdp", "batch"), None),
        P(("fsdp", "batch"), None),
        P(),
        P(),
        P(),
        P(),
        P(),
        P(),
    )
    out_specs = P(("fsdp", "batch"), "seq", None)
    by_heads = mesh.shape["seq"] == 4 and mesh.shape["fsdp"] == 2 and mesh.shape["batch"] > 3

    def mixer(hidden, *rest):
        whole = by_heads and hidden.shape[1] == mesh.shape["seq"] * BLOCK
        return jax.shard_map(
            on_heads if whole else on_sections,
            mesh=mesh,
            in_specs=in_specs,
            out_specs=out_specs,
            check_vma=False,
        )(hidden, *rest)

    return mixer
```

```python
import functools

import jax
import jax.numpy as jnp
from jax import lax
from jax.experimental import pallas as pl
from jax.experimental.pallas import tpu as pltpu
from jax.sharding import PartitionSpec as P

HEADS = 32
HEAD_DIM = 64
STATE = 64
KERNEL = 4
BLOCK = 128
INNER = 2048
CONV_CH = 2176


def prefix(value, axis, join, neutral, backward):
    count, mine = (lax.axis_size(axis), lax.axis_index(axis))
    pieces = jax.tree.map(lambda part: lax.all_gather(part, axis), value)
    if backward:
        pieces = jax.tree.map(lambda part: part[::-1], pieces)
        mine = count - 1 - mine
    running = jax.tree.map(
        lambda part, zero: jnp.full_like(part, 0) + jnp.asarray(zero, part.dtype), value, neutral
    )

    def turn(position, running):
        longer = join(running, jax.tree.map(lambda part: part[position], pieces))
        return jax.tree.map(lambda new, old: jnp.where(position < mine, new, old), longer, running)

    return lax.fori_loop(0, count - 1, turn, running)


def extended_2(value, sides, width):
    for axis, dim in sides:
        size, length = (lax.axis_size(axis), value.shape[dim])
        up = [(i, (i + 1) % size) for i in range(size - 1)]
        down = [(j, i) for i, j in up]
        last = lax.slice_in_dim(value, length - width, length, axis=dim)
        initial = lax.slice_in_dim(value, 0, width, axis=dim)
        before = lax.ppermute(last, axis, up)
        after = lax.ppermute(initial, axis, down)
        value = jnp.concatenate([before, value, after], axis=dim)
    return value


def conv_silu(padded, weight, bias):
    length = padded.shape[0] - weight.shape[0] + 1
    total = jnp.broadcast_to(bias[None, :], (length, bias.shape[0]))
    for tap in range(weight.shape[0]):
        total = total + weight[tap][None, :] * padded[tap : tap + length].astype(jnp.float32)
    return jax.nn.silu(total).astype(jnp.bfloat16)


def block_parts(x_part, b_part, c_part, step_size, log_rate, resets):
    length = x_part.shape[0]
    running = jnp.cumsum(log_rate, axis=0)
    running_heads = running.T
    step_heads = step_size.T
    resets_seen = jnp.cumsum(resets)
    scores = jnp.dot(c_part, b_part.T, preferred_element_type=jnp.float32)
    positions = jnp.arange(length)
    allowed = (positions[:, None] >= positions[None, :]) & (
        resets_seen[:, None] == resets_seen[None, :]
    )
    log_gaps = jnp.minimum(running_heads[:, :, None] - running_heads[:, None, :], 0.0)
    weights = (
        jnp.where(allowed[None, :, :], jnp.exp(log_gaps), 0.0)
        * scores[None, :, :]
        * step_heads[:, None, :]
    )
    weights = weights.astype(jnp.bfloat16)
    values = x_part.reshape(length, HEADS, HEAD_DIM)
    inner_part = jnp.einsum("hts,shp->thp", weights, values, preferred_element_type=jnp.float32)
    last_same = resets_seen == resets_seen[-1]
    tail_weight = (
        jnp.where(last_same[:, None], jnp.exp(running[-1][None, :] - running), 0.0) * step_size
    )
    inputs = (tail_weight[:, :, None] * values.astype(jnp.float32)).astype(jnp.bfloat16)
    local_end = jnp.einsum("shp,sn->hpn", inputs, b_part, preferred_element_type=jnp.float32)
    lead_fade = jnp.where((resets_seen == 0)[:, None], jnp.exp(running), 0.0)
    block_fade = jnp.where(resets_seen[-1] == 0, jnp.exp(running[-1]), 0.0)
    return (inner_part, local_end, lead_fade, block_fade)


def chain_combine(earlier, later):
    return (earlier[0] * later[0], later[0][:, None] * earlier[1] + later[1])


def direction(conv_out, step_cols, resets, bias_step, rates, direct, gains, backward):
    length = conv_out.shape[0]
    blocks = length // BLOCK
    x_part = conv_out[:, :INNER]
    b_part = conv_out[:, INNER : INNER + STATE]
    c_part = conv_out[:, INNER + STATE :]
    step_size = jax.nn.softplus(step_cols.astype(jnp.float32) + bias_step[None, :])
    log_rate = -step_size * rates[None, :]
    inner_part, local_end, lead_fade, block_fade = jax.vmap(block_parts)(
        x_part.reshape(blocks, BLOCK, INNER),
        b_part.reshape(blocks, BLOCK, STATE),
        c_part.reshape(blocks, BLOCK, STATE),
        step_size.reshape(blocks, BLOCK, HEADS),
        log_rate.reshape(blocks, BLOCK, HEADS),
        resets.reshape(blocks, BLOCK),
    )
    carried_state = jnp.zeros((HEADS, HEAD_DIM, STATE), jnp.float32)
    carried_fade = jnp.ones((HEADS,), jnp.float32)
    entering = carried_state
    fades_before = carried_fade
    carried_state = block_fade[0][:, None, None] * carried_state + local_end[0]
    carried_fade = block_fade[0] * carried_fade
    summary = (carried_fade, carried_state.reshape(HEADS, HEAD_DIM * STATE))
    identity = (jnp.ones((HEADS,), jnp.float32), jnp.zeros((HEADS, HEAD_DIM * STATE), jnp.float32))
    if backward:
        incoming = prefix(summary, "seq", chain_combine, identity, True)
    else:
        incoming = prefix(summary, "seq", chain_combine, identity, False)
    incoming_state = incoming[1].reshape(HEADS, HEAD_DIM, STATE)
    states = jnp.stack([fades_before[:, None, None] * incoming_state + entering])
    rounded = states.astype(jnp.bfloat16)
    carried = jnp.einsum(
        "btn,bhpn->bthp",
        c_part.reshape(blocks, BLOCK, STATE),
        rounded,
        preferred_element_type=jnp.float32,
    )
    direct_part = direct[None, None, :, None] * x_part.reshape(
        blocks, BLOCK, HEADS, HEAD_DIM
    ).astype(jnp.float32)
    result = (inner_part + lead_fade[..., None] * carried + direct_part).reshape(
        length, HEADS, HEAD_DIM
    )
    scale = lax.rsqrt(jnp.mean(result * result, axis=-1, keepdims=True) + 1e-05)
    return (result * scale * gains.reshape(HEADS, HEAD_DIM)).reshape(length, INNER)


def project(rows_in, in_weight):
    total = jnp.dot(
        rows_in,
        lax.all_gather(in_weight, ("fsdp", "batch"), axis=0, tiled=True),
        preferred_element_type=jnp.float32,
    )
    return total.astype(jnp.bfloat16)


def on_sections(
    hidden, in_weight, read_starts, conv_weight, conv_bias, dt_bias, decay, skip, norm_gain
):
    tokens = hidden[0]
    length = tokens.shape[0]
    margin = KERNEL - 1
    projected = project(tokens, in_weight)
    extended = extended_2(projected[:, :CONV_CH], (("seq", 0),), margin)
    forward_in = conv_silu(extended[: length + margin], conv_weight[0], conv_bias[0])
    backward_in = conv_silu(jnp.flip(extended[margin:], 0), conv_weight[1], conv_bias[1])
    step_cols = projected[:, CONV_CH:]
    positions = lax.axis_index("seq") * length + jnp.arange(length, dtype=jnp.int32)
    marks = read_starts[0]
    starts_here = jnp.any(positions[:, None] == marks[None, :], axis=1).astype(jnp.float32)
    starts_next = jnp.any((positions + 1)[:, None] == marks[None, :], axis=1).astype(jnp.float32)
    forward_out = direction(
        forward_in, step_cols, starts_here, dt_bias[0], decay[0], skip[0], norm_gain[0], False
    )
    backward_out = direction(
        backward_in,
        jnp.flip(step_cols, 0),
        jnp.flip(starts_next, 0),
        dt_bias[1],
        decay[1],
        skip[1],
        norm_gain[1],
        True,
    )
    mixed = forward_out + jnp.flip(backward_out, 0)
    return mixed.astype(jnp.bfloat16)[None]


LANES = 128
SIDE = 256
EDGE = 8
GROUP = 32
HEADER = 16


def ring_order(count):
    return [i if i < count else 3 * count - 1 - i for i in range(2 * count)]


def split_parts(value, count):
    parts = []
    for _ in range(count):
        parts.append(value.astype(jnp.bfloat16))
        value = value - parts[-1].astype(jnp.float32)
    return parts


def lane_row():
    lane = lax.broadcasted_iota(jnp.int32, (BLOCK, LANES), 1)
    row = lax.broadcasted_iota(jnp.int32, (BLOCK, LANES), 0)
    return lane, row


def shard_at(away, ring):
    fsdp, batch = lax.axis_index("fsdp"), lax.axis_index("batch")
    position = jnp.where(fsdp == 0, batch, 2 * ring - 1 - batch)
    there = lax.rem(position + 2 * ring + away, 2 * ring)
    return jnp.where(there < ring, there, 3 * ring - 1 - there)


def take_rows(pieces, ring, ways, rows_in):
    depth = rows_in.shape[1] // len(ways)
    for n, away in enumerate(ways):
        at = pl.ds(pl.multiple_of(shard_at(away, ring) * depth, depth), depth)
        for mask in range(4):
            rows_in[mask * BLOCK : (mask + 1) * BLOCK, n * depth : (n + 1) * depth] = pieces[mask][:, at]


def times_transposed(a, b):
    return lax.dot_general(a, b, (((1,), (1,)), ((), ())), preferred_element_type=jnp.float32)


def pack_kernel(columns, weight_in, own, side, sems):
    seq = lax.axis_index("seq")
    half = side.shape[0]
    few = own.shape[0] - columns - half
    mine = pl.multiple_of(INNER + seq % 2 * half, half)
    other = pl.multiple_of(INNER + (1 - seq % 2) * half, half)
    steps_at = pl.multiple_of(INNER + 2 * half + seq // 2 * few, few)
    copies = [
        (weight_in.at[pl.ds(pl.multiple_of(seq * columns, columns), columns)], own.at[pl.ds(0, columns)]),
        (weight_in.at[pl.ds(mine, half)], own.at[pl.ds(columns, half)]),
        (weight_in.at[pl.ds(steps_at, few)], own.at[pl.ds(columns + half, few)]),
        (weight_in.at[pl.ds(other, half)], side),
    ]
    copies = [pltpu.make_async_copy(a, b, sems.at[i]) for i, (a, b) in enumerate(copies)]
    for copy in copies:
        copy.start()
    for copy in copies:
        copy.wait()


def first_gather_kernel(columns, own, side, up, down, out, sent):
    rows, depth = own.shape
    half = side.shape[0]
    other = columns + LANES
    out[rows:, :] = jnp.zeros((out.shape[0] - rows, out.shape[1]), out.dtype)
    for n, weight in enumerate((own, up, down)):
        out[:rows, n * depth : (n + 1) * depth] = weight[...]
    out[other : other + half, :depth] = side[...]
    sent[:half, :] = up[columns : columns + half, :]
    sent[half:, :] = down[columns : columns + half, :]


def next_gather_kernel(columns, at, held, swapped, up, down, out, sent):
    del held
    rows, depth = up.shape
    half = swapped.shape[0] // 2
    other = columns + LANES
    for n, weight in enumerate((up, down)):
        out[:rows, (at + n) * depth : (at + n + 1) * depth] = weight[...]
        out[other : other + half, (at + n - 2) * depth : (at + n - 1) * depth] = swapped[n * half : (n + 1) * half, :]
    sent[:half, :] = up[columns : columns + half, :]
    sent[half:, :] = down[columns : columns + half, :]


def split_kernel(columns, up, down, sent, crossing):
    half = crossing.shape[0]
    sent[:half, :] = up[columns : columns + half, :]
    sent[half:, :] = down[columns : columns + half, :]
    crossing[...] = down[columns : columns + half, :]


def early_kernel(columns, ring, ways, first, *refs):
    pieces = refs[:4]
    gathered, swapped, table, partial, rest, rows_in, side = refs[4:]
    length = rows_in.shape[0]
    half, depth = swapped.shape[0] // 2, swapped.shape[1]
    take_rows(pieces, ring, ways[:first], rows_in)
    take_rows(pieces, ring, ways[first:], rest)
    for n in range(columns // SIDE):
        at = slice(n * SIDE, (n + 1) * SIDE)
        partial[:length, at] = times_transposed(rows_in[...], gathered[at, :])
    side[...] = gathered[columns:, :]
    for n in range(2):
        side[LANES : LANES + half, (first - 2 + n) * depth : (first - 1 + n) * depth] = swapped[n * half : (n + 1) * half, :]
    partial[:length, columns:] = times_transposed(rows_in[...], side[...])
    other = columns + LANES
    partial[:BLOCK, other:] = partial[:BLOCK, other:] + pltpu.roll(table[HEADER:, :LANES], half, 1)
    partial[length:, : table.shape[1]] = table[:HEADER, :]


def second_kernel(columns, partial, rest, up, down, swapped, out, w_in, sems):
    rows, depth = up.shape
    length = rest.shape[0]
    half = swapped.shape[0] // 2
    other = columns + LANES
    copies = []
    for n in range(2):
        place = w_in.at[pl.ds(other, half), pl.ds(n * depth, depth)]
        copies.append(pltpu.make_async_copy(swapped.at[pl.ds(n * half, half)], place, sems.at[n]))
        copies[-1].start()
    w_in[rows:other, :] = jnp.zeros((other - rows, w_in.shape[1]), jnp.bfloat16)
    w_in[other + half :, :] = jnp.zeros((w_in.shape[0] - other - half, w_in.shape[1]), jnp.bfloat16)
    for n, weight in enumerate((up, down)):
        w_in[:rows, n * depth : (n + 1) * depth] = weight[...]
    for n in range(w_in.shape[0] // SIDE):
        at = slice(n * SIDE, (n + 1) * SIDE)
        if n == columns // SIDE:
            for copy in copies:
                copy.wait()
        out[:length, at] = partial[:length, at] + times_transposed(rest[:, : 2 * depth], w_in[at, :])
    out[length:, :] = partial[length:, :]


def prepare_kernel(heads, *refs):
    marks_in, conv_w_in, conv_b_in, step_bias_in, decay_in, skip_in, gain_in = refs[:7]
    table, conv_w, conv_b, gains, per_head, marks, sems = refs[7:]
    seq = lax.axis_index("seq")
    columns = heads * HEAD_DIM
    own_lanes = pl.ds(pl.multiple_of(seq * columns, columns), columns)
    side_lanes = pl.ds(INNER, LANES)
    copies = [
        (conv_w_in.at[:, :, own_lanes], conv_w.at[:, :, pl.ds(0, columns)]),
        (conv_w_in.at[:, :, side_lanes], conv_w.at[:, :, pl.ds(columns, LANES)]),
        (conv_b_in.at[:, own_lanes], conv_b.at[:, pl.ds(0, columns)]),
        (conv_b_in.at[:, side_lanes], conv_b.at[:, pl.ds(columns, LANES)]),
        (step_bias_in, per_head.at[0]),
        (decay_in, per_head.at[1]),
        (skip_in, per_head.at[2]),
        (gain_in.at[:, own_lanes], gains),
        (marks_in, marks),
    ]
    copies = [pltpu.make_async_copy(a, b, sems.at[i]) for i, (a, b) in enumerate(copies)]
    for copy in copies:
        copy.start()
    for copy in copies:
        copy.wait()

    lane, row = lane_row()
    within = lane % GROUP
    head_lane = within < 2 * heads
    to_first = lax.rem(LANES - seq * heads, LANES)

    def own_heads(k):
        both = jnp.concatenate([per_head[k], jnp.zeros((2, LANES - HEADS), jnp.float32)], axis=1)
        both = pltpu.roll(both, to_first, 1)
        behind = pltpu.roll(both, heads, 1)
        value = jnp.where(lane[:1] < heads, both[0:1, :], behind[1:2, :])
        return jnp.where(lane[:1] < 2 * heads, value, 0.0)

    for d in range(2):
        table[d * KERNEL : (d + 1) * KERNEL, :] = conv_w[d]
    table[8:10, :] = conv_b[...]
    for k in range(2):
        value = jnp.broadcast_to(own_heads(k), (8, LANES))
        value = sum([pltpu.roll(value, g * GROUP, 1) for g in range(1, LANES // GROUP)], value)
        table[10 + k : 11 + k, :LANES] = value[:1]
    direct = packed(jnp.broadcast_to(own_heads(2), (16, LANES)), 3, heads)
    for d in range(2):
        wide = jnp.dot(direct, head_columns(heads, d), preferred_element_type=jnp.float32)
        table[12 + d : 13 + d, :columns] = wide[:1]
    table[14:16, :columns] = gains[...]

    position = row + lane // GROUP * BLOCK
    here = position == marks[:, 0:1]
    after = position + 1 == marks[:, 0:1]
    for m in range(1, marks.shape[1]):
        here = here | (position == marks[:, m : m + 1])
        after = after | (position + 1 == marks[:, m : m + 1])
    forward_start, backward_start = within == 2 * heads, within == 2 * heads + 1
    starts = jnp.where((here & forward_start) | (after & backward_start), 1.0, 0.0).astype(jnp.bfloat16)
    backward_lane = ((within >= heads) & head_lane) | backward_start
    lower = jnp.where(row >= lane, 1.0, 0.0).astype(jnp.bfloat16)
    upper = jnp.where(row <= lane, 1.0, 0.0).astype(jnp.bfloat16)
    ahead = jnp.dot(lower, starts, preferred_element_type=jnp.float32)
    behind = jnp.dot(upper, starts, preferred_element_type=jnp.float32)
    seen = jnp.where(backward_lane, behind, ahead)
    wanted = lane - within + 2 * heads + jnp.where(backward_lane, 1, 0)
    chosen = jnp.where(row == wanted, 1.0, 0.0).astype(jnp.bfloat16)
    seen = jnp.dot(seen.astype(jnp.bfloat16), chosen, preferred_element_type=jnp.float32)
    chosen = (row == lane // 2 * GROUP + lane % 2 * heads) & (lane < 2 * LANES // GROUP)
    chosen = jnp.where(chosen, 1.0, 0.0).astype(jnp.bfloat16)
    table[HEADER:, :LANES] = jnp.dot(seen.astype(jnp.bfloat16), chosen, preferred_element_type=jnp.float32)


def head_columns(heads, d):
    at_row = lax.broadcasted_iota(jnp.int32, (LANES, heads * HEAD_DIM), 0)
    head = lax.broadcasted_iota(jnp.int32, (LANES, heads * HEAD_DIM), 1) // HEAD_DIM + d * heads
    hit = (at_row == head) | (at_row == head + 2 * heads) | (at_row == head + 4 * heads)
    return jnp.where(hit, 1.0, 0.0).astype(jnp.bfloat16)


def packed(value, count, heads):
    parts = split_parts(value, count)
    joined = parts[0].astype(jnp.float32)
    for k in range(1, count):
        joined = joined + pltpu.roll(parts[k].astype(jnp.float32), 2 * heads * k, 1)
    return joined.astype(jnp.bfloat16)


def mixer_kernel(heads, partial, rest, up_end, down_end, far, *refs):
    outs, refs = refs[:4], refs[4:]
    w_end, padded, xs, cs, bs, widen_in, leads, tails, state, ys, mixed = refs
    seq = lax.axis_index("seq")
    columns = heads * HEAD_DIM
    depth = up_end.shape[1]
    cut, rows = up_end.shape[0], up_end.shape[0] + down_end.shape[0]
    chunks = columns // LANES
    length = rest.shape[0]
    blocks = length // BLOCK
    lane, row = lane_row()

    def table(first, last, lanes):
        return partial[length + first : length + last, lanes]

    half = far.shape[0]
    other = columns + LANES
    w_end[:cut, :] = up_end[...]
    w_end[cut:rows, :] = down_end[...]
    w_end[other : other + half, :] = far[...]
    w_end[rows:other, :] = jnp.zeros((other - rows, depth), jnp.bfloat16)
    w_end[other + half :, :] = jnp.zeros((w_end.shape[0] - other - half, depth), jnp.bfloat16)
    edge = jnp.zeros((EDGE, LANES), jnp.float32)
    for c in range(chunks + 1):
        padded[c, 0:EDGE, :] = edge
        padded[c, EDGE + length :, :] = edge
    state[...] = jnp.zeros_like(state)

    places = [pl.multiple_of((seq ^ mask) * BLOCK, BLOCK) for mask in range(4)]

    def project_in(n):
        at = slice(n * SIDE, (n + 1) * SIDE)
        return times_transposed(rest[:, 2 * depth :], w_end[at, :])

    def rounded(value):
        return value.astype(jnp.bfloat16).astype(jnp.float32)

    def keep(c, value):
        for mask in range(4):
            padded[c, pl.ds(EDGE + places[mask], BLOCK), :] = value[mask * BLOCK : (mask + 1) * BLOCK, :]

    side_out = project_in(columns // SIDE)
    mine = rounded(side_out[:, :LANES] + partial[:length, columns:other])
    others = rounded(side_out[:, LANES:] + partial[:length, other:])
    even = jnp.broadcast_to(seq, mine.shape) % 2 == 0
    low, high = jnp.where(even, mine, others), jnp.where(even, others, mine)
    left = lax.broadcasted_iota(jnp.int32, mine.shape, 1) < half
    keep(chunks, jnp.where(left, low, pltpu.roll(high, half, 1)))
    for n in range(columns // SIDE):
        part_out = rounded(project_in(n) + partial[:length, n * SIDE : (n + 1) * SIDE])
        for k in range(SIDE // LANES):
            keep(n * (SIDE // LANES) + k, part_out[:, k * LANES : (k + 1) * LANES])

    within = lane % GROUP
    head_lane = within < 2 * heads
    backward_lane = (within >= heads) & head_lane
    to_first = LANES - half - seq % 2 * heads
    raw = jnp.zeros((BLOCK, LANES), jnp.float32)
    for mask in range(4):
        own_steps = pltpu.roll(mine[mask * BLOCK : (mask + 1) * BLOCK, :], to_first, 1)
        own_steps = jnp.where(lane < heads, own_steps, 0.0)
        raw = raw + pltpu.roll(own_steps + pltpu.roll(own_steps, heads, 1), (seq ^ mask) * GROUP, 1)
    raw = raw + table(10, 11, slice(0, LANES))
    step = jnp.maximum(raw, 0.0) + jnp.log1p(jnp.exp(-jnp.abs(raw)))
    rate = -step * table(11, 12, slice(0, LANES))
    two = jnp.concatenate(split_parts(rate, 2), axis=1)
    lower = jnp.where(row >= lane, 1.0, 0.0).astype(jnp.bfloat16)
    upper = jnp.where(row <= lane, 1.0, 0.0).astype(jnp.bfloat16)
    sums = jnp.dot(jnp.concatenate([lower, upper], axis=0), two, preferred_element_type=jnp.float32)
    sums = sums[:, :LANES] + sums[:, LANES:]
    cum = jnp.where(backward_lane, sums[BLOCK:], sums[:BLOCK])
    last = jnp.where(backward_lane[:1], cum[:1], cum[BLOCK - 1 :])
    chosen = jnp.where(row == lane // GROUP * 2 + jnp.where(backward_lane, 1, 0), 1.0, 0.0).astype(jnp.bfloat16)
    seen = pltpu.roll(partial[:BLOCK, other:], half, 1).astype(jnp.bfloat16)
    seen = jnp.dot(seen, chosen, preferred_element_type=jnp.float32)
    seen_last = jnp.where(backward_lane[:1], seen[:1], seen[BLOCK - 1 :])
    tail = jnp.where(seen == seen_last, jnp.exp(last - cum) * step, 0.0)
    lead = jnp.where(seen == 0.0, jnp.exp(cum), 0.0)
    last, seen_last = jnp.broadcast_to(last, (8, LANES)), jnp.broadcast_to(seen_last, (8, LANES))
    fade = jnp.where(seen_last == 0.0, jnp.exp(last), 0.0)
    seen_turned = seen.T
    spread = [head_columns(heads, d) for d in range(2)]
    shown, step_turned = (-cum).T, step.T
    fades = []
    for b in range(blocks):
        for k, value in enumerate((lead, tail)):
            if b:
                value = pltpu.roll(value, LANES - b * GROUP, 1)
            at = (k * blocks + b) * BLOCK
            widen_in[at : at + BLOCK, :] = jnp.where(lane < 2 * heads, value, 0.0).astype(jnp.bfloat16)
        value = pltpu.roll(fade, LANES - b * GROUP, 1) if b else fade
        fades.append(packed(jnp.where(lane[:8] < 2 * heads, value, 0.0), 2, heads)[:1])
    fades = jnp.concatenate(fades + [jnp.zeros((16 - blocks, LANES), jnp.bfloat16)], axis=0)
    fade_wide = []
    for d in range(2):
        wide = jnp.dot(widen_in[...], spread[d], preferred_element_type=jnp.float32).astype(jnp.bfloat16)
        leads[d] = wide[:length]
        tails[d] = wide[length:]
        fade_wide.append(jnp.dot(fades, spread[d], preferred_element_type=jnp.float32))

    short = 64

    def convolve(c, i):
        at = i * short
        taps = [padded[c, at + EDGE - 3 + k : at + EDGE - 3 + k + short, :] for k in range(7)]
        rows_at = slice(at, at + short)
        lanes = slice(c * LANES, (c + 1) * LANES)
        for d in range(2):
            acc = table(8 + d, 9 + d, lanes)
            for k in range(KERNEL):
                n = d * KERNEL + k
                acc = acc + table(n, n + 1, lanes) * taps[k if d == 0 else 6 - k]
            half = 0.5 * acc
            value = half + half * jnp.tanh(half)
            if c < chunks:
                xs[d, rows_at, lanes] = value.astype(jnp.bfloat16)
            else:
                high = lax.broadcasted_iota(jnp.int32, (short, LANES), 1) >= STATE
                cs[d, rows_at, :] = jnp.where(high, value, 0.0).astype(jnp.bfloat16)
                bs[d, rows_at, :] = jnp.where(high, pltpu.roll(value, STATE, 1), 0.0).astype(jnp.bfloat16)

    group = SIDE // HEAD_DIM
    lane_head = lax.broadcasted_iota(jnp.int32, (BLOCK, SIDE), 1) // HEAD_DIM
    known = {}

    def scan_block(q, d, b):
        at = slice(b * BLOCK, (b + 1) * BLOCK)
        lanes = slice(q * SIDE, (q + 1) * SIDE)
        c_part = cs[d, at, :]
        b_part = bs[d, at, :]
        if (d, b) not in known:
            ordered = (row >= lane) if d == 0 else (row <= lane)
            n = b * GROUP + d * heads
            bar = jnp.where(ordered & (seen[:, n : n + 1] == seen_turned[n : n + 1, :]), 0.0, -1e30)
            known[d, b] = times_transposed(c_part, b_part), bar
        scores, bar = known[d, b]
        before = state[d, :, lanes]
        carried = jnp.dot(c_part, before.astype(jnp.bfloat16), preferred_element_type=jnp.float32)
        x_part = xs[d, at, lanes]
        local_end = lax.dot_general(
            b_part, tails[d, at, lanes] * x_part, (((0,), (0,)), ((), ())), preferred_element_type=jnp.float32
        )
        state[d, :, lanes] = fade_wide[d][b : b + 1, lanes] * before + local_end
        some = []
        for h in range(q * group, (q + 1) * group):
            n = b * GROUP + d * heads + h
            gap = cum[:, n : n + 1] + (shown[n : n + 1, :] + bar)
            some.append((jnp.exp(gap) * scores * step_turned[n : n + 1, :]).astype(jnp.bfloat16))
        none = jnp.zeros_like(x_part)
        spaced = jnp.concatenate([jnp.where(lane_head == h, x_part, none) for h in range(group)], axis=0)
        inner = jnp.dot(jnp.concatenate(some, axis=1), spaced, preferred_element_type=jnp.float32)
        ys[d, at, lanes] = (
            inner
            + leads[d, at, lanes].astype(jnp.float32) * carried
            + table(12 + d, 13 + d, lanes) * x_part.astype(jnp.float32)
        )

    in_group = SIDE // LANES
    for i in range(length // short):
        for c in (chunks, *range(in_group)):
            convolve(c, i)
    for q in range(columns // SIDE):
        for i in range(blocks):
            for d in range(2):
                scan_block(q, d, i if d == 0 else blocks - 1 - i)
            for c in range((q + 1) * in_group, min((q + 2) * in_group, chunks)):
                for part in range(BLOCK // short):
                    convolve(c, i * (BLOCK // short) + part)

    head_row = lax.broadcasted_iota(jnp.int32, (SIDE, SIDE), 0) // HEAD_DIM
    head_col = lax.broadcasted_iota(jnp.int32, (SIDE, SIDE), 1) // HEAD_DIM
    same = jnp.where(head_row == head_col, 1.0 / HEAD_DIM, 0.0).astype(jnp.bfloat16)
    for q in range(columns // SIDE):
        lanes = slice(q * SIDE, (q + 1) * SIDE)
        both = 0.0
        for d in range(2):
            y = ys[d, :, lanes]
            mean = jnp.dot((y * y).astype(jnp.bfloat16), same, preferred_element_type=jnp.float32)
            both = both + y * lax.rsqrt(mean + 1e-05) * table(14 + d, 15 + d, lanes)
        mixed[:, lanes] = both.astype(jnp.bfloat16)
    for mask in range(4):
        outs[mask][...] = mixed[pl.ds(places[mask], BLOCK), :]


IN_VMEM = pl.BlockSpec(memory_space=pltpu.VMEM)
IN_HBM = pl.BlockSpec(memory_space=pltpu.HBM)
ROOM = 24 * 1024 * 1024


def call(kernel, shapes, scratch, *operands, space=IN_VMEM, apart=0, aliases=None):
    shapes = [jax.ShapeDtypeStruct(*one) for one in shapes]
    return pl.pallas_call(
        kernel,
        out_shape=shapes,
        in_specs=[space] * (len(operands) - apart) + [pl.BlockSpec(memory_space=pl.ANY)] * apart,
        out_specs=[IN_VMEM] * len(shapes),
        scratch_shapes=scratch,
        input_output_aliases=aliases or {},
        compiler_params=pltpu.CompilerParams(vmem_limit_bytes=ROOM),
    )(*operands)


def pack(weight, columns):
    depth = weight.shape[1]
    few = 2 * columns // HEAD_DIM
    shapes = [((columns + STATE + few, depth), weight.dtype), ((STATE, depth), weight.dtype)]
    scratch = [pltpu.SemaphoreType.DMA((4,))]
    return call(functools.partial(pack_kernel, columns), shapes, scratch, weight, space=IN_HBM)


def first_gather(columns, shape, own, side, up, down):
    shapes = [(shape, own.dtype), ((2 * side.shape[0], side.shape[1]), own.dtype)]
    return call(functools.partial(first_gather_kernel, columns), shapes, [], own, side, up, down)


def next_gather(columns, at, held, swapped, up, down):
    shapes = [(held.shape, held.dtype), (swapped.shape, held.dtype)]
    kernel = functools.partial(next_gather_kernel, columns, at)
    return call(kernel, shapes, [], held, swapped, up, down, aliases={0: 0})


def take_kernel(value, out):
    out[...] = value[: out.shape[0], :]


def take(value, rows):
    return call(take_kernel, [((rows, value.shape[1]), value.dtype)], [], value)[0]


def split(columns, up, down):
    rows, depth = up.shape
    shapes = [(2 * STATE, depth), (STATE, depth)]
    shapes = [(one, up.dtype) for one in shapes]
    return call(functools.partial(split_kernel, columns), shapes, [], up, down)


def prepare(heads, params):
    columns = heads * HEAD_DIM
    scratch = [
        pltpu.VMEM((2, KERNEL, columns + LANES), jnp.float32),
        pltpu.VMEM((2, columns + LANES), jnp.float32),
        pltpu.VMEM((2, columns), jnp.float32),
        pltpu.VMEM((3, 2, HEADS), jnp.float32),
        pltpu.VMEM(params[0].shape, jnp.int32),
        pltpu.SemaphoreType.DMA((9,)),
    ]
    shape = ((HEADER + BLOCK, columns + LANES), jnp.float32)
    return call(functools.partial(prepare_kernel, heads), [shape], scratch, *params, space=IN_HBM)[0]


def early(columns, ring, ways, pieces, gathered, swapped, table):
    length = pieces[0].shape[0] * len(pieces)
    wide, known = gathered.shape
    first = 2 * ring - 3
    depth = known // first
    shapes = [
        ((length + HEADER, wide), jnp.float32),
        ((length, depth * len(ways) - known), jnp.bfloat16),
    ]
    scratch = [pltpu.VMEM((length, known), jnp.bfloat16), pltpu.VMEM((SIDE, known), jnp.bfloat16)]
    kernel = functools.partial(early_kernel, columns, ring, ways, first)
    return call(kernel, shapes, scratch, *pieces, gathered, swapped, table)


def second(columns, partial, rest, up, down, swapped):
    scratch = [pltpu.VMEM((partial.shape[1], 2 * up.shape[1]), jnp.bfloat16), pltpu.SemaphoreType.DMA((2,))]
    operands = (partial, rest, up, down, swapped)
    return call(functools.partial(second_kernel, columns), [(partial.shape, jnp.float32)], scratch, *operands, apart=1)[0]


def mix(heads, count, partial, rest, *others):
    columns = heads * HEAD_DIM
    length = rest.shape[0]
    scratch = [
        ((columns + SIDE, others[0].shape[1]), jnp.bfloat16),
        ((columns // LANES + 1, length + 2 * EDGE, LANES), jnp.float32),
        ((2, length, columns), jnp.bfloat16),
        ((2, length, LANES), jnp.bfloat16),
        ((2, length, LANES), jnp.bfloat16),
        ((2 * length, LANES), jnp.bfloat16),
        ((2, length, columns), jnp.bfloat16),
        ((2, length, columns), jnp.bfloat16),
        ((2, LANES, columns), jnp.float32),
        ((2, length, columns), jnp.float32),
        ((length, columns), jnp.bfloat16),
    ]
    shapes = [((length // count, columns), jnp.bfloat16)] * count
    scratch = [pltpu.VMEM(*one) for one in scratch]
    return call(functools.partial(mixer_kernel, heads), shapes, scratch, partial, rest, *others)


def turn(value, way):
    order = ring_order(lax.axis_size("batch"))
    count = len(order)
    return lax.ppermute(value, ("fsdp", "batch"), [(order[i], order[(i + way) % count]) for i in range(count)])


def turn_across(value, way):
    order = ring_order(lax.axis_size("batch"))
    count = len(order)
    pairs = []
    for s in range(lax.axis_size("seq")):
        pairs += [(s * count + order[i], (s ^ 1) * count + order[(i + way) % count]) for i in range(count)]
    return lax.ppermute(value, ("seq", "fsdp", "batch"), pairs)


def swap(value, axis, mask):
    return lax.ppermute(value, axis, [(i, i ^ mask) for i in range(lax.axis_size(axis))])


def on_heads(hidden, in_weight, read_starts, conv_weight, conv_bias, dt_bias, decay, skip, norm_gain):
    tokens = hidden[0]
    count = lax.axis_size("seq")
    seq = lax.axis_index("seq")
    heads = HEADS // count
    columns = heads * HEAD_DIM
    own, side = pack(in_weight.T, columns)

    ring = lax.axis_size("batch")
    late, _ = lax.optimization_barrier((tokens, own))
    across = swap(late, "seq", 2)
    pieces = [tokens, swap(tokens, "seq", 1), across, swap(across, "seq", 1)]
    table = prepare(heads, (read_starts, conv_weight, conv_bias, dt_bias, decay, skip, norm_gain))
    first = 2 * ring - 3
    ways = [0]
    up = down = own
    for away in range(1, ring):
        before = up, down
        up, down = turn(up, 1), turn(down, -1)
        ways += [-away, away]
        if away == 1:
            beside = table
        elif away == 2:
            gathered, sent = first_gather(columns, (columns + SIDE, first * own.shape[1]), own, side, *before)
            beside = swapped = swap(sent, "seq", 1)
        elif away < ring - 1:
            gathered, sent = next_gather(columns, 2 * away - 3, gathered, swapped, *before)
            beside = swapped = swap(sent, "seq", 1)
        else:
            gathered, sent = next_gather(columns, 2 * away - 3, gathered, swapped, *before)
            swapped = swap(sent, "seq", 1)
            partial, rest = early(columns, ring, tuple(ways) + (ring,), pieces, gathered, swapped, table)
            beside = partial
        up, _ = lax.optimization_barrier((up, beside))
        down, _ = lax.optimization_barrier((down, beside))
    cut = own.shape[0] * 2 // 5 // 16 * 16
    ends = [turn(take(up, cut), 1), turn(down[cut:], -1)]
    sent, crossing = split(columns, up, down)
    far = turn_across(crossing, -1)
    partial = second(columns, partial, rest, up, down, swap(sent, "seq", 1))
    results = mix(heads, count, partial, rest, *ends, far)
    received = [results[0]] + [swap(results[mask], "seq", mask) for mask in range(1, count)]
    mixed = jnp.zeros((tokens.shape[0], INNER), jnp.bfloat16)
    for mask in range(count):
        mixed = lax.dynamic_update_slice(mixed, received[mask], (0, (seq ^ mask) * columns))
    return mixed[None]


def solution(mesh):
    in_specs = (
        P(("fsdp", "batch"), "seq", None),
        P(("fsdp", "batch"), None),
        P(("fsdp", "batch"), None),
        P(),
        P(),
        P(),
        P(),
        P(),
        P(),
    )
    out_specs = P(("fsdp", "batch"), "seq", None)
    by_heads = mesh.shape["seq"] == 4 and mesh.shape["fsdp"] == 2 and mesh.shape["batch"] > 3

    def mixer(hidden, *rest):
        whole = by_heads and hidden.shape[1] == mesh.shape["seq"] * BLOCK
        return jax.shard_map(
            on_heads if whole else on_sections,
            mesh=mesh,
            in_specs=in_specs,
            out_specs=out_specs,
            check_vma=False,
        )(hidden, *rest)

    return mixer
```

```python
import functools

import jax
import jax.numpy as jnp
from jax import lax
from jax.experimental import pallas as pl
from jax.experimental.pallas import tpu as pltpu
from jax.sharding import PartitionSpec as P

HEADS = 32
HEAD_DIM = 64
STATE = 64
KERNEL = 4
BLOCK = 128
INNER = 2048
CONV_CH = 2176


def prefix(value, axis, join, neutral, backward):
    count, mine = (lax.axis_size(axis), lax.axis_index(axis))
    pieces = jax.tree.map(lambda part: lax.all_gather(part, axis), value)
    if backward:
        pieces = jax.tree.map(lambda part: part[::-1], pieces)
        mine = count - 1 - mine
    running = jax.tree.map(
        lambda part, zero: jnp.full_like(part, 0) + jnp.asarray(zero, part.dtype), value, neutral
    )

    def turn(position, running):
        longer = join(running, jax.tree.map(lambda part: part[position], pieces))
        return jax.tree.map(lambda new, old: jnp.where(position < mine, new, old), longer, running)

    return lax.fori_loop(0, count - 1, turn, running)


def extended_2(value, sides, width):
    for axis, dim in sides:
        size, length = (lax.axis_size(axis), value.shape[dim])
        up = [(i, (i + 1) % size) for i in range(size - 1)]
        down = [(j, i) for i, j in up]
        last = lax.slice_in_dim(value, length - width, length, axis=dim)
        initial = lax.slice_in_dim(value, 0, width, axis=dim)
        before = lax.ppermute(last, axis, up)
        after = lax.ppermute(initial, axis, down)
        value = jnp.concatenate([before, value, after], axis=dim)
    return value


def conv_silu(padded, weight, bias):
    length = padded.shape[0] - weight.shape[0] + 1
    total = jnp.broadcast_to(bias[None, :], (length, bias.shape[0]))
    for tap in range(weight.shape[0]):
        total = total + weight[tap][None, :] * padded[tap : tap + length].astype(jnp.float32)
    return jax.nn.silu(total).astype(jnp.bfloat16)


def block_parts(x_part, b_part, c_part, step_size, log_rate, resets):
    length = x_part.shape[0]
    running = jnp.cumsum(log_rate, axis=0)
    running_heads = running.T
    step_heads = step_size.T
    resets_seen = jnp.cumsum(resets)
    scores = jnp.dot(c_part, b_part.T, preferred_element_type=jnp.float32)
    positions = jnp.arange(length)
    allowed = (positions[:, None] >= positions[None, :]) & (
        resets_seen[:, None] == resets_seen[None, :]
    )
    log_gaps = jnp.minimum(running_heads[:, :, None] - running_heads[:, None, :], 0.0)
    weights = (
        jnp.where(allowed[None, :, :], jnp.exp(log_gaps), 0.0)
        * scores[None, :, :]
        * step_heads[:, None, :]
    )
    weights = weights.astype(jnp.bfloat16)
    values = x_part.reshape(length, HEADS, HEAD_DIM)
    inner_part = jnp.einsum("hts,shp->thp", weights, values, preferred_element_type=jnp.float32)
    last_same = resets_seen == resets_seen[-1]
    tail_weight = (
        jnp.where(last_same[:, None], jnp.exp(running[-1][None, :] - running), 0.0) * step_size
    )
    inputs = (tail_weight[:, :, None] * values.astype(jnp.float32)).astype(jnp.bfloat16)
    local_end = jnp.einsum("shp,sn->hpn", inputs, b_part, preferred_element_type=jnp.float32)
    lead_fade = jnp.where((resets_seen == 0)[:, None], jnp.exp(running), 0.0)
    block_fade = jnp.where(resets_seen[-1] == 0, jnp.exp(running[-1]), 0.0)
    return (inner_part, local_end, lead_fade, block_fade)


def chain_combine(earlier, later):
    return (earlier[0] * later[0], later[0][:, None] * earlier[1] + later[1])


def direction(conv_out, step_cols, resets, bias_step, rates, direct, gains, backward):
    length = conv_out.shape[0]
    blocks = length // BLOCK
    x_part = conv_out[:, :INNER]
    b_part = conv_out[:, INNER : INNER + STATE]
    c_part = conv_out[:, INNER + STATE :]
    step_size = jax.nn.softplus(step_cols.astype(jnp.float32) + bias_step[None, :])
    log_rate = -step_size * rates[None, :]
    inner_part, local_end, lead_fade, block_fade = jax.vmap(block_parts)(
        x_part.reshape(blocks, BLOCK, INNER),
        b_part.reshape(blocks, BLOCK, STATE),
        c_part.reshape(blocks, BLOCK, STATE),
        step_size.reshape(blocks, BLOCK, HEADS),
        log_rate.reshape(blocks, BLOCK, HEADS),
        resets.reshape(blocks, BLOCK),
    )
    carried_state = jnp.zeros((HEADS, HEAD_DIM, STATE), jnp.float32)
    carried_fade = jnp.ones((HEADS,), jnp.float32)
    entering = carried_state
    fades_before = carried_fade
    carried_state = block_fade[0][:, None, None] * carried_state + local_end[0]
    carried_fade = block_fade[0] * carried_fade
    summary = (carried_fade, carried_state.reshape(HEADS, HEAD_DIM * STATE))
    identity = (jnp.ones((HEADS,), jnp.float32), jnp.zeros((HEADS, HEAD_DIM * STATE), jnp.float32))
    if backward:
        incoming = prefix(summary, "seq", chain_combine, identity, True)
    else:
        incoming = prefix(summary, "seq", chain_combine, identity, False)
    incoming_state = incoming[1].reshape(HEADS, HEAD_DIM, STATE)
    states = jnp.stack([fades_before[:, None, None] * incoming_state + entering])
    rounded = states.astype(jnp.bfloat16)
    carried = jnp.einsum(
        "btn,bhpn->bthp",
        c_part.reshape(blocks, BLOCK, STATE),
        rounded,
        preferred_element_type=jnp.float32,
    )
    direct_part = direct[None, None, :, None] * x_part.reshape(
        blocks, BLOCK, HEADS, HEAD_DIM
    ).astype(jnp.float32)
    result = (inner_part + lead_fade[..., None] * carried + direct_part).reshape(
        length, HEADS, HEAD_DIM
    )
    scale = lax.rsqrt(jnp.mean(result * result, axis=-1, keepdims=True) + 1e-05)
    return (result * scale * gains.reshape(HEADS, HEAD_DIM)).reshape(length, INNER)


def project(rows_in, in_weight):
    total = jnp.dot(
        rows_in,
        lax.all_gather(in_weight, ("fsdp", "batch"), axis=0, tiled=True),
        preferred_element_type=jnp.float32,
    )
    return total.astype(jnp.bfloat16)


def on_sections(
    hidden, in_weight, read_starts, conv_weight, conv_bias, dt_bias, decay, skip, norm_gain
):
    tokens = hidden[0]
    length = tokens.shape[0]
    margin = KERNEL - 1
    projected = project(tokens, in_weight)
    extended = extended_2(projected[:, :CONV_CH], (("seq", 0),), margin)
    forward_in = conv_silu(extended[: length + margin], conv_weight[0], conv_bias[0])
    backward_in = conv_silu(jnp.flip(extended[margin:], 0), conv_weight[1], conv_bias[1])
    step_cols = projected[:, CONV_CH:]
    positions = lax.axis_index("seq") * length + jnp.arange(length, dtype=jnp.int32)
    marks = read_starts[0]
    starts_here = jnp.any(positions[:, None] == marks[None, :], axis=1).astype(jnp.float32)
    starts_next = jnp.any((positions + 1)[:, None] == marks[None, :], axis=1).astype(jnp.float32)
    forward_out = direction(
        forward_in, step_cols, starts_here, dt_bias[0], decay[0], skip[0], norm_gain[0], False
    )
    backward_out = direction(
        backward_in,
        jnp.flip(step_cols, 0),
        jnp.flip(starts_next, 0),
        dt_bias[1],
        decay[1],
        skip[1],
        norm_gain[1],
        True,
    )
    mixed = forward_out + jnp.flip(backward_out, 0)
    return mixed.astype(jnp.bfloat16)[None]


LANES = 128
SIDE = 256
EDGE = 8
GROUP = 32
HEADER = 16


def ring_order(count):
    return [i if i < count else 3 * count - 1 - i for i in range(2 * count)]


def split_parts(value, count):
    parts = []
    for _ in range(count):
        parts.append(value.astype(jnp.bfloat16))
        value = value - parts[-1].astype(jnp.float32)
    return parts


def lane_row():
    lane = lax.broadcasted_iota(jnp.int32, (BLOCK, LANES), 1)
    row = lax.broadcasted_iota(jnp.int32, (BLOCK, LANES), 0)
    return lane, row


def shard_at(away, ring):
    fsdp, batch = lax.axis_index("fsdp"), lax.axis_index("batch")
    position = jnp.where(fsdp == 0, batch, 2 * ring - 1 - batch)
    there = lax.rem(position + 2 * ring + away, 2 * ring)
    return jnp.where(there < ring, there, 3 * ring - 1 - there)


def take_rows(pieces, ring, ways, rows_in):
    depth = rows_in.shape[1] // len(ways)
    for n, away in enumerate(ways):
        at = pl.ds(pl.multiple_of(shard_at(away, ring) * depth, depth), depth)
        for mask in range(4):
            rows_in[mask * BLOCK : (mask + 1) * BLOCK, n * depth : (n + 1) * depth] = pieces[mask][:, at]


def times_transposed(a, b):
    return lax.dot_general(a, b, (((1,), (1,)), ((), ())), preferred_element_type=jnp.float32)


def pack_kernel(columns, weight_in, own, side, sems):
    seq = lax.axis_index("seq")
    half = side.shape[0]
    few = own.shape[0] - columns - half
    mine = pl.multiple_of(INNER + seq % 2 * half, half)
    other = pl.multiple_of(INNER + (1 - seq % 2) * half, half)
    steps_at = pl.multiple_of(INNER + 2 * half + seq // 2 * few, few)
    copies = [
        (weight_in.at[pl.ds(pl.multiple_of(seq * columns, columns), columns)], own.at[pl.ds(0, columns)]),
        (weight_in.at[pl.ds(mine, half)], own.at[pl.ds(columns, half)]),
        (weight_in.at[pl.ds(steps_at, few)], own.at[pl.ds(columns + half, few)]),
        (weight_in.at[pl.ds(other, half)], side),
    ]
    copies = [pltpu.make_async_copy(a, b, sems.at[i]) for i, (a, b) in enumerate(copies)]
    for copy in copies:
        copy.start()
    for copy in copies:
        copy.wait()


def first_gather_kernel(columns, own, side, up, down, out, sent):
    rows, depth = own.shape
    half = side.shape[0]
    other = columns + LANES
    out[rows:, :] = jnp.zeros((out.shape[0] - rows, out.shape[1]), out.dtype)
    for n, weight in enumerate((own, up, down)):
        out[:rows, n * depth : (n + 1) * depth] = weight[...]
    out[other : other + half, :depth] = side[...]
    sent[:half, :] = up[columns : columns + half, :]
    sent[half:, :] = down[columns : columns + half, :]


def next_gather_kernel(columns, at, held, swapped, up, down, out, sent):
    del held
    rows, depth = up.shape
    half = swapped.shape[0] // 2
    other = columns + LANES
    for n, weight in enumerate((up, down)):
        out[:rows, (at + n) * depth : (at + n + 1) * depth] = weight[...]
        out[other : other + half, (at + n - 2) * depth : (at + n - 1) * depth] = swapped[n * half : (n + 1) * half, :]
    sent[:half, :] = up[columns : columns + half, :]
    sent[half:, :] = down[columns : columns + half, :]


def split_kernel(columns, up, down, sent, crossing):
    half = crossing.shape[0]
    sent[:half, :] = up[columns : columns + half, :]
    sent[half:, :] = down[columns : columns + half, :]
    crossing[...] = down[columns : columns + half, :]


def early_kernel(columns, ring, ways, first, *refs):
    pieces = refs[:4]
    gathered, swapped, table, partial, rest, rows_in, side = refs[4:]
    length = rows_in.shape[0]
    half, depth = swapped.shape[0] // 2, swapped.shape[1]
    take_rows(pieces, ring, ways[:first], rows_in)
    take_rows(pieces, ring, ways[first:], rest)
    for n in range(columns // SIDE):
        at = slice(n * SIDE, (n + 1) * SIDE)
        partial[:length, at] = times_transposed(rows_in[...], gathered[at, :])
    side[...] = gathered[columns:, :]
    for n in range(2):
        side[LANES : LANES + half, (first - 2 + n) * depth : (first - 1 + n) * depth] = swapped[n * half : (n + 1) * half, :]
    partial[:length, columns:] = times_transposed(rows_in[...], side[...])
    other = columns + LANES
    partial[:BLOCK, other:] = partial[:BLOCK, other:] + pltpu.roll(table[HEADER:, :LANES], half, 1)
    partial[length:, : table.shape[1]] = table[:HEADER, :]


def second_kernel(columns, partial, rest, up, down, swapped, out, w_in, sems):
    rows, depth = up.shape
    length = rest.shape[0]
    half = swapped.shape[0] // 2
    other = columns + LANES
    copies = []
    for n in range(2):
        place = w_in.at[pl.ds(other, half), pl.ds(n * depth, depth)]
        copies.append(pltpu.make_async_copy(swapped.at[pl.ds(n * half, half)], place, sems.at[n]))
        copies[-1].start()
    w_in[rows:other, :] = jnp.zeros((other - rows, w_in.shape[1]), jnp.bfloat16)
    w_in[other + half :, :] = jnp.zeros((w_in.shape[0] - other - half, w_in.shape[1]), jnp.bfloat16)
    for n, weight in enumerate((up, down)):
        w_in[:rows, n * depth : (n + 1) * depth] = weight[...]
    for n in range(w_in.shape[0] // SIDE):
        at = slice(n * SIDE, (n + 1) * SIDE)
        if n == columns // SIDE:
            for copy in copies:
                copy.wait()
        out[:length, at] = partial[:length, at] + times_transposed(rest[:, : 2 * depth], w_in[at, :])
    out[length:, :] = partial[length:, :]


def prepare_kernel(heads, *refs):
    marks_in, conv_w_in, conv_b_in, step_bias_in, decay_in, skip_in, gain_in = refs[:7]
    table, conv_w, conv_b, gains, per_head, marks, sems = refs[7:]
    seq = lax.axis_index("seq")
    columns = heads * HEAD_DIM
    own_lanes = pl.ds(pl.multiple_of(seq * columns, columns), columns)
    side_lanes = pl.ds(INNER, LANES)
    copies = [
        (conv_w_in.at[:, :, own_lanes], conv_w.at[:, :, pl.ds(0, columns)]),
        (conv_w_in.at[:, :, side_lanes], conv_w.at[:, :, pl.ds(columns, LANES)]),
        (conv_b_in.at[:, own_lanes], conv_b.at[:, pl.ds(0, columns)]),
        (conv_b_in.at[:, side_lanes], conv_b.at[:, pl.ds(columns, LANES)]),
        (step_bias_in, per_head.at[0]),
        (decay_in, per_head.at[1]),
        (skip_in, per_head.at[2]),
        (gain_in.at[:, own_lanes], gains),
        (marks_in, marks),
    ]
    copies = [pltpu.make_async_copy(a, b, sems.at[i]) for i, (a, b) in enumerate(copies)]
    for copy in copies:
        copy.start()
    for copy in copies:
        copy.wait()

    lane, row = lane_row()
    within = lane % GROUP
    head_lane = within < 2 * heads
    to_first = lax.rem(LANES - seq * heads, LANES)

    def own_heads(k):
        both = jnp.concatenate([per_head[k], jnp.zeros((2, LANES - HEADS), jnp.float32)], axis=1)
        both = pltpu.roll(both, to_first, 1)
        behind = pltpu.roll(both, heads, 1)
        value = jnp.where(lane[:1] < heads, both[0:1, :], behind[1:2, :])
        return jnp.where(lane[:1] < 2 * heads, value, 0.0)

    for d in range(2):
        table[d * KERNEL : (d + 1) * KERNEL, :] = conv_w[d]
    table[8:10, :] = conv_b[...]
    for k in range(2):
        value = jnp.broadcast_to(own_heads(k), (8, LANES))
        value = sum([pltpu.roll(value, g * GROUP, 1) for g in range(1, LANES // GROUP)], value)
        table[10 + k : 11 + k, :LANES] = value[:1]
    direct = packed(jnp.broadcast_to(own_heads(2), (16, LANES)), 3, heads)
    for d in range(2):
        wide = jnp.dot(direct, head_columns(heads, d), preferred_element_type=jnp.float32)
        table[12 + d : 13 + d, :columns] = wide[:1]
    table[14:16, :columns] = gains[...]

    position = row + lane // GROUP * BLOCK
    here = position == marks[:, 0:1]
    after = position + 1 == marks[:, 0:1]
    for m in range(1, marks.shape[1]):
        here = here | (position == marks[:, m : m + 1])
        after = after | (position + 1 == marks[:, m : m + 1])
    forward_start, backward_start = within == 2 * heads, within == 2 * heads + 1
    starts = jnp.where((here & forward_start) | (after & backward_start), 1.0, 0.0).astype(jnp.bfloat16)
    backward_lane = ((within >= heads) & head_lane) | backward_start
    lower = jnp.where(row >= lane, 1.0, 0.0).astype(jnp.bfloat16)
    upper = jnp.where(row <= lane, 1.0, 0.0).astype(jnp.bfloat16)
    ahead = jnp.dot(lower, starts, preferred_element_type=jnp.float32)
    behind = jnp.dot(upper, starts, preferred_element_type=jnp.float32)
    seen = jnp.where(backward_lane, behind, ahead)
    wanted = lane - within + 2 * heads + jnp.where(backward_lane, 1, 0)
    chosen = jnp.where(row == wanted, 1.0, 0.0).astype(jnp.bfloat16)
    seen = jnp.dot(seen.astype(jnp.bfloat16), chosen, preferred_element_type=jnp.float32)
    chosen = (row == lane // 2 * GROUP + lane % 2 * heads) & (lane < 2 * LANES // GROUP)
    chosen = jnp.where(chosen, 1.0, 0.0).astype(jnp.bfloat16)
    table[HEADER:, :LANES] = jnp.dot(seen.astype(jnp.bfloat16), chosen, preferred_element_type=jnp.float32)


def head_columns(heads, d):
    at_row = lax.broadcasted_iota(jnp.int32, (LANES, heads * HEAD_DIM), 0)
    head = lax.broadcasted_iota(jnp.int32, (LANES, heads * HEAD_DIM), 1) // HEAD_DIM + d * heads
    hit = (at_row == head) | (at_row == head + 2 * heads) | (at_row == head + 4 * heads)
    return jnp.where(hit, 1.0, 0.0).astype(jnp.bfloat16)


def packed(value, count, heads):
    parts = split_parts(value, count)
    joined = parts[0].astype(jnp.float32)
    for k in range(1, count):
        joined = joined + pltpu.roll(parts[k].astype(jnp.float32), 2 * heads * k, 1)
    return joined.astype(jnp.bfloat16)


def mixer_kernel(heads, partial, rest, up_end, down_end, far, *refs):
    outs, refs = refs[:4], refs[4:]
    w_end, padded, xs, cs, bs, widen_in, leads, tails, state, ys, mixed = refs
    seq = lax.axis_index("seq")
    columns = heads * HEAD_DIM
    depth = up_end.shape[1]
    cut, rows = up_end.shape[0], up_end.shape[0] + down_end.shape[0]
    chunks = columns // LANES
    length = rest.shape[0]
    blocks = length // BLOCK
    lane, row = lane_row()

    def table(first, last, lanes):
        return partial[length + first : length + last, lanes]

    half = far.shape[0]
    other = columns + LANES
    w_end[:cut, :] = up_end[...]
    w_end[cut:rows, :] = down_end[...]
    w_end[other : other + half, :] = far[...]
    w_end[rows:other, :] = jnp.zeros((other - rows, depth), jnp.bfloat16)
    w_end[other + half :, :] = jnp.zeros((w_end.shape[0] - other - half, depth), jnp.bfloat16)
    edge = jnp.zeros((EDGE, LANES), jnp.float32)
    for c in range(chunks + 1):
        padded[c, 0:EDGE, :] = edge
        padded[c, EDGE + length :, :] = edge
    state[...] = jnp.zeros_like(state)

    places = [pl.multiple_of((seq ^ mask) * BLOCK, BLOCK) for mask in range(4)]

    def project_in(n):
        at = slice(n * SIDE, (n + 1) * SIDE)
        return times_transposed(rest[:, 2 * depth :], w_end[at, :])

    def rounded(value):
        return value.astype(jnp.bfloat16).astype(jnp.float32)

    def keep(c, value):
        for mask in range(4):
            padded[c, pl.ds(EDGE + places[mask], BLOCK), :] = value[mask * BLOCK : (mask + 1) * BLOCK, :]

    side_out = project_in(columns // SIDE)
    mine = rounded(side_out[:, :LANES] + partial[:length, columns:other])
    others = rounded(side_out[:, LANES:] + partial[:length, other:])
    even = jnp.broadcast_to(seq, mine.shape) % 2 == 0
    low, high = jnp.where(even, mine, others), jnp.where(even, others, mine)
    left = lax.broadcasted_iota(jnp.int32, mine.shape, 1) < half
    keep(chunks, jnp.where(left, low, pltpu.roll(high, half, 1)))
    for n in range(columns // SIDE):
        part_out = rounded(project_in(n) + partial[:length, n * SIDE : (n + 1) * SIDE])
        for k in range(SIDE // LANES):
            keep(n * (SIDE // LANES) + k, part_out[:, k * LANES : (k + 1) * LANES])

    within = lane % GROUP
    head_lane = within < 2 * heads
    backward_lane = (within >= heads) & head_lane
    to_first = LANES - half - seq % 2 * heads
    raw = jnp.zeros((BLOCK, LANES), jnp.float32)
    for mask in range(4):
        own_steps = pltpu.roll(mine[mask * BLOCK : (mask + 1) * BLOCK, :], to_first, 1)
        own_steps = jnp.where(lane < heads, own_steps, 0.0)
        raw = raw + pltpu.roll(own_steps + pltpu.roll(own_steps, heads, 1), (seq ^ mask) * GROUP, 1)
    raw = raw + table(10, 11, slice(0, LANES))
    step = jnp.maximum(raw, 0.0) + jnp.log1p(jnp.exp(-jnp.abs(raw)))
    rate = -step * table(11, 12, slice(0, LANES))
    two = jnp.concatenate(split_parts(rate, 2), axis=1)
    lower = jnp.where(row >= lane, 1.0, 0.0).astype(jnp.bfloat16)
    upper = jnp.where(row <= lane, 1.0, 0.0).astype(jnp.bfloat16)
    sums = jnp.dot(jnp.concatenate([lower, upper], axis=0), two, preferred_element_type=jnp.float32)
    sums = sums[:, :LANES] + sums[:, LANES:]
    cum = jnp.where(backward_lane, sums[BLOCK:], sums[:BLOCK])
    last = jnp.where(backward_lane[:1], cum[:1], cum[BLOCK - 1 :])
    chosen = jnp.where(row == lane // GROUP * 2 + jnp.where(backward_lane, 1, 0), 1.0, 0.0).astype(jnp.bfloat16)
    seen = pltpu.roll(partial[:BLOCK, other:], half, 1).astype(jnp.bfloat16)
    seen = jnp.dot(seen, chosen, preferred_element_type=jnp.float32)
    seen_last = jnp.where(backward_lane[:1], seen[:1], seen[BLOCK - 1 :])
    tail = jnp.where(seen == seen_last, jnp.exp(last - cum) * step, 0.0)
    lead = jnp.where(seen == 0.0, jnp.exp(cum), 0.0)
    last, seen_last = jnp.broadcast_to(last, (8, LANES)), jnp.broadcast_to(seen_last, (8, LANES))
    fade = jnp.where(seen_last == 0.0, jnp.exp(last), 0.0)
    seen_turned = seen.T
    spread = [head_columns(heads, d) for d in range(2)]
    shown, step_turned = (-cum).T, step.T
    fades = []
    for b in range(blocks):
        for k, value in enumerate((lead, tail)):
            if b:
                value = pltpu.roll(value, LANES - b * GROUP, 1)
            at = (k * blocks + b) * BLOCK
            widen_in[at : at + BLOCK, :] = jnp.where(lane < 2 * heads, value, 0.0).astype(jnp.bfloat16)
        value = pltpu.roll(fade, LANES - b * GROUP, 1) if b else fade
        fades.append(packed(jnp.where(lane[:8] < 2 * heads, value, 0.0), 2, heads)[:1])
    fades = jnp.concatenate(fades + [jnp.zeros((16 - blocks, LANES), jnp.bfloat16)], axis=0)
    fade_wide = []
    for d in range(2):
        wide = jnp.dot(widen_in[...], spread[d], preferred_element_type=jnp.float32).astype(jnp.bfloat16)
        leads[d] = wide[:length]
        tails[d] = wide[length:]
        fade_wide.append(jnp.dot(fades, spread[d], preferred_element_type=jnp.float32))

    short = 64

    def convolve(c, i):
        at = i * short
        taps = [padded[c, at + EDGE - 3 + k : at + EDGE - 3 + k + short, :] for k in range(7)]
        rows_at = slice(at, at + short)
        lanes = slice(c * LANES, (c + 1) * LANES)
        for d in range(2):
            acc = table(8 + d, 9 + d, lanes)
            for k in range(KERNEL):
                n = d * KERNEL + k
                acc = acc + table(n, n + 1, lanes) * taps[k if d == 0 else 6 - k]
            half = 0.5 * acc
            value = half + half * jnp.tanh(half)
            if c < chunks:
                xs[d, rows_at, lanes] = value.astype(jnp.bfloat16)
            else:
                high = lax.broadcasted_iota(jnp.int32, (short, LANES), 1) >= STATE
                cs[d, rows_at, :] = jnp.where(high, value, 0.0).astype(jnp.bfloat16)
                bs[d, rows_at, :] = jnp.where(high, pltpu.roll(value, STATE, 1), 0.0).astype(jnp.bfloat16)

    group = SIDE // HEAD_DIM
    lane_head = lax.broadcasted_iota(jnp.int32, (BLOCK, SIDE), 1) // HEAD_DIM
    known = {}

    def scan_block(q, d, b):
        at = slice(b * BLOCK, (b + 1) * BLOCK)
        lanes = slice(q * SIDE, (q + 1) * SIDE)
        c_part = cs[d, at, :]
        b_part = bs[d, at, :]
        if (d, b) not in known:
            ordered = (row >= lane) if d == 0 else (row <= lane)
            n = b * GROUP + d * heads
            bar = jnp.where(ordered & (seen[:, n : n + 1] == seen_turned[n : n + 1, :]), 0.0, -1e30)
            known[d, b] = times_transposed(c_part, b_part), bar
        scores, bar = known[d, b]
        before = state[d, :, lanes]
        carried = jnp.dot(c_part, before.astype(jnp.bfloat16), preferred_element_type=jnp.float32)
        x_part = xs[d, at, lanes]
        local_end = lax.dot_general(
            b_part, tails[d, at, lanes] * x_part, (((0,), (0,)), ((), ())), preferred_element_type=jnp.float32
        )
        state[d, :, lanes] = fade_wide[d][b : b + 1, lanes] * before + local_end
        some = []
        for h in range(q * group, (q + 1) * group):
            n = b * GROUP + d * heads + h
            gap = cum[:, n : n + 1] + (shown[n : n + 1, :] + bar)
            some.append((jnp.exp(gap) * scores * step_turned[n : n + 1, :]).astype(jnp.bfloat16))
        none = jnp.zeros_like(x_part)
        spaced = jnp.concatenate([jnp.where(lane_head == h, x_part, none) for h in range(group)], axis=0)
        inner = jnp.dot(jnp.concatenate(some, axis=1), spaced, preferred_element_type=jnp.float32)
        ys[d, at, lanes] = (
            inner
            + leads[d, at, lanes].astype(jnp.float32) * carried
            + table(12 + d, 13 + d, lanes) * x_part.astype(jnp.float32)
        )

    in_group = SIDE // LANES
    for i in range(length // short):
        for c in (chunks, *range(in_group)):
            convolve(c, i)
    for q in range(columns // SIDE):
        for i in range(blocks):
            for d in range(2):
                scan_block(q, d, i if d == 0 else blocks - 1 - i)
            for c in range((q + 1) * in_group, min((q + 2) * in_group, chunks)):
                for part in range(BLOCK // short):
                    convolve(c, i * (BLOCK // short) + part)

    head_row = lax.broadcasted_iota(jnp.int32, (SIDE, SIDE), 0) // HEAD_DIM
    head_col = lax.broadcasted_iota(jnp.int32, (SIDE, SIDE), 1) // HEAD_DIM
    same = jnp.where(head_row == head_col, 1.0 / HEAD_DIM, 0.0).astype(jnp.bfloat16)
    for q in range(columns // SIDE):
        lanes = slice(q * SIDE, (q + 1) * SIDE)
        both = 0.0
        for d in range(2):
            y = ys[d, :, lanes]
            mean = jnp.dot((y * y).astype(jnp.bfloat16), same, preferred_element_type=jnp.float32)
            both = both + y * lax.rsqrt(mean + 1e-05) * table(14 + d, 15 + d, lanes)
        mixed[:, lanes] = both.astype(jnp.bfloat16)
    for mask in range(4):
        outs[mask][...] = mixed[pl.ds(places[mask], BLOCK), :]


IN_VMEM = pl.BlockSpec(memory_space=pltpu.VMEM)
IN_HBM = pl.BlockSpec(memory_space=pltpu.HBM)
ROOM = 24 * 1024 * 1024


def call(kernel, shapes, scratch, *operands, space=IN_VMEM, apart=0, aliases=None):
    shapes = [jax.ShapeDtypeStruct(*one) for one in shapes]
    return pl.pallas_call(
        kernel,
        out_shape=shapes,
        in_specs=[space] * (len(operands) - apart) + [pl.BlockSpec(memory_space=pl.ANY)] * apart,
        out_specs=[IN_VMEM] * len(shapes),
        scratch_shapes=scratch,
        input_output_aliases=aliases or {},
        compiler_params=pltpu.CompilerParams(vmem_limit_bytes=ROOM),
    )(*operands)


def pack(weight, columns):
    depth = weight.shape[1]
    few = 2 * columns // HEAD_DIM
    shapes = [((columns + STATE + few, depth), weight.dtype), ((STATE, depth), weight.dtype)]
    scratch = [pltpu.SemaphoreType.DMA((4,))]
    return call(functools.partial(pack_kernel, columns), shapes, scratch, weight, space=IN_HBM)


def first_gather(columns, shape, own, side, up, down):
    shapes = [(shape, own.dtype), ((2 * side.shape[0], side.shape[1]), own.dtype)]
    return call(functools.partial(first_gather_kernel, columns), shapes, [], own, side, up, down)


def next_gather(columns, at, held, swapped, up, down):
    shapes = [(held.shape, held.dtype), (swapped.shape, held.dtype)]
    kernel = functools.partial(next_gather_kernel, columns, at)
    return call(kernel, shapes, [], held, swapped, up, down, aliases={0: 0})


def take_kernel(value, out):
    out[...] = value[: out.shape[0], :]


def take(value, rows):
    return call(take_kernel, [((rows, value.shape[1]), value.dtype)], [], value)[0]


def split(columns, up, down):
    rows, depth = up.shape
    shapes = [(2 * STATE, depth), (STATE, depth)]
    shapes = [(one, up.dtype) for one in shapes]
    return call(functools.partial(split_kernel, columns), shapes, [], up, down)


def prepare(heads, params):
    columns = heads * HEAD_DIM
    scratch = [
        pltpu.VMEM((2, KERNEL, columns + LANES), jnp.float32),
        pltpu.VMEM((2, columns + LANES), jnp.float32),
        pltpu.VMEM((2, columns), jnp.float32),
        pltpu.VMEM((3, 2, HEADS), jnp.float32),
        pltpu.VMEM(params[0].shape, jnp.int32),
        pltpu.SemaphoreType.DMA((9,)),
    ]
    shape = ((HEADER + BLOCK, columns + LANES), jnp.float32)
    return call(functools.partial(prepare_kernel, heads), [shape], scratch, *params, space=IN_HBM)[0]


def early(columns, ring, ways, pieces, gathered, swapped, table):
    length = pieces[0].shape[0] * len(pieces)
    wide, known = gathered.shape
    first = 2 * ring - 3
    depth = known // first
    shapes = [
        ((length + HEADER, wide), jnp.float32),
        ((length, depth * len(ways) - known), jnp.bfloat16),
    ]
    scratch = [pltpu.VMEM((length, known), jnp.bfloat16), pltpu.VMEM((SIDE, known), jnp.bfloat16)]
    kernel = functools.partial(early_kernel, columns, ring, ways, first)
    return call(kernel, shapes, scratch, *pieces, gathered, swapped, table)


def second(columns, partial, rest, up, down, swapped):
    scratch = [pltpu.VMEM((partial.shape[1], 2 * up.shape[1]), jnp.bfloat16), pltpu.SemaphoreType.DMA((2,))]
    operands = (partial, rest, up, down, swapped)
    return call(functools.partial(second_kernel, columns), [(partial.shape, jnp.float32)], scratch, *operands, apart=1)[0]


def mix(heads, count, partial, rest, *others):
    columns = heads * HEAD_DIM
    length = rest.shape[0]
    scratch = [
        ((columns + SIDE, others[0].shape[1]), jnp.bfloat16),
        ((columns // LANES + 1, length + 2 * EDGE, LANES), jnp.float32),
        ((2, length, columns), jnp.bfloat16),
        ((2, length, LANES), jnp.bfloat16),
        ((2, length, LANES), jnp.bfloat16),
        ((2 * length, LANES), jnp.bfloat16),
        ((2, length, columns), jnp.bfloat16),
        ((2, length, columns), jnp.bfloat16),
        ((2, LANES, columns), jnp.float32),
        ((2, length, columns), jnp.float32),
        ((length, columns), jnp.bfloat16),
    ]
    shapes = [((length // count, columns), jnp.bfloat16)] * count
    scratch = [pltpu.VMEM(*one) for one in scratch]
    return call(functools.partial(mixer_kernel, heads), shapes, scratch, partial, rest, *others)


def turn(value, way):
    order = ring_order(lax.axis_size("batch"))
    count = len(order)
    return lax.ppermute(value, ("fsdp", "batch"), [(order[i], order[(i + way) % count]) for i in range(count)])


def turn_across(value, way):
    order = ring_order(lax.axis_size("batch"))
    count = len(order)
    pairs = []
    for s in range(lax.axis_size("seq")):
        pairs += [(s * count + order[i], (s ^ 1) * count + order[(i + way) % count]) for i in range(count)]
    return lax.ppermute(value, ("seq", "fsdp", "batch"), pairs)


def swap(value, axis, mask):
    return lax.ppermute(value, axis, [(i, i ^ mask) for i in range(lax.axis_size(axis))])


def on_heads(hidden, in_weight, read_starts, conv_weight, conv_bias, dt_bias, decay, skip, norm_gain):
    tokens = hidden[0]
    count = lax.axis_size("seq")
    seq = lax.axis_index("seq")
    heads = HEADS // count
    columns = heads * HEAD_DIM
    own, side = pack(in_weight.T, columns)

    ring = lax.axis_size("batch")
    late, _ = lax.optimization_barrier((tokens, own))
    across = swap(late, "seq", 2)
    hc = swap(tokens, "seq", 1)
    hyc = swap(across, "seq", 1)
    table = prepare(heads, (read_starts, conv_weight, conv_bias, dt_bias, decay, skip, norm_gain))
    first = 2 * ring - 3
    ways = [0]
    up = down = own
    for away in range(1, ring):
        before = up, down
        up, down = turn(up, 1), turn(down, -1)
        ways += [-away, away]
        if away == 1:
            continue
        elif away == 2:
            gathered, sent = first_gather(columns, (columns + SIDE, first * own.shape[1]), own, side, *before)
            beside = swapped = swap(sent, "seq", 1)
        elif away < ring - 1:
            gathered, sent = next_gather(columns, 2 * away - 3, gathered, swapped, *before)
            beside = swapped = swap(sent, "seq", 1)
        else:
            gathered, sent = next_gather(columns, 2 * away - 3, gathered, swapped, *before)
            swapped = swap(sent, "seq", 1)
            pieces = [tokens, hc, across, hyc]
            partial, rest = early(columns, ring, tuple(ways) + (ring,), pieces, gathered, swapped, table)
            beside = partial
        up, _ = lax.optimization_barrier((up, beside))
        down, _ = lax.optimization_barrier((down, beside))
    cut = own.shape[0] * 2 // 5 // 16 * 16
    ends = [turn(take(up, cut), 1), turn(down[cut:], -1)]
    sent, crossing = split(columns, up, down)
    far = turn_across(crossing, -1)
    partial = second(columns, partial, rest, up, down, swap(sent, "seq", 1))
    results = mix(heads, count, partial, rest, *ends, far)
    received = [results[0]] + [swap(results[mask], "seq", mask) for mask in range(1, count)]
    mixed = jnp.zeros((tokens.shape[0], INNER), jnp.bfloat16)
    for mask in range(count):
        mixed = lax.dynamic_update_slice(mixed, received[mask], (0, (seq ^ mask) * columns))
    return mixed[None]


def solution(mesh):
    in_specs = (
        P(("fsdp", "batch"), "seq", None),
        P(("fsdp", "batch"), None),
        P(("fsdp", "batch"), None),
        P(),
        P(),
        P(),
        P(),
        P(),
        P(),
    )
    out_specs = P(("fsdp", "batch"), "seq", None)
    by_heads = mesh.shape["seq"] == 4 and mesh.shape["fsdp"] == 2 and mesh.shape["batch"] > 3

    def mixer(hidden, *rest):
        whole = by_heads and hidden.shape[1] == mesh.shape["seq"] * BLOCK
        return jax.shard_map(
            on_heads if whole else on_sections,
            mesh=mesh,
            in_specs=in_specs,
            out_specs=out_specs,
            check_vma=False,
        )(hidden, *rest)

    return mixer
```
